32 devices in a mesh: seq: 2 (over x), ctx: 4 (over y, core), fsdp: 4 (over z).
Axes of the slice: x: 2, y: 2, z: 4, core: 2. Of those that a mesh axis runs over, the one named last changes fastest.
Arguments:
- tokens: bfloat16 [8, 1024, 2048], P(('seq', 'fsdp'), 'ctx'), may hold values from -6 to 6
- doc_lengths: int32 [8, 8], P(('seq', 'fsdp')), may hold values from 1 to 832, 1024 in all within a row
- keep_mask: int32 [8, 1024], P(('seq', 'fsdp'), 'ctx'), may hold values 0 or 1
- ln_gain: bfloat16 [2, 2048], P(None, ('ctx', 'fsdp')), may hold values from 0.5 to 1.5
- ln_bias: bfloat16 [2, 2048], P(None, ('ctx', 'fsdp')), may hold values from -2 to 2
- qkv_weight: bfloat16 [2, 2048, 6144], P(None, ('ctx', 'fsdp')), may hold values from -0.125 to 0.125
- qkv_bias: bfloat16 [2, 6144], P(None, ('ctx', 'fsdp')), may hold values from -2 to 2
- out_weight: bfloat16 [2, 2048, 2048], P(None, ('ctx', 'fsdp')), may hold values from -0.5 to 0.5
- out_bias: bfloat16 [2, 2048], P(None, ('ctx', 'fsdp')), may hold values from -2 to 2
- up_weight: bfloat16 [2, 2048, 8192], P(None, ('ctx', 'fsdp')), may hold values from -0.125 to 0.125
- up_bias: bfloat16 [2, 8192], P(None, ('ctx', 'fsdp')), may hold values from -2 to 2
- down_weight: bfloat16 [2, 8192, 2048], P(None, ('ctx', 'fsdp')), may hold values from -0.0625 to 0.0625
- down_bias: bfloat16 [2, 2048], P(None, ('ctx', 'fsdp')), may hold values from -2 to 2
- cotangent: bfloat16 [8, 1024, 2048], P(('seq', 'fsdp'), 'ctx'), may hold values from -6 to 6
Outputs:
- result: bfloat16 [8, 1024, 2048], P(('seq', 'fsdp'), 'ctx')
- grad_tokens: float32 [8, 1024, 2048], P(('seq', 'fsdp'), 'ctx')
- grad_ln_gain: float32 [2, 2048], P(None, ('ctx', 'fsdp'))
- grad_ln_bias: float32 [2, 2048], P(None, ('ctx', 'fsdp'))
- grad_qkv_weight: float32 [2, 2048, 6144], P(None, ('ctx', 'fsdp'))
- grad_qkv_bias: float32 [2, 6144], P(None, ('ctx', 'fsdp'))
- grad_out_weight: float32 [2, 2048, 2048], P(None, ('ctx', 'fsdp'))
- grad_out_bias: float32 [2, 2048], P(None, ('ctx', 'fsdp'))
- grad_up_weight: float32 [2, 2048, 8192], P(None, ('ctx', 'fsdp'))
- grad_up_bias: float32 [2, 8192], P(None, ('ctx', 'fsdp'))
- grad_down_weight: float32 [2, 8192, 2048], P(None, ('ctx', 'fsdp'))
- grad_down_bias: float32 [2, 2048], P(None, ('ctx', 'fsdp'))
The draws below stay inside these ranges and needn't reach their ends.
Inputs may be any that keep to these rules, and one draw needn't show every extreme that they name: `doc_lengths`: each row lists the 8 document lengths of one sequence in order; they sum to 1024, and the longest is exactly 832.
All inputs are finite; a program needn't handle non-finite values. No bound on the sum of `keep_mask` on one device may be relied on, other than what follows from the above.
Results may differ from the reference program's by a relative error of at most 0.02.
Values may be sent and summed in bfloat16 or wider, within the bound.
A program may use at most 960 MiB of HBM per device.

```python
import math
import jax
import jax.numpy as jnp
import numpy as np
from jax import lax

D = 2048
HEADS = 32
HEAD_DIM = 64
ROT = 32
FF = 8192
LAYERS = 2
DOCS = 8
SEQS = 8
SEQ_LEN = 1024
LONGEST = 832


def touch_ends(entries, stream_key, low, top_value):
    shape = entries.shape
    spot = [jax.random.randint(jax.random.fold_in(stream_key, axis), (), 0, shape[axis]) for axis in range(len(shape))]
    entries = entries.at[tuple(spot)].set(low)
    longest = shape.index(max(shape))
    spot[longest] = (spot[longest] + 1) % shape[longest]
    return entries.at[tuple(spot)].set(top_value)


def level_of(stream_key, extent, shards, smallest, largest):
    factor_of, own = 1.0, jax.random.fold_in(stream_key, 6)
    for axis_at, parts in shards:
        draws = jnp.exp(jax.random.uniform(jax.random.fold_in(own, axis_at), (parts,), jnp.float32, smallest / len(shards), largest / len(shards)))
        factor_of = factor_of * jnp.repeat(draws, extent[axis_at] // parts).reshape([-1 if axis == axis_at else 1 for axis in range(len(extent))])
    return factor_of


def split_up(amount, total, bound, lean):
    portions = [(1 << 20) // math.isqrt(rank ** lean) + 1 for rank in range(2, amount + 1)]
    rest, given = total - bound - (amount - 1), [1] * (amount - 1)
    while rest > 0:
        candidates = [i for i in range(amount - 1) if given[i] < bound]
        pool, remaining = sum([portions[i] for i in candidates]), rest
        for i in candidates:
            addition = min(bound - given[i], max(1, remaining * portions[i] // pool), rest)
            given[i] = given[i] + addition
            rest = rest - addition
    return np.array([bound] + given)


def ragged(key, number_of, total, most, lean):
    if number_of == 2:
        one = jax.random.randint(key, (), max(1, total - most), min(most, total - 1) + 1)
        return jnp.stack([one, total - one])
    sizes = jnp.asarray(split_up(number_of, total, most, lean), jnp.int32)
    pairs = (number_of - 1) // 2
    source_of, sink = sizes[1:1 + 2 * pairs:2], sizes[2:2 + 2 * pairs:2]
    margin = jnp.minimum(source_of - 1, most - sink)
    shifted = jax.random.randint(jax.random.fold_in(key, 1), (pairs,), 0, 1 << 20) % (margin + 1)
    sizes = sizes.at[1:1 + 2 * pairs:2].set(source_of - shifted).at[2:2 + 2 * pairs:2].set(sink + shifted)
    return sizes[jax.random.permutation(jax.random.fold_in(key, 2), number_of)]


def bell_draw(key, shape, scale, reach, split=(), kind=jnp.bfloat16):
    drawn = jax.random.normal(key, shape, jnp.float32) * scale
    if len(split) > 0:
        drawn = level_of(key, shape, split, -0.22, 0.18) * drawn
    return jnp.clip(drawn, min=-reach, max=reach).astype(kind)


def setup_inputs(seed: int = 0) -> dict:
    arg_keys = jax.random.split(jax.random.key(seed), 15)
    return {
        "tokens": bell_draw(arg_keys[0], (SEQS, SEQ_LEN, D), 1.0, 6.0, ((0, 8), (1, 4))),
        "doc_lengths": jax.vmap(lambda own: ragged(own, DOCS, SEQ_LEN, LONGEST, 2))(jax.random.split(arg_keys[1], SEQS)).reshape((SEQS, DOCS)).astype(jnp.int32),
        "keep_mask": touch_ends((jax.random.randint(arg_keys[2], (SEQS, SEQ_LEN), 0, 8) < 7).astype(jnp.int32), jax.random.fold_in(arg_keys[2], 1), 0, 1),
        "ln_gain": jnp.clip(1.0 + 0.1 * jax.random.normal(arg_keys[3], (LAYERS, D), jnp.float32), 0.5, 1.5).astype(jnp.bfloat16),
        "ln_bias": bell_draw(arg_keys[4], (LAYERS, D), 0.3, 2.0, ((1, 16),)),
        "qkv_weight": bell_draw(arg_keys[5], (LAYERS, D, 3 * D), D ** -0.5, 0.125, ((1, 16),)),
        "qkv_bias": bell_draw(arg_keys[6], (LAYERS, 3 * D), 0.3, 2.0, ((1, 16),)),
        "out_weight": bell_draw(arg_keys[7], (LAYERS, D, D), (D // 16) ** -0.5, 0.5, ((1, 16),)),
        "out_bias": bell_draw(arg_keys[8], (LAYERS, D), 0.3, 2.0, ((1, 16),)),
        "up_weight": bell_draw(arg_keys[9], (LAYERS, D, FF), D ** -0.5, 0.125, ((1, 16),)),
        "up_bias": bell_draw(arg_keys[10], (LAYERS, FF), 0.3, 2.0, ((1, 16),)),
        "down_weight": bell_draw(arg_keys[11], (LAYERS, FF, D), FF ** -0.5, 0.0625, ((1, 16),)),
        "down_bias": bell_draw(arg_keys[12], (LAYERS, D), 0.3, 2.0, ((1, 16),)),
        "cotangent": bell_draw(arg_keys[13], (SEQS, SEQ_LEN, D), 1.0, 6.0, ((0, 8), (1, 4))),
    }


EPS = 1e-05
NEG = -1e+30
HIGH = lax.Precision.HIGHEST

@jax.custom_vjp
def low(v):
    return lax.optimization_barrier(v.astype(jnp.bfloat16)).astype(jnp.float32)

@jax.custom_vjp
def low_back(v):
    return v

def low_keep(v):
    return (low(v), None)

def low_pass(kept, grad):
    return (grad,)

def back_keep(v):
    return (v, None)

def back_low(kept, grad):
    return (low(grad),)
low.defvjp(low_keep, low_pass)
low_back.defvjp(back_keep, back_low)

def place_tokens(lengths):
    bounds = jnp.cumsum(lengths).astype(jnp.int32)
    starts = (bounds - lengths).astype(jnp.int32)
    token_index = jnp.arange(SEQ_LEN, dtype=jnp.int32)
    segment = lax.optimization_barrier(jnp.sum((token_index[:, None] >= bounds[None, :]).astype(jnp.int32), axis=1)).astype(jnp.int32)
    chosen = segment[:, None] == jnp.arange(DOCS, dtype=jnp.int32)[None, :]
    position = (token_index - lax.optimization_barrier(jnp.sum(jnp.where(chosen, starts[None, :], 0), axis=1))).astype(jnp.int32)
    return (token_index, segment, position)

def angles(position):
    indices = jnp.arange(0, ROT, 2, dtype=jnp.float32) / ROT
    inverse = 1.0 / 10000.0 ** indices
    turned = position.astype(jnp.float32)[:, None] * inverse[None, :]
    turned = jnp.concatenate([turned, turned], axis=1)
    return (jnp.cos(turned), jnp.sin(turned))

def rotate(values, cosine, sine):
    rotary = values[..., :ROT]
    middle = ROT // 2
    turned = jnp.concatenate([-rotary[..., middle:], rotary[..., :middle]], axis=-1)
    mixed = rotary * cosine[:, None, :] + turned * sine[:, None, :]
    return jnp.concatenate([mixed, values[..., ROT:]], axis=-1)

def head_attention(query_rows, key_rows, value_rows, allowed):
    scores = low_back(jnp.dot(query_rows, key_rows.T, precision=HIGH) * (1.0 / math.sqrt(HEAD_DIM)))
    masked = jnp.where(allowed, scores, NEG)
    maxima = lax.optimization_barrier(jnp.max(masked, axis=1, keepdims=True))
    weights = jnp.where(allowed, jnp.exp(masked - maxima), 0.0)
    normaliser = lax.optimization_barrier(jnp.sum(weights, axis=1, keepdims=True))
    weighted = low_back(jnp.dot(low(weights), value_rows, precision=HIGH))
    return weighted / normaliser

def layer_forward(hidden, weights, allowed, cosine, sine):
    norm_gain, norm_shift, joint_weight, joint_bias, output_weight, output_bias, upper_weight, upper_bias, lower_weight, lower_bias = weights
    length = hidden.shape[0]
    average = lax.optimization_barrier(jnp.mean(hidden, axis=1, keepdims=True))
    centred = hidden - average
    spread = lax.optimization_barrier(jnp.mean(centred * centred, axis=1, keepdims=True))
    normed = low(centred * lax.rsqrt(spread + EPS) * norm_gain + norm_shift)
    joint = low_back(jnp.dot(normed, joint_weight, precision=HIGH) + joint_bias)
    queries = low(rotate(joint[:, :D].reshape(length, HEADS, HEAD_DIM), cosine, sine))
    keys_all = low(rotate(joint[:, D:2 * D].reshape(length, HEADS, HEAD_DIM), cosine, sine))
    values_all = low(joint[:, 2 * D:].reshape(length, HEADS, HEAD_DIM))

    def one_head(blocks):
        return head_attention(blocks[0], blocks[1], blocks[2], allowed)
    per_head = lax.map(jax.checkpoint(one_head), (queries.transpose(1, 0, 2), keys_all.transpose(1, 0, 2), values_all.transpose(1, 0, 2)))
    mixed = per_head.transpose(1, 0, 2).reshape(length, D)
    attention_out = jnp.dot(low(mixed), output_weight, precision=HIGH) + output_bias
    inner = low_back(jnp.dot(normed, upper_weight, precision=HIGH) + upper_bias)
    activated = low(jax.nn.gelu(inner, approximate=True))
    feed_out = jnp.dot(activated, lower_weight, precision=HIGH) + lower_bias
    return hidden + low_back(attention_out + feed_out)

def one_sequence(hidden, parameters, lengths_row, keep_row):
    token_index, segment, position = place_tokens(lengths_row)
    allowed = (segment[:, None] == segment[None, :]) & (token_index[None, :] <= token_index[:, None]) & ((keep_row[None, :] > 0) | (token_index[:, None] == token_index[None, :]))
    cosine, sine = angles(position)
    for layer_index in range(LAYERS):
        hidden = layer_forward(hidden, tuple((weight[layer_index] for weight in parameters)), allowed, cosine, sine)
    return hidden

def reference(tokens, doc_lengths, keep_mask, ln_gain, ln_bias, qkv_weight, qkv_bias, out_weight, out_bias, up_weight, up_bias, down_weight, down_bias, cotangent):
    parameters = tuple((weight.astype(jnp.float32) for weight in (ln_gain, ln_bias, qkv_weight, qkv_bias, out_weight, out_bias, up_weight, up_bias, down_weight, down_bias)))
    grouped = math.gcd(SEQS, max(1, 4096 // SEQ_LEN))
    blocks = SEQS // grouped
    hiddens = tokens.astype(jnp.float32).reshape(blocks, grouped, SEQ_LEN, D)
    cotangents = (cotangent.astype(jnp.float32) * keep_mask.astype(jnp.float32)[:, :, None]).reshape(blocks, grouped, SEQ_LEN, D)
    lengths = doc_lengths.reshape(blocks, grouped, DOCS)
    keeps = keep_mask.reshape(blocks, grouped, SEQ_LEN)

    def accumulate(totals, record):
        hidden_rows, cotangent_rows, lengths_rows, keep_rows = record

        def forward(states, weights):
            return jax.vmap(one_sequence, in_axes=(0, None, 0, 0))(states, weights, lengths_rows, keep_rows)
        output, pullback = jax.vjp(forward, hidden_rows, parameters)
        grad_hidden, grad_weights = pullback(cotangent_rows)
        totals = tuple((running + update for running, update in zip(totals, grad_weights)))
        return (totals, (output, grad_hidden))
    initial = tuple((jnp.zeros_like(weight) for weight in parameters))
    totals, (outputs, gradients) = lax.scan(accumulate, initial, (hiddens, cotangents, lengths, keeps))
    return (outputs.reshape(SEQS, SEQ_LEN, D).astype(jnp.bfloat16), gradients.reshape(SEQS, SEQ_LEN, D), totals[0], totals[1], totals[2], totals[3], totals[4], totals[5], totals[6], totals[7], totals[8], totals[9])
```

```python
import functools
import math

import jax
import jax.numpy as jnp
import numpy as np
from jax import lax
from jax.experimental import pallas as pl
from jax.experimental.pallas import tpu as pltpu
from jax.sharding import PartitionSpec as P

D = 2048
HEADS = 32
HEAD_DIM = 64
ROT = 32
FF = 8192
LAYERS = 2


EPS = 1e-05
NEG = -1e30


def place_tokens(token_index, lengths):
    bounds = jnp.cumsum(lengths)
    starts = bounds - lengths
    segment = jnp.sum((token_index[:, None] >= bounds[None, :]).astype(jnp.int32), axis=1)
    chosen = segment[:, None] == jnp.arange(lengths.shape[0], dtype=jnp.int32)[None, :]
    position = token_index - jnp.sum(jnp.where(chosen, starts[None, :], 0), axis=1)
    return (segment, position)


def angles(position):
    indices = jnp.arange(0, ROT, 2, dtype=jnp.float32) / ROT
    inverse = 1.0 / 10000.0**indices
    turned = position.astype(jnp.float32)[:, None] * inverse[None, :]
    turned = jnp.concatenate([turned, turned], axis=1)
    return (jnp.cos(turned), jnp.sin(turned))


def rotate(values, cosine, sine):
    rotary = values[..., :ROT]
    middle = ROT // 2
    turned = jnp.concatenate([-rotary[..., middle:], rotary[..., :middle]], axis=-1)
    mixed = rotary * cosine[:, None, :] + turned * sine[:, None, :]
    return jnp.concatenate([mixed, values[..., ROT:]], axis=-1)


def normalize(hidden, gain_row, shift_row):
    average = jnp.mean(hidden, axis=1, keepdims=True)
    centred = hidden - average
    spread = jnp.mean(centred * centred, axis=1, keepdims=True)
    return centred * lax.rsqrt(spread + EPS) * gain_row + shift_row


def block_scores(queries, travelling, start, query_index, query_segment, lengths):
    key_flat, value_flat, key_keep = travelling
    count = key_flat.shape[0]
    key_index = start + jnp.arange(count, dtype=jnp.int32)
    key_segment = place_tokens(key_index, lengths)[0]
    allowed = (
        (query_segment[:, None] == key_segment[None, :])
        & (key_index[None, :] <= query_index[:, None])
        & ((key_keep[None, :] > 0) | (key_index[None, :] == query_index[:, None]))
    )
    key_rows = key_flat.reshape(count, HEADS, HEAD_DIM)
    value_rows = value_flat.reshape(count, HEADS, HEAD_DIM)
    scores = jnp.einsum("qhd,khd->hqk", queries, key_rows, preferred_element_type=jnp.float32) * (
        1.0 / math.sqrt(HEAD_DIM)
    )
    return (scores, allowed, key_rows, value_rows)


def attend(running, travelling, start, queries, query_index, query_segment, lengths):
    maxima, totals, weighted = running
    scores, allowed, key_rows, value_rows = block_scores(
        queries, travelling, start, query_index, query_segment, lengths
    )
    masked = jnp.where(allowed[None], scores, NEG)
    new_max = jnp.maximum(maxima, jnp.max(masked, axis=2))
    probs = jnp.where(allowed[None], jnp.exp(masked - new_max[:, :, None]), 0.0)
    totals = jnp.sum(probs, axis=2)
    weighted = jnp.einsum(
        "hqk,khd->hqd", probs.astype(jnp.bfloat16), value_rows, preferred_element_type=jnp.float32
    )
    return (new_max, totals, weighted)


def attend_back(
    travelling, start, queries, maxima, grad_numer, drift, query_index, query_segment, lengths
):
    scores, allowed, key_rows, value_rows = block_scores(
        queries, travelling, start, query_index, query_segment, lengths
    )
    count = key_rows.shape[0]
    scale = 1.0 / math.sqrt(HEAD_DIM)
    probs = jnp.where(allowed[None], jnp.exp(scores - maxima[:, :, None]), 0.0)
    grad_probs = jnp.einsum(
        "hqd,khd->hqk", grad_numer, value_rows, preferred_element_type=jnp.float32
    )
    grad_scores = (probs * (grad_probs - drift[:, :, None])).astype(jnp.bfloat16)
    grad_query = (
        jnp.einsum("hqk,khd->qhd", grad_scores, key_rows, preferred_element_type=jnp.float32)
        * scale
    )
    grad_key = (
        jnp.einsum("hqk,qhd->khd", grad_scores, queries, preferred_element_type=jnp.float32) * scale
    )
    grad_value = jnp.einsum(
        "hqk,hqd->khd", probs.astype(jnp.bfloat16), grad_numer, preferred_element_type=jnp.float32
    )
    return (
        grad_query,
        grad_key.reshape(count, HEADS * HEAD_DIM),
        grad_value.reshape(count, HEADS * HEAD_DIM),
    )


def attention_forward(queries, key_flat, value_flat, key_keep, query_index, query_segment, lengths):
    row_count = key_flat.shape[0]
    initial = (
        jnp.full((HEADS, row_count), NEG, jnp.float32),
        jnp.zeros((HEADS, row_count), jnp.float32),
        jnp.zeros((HEADS, row_count, HEAD_DIM), jnp.float32),
    )
    return attend(
        initial,
        (
            lax.all_gather(key_flat, "ctx", axis=0, tiled=True),
            lax.all_gather(value_flat, "ctx", axis=0, tiled=True),
            lax.all_gather(key_keep, "ctx", axis=0, tiled=True),
        ),
        jnp.int32(0),
        queries,
        query_index,
        query_segment,
        lengths,
    )


def attention_backward(
    queries,
    key_flat,
    value_flat,
    key_keep,
    maxima,
    grad_numer,
    drift,
    query_index,
    query_segment,
    lengths,
):
    whole = (
        lax.all_gather(key_flat, "ctx", axis=0, tiled=True),
        lax.all_gather(value_flat, "ctx", axis=0, tiled=True),
        lax.all_gather(key_keep, "ctx", axis=0, tiled=True),
    )
    grad_query, every_key, every_value = attend_back(
        whole, 0, queries, maxima, grad_numer, drift, query_index, query_segment, lengths
    )
    grad_key, grad_value = (
        lax.psum_scatter(
            every_key.astype(jnp.bfloat16), "ctx", scatter_dimension=0, tiled=True
        ).astype(jnp.float32),
        lax.psum_scatter(
            every_value.astype(jnp.bfloat16), "ctx", scatter_dimension=0, tiled=True
        ).astype(jnp.float32),
    )
    return (grad_query, grad_key, grad_value)


def layer_forward(hidden, weights, cosine, sine, key_keep, query_index, query_segment, lengths):
    (
        norm_gain,
        norm_shift,
        joint_weight,
        joint_bias,
        output_weight,
        output_bias,
        upper_weight,
        upper_bias,
        lower_weight,
        lower_bias,
    ) = weights
    row_count = hidden.shape[0]
    width = HEADS * HEAD_DIM
    normed = normalize(
        hidden, norm_gain.astype(jnp.float32), norm_shift.astype(jnp.float32)
    ).astype(jnp.bfloat16)
    joint = jnp.dot(normed, joint_weight, preferred_element_type=jnp.float32) + joint_bias.astype(
        jnp.float32
    )
    queries = rotate(joint[:, :width].reshape(row_count, HEADS, HEAD_DIM), cosine, sine).astype(
        jnp.bfloat16
    )
    key_flat = (
        rotate(joint[:, width : 2 * width].reshape(row_count, HEADS, HEAD_DIM), cosine, sine)
        .astype(jnp.bfloat16)
        .reshape(row_count, width)
    )
    value_flat = joint[:, 2 * width :].astype(jnp.bfloat16)
    maxima, totals, weighted = attention_forward(
        queries, key_flat, value_flat, key_keep, query_index, query_segment, lengths
    )
    mixed = (weighted / totals[:, :, None]).transpose(1, 0, 2).reshape(row_count, width)
    attention_out = jnp.dot(
        mixed.astype(jnp.bfloat16), output_weight, preferred_element_type=jnp.float32
    ) + output_bias.astype(jnp.float32)
    inner = jnp.dot(normed, upper_weight, preferred_element_type=jnp.float32) + upper_bias.astype(
        jnp.float32
    )
    activated = jax.nn.gelu(inner, approximate=True).astype(jnp.bfloat16)
    feed_out = jnp.dot(
        activated, lower_weight, preferred_element_type=jnp.float32
    ) + lower_bias.astype(jnp.float32)
    saved = (hidden, normed, queries, key_flat, value_flat, maxima, totals, mixed, inner, activated)
    return (hidden + (attention_out + feed_out), saved)


def layer_backward(
    grad_out, saved, weights, cosine, sine, key_keep, query_index, query_segment, lengths
):
    hidden, normed, queries, key_flat, value_flat, maxima, totals, mixed, inner, activated = saved
    (
        norm_gain,
        norm_shift,
        joint_weight,
        joint_bias,
        output_weight,
        output_bias,
        upper_weight,
        upper_bias,
        lower_weight,
        lower_bias,
    ) = weights
    row_count = hidden.shape[0]
    width = HEADS * HEAD_DIM
    ratio = FF // D
    grad_branch = grad_out.astype(jnp.bfloat16)
    mixed_low = mixed.astype(jnp.bfloat16)
    branch_bias = jnp.sum(grad_branch, axis=0, dtype=jnp.float32)
    grad_activated = jnp.einsum(
        "td,fd->tf", grad_branch, lower_weight, preferred_element_type=jnp.float32
    )
    gelu_pull = jax.vjp(functools.partial(jax.nn.gelu, approximate=True), inner)[1]
    grad_inner = gelu_pull(grad_activated)[0].astype(jnp.bfloat16)
    upper_bias_grad = jnp.sum(grad_inner, axis=0, dtype=jnp.float32)
    grad_normed = jnp.einsum(
        "tf,df->td", grad_inner, upper_weight, preferred_element_type=jnp.float32
    )
    upper_bias_rows = upper_bias_grad.reshape(D, ratio)
    normed_cols = normed
    upper_part = jnp.einsum(
        "tc,tf->cf", normed_cols, grad_inner, preferred_element_type=jnp.float32
    )
    lower_part = jnp.einsum(
        "tc,td->cd", activated, grad_branch, preferred_element_type=jnp.float32
    ).reshape(lax.axis_size(("ctx", "fsdp")) * (D // lax.axis_size(("ctx", "fsdp"))), ratio * width)
    bias_part = upper_bias_rows
    branch_part = branch_bias[:, None]
    feed_share = lax.psum_scatter(
        jnp.concatenate([upper_part, lower_part, bias_part, branch_part], axis=1),
        ("ctx", "fsdp"),
        scatter_dimension=0,
        tiled=True,
    )
    share_rows = feed_share.shape[0]
    upper_share = feed_share[:, :FF]
    lower_share = feed_share[:, FF : FF + ratio * width].reshape(share_rows * ratio, width)
    upper_bias_share = feed_share[:, FF + ratio * width : FF + ratio * width + ratio].reshape(
        share_rows * ratio
    )
    branch_share = feed_share[:, FF + ratio * width + ratio]
    feed_parts = (upper_share, upper_bias_share, lower_share, branch_share)
    output_share = None
    grad_mixed = jnp.einsum(
        "te,de->td", grad_branch, output_weight, preferred_element_type=jnp.float32
    )
    head_mixed = mixed.reshape(row_count, HEADS, HEAD_DIM).transpose(1, 0, 2)
    head_grad = grad_mixed.reshape(row_count, HEADS, HEAD_DIM).transpose(1, 0, 2)
    drift = jnp.sum(head_grad * head_mixed, axis=2) / totals
    grad_numer = (head_grad / totals[:, :, None]).astype(jnp.bfloat16)
    grad_query, grad_key, grad_value = attention_backward(
        queries,
        key_flat,
        value_flat,
        key_keep,
        maxima,
        grad_numer,
        drift,
        query_index,
        query_segment,
        lengths,
    )
    grad_query = rotate(grad_query, cosine, -sine).reshape(row_count, width)
    grad_key = rotate(grad_key.reshape(row_count, HEADS, HEAD_DIM), cosine, -sine).reshape(
        row_count, width
    )
    grad_joint = jnp.concatenate([grad_query, grad_key, grad_value], axis=1).astype(jnp.bfloat16)
    joint_bias_grad = jnp.sum(grad_joint, axis=0, dtype=jnp.float32)
    grad_normed = grad_normed + jnp.einsum(
        "te,de->td", grad_joint, joint_weight, preferred_element_type=jnp.float32
    )
    norm_pull = jax.vjp(
        normalize, hidden, norm_gain.astype(jnp.float32), norm_shift.astype(jnp.float32)
    )[1]
    grad_hidden, gain_grad, shift_grad = norm_pull(grad_normed)
    joint_bias_rows = joint_bias_grad.reshape(D, 3)
    normed_cols = normed
    joint_part = jnp.einsum(
        "tc,te->ce", normed_cols, grad_joint, preferred_element_type=jnp.float32
    )
    output_part = jnp.einsum(
        "tc,te->ce", mixed_low, grad_branch, preferred_element_type=jnp.float32
    )
    bias_part = joint_bias_rows
    gain_part = gain_grad[:, None]
    shift_part = shift_grad[:, None]
    attn_share = lax.psum_scatter(
        jnp.concatenate([joint_part, output_part, bias_part, gain_part, shift_part], axis=1),
        ("ctx", "fsdp"),
        scatter_dimension=0,
        tiled=True,
    )
    share_rows = attn_share.shape[0]
    joint_share = attn_share[:, : 3 * width]
    output_share = attn_share[:, 3 * width : 4 * width]
    joint_bias_share = attn_share[:, 4 * width : 4 * width + 3].reshape(share_rows * 3)
    gain_share = attn_share[:, 4 * width + 3]
    shift_share = attn_share[:, 4 * width + 4]
    attention_parts = (gain_share, shift_share, joint_share, joint_bias_share, output_share)
    return (grad_out + grad_hidden, attention_parts, feed_parts)


def on_device_gathered(
    tokens,
    doc_lengths,
    keep_mask,
    ln_gain,
    ln_bias,
    qkv_weight,
    qkv_bias,
    out_weight,
    out_bias,
    up_weight,
    up_bias,
    down_weight,
    down_bias,
    cotangent,
):
    row_count = tokens.shape[1]
    position = lax.axis_index("ctx")
    query_index = position * row_count + jnp.arange(row_count, dtype=jnp.int32)
    lengths = doc_lengths[0]
    query_segment, query_position = place_tokens(query_index, lengths)
    cosine, sine = angles(query_position)
    key_keep = keep_mask[0].astype(jnp.bfloat16)
    shards = (
        ln_gain,
        ln_bias,
        qkv_weight,
        qkv_bias,
        out_weight,
        out_bias,
        up_weight,
        up_bias,
        down_weight,
        down_bias,
    )

    def fetch(layer_index):
        return (
            lax.all_gather(shards[0][layer_index], ("ctx", "fsdp"), axis=0, tiled=True),
            lax.all_gather(shards[1][layer_index], ("ctx", "fsdp"), axis=0, tiled=True),
            lax.all_gather(shards[2][layer_index], ("ctx", "fsdp"), axis=0, tiled=True),
            lax.all_gather(shards[3][layer_index], ("ctx", "fsdp"), axis=0, tiled=True),
            lax.all_gather(shards[4][layer_index], ("ctx", "fsdp"), axis=0, tiled=True),
            lax.all_gather(shards[5][layer_index], ("ctx", "fsdp"), axis=0, tiled=True),
            lax.all_gather(shards[6][layer_index], ("ctx", "fsdp"), axis=0, tiled=True),
            lax.all_gather(shards[7][layer_index], ("ctx", "fsdp"), axis=0, tiled=True),
            lax.all_gather(shards[8][layer_index], ("ctx", "fsdp"), axis=0, tiled=True),
            lax.all_gather(shards[9][layer_index], ("ctx", "fsdp"), axis=0, tiled=True),
        )

    hidden = tokens[0].astype(jnp.float32)
    saved_layers = []
    weights = None
    for layer_index in range(LAYERS):
        weights = fetch(layer_index)
        hidden, saved = layer_forward(
            hidden, weights, cosine, sine, key_keep, query_index, query_segment, lengths
        )
        saved_layers.append(saved)
    result = hidden.astype(jnp.bfloat16)[None]
    grad_hidden = cotangent[0].astype(jnp.float32) * keep_mask[0].astype(jnp.float32)[:, None]
    attention_list = [None] * LAYERS
    feed_list = [None] * LAYERS
    for layer_index in reversed(range(LAYERS)):
        weights = weights if layer_index == LAYERS - 1 else fetch(layer_index)
        grad_hidden, attention_parts, feed_parts = layer_backward(
            grad_hidden,
            saved_layers[layer_index],
            weights,
            cosine,
            sine,
            key_keep,
            query_index,
            query_segment,
            lengths,
        )
        attention_list[layer_index] = attention_parts
        feed_list[layer_index] = feed_parts
    gain_stack = jnp.stack([attention_list[layer_index][0] for layer_index in range(LAYERS)])
    shift_stack = jnp.stack([attention_list[layer_index][1] for layer_index in range(LAYERS)])
    joint_stack = jnp.stack([attention_list[layer_index][2] for layer_index in range(LAYERS)])
    joint_bias_stack = jnp.stack([attention_list[layer_index][3] for layer_index in range(LAYERS)])
    output_stack = jnp.stack([attention_list[layer_index][4] for layer_index in range(LAYERS)])
    upper_stack = jnp.stack([feed_list[layer_index][0] for layer_index in range(LAYERS)])
    upper_bias_stack = jnp.stack([feed_list[layer_index][1] for layer_index in range(LAYERS)])
    lower_stack = jnp.stack([feed_list[layer_index][2] for layer_index in range(LAYERS)])
    branch_stack = jnp.stack([feed_list[layer_index][3] for layer_index in range(LAYERS)])
    summed = (
        lax.psum(gain_stack.astype(jnp.bfloat16), "seq").astype(jnp.float32),
        lax.psum(shift_stack.astype(jnp.bfloat16), "seq").astype(jnp.float32),
        lax.psum(joint_stack.astype(jnp.bfloat16), "seq").astype(jnp.float32),
        lax.psum(joint_bias_stack.astype(jnp.bfloat16), "seq").astype(jnp.float32),
        lax.psum(output_stack.astype(jnp.bfloat16), "seq").astype(jnp.float32),
        lax.psum(upper_stack.astype(jnp.bfloat16), "seq").astype(jnp.float32),
        lax.psum(upper_bias_stack.astype(jnp.bfloat16), "seq").astype(jnp.float32),
        lax.psum(lower_stack.astype(jnp.bfloat16), "seq").astype(jnp.float32),
        lax.psum(branch_stack.astype(jnp.bfloat16), "seq").astype(jnp.float32),
    )
    return (
        result,
        grad_hidden[None],
        summed[0],
        summed[1],
        summed[2],
        summed[3],
        summed[4],
        summed[8],
        summed[5],
        summed[6],
        summed[7],
        summed[8],
    )


SIDE = 4
GROUP = SIDE * SIDE
OWN = HEADS // GROUP
HEAD_COLS = OWN * HEAD_DIM
JOINT_COLS = 3 * HEAD_COLS
FEED_COLS = FF // GROUP
COLS = JOINT_COLS + FEED_COLS
BACK_COLS = HEAD_COLS + FEED_COLS
SHARE = D // GROUP
VMEM = pl.BlockSpec(memory_space=pltpu.VMEM)
HBM = pl.BlockSpec(memory_space=pl.ANY)
MESH = pl.DeviceIdType.MESH
ROOM = 60 * 2**20


def dot(left, right, left_dim=1, right_dim=0):
    return lax.dot_general(
        left, right, (((left_dim,), (right_dim,)), ((), ())), preferred_element_type=jnp.float32
    )


def digit(entries, index):
    words = [
        sum(entry << (2 * place) for place, entry in enumerate(entries[start : start + 8]))
        for start in range(0, len(entries), 8)
    ]
    word = jnp.int32(words[0])
    for number in range(1, len(words)):
        word = jnp.where(index >= 8 * number, jnp.int32(words[number]), word)
    return lax.rem(lax.shift_right_logical(word, 2 * lax.rem(index, 8)), 4)


def digit_of_row(table, row, index):
    value = digit(table[0], index)
    for number in range(1, len(table)):
        value = jnp.where(row == number, digit(table[number], index), value)
    return value


NEAR = ((0, 1, 2, 3), (1, 0, 2, 3), (2, 3, 1, 0), (3, 2, 1, 0))
FAR = ((3, 2, 1, 0), (3, 0, 2, 1), (0, 3, 1, 2), (0, 1, 2, 3))


def neighbours():
    ctx, place = lax.axis_index("ctx"), lax.axis_index("fsdp")
    twin = ctx + 1 - 2 * lax.rem(ctx, 2)
    across = lax.rem(ctx + 2, 4)
    return ctx, place, twin, across, lax.rem(twin + 2, 4)


def greet_neighbours():
    ctx, place, twin, across, _ = neighbours()
    barrier = pltpu.get_barrier_semaphore()
    pl.semaphore_signal(barrier, inc=1, device_id={"ctx": twin}, device_id_type=MESH)
    pl.semaphore_signal(barrier, inc=1, device_id={"ctx": across}, device_id_type=MESH)

    @pl.when(place > 0)
    def _():
        pl.semaphore_signal(barrier, inc=1, device_id={"fsdp": place - 1}, device_id_type=MESH)

    @pl.when(place < SIDE - 1)
    def _():
        pl.semaphore_signal(barrier, inc=1, device_id={"fsdp": place + 1}, device_id_type=MESH)

    inner = jnp.int32(2) + jnp.where(place > 0, 1, 0) + jnp.where(place < SIDE - 1, 1, 0)
    pl.semaphore_wait(barrier, inner)


def greet_plane(steps, cross=True):
    ctx, place = lax.axis_index("ctx"), lax.axis_index("fsdp")
    me = ctx * SIDE + place
    barrier = pltpu.get_barrier_semaphore()
    for step in range(1, steps):
        peer = lax.rem(me + step, GROUP)
        pl.semaphore_signal(
            barrier,
            inc=1,
            device_id={"ctx": peer // SIDE, "fsdp": lax.rem(peer, SIDE)},
            device_id_type=MESH,
        )
    if cross:
        pl.semaphore_signal(
            barrier, inc=1, device_id={"seq": 1 - lax.axis_index("seq")}, device_id_type=MESH
        )
    pl.semaphore_wait(barrier, steps if cross else steps - 1)


def to_peer(source, target, send, recv, peer):
    return pltpu.make_async_remote_copy(
        src_ref=source,
        dst_ref=target,
        send_sem=send,
        recv_sem=recv,
        device_id={"ctx": peer // SIDE, "fsdp": lax.rem(peer, SIDE)},
        device_id_type=MESH,
    )


def to_axis(source, target, send, recv, axis, index):
    return pltpu.make_async_remote_copy(
        src_ref=source,
        dst_ref=target,
        send_sem=send,
        recv_sem=recv,
        device_id={axis: index},
        device_id_type=MESH,
    )


PARTS = ((0, 112), (112, 96), (208, 48))
LAST = len(PARTS) - 1
GATHER_KIND = (
    (0, 0, 0, 0, 0, 1, 0, 0, 1, 0, 2, 0, 1, 1, 1, 2, 0, 0, 1, 0, 1, 3, 2, 1, 0, 3, 1, 1, 1, 1, 0, 3, 0, 0, 1, 1, 1, 1, 2, 3),
    (0, 0, 0, 1, 0, 0, 0, 0, 0, 0, 0, 0, 1, 0, 2, 1, 2, 1, 0, 1, 1, 2, 0, 3, 1, 1, 0, 1, 1, 1, 3, 1, 1, 0, 1, 3, 1, 1, 2, 3),
)
GATHER_STEP = (
    (0, 0, 1, 0, 0, 0, 1, 1, 0, 1, 0, 2, 0, 0, 1, 1, 2, 2, 1, 2, 1, 0, 2, 1, 3, 1, 2, 2, 2, 2, 3, 2, 3, 3, 3, 3, 3, 3, 3, 3),
    (0, 0, 0, 0, 2, 2, 1, 0, 1, 2, 1, 1, 0, 2, 0, 0, 2, 0, 3, 2, 2, 1, 3, 0, 2, 1, 3, 1, 2, 1, 2, 3, 1, 3, 3, 1, 3, 3, 3, 3),
)
GATHER_PART = (
    (1, 0, 1, 2, 3, 1, 2, 0, 0, 3, 3, 2, 2, 3, 0, 3, 1, 0, 1, 3, 2, 3, 3, 3, 0, 3, 1, 2, 0, 3, 1, 3, 2, 3, 1, 0, 2, 3, 3, 3),
    (1, 0, 2, 0, 2, 0, 2, 3, 1, 1, 0, 3, 2, 3, 3, 1, 3, 3, 0, 0, 2, 3, 1, 3, 1, 1, 2, 2, 3, 0, 3, 2, 3, 3, 0, 3, 1, 3, 3, 3),
)
OPS = len(GATHER_KIND[0])
WORKS = tuple(
    tuple(
        number for number in range(OPS) if parts[number] == 3
    )
    for parts in GATHER_PART
)


def by_place(tables, index):
    place = lax.axis_index("fsdp")
    at_end = (place == 0) | (place == SIDE - 1)
    return jnp.where(at_end, digit(tables[0], index), digit(tables[1], index))


def gather_slot(kind, step):
    ctx, place, twin, across, twin_across = neighbours()
    line = digit_of_row(NEAR, place, step)
    owner = jnp.where(
        kind == 0, ctx, jnp.where(kind == 1, across, jnp.where(kind == 2, twin, twin_across))
    )
    return line, owner * SIDE + line


def work_slot(number):
    kind = by_place(
        tuple(tuple(row[at] for at in places) for row, places in zip(GATHER_KIND, WORKS)), number
    )
    step = by_place(
        tuple(tuple(row[at] for at in places) for row, places in zip(GATHER_STEP, WORKS)), number
    )
    return gather_slot(kind, step)[1]


def gather_blocks(land, every, up, down, side, core, arrived, core_arrived, kept, work):
    ctx, place, twin, across, _ = neighbours()

    def copies(kind, line, slot, part):
        start, size = PARTS[part]
        block = land.at[slot, pl.ds(start, size)]
        row, met = kind * SIDE + line, arrived.at[slot, part]
        return (
            lambda: to_axis(block, block, up.at[row, part], met, "fsdp", place + 1),
            lambda: to_axis(block, block, down.at[row, part], met, "fsdp", place - 1),
            lambda: to_axis(block, block, side.at[line, part], met, "ctx", across),
        )

    def routes(kind, line, part):
        goes_up = (line <= place) & (place < SIDE - 1)
        goes_down = (line >= place) & (place > 0)
        if part == LAST:
            return goes_up, goes_down, (kind == 0) & (line == place)
        return goes_up & (kind == 0), goes_down & (kind == 0), kind == 0

    def core_copy(kind, line, slot):
        block = land.at[slot]
        return to_axis(
            block, block, core.at[kind * SIDE + line], core_arrived.at[slot], "ctx", twin
        )

    def step_op(number, worked):
        kind, step = by_place(GATHER_KIND, number), by_place(GATHER_STEP, number)
        part = by_place(GATHER_PART, number)
        line, slot = gather_slot(kind, step)
        for which in range(len(PARTS)):

            @pl.when(part == which)
            def _(which=which):
                @pl.when((kind == 1) | (line != place))
                def _():
                    copies(kind, line, slot, which)[2]().wait_recv()

                for copy, goes in zip(
                    copies(kind, line, slot, which), routes(kind, line, which)
                ):

                    @pl.when(goes)
                    def _(copy=copy):
                        copy().start()

        @pl.when(part == 3)
        def _():
            @pl.when(kind <= 1)
            def _():
                core_copy(kind, line, slot).start()

            @pl.when(kind >= 2)
            def _():
                core_copy(kind - 2, line, slot).wait_recv()

            if every is not None:
                pltpu.make_async_copy(land.at[slot], every.at[slot], kept.at[slot]).start()
            work(worked, slot)

        return worked + jnp.where(part == 3, 1, 0)

    lax.fori_loop(0, OPS, step_op, jnp.int32(0))

    def finish(number, carry):
        kind, line = number // SIDE, lax.rem(number, SIDE)
        slot = jnp.where(kind == 0, ctx, across) * SIDE + line
        for which in range(len(PARTS)):
            for copy, goes in zip(copies(kind, line, slot, which), routes(kind, line, which)):

                @pl.when(goes)
                def _(copy=copy):
                    copy().wait_send()

        core_copy(kind, line, slot).wait_send()
        return carry

    lax.fori_loop(0, 2 * SIDE, finish, 0)

    def finish_kept(slot, carry):
        pltpu.make_async_copy(land.at[slot], every.at[slot], kept.at[slot]).wait()
        return carry

    if every is not None:
        lax.fori_loop(0, GROUP, finish_kept, 0)


def gather_scratch(rows):
    parts = len(PARTS)
    return [
        pltpu.VMEM((GROUP, rows, D), jnp.bfloat16),
        pltpu.SemaphoreType.DMA((2 * SIDE, parts)),
        pltpu.SemaphoreType.DMA((2 * SIDE, parts)),
        pltpu.SemaphoreType.DMA((SIDE, parts)),
        pltpu.SemaphoreType.DMA((2 * SIDE,)),
        pltpu.SemaphoreType.DMA((GROUP, parts)),
        pltpu.SemaphoreType.DMA((GROUP,)),
        pltpu.SemaphoreType.DMA((GROUP,)),
    ]


def spin(values, cosine, sine, sign):
    lane = lax.rem(lax.broadcasted_iota(jnp.int32, values.shape, 1), HEAD_DIM)
    partner = jnp.where(
        lane < ROT // 2,
        -pltpu.roll(values, HEAD_COLS - ROT // 2, 1),
        pltpu.roll(values, ROT // 2, 1),
    )
    return values * cosine + sign * (partner * sine)


STRIP = 32


def each_strip(rows, body, start):
    def step(number, carry):
        return body(pl.ds(pl.multiple_of(number * STRIP, STRIP), STRIP), carry)

    return lax.fori_loop(0, rows // STRIP, step, start)


def column_places(block):
    return [
        (0, pl.multiple_of(part * D + block * HEAD_COLS, HEAD_COLS), part * HEAD_COLS, HEAD_COLS)
        for part in range(3)
    ] + [(1, pl.multiple_of(block * FEED_COLS, FEED_COLS), JOINT_COLS, FEED_COLS)]


PLACES = 4


def forward_gather(hidden, gain, shift, bias, turns, sources, layer):
    rows = hidden.shape[0]
    half = SHARE // 2
    first = layer == 0

    def kernel(hidden, gain, shift, bias, turn_a, turn_b, source_a, source_b, *refs):
        every, columns_out, query, key, value, inner, active = refs[:7]
        refs = refs[7:]
        if first:
            cosine, sine = refs[:2]
            refs = refs[2:]
        else:
            cosine, sine = turn_a, turn_b
        columns, plane_send, plane_recv, cross_send, cross_recv, own_sem, saved = refs[:7]
        land = refs[7]
        ctx, place, seq = lax.axis_index("ctx"), lax.axis_index("fsdp"), lax.axis_index("seq")
        me = ctx * SIDE + place
        part_rows = pl.ds(pl.multiple_of(seq * half, half), half)
        other_rows = pl.ds(pl.multiple_of((1 - seq) * half, half), half)
        if first:
            greet_plane(GROUP)
        else:
            greet_neighbours()
        sources = (source_a, source_b)
        halves = ()
        if not first:
            halves = (
                pltpu.make_async_copy(source_a, columns.at[:, part_rows], own_sem.at[0]),
                pltpu.make_async_copy(source_b, columns.at[:, other_rows], own_sem.at[1]),
            )

        def piece(step, number):
            peer = lax.rem(me + step, GROUP)
            which, start, at, width = column_places(peer)[number]
            return (
                peer,
                sources[which].at[layer, part_rows, pl.ds(start, width)],
                columns.at[me, part_rows, pl.ds(at, width)],
            )

        def send_piece(step, number):
            peer, source, target = piece(step, number)
            return to_peer(
                source, target, plane_send.at[step, number], plane_recv.at[me, number], peer
            )

        def own_piece(number):
            _, source, target = piece(0, number)
            return pltpu.make_async_copy(source, target, own_sem.at[number])

        def cross(source):
            block = columns.at[source, part_rows]
            return to_axis(
                block, block, cross_send.at[source], cross_recv.at[source], "seq", 1 - seq
            )

        if first:
            for number in range(PLACES):
                own_piece(number).start()
        else:
            for copy in halves:
                copy.start()

        def send_columns(step, carry):
            for number in range(PLACES):
                send_piece(step, number).start()
            return carry

        def strip(part, carry):
            values = hidden[part].astype(jnp.float32)
            centred = values - jnp.mean(values, axis=1, keepdims=True)
            spread = jnp.mean(centred * centred, axis=1, keepdims=True)
            normed = centred * lax.rsqrt(spread + EPS) * gain[...] + shift[...]
            land[me, part] = normed.astype(jnp.bfloat16)
            return carry

        each_strip(rows, strip, 0)

        def pass_on(step):
            source = lax.rem(me + GROUP - step, GROUP)

            @pl.when(step == 0)
            def _():
                for number in range(PLACES):
                    own_piece(number).wait()

            @pl.when(step > 0)
            def _():
                for number in range(PLACES):
                    _, _, at, width = column_places(0)[number]
                    target = columns.at[source, part_rows, pl.ds(at, width)]
                    to_peer(
                        target, target, plane_send.at[0, number], plane_recv.at[source, number], source
                    ).wait_recv()

            cross(source).start()

        def product(slot):
            whole = dot(land[slot], columns[...].reshape(D, COLS)) + bias[...]
            one, two = HEAD_COLS, 2 * HEAD_COLS
            query[slot] = spin(whole[:, :one], cosine[slot], sine[slot], 1.0).astype(jnp.bfloat16)
            key[slot] = spin(whole[:, one:two], cosine[slot], sine[slot], 1.0).astype(jnp.bfloat16)
            value[slot] = whole[:, two:JOINT_COLS].astype(jnp.bfloat16)
            units = whole[:, JOINT_COLS:]
            inner[slot] = units
            active[slot] = jax.nn.gelu(units, approximate=True).astype(jnp.bfloat16)

        save = pltpu.make_async_copy(columns, columns_out, saved)

        def work_as_columns_come(number, slot):
            @pl.when(number == 0)
            def _():
                lax.fori_loop(1, GROUP, send_columns, 0)

            angle = turn_a[slot] * turn_b[...]
            cosine[slot] = jnp.cos(angle)
            sine[slot] = jnp.sin(angle)

            @pl.when(number < GROUP // 2)
            def _():
                pass_on(2 * number)
                pass_on(2 * number + 1)

            @pl.when(number == GROUP // 2)
            def _():
                def arrive(source, carry):
                    block = columns.at[source, part_rows]
                    to_axis(
                        block, block, cross_send.at[source], cross_recv.at[source], "seq", 1 - seq
                    ).wait_recv()
                    return carry

                lax.fori_loop(0, GROUP, arrive, 0)
                save.start()

            @pl.when(number >= GROUP // 2)
            def _():
                def two_products(more, carry):
                    product(work_slot(2 * number - GROUP + more))
                    return carry

                lax.fori_loop(0, 2, two_products, 0)

        def work(number, slot):
            @pl.when(number == 0)
            def _():
                for copy in halves:
                    copy.wait()
                save.start()

            product(slot)

        gather_blocks(land, every, *refs[8:], work_as_columns_come if first else work)
        save.wait()

        def end(step, carry):
            cross(step).wait_send()

            @pl.when(step > 0)
            def _():
                for number in range(PLACES):
                    send_piece(step, number).wait_send()

            return carry

        if first:
            lax.fori_loop(0, GROUP, end, 0)

    def out(width, dtype):
        return jax.ShapeDtypeStruct((GROUP, rows, width), dtype)

    out_shape = [
        out(D, jnp.bfloat16),
        jax.ShapeDtypeStruct((GROUP, SHARE, COLS), jnp.bfloat16),
        out(HEAD_COLS, jnp.bfloat16),
        out(HEAD_COLS, jnp.bfloat16),
        out(HEAD_COLS, jnp.bfloat16),
        out(FEED_COLS, jnp.float32),
        out(FEED_COLS, jnp.bfloat16),
    ] + [out(HEAD_COLS, jnp.float32)] * (2 if first else 0)
    return pl.pallas_call(
        kernel,
        out_shape=out_shape,
        in_specs=[VMEM] * 6 + [HBM] * 2,
        out_specs=[HBM, HBM] + [VMEM] * (len(out_shape) - 2),
        scratch_shapes=[
            pltpu.VMEM((GROUP, SHARE, COLS), jnp.bfloat16),
            pltpu.SemaphoreType.DMA((GROUP, PLACES)),
            pltpu.SemaphoreType.DMA((GROUP, PLACES)),
            pltpu.SemaphoreType.DMA((GROUP,)),
            pltpu.SemaphoreType.DMA((GROUP,)),
            pltpu.SemaphoreType.DMA((PLACES,)),
            pltpu.SemaphoreType.DMA,
        ]
        + gather_scratch(rows),
        compiler_params=pltpu.CompilerParams(
            collective_id=30 + layer, has_side_effects=True, vmem_limit_bytes=ROOM
        ),
    )(hidden, gain, shift, bias, *turns, *sources)


def backward_gather(grad, out_weight, down_weight, inner, mixed, active):
    rows = grad.shape[0]

    def kernel(
        own,
        out_weight,
        down_weight,
        inner,
        mixed,
        active,
        grad_mixed,
        grad_inner,
        branch,
        total,
        land,
        *sems,
    ):
        ctx, place, _, _, _ = neighbours()
        greet_neighbours()
        land[ctx * SIDE + place] = own[...]
        total[...] = jnp.zeros_like(total)

        def work(number, slot):
            block = land[slot]
            grad_mixed[slot] = dot(block, out_weight[...], 1, 1)
            value = inner[slot]
            factor = math.sqrt(2.0 / math.pi)
            square = value * value
            bend = jnp.tanh(factor * value * (1.0 + 0.044715 * square))
            slope = 0.5 * (1.0 + bend) + 0.5 * value * (1.0 - bend * bend) * (
                factor * (1.0 + 3 * 0.044715 * square)
            )
            grad_inner[slot] = (dot(block, down_weight[...], 1, 1) * slope).astype(jnp.bfloat16)
            total[:HEAD_COLS] += dot(mixed[slot], block, 0, 0)
            total[HEAD_COLS:] += dot(active[slot], block, 0, 0)

        gather_blocks(land, None, *sems, work)
        branch[...] = total[...].astype(jnp.bfloat16)

    return pl.pallas_call(
        kernel,
        out_shape=(
            jax.ShapeDtypeStruct((GROUP, rows, HEAD_COLS), jnp.float32),
            jax.ShapeDtypeStruct((GROUP, rows, FEED_COLS), jnp.bfloat16),
            jax.ShapeDtypeStruct((BACK_COLS, D), jnp.bfloat16),
        ),
        in_specs=[VMEM] * 6,
        out_specs=(VMEM, VMEM, VMEM),
        scratch_shapes=[pltpu.VMEM((BACK_COLS, D), jnp.float32)] + gather_scratch(rows),
        compiler_params=pltpu.CompilerParams(
            collective_id=4, has_side_effects=True, vmem_limit_bytes=ROOM
        ),
    )(grad, out_weight, down_weight, inner, mixed, active)


SCATTER_OPS = (
    ((0, 0), (0, 1), (1, 0), (2, 0), (1, 1), (0, 2), (2, 1), (3, 0), (1, 2), (2, 2), (4, 0), (6, 0), (5, 0), (0, 3), (3, 1), (3, 2), (1, 3), (3, 3), (4, 1), (5, 1), (6, 1), (4, 2), (5, 2), (6, 2), (2, 3), (4, 3), (5, 3), (6, 3)),
    ((0, 0), (0, 2), (3, 2), (1, 0), (3, 0), (0, 1), (0, 3), (1, 1), (2, 0), (1, 2), (3, 1), (1, 3), (4, 0), (6, 0), (5, 0), (3, 3), (2, 1), (2, 2), (4, 1), (6, 1), (5, 1), (4, 2), (5, 2), (6, 2), (2, 3), (4, 3), (5, 3), (6, 3)),
)
SCATTER_OPS_WORK = (
    ((0, 0), (0, 1), (1, 0), (2, 0), (1, 1), (0, 2), (2, 1), (3, 0), (1, 2), (2, 2), (4, 0), (6, 0), (7, 0), (5, 0), (0, 3), (3, 1), (3, 2), (1, 3), (3, 3), (4, 1), (7, 0), (5, 1), (7, 0), (7, 0), (7, 0), (7, 0), (7, 0), (6, 1), (4, 2), (7, 0), (5, 2), (7, 0), (7, 0), (7, 0), (6, 2), (2, 3), (7, 0), (7, 0), (7, 0), (7, 0), (7, 0), (4, 3), (5, 3), (6, 3)),
    ((0, 0), (0, 2), (3, 2), (1, 0), (3, 0), (7, 0), (0, 1), (0, 3), (1, 1), (2, 0), (1, 2), (3, 1), (7, 0), (7, 0), (1, 3), (4, 0), (6, 0), (7, 0), (5, 0), (7, 0), (7, 0), (3, 3), (2, 1), (7, 0), (2, 2), (7, 0), (7, 0), (4, 1), (6, 1), (5, 1), (4, 2), (5, 2), (7, 0), (7, 0), (7, 0), (6, 2), (7, 0), (7, 0), (7, 0), (2, 3), (7, 0), (4, 3), (5, 3), (6, 3)),
)
SCATTER_OPS_EARLY = (
    ((0, 0), (0, 1), (1, 0), (2, 0), (0, 2), (1, 1), (2, 1), (3, 0), (1, 2), (2, 2), (4, 0), (6, 0), (7, 0), (5, 0), (0, 3), (7, 0), (7, 0), (3, 1), (3, 2), (3, 3), (4, 1), (7, 0), (5, 1), (7, 0), (7, 0), (6, 1), (1, 3), (7, 0), (4, 2), (7, 0), (7, 0), (5, 2), (7, 0), (7, 0), (7, 0), (6, 2), (7, 0), (7, 0), (7, 0), (7, 0), (2, 3), (4, 3), (5, 3), (6, 3)),
    ((0, 1), (0, 0), (1, 1), (0, 3), (1, 0), (0, 2), (3, 0), (1, 2), (2, 0), (7, 0), (1, 3), (3, 3), (2, 2), (3, 1), (3, 2), (4, 0), (7, 0), (6, 0), (7, 0), (2, 1), (2, 3), (7, 0), (5, 0), (7, 0), (7, 0), (4, 1), (7, 0), (7, 0), (6, 1), (7, 0), (7, 0), (5, 1), (4, 2), (5, 2), (7, 0), (7, 0), (7, 0), (7, 0), (7, 0), (7, 0), (6, 2), (4, 3), (5, 3), (6, 3)),
)
SPLIT = ((0, 208), (208, 48))


def nibble(entries, index):
    word = jnp.int32(0)
    for start in range(0, len(entries), 7):
        packed = sum(entry << (4 * place) for place, entry in enumerate(entries[start : start + 7]))
        word = jnp.where(index >= start, jnp.int32(packed), word)
    return lax.rem(lax.shift_right_logical(word, 4 * lax.rem(index, 7)), 16)


def scatter_events(partial, other_work, ops, scratch):
    total, give, take, side_take, line_take, other_take = scratch[:6]
    core_send, core_recv, side_send, side_recv, line_send, line_recv = scratch[6:12]
    other_send, other_recv = scratch[12:]
    ctx, place, twin, across, twin_across = neighbours()
    below, above = place - 1, place + 1
    has_below, has_above = place > 0, place < SIDE - 1
    at_end = (place == 0) | (place == SIDE - 1)

    def rows_of(part):
        return pl.ds(*SPLIT[part])

    def core_copy(step, store):
        return to_axis(
            give.at[step], take.at[store], core_send.at[store], core_recv.at[store], "ctx", twin
        )

    def side_copy(step, part):
        return to_axis(
            take.at[step, rows_of(part)],
            side_take.at[step, rows_of(part)],
            side_send.at[step, part],
            side_recv.at[step, part],
            "ctx",
            across,
        )

    def line_copy(step, line, slot, target, part):
        return to_axis(
            take.at[SIDE + step, rows_of(part)],
            line_take.at[slot, rows_of(part)],
            line_send.at[line, part],
            line_recv.at[slot, part],
            "fsdp",
            target,
        )

    def other_copy(step, line, slot, target):
        return to_axis(
            take.at[step, rows_of(1)],
            other_take.at[slot],
            other_send.at[line],
            other_recv.at[slot],
            "fsdp",
            target,
        )

    def from_above(line):
        return jnp.where(line == place, SIDE, line)

    def to_below(line):
        return jnp.where(line == place - 1, SIDE, line)

    def one(number, turn):
        def by_end(field):
            ends, middle = (tuple(entry[field] for entry in table) for table in ops)
            return jnp.where(at_end, nibble(ends, number), nibble(middle, number))

        what, step = by_end(0), by_end(1)
        line = digit_of_row(FAR, place, step)

        @pl.when((what <= 1) | (what == 3) | (what == 4))
        def _():
            owner = jnp.where(
                what == 0,
                twin_across,
                jnp.where(what == 1, across, jnp.where(what == 3, twin, ctx)),
            )
            total[...] = partial(owner * SIDE + line)

        @pl.when(what == 0)
        def _():
            give[step] = total[...].astype(jnp.bfloat16)
            core_copy(step, step).start()

        @pl.when(what == 1)
        def _():
            core_copy(step, step).wait_recv()
            take[step] = (total[...] + take[step].astype(jnp.float32)).astype(jnp.bfloat16)
            side_copy(step, 0).start()

        @pl.when(what == 2)
        def _():
            rows = rows_of(1)

            @pl.when((line >= place) & has_below)
            def _():
                other_copy(step, line, line, below).wait_recv()
                take[step, rows] = (
                    take[step, rows].astype(jnp.float32) + other_take[line].astype(jnp.float32)
                ).astype(jnp.bfloat16)

            @pl.when((line <= place) & has_above)
            def _():
                other_copy(step, line, from_above(line), above).wait_recv()
                take[step, rows] = (
                    take[step, rows].astype(jnp.float32)
                    + other_take[from_above(line)].astype(jnp.float32)
                ).astype(jnp.bfloat16)

            @pl.when(line > place)
            def _():
                other_copy(step, line, line, above).start()

            @pl.when(line < place)
            def _():
                other_copy(step, line, to_below(line), below).start()

            @pl.when(line == place)
            def _():
                side_copy(step, 1).start()

        @pl.when(what == 3)
        def _():
            core_copy(step, step).wait_send()
            give[step] = total[...].astype(jnp.bfloat16)
            core_copy(step, SIDE + step).start()

        @pl.when(what == 4)
        def _():
            core_copy(step, SIDE + step).wait_recv()
            total[...] += take[SIDE + step].astype(jnp.float32)

        for part in range(2):
            rows = rows_of(part)

            @pl.when(what == 5 + part)
            def _(rows=rows, part=part):
                crossed = line == place if part == 1 else line >= 0

                @pl.when(crossed)
                def _():
                    side_copy(step, part).wait_recv()
                    total[rows] += side_take[step, rows].astype(jnp.float32)

                @pl.when((line >= place) & has_below)
                def _():
                    line_copy(step, line, line, below, part).wait_recv()
                    total[rows] += line_take[line, rows].astype(jnp.float32)

                @pl.when((line <= place) & has_above)
                def _():
                    line_copy(step, line, from_above(line), above, part).wait_recv()
                    total[rows] += line_take[from_above(line), rows].astype(jnp.float32)

                @pl.when(line > place)
                def _():
                    take[SIDE + step, rows] = total[rows].astype(jnp.bfloat16)
                    line_copy(step, line, line, above, part).start()

                @pl.when(line < place)
                def _():
                    take[SIDE + step, rows] = total[rows].astype(jnp.bfloat16)
                    line_copy(step, line, to_below(line), below, part).start()

        if other_work is not None:

            @pl.when(what == 7)
            def _():
                other_work(turn)

        return turn + jnp.where(what == 7, 1, 0)

    lax.fori_loop(0, len(ops[0]), one, jnp.int32(0))

    def finish(step, carry):
        line = digit_of_row(FAR, place, step)
        core_copy(step, SIDE + step).wait_send()
        side_copy(step, 0).wait_send()

        @pl.when(line == place)
        def _():
            side_copy(step, 1).wait_send()

        @pl.when(line != place)
        def _():
            for part in range(2):
                line_copy(step, line, line, place, part).wait_send()
            other_copy(step, line, line, place).wait_send()

        return carry

    lax.fori_loop(0, SIDE, finish, 0)


def scatter_scratch(rows):
    return [
        pltpu.VMEM((rows, D), jnp.float32),
        pltpu.VMEM((SIDE, rows, D), jnp.bfloat16),
        pltpu.VMEM((2 * SIDE, rows, D), jnp.bfloat16),
        pltpu.VMEM((SIDE, rows, D), jnp.bfloat16),
        pltpu.VMEM((SIDE + 1, rows, D), jnp.bfloat16),
        pltpu.VMEM((SIDE + 1, SPLIT[1][1], D), jnp.bfloat16),
        pltpu.SemaphoreType.DMA((2 * SIDE,)),
        pltpu.SemaphoreType.DMA((2 * SIDE,)),
        pltpu.SemaphoreType.DMA((SIDE, 2)),
        pltpu.SemaphoreType.DMA((SIDE, 2)),
        pltpu.SemaphoreType.DMA((SIDE, 2)),
        pltpu.SemaphoreType.DMA((SIDE + 1, 2)),
        pltpu.SemaphoreType.DMA((SIDE,)),
        pltpu.SemaphoreType.DMA((SIDE + 1,)),
    ]


def forward_scatter(hidden, bias, mixed, active, out_weight, down_weight, layer):
    rows = hidden.shape[0]

    def kernel(hidden, bias, mixed, active, out_weight, down_weight, out, *scratch):
        greet_neighbours()

        def partial(slot):
            return dot(mixed[slot], out_weight[...]) + dot(active[slot], down_weight[...])

        scatter_events(partial, None, SCATTER_OPS, scratch)
        out[...] = hidden[...].astype(jnp.float32) + (scratch[0][...] + bias[...])

    return pl.pallas_call(
        kernel,
        out_shape=jax.ShapeDtypeStruct((rows, D), jnp.float32),
        in_specs=[VMEM] * 6,
        out_specs=VMEM,
        scratch_shapes=scatter_scratch(rows),
        compiler_params=pltpu.CompilerParams(
            collective_id=10 + layer, has_side_effects=True, vmem_limit_bytes=ROOM
        ),
    )(hidden, bias, mixed, active, out_weight, down_weight)


SMALL_ROWS = 16


def backward_scatter(hidden, grad, gain, grad_joint, grad_inner, columns, every, layer):
    rows = hidden.shape[0]
    half = SHARE // 2
    collects = layer == 0

    def kernel(
        hidden,
        grad,
        gain,
        grad_joint,
        grad_inner,
        columns,
        every,
        out,
        small_out,
        *refs,
    ):
        if collects:
            joint_out, upper_out, mine, strips, other, summed, arrived = refs[:7]
            refs = refs[7:]
        else:
            mine, strips = refs[:2]
            joint_out = upper_out = other = summed = arrived = mine
            refs = refs[2:]
        (
        shares,
        small_land,
        small_mine,
        small_other,
        load,
        cross_send,
        cross_recv,
        plane_send,
        plane_recv,
        back_send,
        back_recv,
        keep,
        small_send,
        small_recv,
        swap_send,
        swap_recv,
        *scratch,
        ) = refs
        total = scratch[0]
        ctx, place, seq = lax.axis_index("ctx"), lax.axis_index("fsdp"), lax.axis_index("seq")
        me = ctx * SIDE + place
        part_rows = pl.ds(pl.multiple_of(seq * half, half), half)
        other_rows = pl.ds(pl.multiple_of((1 - seq) * half, half), half)
        outputs = (joint_out, upper_out)
        greet_plane(GROUP)

        def block_of(turn):
            return lax.rem(me + 1 + turn, GROUP)

        def load_strip(turn):
            start = pl.multiple_of(block_of(turn) * SHARE, SHARE)
            buffer = lax.rem(turn, 2)
            return pltpu.make_async_copy(
                every.at[:, :, pl.ds(start, SHARE)], strips.at[buffer], load.at[buffer]
            )

        def cross_copy(block):
            return to_axis(
                mine.at[block, other_rows],
                other.at[block],
                cross_send.at[block],
                cross_recv.at[block],
                "seq",
                1 - seq,
            )

        def plane_copy(block):
            return to_peer(
                summed.at[block], arrived.at[me], plane_send.at[block], plane_recv.at[me], block
            )

        def final_pieces(source):
            return [
                (
                    number,
                    arrived.at[source, :, pl.ds(at, width)],
                    outputs[which].at[part_rows, pl.ds(start, width)],
                )
                for number, (which, start, at, width) in enumerate(column_places(source))
            ]

        def back_copies(source):
            return [
                to_axis(
                    piece,
                    target,
                    back_send.at[source, number],
                    back_recv.at[source, number],
                    "seq",
                    1 - seq,
                )
                for number, piece, target in final_pieces(source)
            ]

        def keep_copies(source):
            return [
                pltpu.make_async_copy(piece, target, keep.at[source, number])
                for number, piece, target in final_pieces(source)
            ]

        def partial(slot):
            return dot(grad_joint[slot], columns[:, :JOINT_COLS], 1, 1) + dot(
                grad_inner[slot], columns[:, JOINT_COLS:], 1, 1
            )

        def product(turn):
            block = block_of(turn)
            load_strip(turn).wait()

            @pl.when(turn + 1 < GROUP)
            def _():
                load_strip(turn + 1).start()

            strip = strips[lax.rem(turn, 2)].reshape(GROUP * rows, SHARE)
            mine[block, :, :JOINT_COLS] = dot(
                strip, grad_joint[...].reshape(GROUP * rows, JOINT_COLS), 0, 0
            ).astype(jnp.bfloat16)
            mine[block, :, JOINT_COLS:] = dot(
                strip, grad_inner[...].reshape(GROUP * rows, FEED_COLS), 0, 0
            ).astype(jnp.bfloat16)
            if collects:
                cross_copy(block).start()

        def add(turn):
            block = block_of(turn)
            cross_copy(block).wait_recv()
            summed[block] = (
                mine[block, part_rows].astype(jnp.float32) + other[block].astype(jnp.float32)
            ).astype(jnp.bfloat16)

            @pl.when(turn < GROUP - 1)
            def _():
                plane_copy(block).start()

        def other_work(turn):
            product(turn)
            if collects:

                @pl.when(turn >= SIDE)
                def _():
                    add(turn - SIDE)

        def last_adds(turn, carry):
            add(turn)
            return carry

        load_strip(0).start()
        scatter_events(
            partial, other_work, SCATTER_OPS_EARLY if collects else SCATTER_OPS_WORK, scratch
        )
        if collects:
            lax.fori_loop(GROUP - SIDE, GROUP, last_adds, 0)
            arrived[me] = summed[me]

        def norm_back(part, sums):
            values = hidden[part].astype(jnp.float32)
            centred = values - jnp.mean(values, axis=1, keepdims=True)
            spread = jnp.mean(centred * centred, axis=1, keepdims=True)
            root = lax.rsqrt(spread + EPS)
            normed = centred * root
            above = total[part]
            scaled = above * gain[...]
            down = jnp.mean(scaled, axis=1, keepdims=True)
            along = jnp.mean(scaled * normed, axis=1, keepdims=True)
            passing = grad[part]
            out[part] = passing + root * (scaled - down - normed * along)
            low = passing.astype(jnp.bfloat16).astype(jnp.float32)

            def fold(values):
                return jnp.sum(values.reshape(STRIP // 8, 8, D), axis=0)

            return (sums[0] + fold(above * normed), sums[1] + fold(above), sums[2] + fold(low))

        zeros = jnp.zeros((8, D), jnp.float32)
        sums = each_strip(rows, norm_back, (zeros, zeros, zeros))
        shares[...] = jnp.zeros_like(shares)
        for number, folded in enumerate(sums):
            row = jnp.sum(folded, axis=0, keepdims=True)
            for block in range(GROUP):
                shares[block, number : number + 1] = row[:, block * SHARE : (block + 1) * SHARE]
        ones = jnp.ones((16, GROUP * rows), jnp.bfloat16)
        joint_bias = dot(ones, grad_joint[...].reshape(GROUP * rows, JOINT_COLS))[:1]
        upper_bias = dot(ones, grad_inner[...].reshape(GROUP * rows, FEED_COLS))[:1]
        for part in range(3):
            at = part * GROUP + me
            shares[at // 3, pl.ds(3 + lax.rem(at, 3), 1)] = joint_bias[
                :, part * HEAD_COLS : (part + 1) * HEAD_COLS
            ]
        for part in range(FEED_COLS // SHARE):
            shares[me, 6 + part : 7 + part] = upper_bias[:, part * SHARE : (part + 1) * SHARE]

        def small_copy(step):
            peer = lax.rem(me + step, GROUP)
            return to_peer(
                shares.at[peer], small_land.at[me], small_send.at[step], small_recv.at[me], peer
            )

        def small_begin(step, carry):
            small_copy(step).start()
            return carry

        lax.fori_loop(1, GROUP, small_begin, 0)
        small_land[me] = shares[me]

        def pass_on(step, carry):
            source = lax.rem(me + GROUP - step, GROUP)

            @pl.when(step > 0)
            def _():
                to_peer(
                    summed.at[source],
                    arrived.at[source],
                    plane_send.at[source],
                    plane_recv.at[source],
                    source,
                ).wait_recv()

            for copy in back_copies(source) + keep_copies(source):
                copy.start()
            return carry

        if collects:
            lax.fori_loop(0, GROUP, pass_on, 0)

        def small_end(step, carry):
            source = lax.rem(me + GROUP - step, GROUP)
            to_peer(
                shares.at[source],
                small_land.at[source],
                small_send.at[step],
                small_recv.at[source],
                source,
            ).wait_recv()
            small_copy(step).wait_send()
            return carry

        lax.fori_loop(1, GROUP, small_end, 0)
        small_mine[...] = jnp.sum(small_land[...], axis=0)
        swap = to_axis(small_mine, small_other, swap_send, swap_recv, "seq", 1 - seq)
        swap.start()
        swap.wait()
        small_out[...] = small_mine[...] + small_other[...]

        def end(block, carry):
            cross_copy(block).wait_send()

            @pl.when(block != me)
            def _():
                plane_copy(block).wait_send()

            for copy in back_copies(block) + keep_copies(block):
                copy.wait()
            return carry

        if collects:
            lax.fori_loop(0, GROUP, end, 0)

    part = pltpu.VMEM((GROUP, half, COLS), jnp.bfloat16)
    whole = (GROUP, SHARE, COLS)
    small = (SMALL_ROWS, SHARE)
    return pl.pallas_call(
        kernel,
        out_shape=(
            jax.ShapeDtypeStruct((rows, D), jnp.float32),
            jax.ShapeDtypeStruct(small, jnp.float32),
        )
        + (
            (
                jax.ShapeDtypeStruct((SHARE, 3 * D), jnp.bfloat16),
                jax.ShapeDtypeStruct((SHARE, FF), jnp.bfloat16),
            )
            if collects
            else (jax.ShapeDtypeStruct(whole, jnp.bfloat16),)
        ),
        in_specs=[VMEM] * 6 + [HBM],
        out_specs=(VMEM, VMEM) + ((HBM, HBM) if collects else (VMEM,)),
        scratch_shapes=([pltpu.VMEM(whole, jnp.bfloat16)] if collects else [])
        + [pltpu.VMEM((2, GROUP, rows, SHARE), jnp.bfloat16)]
        + ([part] * 3 if collects else [])
        + [
            pltpu.VMEM((GROUP,) + small, jnp.float32),
            pltpu.VMEM((GROUP,) + small, jnp.float32),
            pltpu.VMEM(small, jnp.float32),
            pltpu.VMEM(small, jnp.float32),
            pltpu.SemaphoreType.DMA((2,)),
        ]
        + [pltpu.SemaphoreType.DMA((GROUP,))] * 4
        + [pltpu.SemaphoreType.DMA((GROUP, PLACES))] * 3
        + [pltpu.SemaphoreType.DMA((GROUP,))] * 2
        + [pltpu.SemaphoreType.DMA] * 2
        + scatter_scratch(rows),
        compiler_params=pltpu.CompilerParams(
            collective_id=20 + layer, has_side_effects=True, vmem_limit_bytes=ROOM
        ),
    )(hidden, grad, gain, grad_joint, grad_inner, columns, every)


def gather_small(packed):
    def kernel(packed, out, send, recv):
        ctx, place = lax.axis_index("ctx"), lax.axis_index("fsdp")
        me = ctx * SIDE + place
        greet_plane(GROUP, False)
        out[me] = packed[...]

        def copy(step):
            return to_peer(
                packed, out.at[me], send.at[step], recv.at[me], lax.rem(me + step, GROUP)
            )

        def begin(step, carry):
            copy(step).start()
            return carry

        lax.fori_loop(1, GROUP, begin, 0)

        def end(step, carry):
            source = lax.rem(me + GROUP - step, GROUP)
            to_peer(packed, out.at[source], send.at[step], recv.at[source], source).wait_recv()
            copy(step).wait_send()
            return carry

        lax.fori_loop(1, GROUP, end, 0)

    return pl.pallas_call(
        kernel,
        out_shape=jax.ShapeDtypeStruct((GROUP,) + packed.shape, packed.dtype),
        in_specs=[VMEM],
        out_specs=VMEM,
        scratch_shapes=[pltpu.SemaphoreType.DMA((GROUP,))] * 2,
        compiler_params=pltpu.CompilerParams(
            collective_id=6, has_side_effects=True, vmem_limit_bytes=ROOM
        ),
    )(packed)


def mask_rest(rows, begin, spot, first, lead):
    if lead:
        old = jnp.where(spot[:lead] >= begin, rows[:lead], NEG)
    key_at = lax.broadcasted_iota(jnp.int32, (first, first), 0) + lead
    query_at = lax.broadcasted_iota(jnp.int32, (first, first), 1) + lead
    near = spot[lead:]
    seen = ((near >= begin) & (near <= query_at)) | (key_at == query_at)
    new = jnp.where(seen, rows[lead:], NEG)
    return jnp.concatenate([old, new], axis=0) if lead else new


def head_lanes(head, rows):
    lane = lax.broadcasted_iota(jnp.int32, (rows, HEAD_COLS), 1)
    return (lane >= head * HEAD_DIM) & (lane < (head + 1) * HEAD_DIM)


def column_exchange(sources, land, sems, layer):
    plane_send, plane_recv, own_sem = sems
    ctx, place, seq = lax.axis_index("ctx"), lax.axis_index("fsdp"), lax.axis_index("seq")
    me = ctx * SIDE + place
    half = SHARE // 2
    part_rows = pl.ds(pl.multiple_of(seq * half, half), half)

    def piece(peer, number):
        which, start, at, width = column_places(peer)[number]
        return (
            sources[which].at[layer, part_rows, pl.ds(start, width)],
            land.at[me, :, pl.ds(at, width)],
        )

    def send_piece(step, number):
        peer = lax.rem(me + step, GROUP)
        source, target = piece(peer, number)
        return to_peer(source, target, plane_send.at[step, number], plane_recv.at[me, number], peer)

    def own_piece(number):
        return pltpu.make_async_copy(*piece(me, number), own_sem.at[number])

    def begin():
        greet_plane(GROUP, False)

        def send(step, carry):
            for number in range(PLACES):
                send_piece(step, number).start()
            return carry

        lax.fori_loop(1, GROUP, send, 0)
        for number in range(PLACES):
            own_piece(number).start()

    def end():
        def arrive(step, carry):
            source = lax.rem(me + GROUP - step, GROUP)
            for number in range(PLACES):
                _, _, at, width = column_places(0)[number]
                target = land.at[source, :, pl.ds(at, width)]
                to_peer(
                    target, target, plane_send.at[0, number], plane_recv.at[source, number], source
                ).wait_recv()
                send_piece(step, number).wait_send()
            return carry

        lax.fori_loop(1, GROUP, arrive, 0)
        for number in range(PLACES):
            own_piece(number).wait()

    return begin, end


def row_exchange(summed, outputs, sems):
    plane_send, plane_recv, own_sem = sems
    me = lax.axis_index("ctx") * SIDE + lax.axis_index("fsdp")

    def piece(peer, number):
        which, start, at, width = column_places(me)[number]
        return summed.at[peer, :, pl.ds(at, width)], outputs[which].at[:, pl.ds(start, width)]

    def send_piece(step, number):
        peer = lax.rem(me + step, GROUP)
        source, target = piece(peer, number)
        return to_peer(source, target, plane_send.at[step, number], plane_recv.at[me, number], peer)

    def own_piece(number):
        return pltpu.make_async_copy(*piece(me, number), own_sem.at[number])

    def begin():
        greet_plane(GROUP, False)

        def send(step, carry):
            for number in range(PLACES):
                send_piece(step, number).start()
            return carry

        lax.fori_loop(1, GROUP, send, 0)
        for number in range(PLACES):
            own_piece(number).start()

    def end():
        def arrive(step, carry):
            source = lax.rem(me + GROUP - step, GROUP)
            for number in range(PLACES):
                which, start, _, width = column_places(source)[number]
                target = outputs[which].at[:, pl.ds(start, width)]
                to_peer(
                    target, target, plane_send.at[0, number], plane_recv.at[source, number], source
                ).wait_recv()
                send_piece(step, number).wait_send()
            return carry

        lax.fori_loop(1, GROUP, arrive, 0)
        for number in range(PLACES):
            own_piece(number).wait()

    return begin, end


EXCHANGE_SEMS = [
    pltpu.SemaphoreType.DMA((GROUP, PLACES)),
    pltpu.SemaphoreType.DMA((GROUP, PLACES)),
    pltpu.SemaphoreType.DMA((PLACES,)),
]


def attend_plane(query, key, value, begin, spot, weights=None, layer=0):
    rows = query.shape[1]
    length = SIDE * rows
    scale = 1.0 / math.sqrt(HEAD_DIM)

    def kernel(query, key, value, begin, spot, *refs):
        if weights is None:
            mixed, turned, stats = refs
        else:
            mixed, turned, stats, land = refs[2:6]
            begin_exchange, end_exchange = column_exchange(refs[:2], land, refs[6:], layer)
            pl.when(pl.program_id(0) == 0)(begin_exchange)
        keys = key[:, 0].reshape(length, HEAD_COLS)
        values = value[:, 0].reshape(length, HEAD_COLS)
        for chunk in range(SIDE):
            lead = chunk * rows
            seen = lead + rows
            scaled = query[chunk, 0] * jnp.bfloat16(scale)
            start = begin[0, :, lead:seen]
            outs = []
            for head in range(OWN):
                own = jnp.where(head_lanes(head, rows), scaled, jnp.bfloat16(0))
                scores = mask_rest(
                    dot(keys[:seen], own, 1, 1), start, spot[0, :seen], rows, lead
                )
                peak = jnp.max(scores, axis=0, keepdims=True)
                probs = jnp.exp(scores - peak)
                norm = jnp.sum(probs, axis=0, keepdims=True)
                stats[0, head : head + 1, lead:seen] = peak
                stats[0, OWN + head : OWN + head + 1, lead:seen] = norm
                whole = dot(values[:seen], probs.astype(jnp.bfloat16), 0, 0)
                outs.append(whole[head * HEAD_DIM : (head + 1) * HEAD_DIM] / norm)
            joined = jnp.concatenate(outs, axis=0)
            turned[chunk, 0] = joined
            mixed[chunk, 0] = joined.T.astype(jnp.bfloat16)
        if weights is not None:
            pl.when(pl.program_id(0) == SIDE - 1)(end_exchange)

    def spec(height, width):
        return pl.BlockSpec((SIDE, 1, height, width), lambda step: (0, step, 0, 0))

    def shape(height, width, dtype):
        return jax.ShapeDtypeStruct((SIDE, SIDE, height, width), dtype)

    extra = weights is not None
    land = (jax.ShapeDtypeStruct((GROUP, SHARE // 2, COLS), jnp.bfloat16),) if extra else ()
    mixed, turned, stats, *land = pl.pallas_call(
        kernel,
        grid=(SIDE,),
        out_shape=(
            shape(rows, HEAD_COLS, jnp.bfloat16),
            shape(HEAD_COLS, rows, jnp.float32),
            jax.ShapeDtypeStruct((SIDE, 2 * OWN, length), jnp.float32),
        )
        + land,
        in_specs=[spec(rows, HEAD_COLS)] * 3
        + [
            pl.BlockSpec((1, 1, length), lambda step: (step, 0, 0)),
            pl.BlockSpec((1, length, 1), lambda step: (step, 0, 0)),
        ]
        + [HBM] * (2 if extra else 0),
        out_specs=(
            spec(rows, HEAD_COLS),
            spec(HEAD_COLS, rows),
            pl.BlockSpec((1, 2 * OWN, length), lambda step: (step, 0, 0)),
        )
        + ((HBM,) if extra else ()),
        scratch_shapes=EXCHANGE_SEMS if extra else [],
        compiler_params=pltpu.CompilerParams(
            collective_id=40, has_side_effects=True, vmem_limit_bytes=ROOM
        )
        if extra
        else pltpu.CompilerParams(vmem_limit_bytes=ROOM),
    )(
        *(array.reshape(SIDE, SIDE, rows, HEAD_COLS) for array in (query, key, value)),
        begin,
        spot,
        *(weights or ()),
    )
    return mixed.reshape(GROUP, rows, HEAD_COLS), turned, stats, *land


def attend_plane_back(query, key, value, begin, spot, turned, stats, grad, tables, summed=None):
    rows = query.shape[1]
    length = SIDE * rows
    scale = 1.0 / math.sqrt(HEAD_DIM)

    extra = summed is not None

    def kernel(query, key, value, grad, cosine, sine, begin, spot, turned, stats, *refs):
        if extra:
            out, grad_k, grad_v = refs[1], refs[4], refs[5]
            begin_exchange, end_exchange = row_exchange(refs[0], refs[2:4], refs[6:])
            pl.when(pl.program_id(0) == 0)(begin_exchange)
        else:
            out, grad_k, grad_v = refs
        keys = key[:, 0].reshape(length, HEAD_COLS)
        values = value[:, 0].reshape(length, HEAD_COLS)
        for chunk in range(SIDE):
            lead = chunk * rows
            seen = lead + rows
            if chunk == 0:
                grad_k[...] = jnp.zeros_like(grad_k)
                grad_v[...] = jnp.zeros_like(grad_v)
            scaled = query[chunk, 0] * jnp.bfloat16(scale)
            start = begin[0, :, lead:seen]
            flipped = grad[chunk, 0].T
            grad_q, drifts, numers = [], [], []
            for head in range(OWN):
                part = slice(head * HEAD_DIM, (head + 1) * HEAD_DIM)
                norm = stats[0, OWN + head : OWN + head + 1, lead:seen]
                drifts.append(
                    jnp.sum(flipped[part] * turned[chunk, 0, part], axis=0, keepdims=True) / norm
                )
                numers.append(flipped[part] / norm)
            numer = jnp.concatenate(numers, axis=0).T.astype(jnp.bfloat16)
            for head in range(OWN):
                part = slice(head * HEAD_DIM, (head + 1) * HEAD_DIM)
                lanes = head_lanes(head, rows)
                own = jnp.where(lanes, scaled, jnp.bfloat16(0))
                own_numer = jnp.where(lanes, numer, jnp.bfloat16(0))
                scores = mask_rest(
                    dot(keys[:seen], own, 1, 1), start, spot[0, :seen], rows, lead
                )
                probs = jnp.exp(scores - stats[0, head : head + 1, lead:seen])
                grad_probs = dot(values[:seen], own_numer, 1, 1)
                grad_scores = (probs * (grad_probs - drifts[head])).astype(jnp.bfloat16)
                grad_q.append(dot(keys[:seen], grad_scores, 0, 0)[part])
                grad_k[:seen] += dot(grad_scores, own)
                grad_v[:seen] += dot(probs.astype(jnp.bfloat16), own_numer)
            turns = (cosine[chunk, 0], sine[chunk, 0])
            whole = jnp.concatenate(grad_q, axis=0).T * scale
            out[chunk, 0, :, :HEAD_COLS] = spin(whole, *turns, -1.0).astype(jnp.bfloat16)
        for chunk in range(SIDE):
            place = slice(chunk * rows, (chunk + 1) * rows)
            turns = (cosine[chunk, 0], sine[chunk, 0])
            out[chunk, 0, :, HEAD_COLS : 2 * HEAD_COLS] = spin(grad_k[place], *turns, -1.0).astype(
                jnp.bfloat16
            )
            out[chunk, 0, :, 2 * HEAD_COLS :] = grad_v[place].astype(jnp.bfloat16)
        if extra:
            pl.when(pl.program_id(0) == SIDE - 1)(end_exchange)

    def spec(height, width):
        return pl.BlockSpec((SIDE, 1, height, width), lambda step: (0, step, 0, 0))

    half = SHARE // 2
    halves = (
        jax.ShapeDtypeStruct((half, 3 * D), jnp.bfloat16),
        jax.ShapeDtypeStruct((half, FF), jnp.bfloat16),
    )
    out, *halves = pl.pallas_call(
        kernel,
        grid=(SIDE,),
        out_shape=(jax.ShapeDtypeStruct((SIDE, SIDE, rows, JOINT_COLS), jnp.bfloat16),)
        + (halves if extra else ()),
        in_specs=[spec(rows, HEAD_COLS)] * 6
        + [
            pl.BlockSpec((1, 1, length), lambda step: (step, 0, 0)),
            pl.BlockSpec((1, length, 1), lambda step: (step, 0, 0)),
            spec(HEAD_COLS, rows),
            pl.BlockSpec((1, 2 * OWN, length), lambda step: (step, 0, 0)),
        ]
        + [HBM] * (1 if extra else 0),
        out_specs=(spec(rows, JOINT_COLS),) + ((HBM, HBM) if extra else ()),
        scratch_shapes=[pltpu.VMEM((length, HEAD_COLS), jnp.float32)] * 2
        + (EXCHANGE_SEMS if extra else []),
        compiler_params=pltpu.CompilerParams(
            collective_id=41, has_side_effects=True, vmem_limit_bytes=ROOM
        )
        if extra
        else pltpu.CompilerParams(vmem_limit_bytes=ROOM),
    )(
        *(
            array.reshape(SIDE, SIDE, rows, HEAD_COLS)
            for array in (query, key, value, grad) + tuple(tables)
        ),
        begin,
        spot,
        turned,
        stats,
        *((summed,) if extra else ()),
    )
    return out.reshape(GROUP, rows, JOINT_COLS), *halves


def on_device_split(
    tokens,
    doc_lengths,
    keep_mask,
    ln_gain,
    ln_bias,
    qkv_weight,
    qkv_bias,
    out_weight,
    out_bias,
    up_weight,
    up_bias,
    down_weight,
    down_bias,
    cotangent,
):
    rows = tokens.shape[1]
    length = SIDE * rows
    docs = doc_lengths.shape[1]
    me = lax.axis_index("ctx") * SIDE + lax.axis_index("fsdp")

    high = (doc_lengths[0] // 32).astype(jnp.bfloat16)
    low = (doc_lengths[0] % 32).astype(jnp.bfloat16)
    fields = [ln_gain, ln_bias, qkv_bias, out_bias, down_bias]
    packed = jnp.concatenate(
        [field.reshape(-1) for field in fields]
        + [keep_mask[0].astype(jnp.bfloat16), high, low]
    )
    tile = 16 * 128
    packed = jnp.pad(packed, (0, -packed.shape[0] % tile)).reshape(-1, 128)
    everyone = gather_small(packed).reshape(GROUP, -1)
    at = 0
    whole = []
    for field in fields:
        width = field.shape[1]
        part = everyone[:, at : at + LAYERS * width].reshape(GROUP, LAYERS, width)
        whole.append(part.transpose(1, 0, 2).reshape(LAYERS, 1, GROUP * width).astype(jnp.float32))
        at += LAYERS * width
    gain, shift, joint_bias, output_bias, lower_bias = whole
    keep = everyone[:, at : at + rows].reshape(SIDE, SIDE, rows)
    keep = keep.transpose(1, 0, 2).reshape(SIDE, length)
    at += rows
    lengths = (
        everyone[:SIDE, at : at + docs].astype(jnp.int32) * 32
        + everyone[:SIDE, at + docs : at + 2 * docs].astype(jnp.int32)
    )
    own_bias = lax.dynamic_slice_in_dim(
        joint_bias.reshape(LAYERS, 3, GROUP, HEAD_COLS), me, 1, axis=2
    ).reshape(LAYERS, JOINT_COLS)
    column_bias = jnp.concatenate([own_bias, up_bias.astype(jnp.float32)], axis=1)

    index = jnp.arange(length, dtype=jnp.int32)
    ends = jnp.cumsum(lengths, axis=1)
    passed = jnp.where(index[None, None, :] >= ends[:, :, None], ends[:, :, None], 0)
    begin = jnp.max(passed, axis=1)[:, None, :]
    spot = jnp.where(keep > 0, index[None, :], -1)[:, :, None]
    position = (index[None, None, :] - begin).astype(jnp.float32)
    position = position.reshape(SIDE, SIDE, rows).transpose(1, 0, 2).reshape(GROUP, rows, 1)
    lane = np.arange(HEAD_COLS) % HEAD_DIM
    inverse = 1.0 / 10000.0 ** (np.arange(0, ROT, 2, dtype=np.float32) / np.float32(ROT))
    inverse = np.where(lane < ROT, inverse[lane % (ROT // 2)], 0.0).astype(np.float32)
    inverse = jnp.asarray(inverse)[None, :]

    seq = lax.axis_index("seq")
    half = SHARE // 2
    swap = [(0, 1), (1, 0)]

    def swapped(values):
        return lax.ppermute(values, "seq", swap)

    hidden = tokens[0]
    saved, tables = [], None
    sources = (qkv_weight, up_weight)
    for layer in range(LAYERS):
        out = forward_gather(
            hidden,
            gain[layer],
            shift[layer],
            column_bias[layer][None, :],
            tables or (position, inverse),
            sources,
            layer,
        )
        every, columns, query, key, value, inner, active = out[:7]
        tables = tables or tuple(out[7:])
        if layer + 1 < LAYERS:
            mixed, turned, stats, arrived = attend_plane(
                query, key, value, begin, spot, (qkv_weight, up_weight), layer + 1
            )
            sources = (arrived, swapped(arrived))
        else:
            mixed, turned, stats = attend_plane(query, key, value, begin, spot)
        saved.append(
            (hidden, every, columns, query, key, value, inner, active, mixed, turned, stats)
        )
        hidden = forward_scatter(
            hidden,
            output_bias[layer] + lower_bias[layer],
            mixed,
            active,
            out_weight[layer],
            down_weight[layer],
            layer,
        )
    result = hidden.astype(jnp.bfloat16)[None]

    grad_hidden = cotangent[0].astype(jnp.float32) * keep_mask[0].astype(jnp.float32)[:, None]
    joint_grads, upper_grads, branch_grads, small_grads = [], [], [], []
    summed = None
    for layer in reversed(range(LAYERS)):
        before, every, columns, query, key, value, inner, active, mixed, turned, stats = saved[layer]
        grad_mixed, grad_inner, branch = backward_gather(
            grad_hidden.astype(jnp.bfloat16),
            out_weight[layer],
            down_weight[layer],
            inner,
            mixed,
            active,
        )
        branch_grads.insert(
            0, branch.astype(jnp.float32) + swapped(branch).astype(jnp.float32)
        )
        grad_joint, *halves = attend_plane_back(
            query, key, value, begin, spot, turned, stats, grad_mixed, tables, summed
        )
        for grads, own in zip((joint_grads, upper_grads), halves):
            other = swapped(own)
            grads.insert(
                0,
                jnp.concatenate(
                    [jnp.where(seq == 0, own, other), jnp.where(seq == 0, other, own)], axis=0
                ),
            )
        grad_hidden, small, *grads = backward_scatter(
            before,
            grad_hidden,
            gain[layer],
            grad_joint,
            grad_inner,
            columns.reshape(D, COLS),
            every,
            layer,
        )
        small_grads.insert(0, small)
        if layer > 0:
            own = lax.dynamic_slice_in_dim(grads[0], seq * half, half, axis=1)
            other = swapped(lax.dynamic_slice_in_dim(grads[0], (1 - seq) * half, half, axis=1))
            summed = (own.astype(jnp.float32) + other.astype(jnp.float32)).astype(jnp.bfloat16)
        else:
            joint_grads.insert(0, grads[0])
            upper_grads.insert(0, grads[1])
    branch_grad = jnp.stack(branch_grads)
    small = jnp.stack(small_grads)
    return (
        result,
        grad_hidden[None],
        small[:, 0],
        small[:, 1],
        jnp.stack(joint_grads).astype(jnp.float32),
        small[:, 3:6].reshape(LAYERS, JOINT_COLS),
        branch_grad[:, :HEAD_COLS],
        small[:, 2],
        jnp.stack(upper_grads).astype(jnp.float32),
        small[:, 6:10].reshape(LAYERS, FEED_COLS),
        branch_grad[:, HEAD_COLS:],
        small[:, 2],
    )


def solution(mesh):
    small = mesh.shape["ctx"] == SIDE and mesh.shape["fsdp"] == SIDE and mesh.shape["seq"] == 2
    on_device = on_device_split if small else on_device_gathered
    return jax.shard_map(
        on_device,
        mesh=mesh,
        in_specs=(
            P(("seq", "fsdp"), "ctx", None),
            P(("seq", "fsdp"), None),
            P(("seq", "fsdp"), "ctx"),
            P(None, ("ctx", "fsdp")),
            P(None, ("ctx", "fsdp")),
            P(None, ("ctx", "fsdp"), None),
            P(None, ("ctx", "fsdp")),
            P(None, ("ctx", "fsdp"), None),
            P(None, ("ctx", "fsdp")),
            P(None, ("ctx", "fsdp"), None),
            P(None, ("ctx", "fsdp")),
            P(None, ("ctx", "fsdp"), None),
            P(None, ("ctx", "fsdp")),
            P(("seq", "fsdp"), "ctx", None),
        ),
        out_specs=(
            P(("seq", "fsdp"), "ctx", None),
            P(("seq", "fsdp"), "ctx", None),
            P(None, ("ctx", "fsdp")),
            P(None, ("ctx", "fsdp")),
            P(None, ("ctx", "fsdp"), None),
            P(None, ("ctx", "fsdp")),
            P(None, ("ctx", "fsdp"), None),
            P(None, ("ctx", "fsdp")),
            P(None, ("ctx", "fsdp"), None),
            P(None, ("ctx", "fsdp")),
            P(None, ("ctx", "fsdp"), None),
            P(None, ("ctx", "fsdp")),
        ),
        check_vma=False,
    )
```

```python
import functools
import math

import jax
import jax.numpy as jnp
import numpy as np
from jax import lax
from jax.experimental import pallas as pl
from jax.experimental.pallas import tpu as pltpu
from jax.sharding import PartitionSpec as P

D = 2048
HEADS = 32
HEAD_DIM = 64
ROT = 32
FF = 8192
LAYERS = 2


EPS = 1e-05
NEG = -1e30


def place_tokens(token_index, lengths):
    bounds = jnp.cumsum(lengths)
    starts = bounds - lengths
    segment = jnp.sum((token_index[:, None] >= bounds[None, :]).astype(jnp.int32), axis=1)
    chosen = segment[:, None] == jnp.arange(lengths.shape[0], dtype=jnp.int32)[None, :]
    position = token_index - jnp.sum(jnp.where(chosen, starts[None, :], 0), axis=1)
    return (segment, position)


def angles(position):
    indices = jnp.arange(0, ROT, 2, dtype=jnp.float32) / ROT
    inverse = 1.0 / 10000.0**indices
    turned = position.astype(jnp.float32)[:, None] * inverse[None, :]
    turned = jnp.concatenate([turned, turned], axis=1)
    return (jnp.cos(turned), jnp.sin(turned))


def rotate(values, cosine, sine):
    rotary = values[..., :ROT]
    middle = ROT // 2
    turned = jnp.concatenate([-rotary[..., middle:], rotary[..., :middle]], axis=-1)
    mixed = rotary * cosine[:, None, :] + turned * sine[:, None, :]
    return jnp.concatenate([mixed, values[..., ROT:]], axis=-1)


def normalize(hidden, gain_row, shift_row):
    average = jnp.mean(hidden, axis=1, keepdims=True)
    centred = hidden - average
    spread = jnp.mean(centred * centred, axis=1, keepdims=True)
    return centred * lax.rsqrt(spread + EPS) * gain_row + shift_row


def block_scores(queries, travelling, start, query_index, query_segment, lengths):
    key_flat, value_flat, key_keep = travelling
    count = key_flat.shape[0]
    key_index = start + jnp.arange(count, dtype=jnp.int32)
    key_segment = place_tokens(key_index, lengths)[0]
    allowed = (
        (query_segment[:, None] == key_segment[None, :])
        & (key_index[None, :] <= query_index[:, None])
        & ((key_keep[None, :] > 0) | (key_index[None, :] == query_index[:, None]))
    )
    key_rows = key_flat.reshape(count, HEADS, HEAD_DIM)
    value_rows = value_flat.reshape(count, HEADS, HEAD_DIM)
    scores = jnp.einsum("qhd,khd->hqk", queries, key_rows, preferred_element_type=jnp.float32) * (
        1.0 / math.sqrt(HEAD_DIM)
    )
    return (scores, allowed, key_rows, value_rows)


def attend(running, travelling, start, queries, query_index, query_segment, lengths):
    maxima, totals, weighted = running
    scores, allowed, key_rows, value_rows = block_scores(
        queries, travelling, start, query_index, query_segment, lengths
    )
    masked = jnp.where(allowed[None], scores, NEG)
    new_max = jnp.maximum(maxima, jnp.max(masked, axis=2))
    probs = jnp.where(allowed[None], jnp.exp(masked - new_max[:, :, None]), 0.0)
    totals = jnp.sum(probs, axis=2)
    weighted = jnp.einsum(
        "hqk,khd->hqd", probs.astype(jnp.bfloat16), value_rows, preferred_element_type=jnp.float32
    )
    return (new_max, totals, weighted)


def attend_back(
    travelling, start, queries, maxima, grad_numer, drift, query_index, query_segment, lengths
):
    scores, allowed, key_rows, value_rows = block_scores(
        queries, travelling, start, query_index, query_segment, lengths
    )
    count = key_rows.shape[0]
    scale = 1.0 / math.sqrt(HEAD_DIM)
    probs = jnp.where(allowed[None], jnp.exp(scores - maxima[:, :, None]), 0.0)
    grad_probs = jnp.einsum(
        "hqd,khd->hqk", grad_numer, value_rows, preferred_element_type=jnp.float32
    )
    grad_scores = (probs * (grad_probs - drift[:, :, None])).astype(jnp.bfloat16)
    grad_query = (
        jnp.einsum("hqk,khd->qhd", grad_scores, key_rows, preferred_element_type=jnp.float32)
        * scale
    )
    grad_key = (
        jnp.einsum("hqk,qhd->khd", grad_scores, queries, preferred_element_type=jnp.float32) * scale
    )
    grad_value = jnp.einsum(
        "hqk,hqd->khd", probs.astype(jnp.bfloat16), grad_numer, preferred_element_type=jnp.float32
    )
    return (
        grad_query,
        grad_key.reshape(count, HEADS * HEAD_DIM),
        grad_value.reshape(count, HEADS * HEAD_DIM),
    )


def attention_forward(queries, key_flat, value_flat, key_keep, query_index, query_segment, lengths):
    row_count = key_flat.shape[0]
    initial = (
        jnp.full((HEADS, row_count), NEG, jnp.float32),
        jnp.zeros((HEADS, row_count), jnp.float32),
        jnp.zeros((HEADS, row_count, HEAD_DIM), jnp.float32),
    )
    return attend(
        initial,
        (
            lax.all_gather(key_flat, "ctx", axis=0, tiled=True),
            lax.all_gather(value_flat, "ctx", axis=0, tiled=True),
            lax.all_gather(key_keep, "ctx", axis=0, tiled=True),
        ),
        jnp.int32(0),
        queries,
        query_index,
        query_segment,
        lengths,
    )


def attention_backward(
    queries,
    key_flat,
    value_flat,
    key_keep,
    maxima,
    grad_numer,
    drift,
    query_index,
    query_segment,
    lengths,
):
    whole = (
        lax.all_gather(key_flat, "ctx", axis=0, tiled=True),
        lax.all_gather(value_flat, "ctx", axis=0, tiled=True),
        lax.all_gather(key_keep, "ctx", axis=0, tiled=True),
    )
    grad_query, every_key, every_value = attend_back(
        whole, 0, queries, maxima, grad_numer, drift, query_index, query_segment, lengths
    )
    grad_key, grad_value = (
        lax.psum_scatter(
            every_key.astype(jnp.bfloat16), "ctx", scatter_dimension=0, tiled=True
        ).astype(jnp.float32),
        lax.psum_scatter(
            every_value.astype(jnp.bfloat16), "ctx", scatter_dimension=0, tiled=True
        ).astype(jnp.float32),
    )
    return (grad_query, grad_key, grad_value)


def layer_forward(hidden, weights, cosine, sine, key_keep, query_index, query_segment, lengths):
    (
        norm_gain,
        norm_shift,
        joint_weight,
        joint_bias,
        output_weight,
        output_bias,
        upper_weight,
        upper_bias,
        lower_weight,
        lower_bias,
    ) = weights
    row_count = hidden.shape[0]
    width = HEADS * HEAD_DIM
    normed = normalize(
        hidden, norm_gain.astype(jnp.float32), norm_shift.astype(jnp.float32)
    ).astype(jnp.bfloat16)
    joint = jnp.dot(normed, joint_weight, preferred_element_type=jnp.float32) + joint_bias.astype(
        jnp.float32
    )
    queries = rotate(joint[:, :width].reshape(row_count, HEADS, HEAD_DIM), cosine, sine).astype(
        jnp.bfloat16
    )
    key_flat = (
        rotate(joint[:, width : 2 * width].reshape(row_count, HEADS, HEAD_DIM), cosine, sine)
        .astype(jnp.bfloat16)
        .reshape(row_count, width)
    )
    value_flat = joint[:, 2 * width :].astype(jnp.bfloat16)
    maxima, totals, weighted = attention_forward(
        queries, key_flat, value_flat, key_keep, query_index, query_segment, lengths
    )
    mixed = (weighted / totals[:, :, None]).transpose(1, 0, 2).reshape(row_count, width)
    attention_out = jnp.dot(
        mixed.astype(jnp.bfloat16), output_weight, preferred_element_type=jnp.float32
    ) + output_bias.astype(jnp.float32)
    inner = jnp.dot(normed, upper_weight, preferred_element_type=jnp.float32) + upper_bias.astype(
        jnp.float32
    )
    activated = jax.nn.gelu(inner, approximate=True).astype(jnp.bfloat16)
    feed_out = jnp.dot(
        activated, lower_weight, preferred_element_type=jnp.float32
    ) + lower_bias.astype(jnp.float32)
    saved = (hidden, normed, queries, key_flat, value_flat, maxima, totals, mixed, inner, activated)
    return (hidden + (attention_out + feed_out), saved)


def layer_backward(
    grad_out, saved, weights, cosine, sine, key_keep, query_index, query_segment, lengths
):
    hidden, normed, queries, key_flat, value_flat, maxima, totals, mixed, inner, activated = saved
    (
        norm_gain,
        norm_shift,
        joint_weight,
        joint_bias,
        output_weight,
        output_bias,
        upper_weight,
        upper_bias,
        lower_weight,
        lower_bias,
    ) = weights
    row_count = hidden.shape[0]
    width = HEADS * HEAD_DIM
    ratio = FF // D
    grad_branch = grad_out.astype(jnp.bfloat16)
    mixed_low = mixed.astype(jnp.bfloat16)
    branch_bias = jnp.sum(grad_branch, axis=0, dtype=jnp.float32)
    grad_activated = jnp.einsum(
        "td,fd->tf", grad_branch, lower_weight, preferred_element_type=jnp.float32
    )
    gelu_pull = jax.vjp(functools.partial(jax.nn.gelu, approximate=True), inner)[1]
    grad_inner = gelu_pull(grad_activated)[0].astype(jnp.bfloat16)
    upper_bias_grad = jnp.sum(grad_inner, axis=0, dtype=jnp.float32)
    grad_normed = jnp.einsum(
        "tf,df->td", grad_inner, upper_weight, preferred_element_type=jnp.float32
    )
    upper_bias_rows = upper_bias_grad.reshape(D, ratio)
    normed_cols = normed
    upper_part = jnp.einsum(
        "tc,tf->cf", normed_cols, grad_inner, preferred_element_type=jnp.float32
    )
    lower_part = jnp.einsum(
        "tc,td->cd", activated, grad_branch, preferred_element_type=jnp.float32
    ).reshape(lax.axis_size(("ctx", "fsdp")) * (D // lax.axis_size(("ctx", "fsdp"))), ratio * width)
    bias_part = upper_bias_rows
    branch_part = branch_bias[:, None]
    feed_share = lax.psum_scatter(
        jnp.concatenate([upper_part, lower_part, bias_part, branch_part], axis=1),
        ("ctx", "fsdp"),
        scatter_dimension=0,
        tiled=True,
    )
    share_rows = feed_share.shape[0]
    upper_share = feed_share[:, :FF]
    lower_share = feed_share[:, FF : FF + ratio * width].reshape(share_rows * ratio, width)
    upper_bias_share = feed_share[:, FF + ratio * width : FF + ratio * width + ratio].reshape(
        share_rows * ratio
    )
    branch_share = feed_share[:, FF + ratio * width + ratio]
    feed_parts = (upper_share, upper_bias_share, lower_share, branch_share)
    output_share = None
    grad_mixed = jnp.einsum(
        "te,de->td", grad_branch, output_weight, preferred_element_type=jnp.float32
    )
    head_mixed = mixed.reshape(row_count, HEADS, HEAD_DIM).transpose(1, 0, 2)
    head_grad = grad_mixed.reshape(row_count, HEADS, HEAD_DIM).transpose(1, 0, 2)
    drift = jnp.sum(head_grad * head_mixed, axis=2) / totals
    grad_numer = (head_grad / totals[:, :, None]).astype(jnp.bfloat16)
    grad_query, grad_key, grad_value = attention_backward(
        queries,
        key_flat,
        value_flat,
        key_keep,
        maxima,
        grad_numer,
        drift,
        query_index,
        query_segment,
        lengths,
    )
    grad_query = rotate(grad_query, cosine, -sine).reshape(row_count, width)
    grad_key = rotate(grad_key.reshape(row_count, HEADS, HEAD_DIM), cosine, -sine).reshape(
        row_count, width
    )
    grad_joint = jnp.concatenate([grad_query, grad_key, grad_value], axis=1).astype(jnp.bfloat16)
    joint_bias_grad = jnp.sum(grad_joint, axis=0, dtype=jnp.float32)
    grad_normed = grad_normed + jnp.einsum(
        "te,de->td", grad_joint, joint_weight, preferred_element_type=jnp.float32
    )
    norm_pull = jax.vjp(
        normalize, hidden, norm_gain.astype(jnp.float32), norm_shift.astype(jnp.float32)
    )[1]
    grad_hidden, gain_grad, shift_grad = norm_pull(grad_normed)
    joint_bias_rows = joint_bias_grad.reshape(D, 3)
    normed_cols = normed
    joint_part = jnp.einsum(
        "tc,te->ce", normed_cols, grad_joint, preferred_element_type=jnp.float32
    )
    output_part = jnp.einsum(
        "tc,te->ce", mixed_low, grad_branch, preferred_element_type=jnp.float32
    )
    bias_part = joint_bias_rows
    gain_part = gain_grad[:, None]
    shift_part = shift_grad[:, None]
    attn_share = lax.psum_scatter(
        jnp.concatenate([joint_part, output_part, bias_part, gain_part, shift_part], axis=1),
        ("ctx", "fsdp"),
        scatter_dimension=0,
        tiled=True,
    )
    share_rows = attn_share.shape[0]
    joint_share = attn_share[:, : 3 * width]
    output_share = attn_share[:, 3 * width : 4 * width]
    joint_bias_share = attn_share[:, 4 * width : 4 * width + 3].reshape(share_rows * 3)
    gain_share = attn_share[:, 4 * width + 3]
    shift_share = attn_share[:, 4 * width + 4]
    attention_parts = (gain_share, shift_share, joint_share, joint_bias_share, output_share)
    return (grad_out + grad_hidden, attention_parts, feed_parts)


def on_device_gathered(
    tokens,
    doc_lengths,
    keep_mask,
    ln_gain,
    ln_bias,
    qkv_weight,
    qkv_bias,
    out_weight,
    out_bias,
    up_weight,
    up_bias,
    down_weight,
    down_bias,
    cotangent,
):
    row_count = tokens.shape[1]
    position = lax.axis_index("ctx")
    query_index = position * row_count + jnp.arange(row_count, dtype=jnp.int32)
    lengths = doc_lengths[0]
    query_segment, query_position = place_tokens(query_index, lengths)
    cosine, sine = angles(query_position)
    key_keep = keep_mask[0].astype(jnp.bfloat16)
    shards = (
        ln_gain,
        ln_bias,
        qkv_weight,
        qkv_bias,
        out_weight,
        out_bias,
        up_weight,
        up_bias,
        down_weight,
        down_bias,
    )

    def fetch(layer_index):
        return (
            lax.all_gather(shards[0][layer_index], ("ctx", "fsdp"), axis=0, tiled=True),
            lax.all_gather(shards[1][layer_index], ("ctx", "fsdp"), axis=0, tiled=True),
            lax.all_gather(shards[2][layer_index], ("ctx", "fsdp"), axis=0, tiled=True),
            lax.all_gather(shards[3][layer_index], ("ctx", "fsdp"), axis=0, tiled=True),
            lax.all_gather(shards[4][layer_index], ("ctx", "fsdp"), axis=0, tiled=True),
            lax.all_gather(shards[5][layer_index], ("ctx", "fsdp"), axis=0, tiled=True),
            lax.all_gather(shards[6][layer_index], ("ctx", "fsdp"), axis=0, tiled=True),
            lax.all_gather(shards[7][layer_index], ("ctx", "fsdp"), axis=0, tiled=True),
            lax.all_gather(shards[8][layer_index], ("ctx", "fsdp"), axis=0, tiled=True),
            lax.all_gather(shards[9][layer_index], ("ctx", "fsdp"), axis=0, tiled=True),
        )

    hidden = tokens[0].astype(jnp.float32)
    saved_layers = []
    weights = None
    for layer_index in range(LAYERS):
        weights = fetch(layer_index)
        hidden, saved = layer_forward(
            hidden, weights, cosine, sine, key_keep, query_index, query_segment, lengths
        )
        saved_layers.append(saved)
    result = hidden.astype(jnp.bfloat16)[None]
    grad_hidden = cotangent[0].astype(jnp.float32) * keep_mask[0].astype(jnp.float32)[:, None]
    attention_list = [None] * LAYERS
    feed_list = [None] * LAYERS
    for layer_index in reversed(range(LAYERS)):
        weights = weights if layer_index == LAYERS - 1 else fetch(layer_index)
        grad_hidden, attention_parts, feed_parts = layer_backward(
            grad_hidden,
            saved_layers[layer_index],
            weights,
            cosine,
            sine,
            key_keep,
            query_index,
            query_segment,
            lengths,
        )
        attention_list[layer_index] = attention_parts
        feed_list[layer_index] = feed_parts
    gain_stack = jnp.stack([attention_list[layer_index][0] for layer_index in range(LAYERS)])
    shift_stack = jnp.stack([attention_list[layer_index][1] for layer_index in range(LAYERS)])
    joint_stack = jnp.stack([attention_list[layer_index][2] for layer_index in range(LAYERS)])
    joint_bias_stack = jnp.stack([attention_list[layer_index][3] for layer_index in range(LAYERS)])
    output_stack = jnp.stack([attention_list[layer_index][4] for layer_index in range(LAYERS)])
    upper_stack = jnp.stack([feed_list[layer_index][0] for layer_index in range(LAYERS)])
    upper_bias_stack = jnp.stack([feed_list[layer_index][1] for layer_index in range(LAYERS)])
    lower_stack = jnp.stack([feed_list[layer_index][2] for layer_index in range(LAYERS)])
    branch_stack = jnp.stack([feed_list[layer_index][3] for layer_index in range(LAYERS)])
    summed = (
        lax.psum(gain_stack.astype(jnp.bfloat16), "seq").astype(jnp.float32),
        lax.psum(shift_stack.astype(jnp.bfloat16), "seq").astype(jnp.float32),
        lax.psum(joint_stack.astype(jnp.bfloat16), "seq").astype(jnp.float32),
        lax.psum(joint_bias_stack.astype(jnp.bfloat16), "seq").astype(jnp.float32),
        lax.psum(output_stack.astype(jnp.bfloat16), "seq").astype(jnp.float32),
        lax.psum(upper_stack.astype(jnp.bfloat16), "seq").astype(jnp.float32),
        lax.psum(upper_bias_stack.astype(jnp.bfloat16), "seq").astype(jnp.float32),
        lax.psum(lower_stack.astype(jnp.bfloat16), "seq").astype(jnp.float32),
        lax.psum(branch_stack.astype(jnp.bfloat16), "seq").astype(jnp.float32),
    )
    return (
        result,
        grad_hidden[None],
        summed[0],
        summed[1],
        summed[2],
        summed[3],
        summed[4],
        summed[8],
        summed[5],
        summed[6],
        summed[7],
        summed[8],
    )


SIDE = 4
GROUP = SIDE * SIDE
OWN = HEADS // GROUP
HEAD_COLS = OWN * HEAD_DIM
JOINT_COLS = 3 * HEAD_COLS
FEED_COLS = FF // GROUP
COLS = JOINT_COLS + FEED_COLS
BACK_COLS = HEAD_COLS + FEED_COLS
SHARE = D // GROUP
VMEM = pl.BlockSpec(memory_space=pltpu.VMEM)
HBM = pl.BlockSpec(memory_space=pl.ANY)
MESH = pl.DeviceIdType.MESH
ROOM = 60 * 2**20


def dot(left, right, left_dim=1, right_dim=0):
    return lax.dot_general(
        left, right, (((left_dim,), (right_dim,)), ((), ())), preferred_element_type=jnp.float32
    )


def digit(entries, index):
    words = [
        sum(entry << (2 * place) for place, entry in enumerate(entries[start : start + 8]))
        for start in range(0, len(entries), 8)
    ]
    word = jnp.int32(words[0])
    for number in range(1, len(words)):
        word = jnp.where(index >= 8 * number, jnp.int32(words[number]), word)
    return lax.rem(lax.shift_right_logical(word, 2 * lax.rem(index, 8)), 4)


def digit_of_row(table, row, index):
    value = digit(table[0], index)
    for number in range(1, len(table)):
        value = jnp.where(row == number, digit(table[number], index), value)
    return value


NEAR = ((0, 1, 2, 3), (1, 0, 2, 3), (2, 3, 1, 0), (3, 2, 1, 0))
FAR = ((3, 2, 1, 0), (3, 0, 2, 1), (0, 3, 1, 2), (0, 1, 2, 3))


def neighbours():
    ctx, place = lax.axis_index("ctx"), lax.axis_index("fsdp")
    twin = ctx + 1 - 2 * lax.rem(ctx, 2)
    across = lax.rem(ctx + 2, 4)
    return ctx, place, twin, across, lax.rem(twin + 2, 4)


def greet_neighbours():
    ctx, place, twin, across, _ = neighbours()
    barrier = pltpu.get_barrier_semaphore()
    pl.semaphore_signal(barrier, inc=1, device_id={"ctx": twin}, device_id_type=MESH)
    pl.semaphore_signal(barrier, inc=1, device_id={"ctx": across}, device_id_type=MESH)

    @pl.when(place > 0)
    def _():
        pl.semaphore_signal(barrier, inc=1, device_id={"fsdp": place - 1}, device_id_type=MESH)

    @pl.when(place < SIDE - 1)
    def _():
        pl.semaphore_signal(barrier, inc=1, device_id={"fsdp": place + 1}, device_id_type=MESH)

    inner = jnp.int32(2) + jnp.where(place > 0, 1, 0) + jnp.where(place < SIDE - 1, 1, 0)
    pl.semaphore_wait(barrier, inner)


def greet_plane(steps, cross=True):
    ctx, place = lax.axis_index("ctx"), lax.axis_index("fsdp")
    me = ctx * SIDE + place
    barrier = pltpu.get_barrier_semaphore()
    for step in range(1, steps):
        peer = lax.rem(me + step, GROUP)
        pl.semaphore_signal(
            barrier,
            inc=1,
            device_id={"ctx": peer // SIDE, "fsdp": lax.rem(peer, SIDE)},
            device_id_type=MESH,
        )
    if cross:
        pl.semaphore_signal(
            barrier, inc=1, device_id={"seq": 1 - lax.axis_index("seq")}, device_id_type=MESH
        )
    pl.semaphore_wait(barrier, steps if cross else steps - 1)


def to_peer(source, target, send, recv, peer):
    return pltpu.make_async_remote_copy(
        src_ref=source,
        dst_ref=target,
        send_sem=send,
        recv_sem=recv,
        device_id={"ctx": peer // SIDE, "fsdp": lax.rem(peer, SIDE)},
        device_id_type=MESH,
    )


def to_axis(source, target, send, recv, axis, index):
    return pltpu.make_async_remote_copy(
        src_ref=source,
        dst_ref=target,
        send_sem=send,
        recv_sem=recv,
        device_id={axis: index},
        device_id_type=MESH,
    )


PARTS = ((0, 112), (112, 96), (208, 48))
LAST = len(PARTS) - 1
GATHER_KIND = (
    (0, 0, 0, 0, 0, 1, 0, 0, 1, 0, 2, 0, 1, 1, 1, 2, 0, 0, 1, 0, 1, 3, 2, 1, 0, 3, 1, 1, 1, 1, 0, 3, 0, 0, 1, 1, 1, 1, 2, 3),
    (0, 0, 0, 1, 0, 0, 0, 0, 0, 0, 0, 0, 1, 0, 2, 1, 2, 1, 0, 1, 1, 2, 0, 3, 1, 1, 0, 1, 1, 1, 3, 1, 1, 0, 1, 3, 1, 1, 2, 3),
)
GATHER_STEP = (
    (0, 0, 1, 0, 0, 0, 1, 1, 0, 1, 0, 2, 0, 0, 1, 1, 2, 2, 1, 2, 1, 0, 2, 1, 3, 1, 2, 2, 2, 2, 3, 2, 3, 3, 3, 3, 3, 3, 3, 3),
    (0, 0, 0, 0, 2, 2, 1, 0, 1, 2, 1, 1, 0, 2, 0, 0, 2, 0, 3, 2, 2, 1, 3, 0, 2, 1, 3, 1, 2, 1, 2, 3, 1, 3, 3, 1, 3, 3, 3, 3),
)
GATHER_PART = (
    (1, 0, 1, 2, 3, 1, 2, 0, 0, 3, 3, 2, 2, 3, 0, 3, 1, 0, 1, 3, 2, 3, 3, 3, 0, 3, 1, 2, 0, 3, 1, 3, 2, 3, 1, 0, 2, 3, 3, 3),
    (1, 0, 2, 0, 2, 0, 2, 3, 1, 1, 0, 3, 2, 3, 3, 1, 3, 3, 0, 0, 2, 3, 1, 3, 1, 1, 2, 2, 3, 0, 3, 2, 3, 3, 0, 3, 1, 3, 3, 3),
)
OPS = len(GATHER_KIND[0])
WORKS = tuple(
    tuple(
        number for number in range(OPS) if parts[number] == 3
    )
    for parts in GATHER_PART
)


def by_place(tables, index):
    place = lax.axis_index("fsdp")
    at_end = (place == 0) | (place == SIDE - 1)
    return jnp.where(at_end, digit(tables[0], index), digit(tables[1], index))


def gather_slot(kind, step):
    ctx, place, twin, across, twin_across = neighbours()
    line = digit_of_row(NEAR, place, step)
    owner = jnp.where(
        kind == 0, ctx, jnp.where(kind == 1, across, jnp.where(kind == 2, twin, twin_across))
    )
    return line, owner * SIDE + line


def work_slot(number):
    kind = by_place(
        tuple(tuple(row[at] for at in places) for row, places in zip(GATHER_KIND, WORKS)), number
    )
    step = by_place(
        tuple(tuple(row[at] for at in places) for row, places in zip(GATHER_STEP, WORKS)), number
    )
    return gather_slot(kind, step)[1]


def gather_blocks(land, every, up, down, side, core, arrived, core_arrived, kept, work):
    ctx, place, twin, across, _ = neighbours()

    def copies(kind, line, slot, part):
        start, size = PARTS[part]
        block = land.at[slot, pl.ds(start, size)]
        row, met = kind * SIDE + line, arrived.at[slot, part]
        return (
            lambda: to_axis(block, block, up.at[row, part], met, "fsdp", place + 1),
            lambda: to_axis(block, block, down.at[row, part], met, "fsdp", place - 1),
            lambda: to_axis(block, block, side.at[line, part], met, "ctx", across),
        )

    def routes(kind, line, part):
        goes_up = (line <= place) & (place < SIDE - 1)
        goes_down = (line >= place) & (place > 0)
        if part == LAST:
            return goes_up, goes_down, (kind == 0) & (line == place)
        return goes_up & (kind == 0), goes_down & (kind == 0), kind == 0

    def core_copy(kind, line, slot):
        block = land.at[slot]
        return to_axis(
            block, block, core.at[kind * SIDE + line], core_arrived.at[slot], "ctx", twin
        )

    def step_op(number, worked):
        kind, step = by_place(GATHER_KIND, number), by_place(GATHER_STEP, number)
        part = by_place(GATHER_PART, number)
        line, slot = gather_slot(kind, step)
        for which in range(len(PARTS)):

            @pl.when(part == which)
            def _(which=which):
                @pl.when((kind == 1) | (line != place))
                def _():
                    copies(kind, line, slot, which)[2]().wait_recv()

                for copy, goes in zip(
                    copies(kind, line, slot, which), routes(kind, line, which)
                ):

                    @pl.when(goes)
                    def _(copy=copy):
                        copy().start()

        @pl.when(part == 3)
        def _():
            @pl.when(kind <= 1)
            def _():
                core_copy(kind, line, slot).start()

            @pl.when(kind >= 2)
            def _():
                core_copy(kind - 2, line, slot).wait_recv()

            if every is not None:
                pltpu.make_async_copy(land.at[slot], every.at[slot], kept.at[slot]).start()
            work(worked, slot)

        return worked + jnp.where(part == 3, 1, 0)

    lax.fori_loop(0, OPS, step_op, jnp.int32(0))

    def finish(number, carry):
        kind, line = number // SIDE, lax.rem(number, SIDE)
        slot = jnp.where(kind == 0, ctx, across) * SIDE + line
        for which in range(len(PARTS)):
            for copy, goes in zip(copies(kind, line, slot, which), routes(kind, line, which)):

                @pl.when(goes)
                def _(copy=copy):
                    copy().wait_send()

        core_copy(kind, line, slot).wait_send()
        return carry

    lax.fori_loop(0, 2 * SIDE, finish, 0)

    def finish_kept(slot, carry):
        pltpu.make_async_copy(land.at[slot], every.at[slot], kept.at[slot]).wait()
        return carry

    if every is not None:
        lax.fori_loop(0, GROUP, finish_kept, 0)


def gather_scratch(rows):
    parts = len(PARTS)
    return [
        pltpu.VMEM((GROUP, rows, D), jnp.bfloat16),
        pltpu.SemaphoreType.DMA((2 * SIDE, parts)),
        pltpu.SemaphoreType.DMA((2 * SIDE, parts)),
        pltpu.SemaphoreType.DMA((SIDE, parts)),
        pltpu.SemaphoreType.DMA((2 * SIDE,)),
        pltpu.SemaphoreType.DMA((GROUP, parts)),
        pltpu.SemaphoreType.DMA((GROUP,)),
        pltpu.SemaphoreType.DMA((GROUP,)),
    ]


def spin(values, cosine, sine, sign):
    lane = lax.rem(lax.broadcasted_iota(jnp.int32, values.shape, 1), HEAD_DIM)
    partner = jnp.where(
        lane < ROT // 2,
        -pltpu.roll(values, HEAD_COLS - ROT // 2, 1),
        pltpu.roll(values, ROT // 2, 1),
    )
    return values * cosine + sign * (partner * sine)


STRIP = 32


def each_strip(rows, body, start):
    def step(number, carry):
        return body(pl.ds(pl.multiple_of(number * STRIP, STRIP), STRIP), carry)

    return lax.fori_loop(0, rows // STRIP, step, start)


def column_places(block):
    return [
        (0, pl.multiple_of(part * D + block * HEAD_COLS, HEAD_COLS), part * HEAD_COLS, HEAD_COLS)
        for part in range(3)
    ] + [(1, pl.multiple_of(block * FEED_COLS, FEED_COLS), JOINT_COLS, FEED_COLS)]


PLACES = 4


def load_all(pairs, sems):
    copies = [
        pltpu.make_async_copy(source, target, sems.at[number])
        for number, (source, target) in enumerate(pairs)
    ]
    for copy in copies:
        copy.start()
    return copies


def wait_all(copies):
    for copy in copies:
        copy.wait()


def forward_gather(hidden, gain, shift, bias, turns, sources, layer):
    rows = hidden.shape[0]
    half = SHARE // 2
    first = layer == 0

    def kernel(hidden, gain, shift, bias, turn_a, turn_b, source_a, source_b, *refs):
        every, columns_out, results, refs = refs[0], refs[1], refs[2:7], refs[7:]
        rings, ring_sem, refs = refs[-6:-1], refs[-1], refs[:-6]
        cosine, sine, refs = refs[0], refs[1], refs[2:]
        columns, plane_send, plane_recv, cross_send, cross_recv, own_sem, saved = refs[:7]
        land = refs[7]
        query, key, value, inner, active = rings
        ctx, place, seq = lax.axis_index("ctx"), lax.axis_index("fsdp"), lax.axis_index("seq")
        me = ctx * SIDE + place
        part_rows = pl.ds(pl.multiple_of(seq * half, half), half)
        other_rows = pl.ds(pl.multiple_of((1 - seq) * half, half), half)
        if first:
            greet_plane(GROUP)
        else:
            greet_neighbours()
        sources = (source_a, source_b)

        def piece(step, number):
            peer = lax.rem(me + step, GROUP)
            which, start, at, width = column_places(peer)[number]
            return (
                peer,
                sources[which].at[layer, part_rows, pl.ds(start, width)],
                columns.at[me, part_rows, pl.ds(at, width)],
            )

        def send_piece(step, number):
            peer, source, target = piece(step, number)
            return to_peer(
                source, target, plane_send.at[step, number], plane_recv.at[me, number], peer
            )

        def own_piece(number):
            _, source, target = piece(0, number)
            return pltpu.make_async_copy(source, target, own_sem.at[number])

        def cross(source):
            block = columns.at[source, part_rows]
            return to_axis(
                block, block, cross_send.at[source], cross_recv.at[source], "seq", 1 - seq
            )

        if first:
            for number in range(PLACES):
                own_piece(number).start()
        else:
            halves = load_all(
                (
                    (source_a, columns.at[:, part_rows]),
                    (source_b, columns.at[:, other_rows]),
                    (turn_a, cosine),
                    (turn_b, sine),
                ),
                own_sem,
            )

        def send_columns(step, carry):
            for number in range(PLACES):
                send_piece(step, number).start()
            return carry

        def strip(part, carry):
            values = hidden[part].astype(jnp.float32)
            centred = values - jnp.mean(values, axis=1, keepdims=True)
            spread = jnp.mean(centred * centred, axis=1, keepdims=True)
            normed = centred * lax.rsqrt(spread + EPS) * gain[...] + shift[...]
            land[me, part] = normed.astype(jnp.bfloat16)
            return carry

        each_strip(rows, strip, 0)

        def pass_on(step):
            source = lax.rem(me + GROUP - step, GROUP)

            @pl.when(step == 0)
            def _():
                for number in range(PLACES):
                    own_piece(number).wait()

            @pl.when(step > 0)
            def _():
                for number in range(PLACES):
                    _, _, at, width = column_places(0)[number]
                    target = columns.at[source, part_rows, pl.ds(at, width)]
                    to_peer(
                        target, target, plane_send.at[0, number], plane_recv.at[source, number], source
                    ).wait_recv()

            cross(source).start()

        def leave(number):
            at = lax.rem(number, 2)
            return [
                pltpu.make_async_copy(
                    ring.at[at], result.at[work_slot(number)], ring_sem.at[at, which]
                )
                for which, (ring, result) in enumerate(zip(rings, results))
            ]

        def product(number, slot):
            whole = dot(land[slot], columns[...].reshape(D, COLS)) + bias[...]
            one, two = HEAD_COLS, 2 * HEAD_COLS
            at = lax.rem(number, 2)

            @pl.when(number >= 2)
            def _():
                wait_all(leave(number - 2))

            query[at] = spin(whole[:, :one], cosine[slot], sine[slot], 1.0).astype(jnp.bfloat16)
            key[at] = spin(whole[:, one:two], cosine[slot], sine[slot], 1.0).astype(jnp.bfloat16)
            value[at] = whole[:, two:JOINT_COLS].astype(jnp.bfloat16)
            units = whole[:, JOINT_COLS:]
            inner[at] = units
            active[at] = jax.nn.gelu(units, approximate=True).astype(jnp.bfloat16)
            for copy in leave(number):
                copy.start()

        save = pltpu.make_async_copy(columns, columns_out, saved)

        def work_as_columns_come(number, slot):
            @pl.when(number == 0)
            def _():
                lax.fori_loop(1, GROUP, send_columns, 0)

            angle = turn_a[slot] * turn_b[...]
            cosine[slot] = jnp.cos(angle)
            sine[slot] = jnp.sin(angle)

            @pl.when(number < GROUP // 2)
            def _():
                pass_on(2 * number)
                pass_on(2 * number + 1)

            @pl.when(number == GROUP // 2)
            def _():
                def arrive(source, carry):
                    block = columns.at[source, part_rows]
                    to_axis(
                        block, block, cross_send.at[source], cross_recv.at[source], "seq", 1 - seq
                    ).wait_recv()
                    return carry

                lax.fori_loop(0, GROUP, arrive, 0)
                save.start()

            @pl.when(number >= GROUP // 2)
            def _():
                def two_products(more, carry):
                    which = 2 * number - GROUP + more
                    product(which, work_slot(which))
                    return carry

                lax.fori_loop(0, 2, two_products, 0)

        def work(number, slot):
            @pl.when(number == 0)
            def _():
                wait_all(halves)
                save.start()

            product(number, slot)

        gather_blocks(land, every, *refs[8:], work_as_columns_come if first else work)
        save.wait()
        for number in (GROUP - 2, GROUP - 1):
            wait_all(leave(jnp.int32(number)))

        def end(step, carry):
            cross(step).wait_send()

            @pl.when(step > 0)
            def _():
                for number in range(PLACES):
                    send_piece(step, number).wait_send()

            return carry

        if first:
            lax.fori_loop(0, GROUP, end, 0)

    def out(width, dtype):
        return jax.ShapeDtypeStruct((GROUP, rows, width), dtype)

    out_shape = [
        out(D, jnp.bfloat16),
        jax.ShapeDtypeStruct((GROUP, SHARE, COLS), jnp.bfloat16),
        out(HEAD_COLS, jnp.bfloat16),
        out(HEAD_COLS, jnp.bfloat16),
        out(HEAD_COLS, jnp.bfloat16),
        out(FEED_COLS, jnp.float32),
        out(FEED_COLS, jnp.bfloat16),
    ] + [out(HEAD_COLS, jnp.float32)] * (2 if first else 0)
    return pl.pallas_call(
        kernel,
        out_shape=out_shape,
        in_specs=[VMEM] * 4 + [VMEM if first else HBM] * 2 + [HBM] * 2,
        out_specs=[HBM] * 7 + [VMEM] * (len(out_shape) - 7),
        scratch_shapes=([] if first else [pltpu.VMEM((GROUP, rows, HEAD_COLS), jnp.float32)] * 2)
        + [
            pltpu.VMEM((GROUP, SHARE, COLS), jnp.bfloat16),
            pltpu.SemaphoreType.DMA((GROUP, PLACES)),
            pltpu.SemaphoreType.DMA((GROUP, PLACES)),
            pltpu.SemaphoreType.DMA((GROUP,)),
            pltpu.SemaphoreType.DMA((GROUP,)),
            pltpu.SemaphoreType.DMA((PLACES,)),
            pltpu.SemaphoreType.DMA,
        ]
        + gather_scratch(rows)
        + [
            pltpu.VMEM((2, rows, HEAD_COLS), jnp.bfloat16),
            pltpu.VMEM((2, rows, HEAD_COLS), jnp.bfloat16),
            pltpu.VMEM((2, rows, HEAD_COLS), jnp.bfloat16),
            pltpu.VMEM((2, rows, FEED_COLS), jnp.float32),
            pltpu.VMEM((2, rows, FEED_COLS), jnp.bfloat16),
            pltpu.SemaphoreType.DMA((2, 5)),
        ],
        compiler_params=pltpu.CompilerParams(
            collective_id=30 + layer, has_side_effects=True, vmem_limit_bytes=ROOM
        ),
    )(hidden, gain, shift, bias, *turns, *sources)


def backward_gather(grad, out_weight, down_weight, inner, mixed, active):
    rows = grad.shape[0]

    def kernel(own, out_weight, down_weight, inner, mixed, active, grad_mixed, grad_inner, branch, *refs):
        out_part, down_part, weight_sem, total = refs[:4]
        fetched, fetch_sem, rings, ring_sem = refs[4:7], refs[7], refs[8:10], refs[10]
        land, sems = refs[11], refs[12:]
        inner_part, mixed_part, active_part = fetched
        ctx, place, _, _, _ = neighbours()

        def fetch(number):
            at, slot = lax.rem(number, 2), work_slot(number)
            return [
                pltpu.make_async_copy(source.at[slot], target.at[at], fetch_sem.at[at, which])
                for which, (source, target) in enumerate(zip((inner, mixed, active), fetched))
            ]

        def leave(number):
            at, slot = lax.rem(number, 2), work_slot(number)
            return [
                pltpu.make_async_copy(ring.at[at], result.at[slot], ring_sem.at[at, which])
                for which, (ring, result) in enumerate(zip(rings, (grad_mixed, grad_inner)))
            ]

        weights = load_all(((out_weight, out_part), (down_weight, down_part)), weight_sem)
        for copy in fetch(jnp.int32(0)):
            copy.start()
        greet_neighbours()
        land[ctx * SIDE + place] = own[...]
        total[...] = jnp.zeros_like(total)

        def work(number, slot):
            at = lax.rem(number, 2)

            @pl.when(number == 0)
            def _():
                wait_all(weights)

            @pl.when(number + 1 < GROUP)
            def _():
                for copy in fetch(number + 1):
                    copy.start()

            @pl.when(number >= 2)
            def _():
                wait_all(leave(number - 2))

            wait_all(fetch(number))
            block = land[slot]
            rings[0][at] = dot(block, out_part[...], 1, 1)
            value = inner_part[at]
            factor = math.sqrt(2.0 / math.pi)
            square = value * value
            bend = jnp.tanh(factor * value * (1.0 + 0.044715 * square))
            slope = 0.5 * (1.0 + bend) + 0.5 * value * (1.0 - bend * bend) * (
                factor * (1.0 + 3 * 0.044715 * square)
            )
            rings[1][at] = (dot(block, down_part[...], 1, 1) * slope).astype(jnp.bfloat16)
            for copy in leave(number):
                copy.start()
            total[:HEAD_COLS] += dot(mixed_part[at], block, 0, 0)
            total[HEAD_COLS:] += dot(active_part[at], block, 0, 0)

        gather_blocks(land, None, *sems, work)
        branch[...] = total[...].astype(jnp.bfloat16)
        for number in (GROUP - 2, GROUP - 1):
            wait_all(leave(jnp.int32(number)))

    return pl.pallas_call(
        kernel,
        out_shape=(
            jax.ShapeDtypeStruct((GROUP, rows, HEAD_COLS), jnp.float32),
            jax.ShapeDtypeStruct((GROUP, rows, FEED_COLS), jnp.bfloat16),
            jax.ShapeDtypeStruct((BACK_COLS, D), jnp.bfloat16),
        ),
        in_specs=[VMEM] + [HBM] * 5,
        out_specs=(HBM, HBM, VMEM),
        scratch_shapes=[
            pltpu.VMEM(out_weight.shape, jnp.bfloat16),
            pltpu.VMEM(down_weight.shape, jnp.bfloat16),
            pltpu.SemaphoreType.DMA((2,)),
            pltpu.VMEM((BACK_COLS, D), jnp.float32),
            pltpu.VMEM((2, rows, FEED_COLS), jnp.float32),
            pltpu.VMEM((2, rows, HEAD_COLS), jnp.bfloat16),
            pltpu.VMEM((2, rows, FEED_COLS), jnp.bfloat16),
            pltpu.SemaphoreType.DMA((2, 3)),
            pltpu.VMEM((2, rows, HEAD_COLS), jnp.float32),
            pltpu.VMEM((2, rows, FEED_COLS), jnp.bfloat16),
            pltpu.SemaphoreType.DMA((2, 2)),
        ]
        + gather_scratch(rows),
        compiler_params=pltpu.CompilerParams(
            collective_id=4, has_side_effects=True, vmem_limit_bytes=ROOM
        ),
    )(grad, out_weight, down_weight, inner, mixed, active)


SCATTER_OPS = (
    ((0, 0), (0, 1), (1, 0), (2, 0), (1, 1), (0, 2), (2, 1), (3, 0), (1, 2), (2, 2), (4, 0), (6, 0), (5, 0), (0, 3), (3, 1), (3, 2), (1, 3), (3, 3), (4, 1), (5, 1), (6, 1), (4, 2), (5, 2), (6, 2), (2, 3), (4, 3), (5, 3), (6, 3)),
    ((0, 0), (0, 2), (3, 2), (1, 0), (3, 0), (0, 1), (0, 3), (1, 1), (2, 0), (1, 2), (3, 1), (1, 3), (4, 0), (6, 0), (5, 0), (3, 3), (2, 1), (2, 2), (4, 1), (6, 1), (5, 1), (4, 2), (5, 2), (6, 2), (2, 3), (4, 3), (5, 3), (6, 3)),
)
SCATTER_OPS_WORK = (
    ((0, 0), (0, 1), (1, 0), (2, 0), (1, 1), (0, 2), (2, 1), (3, 0), (1, 2), (2, 2), (4, 0), (6, 0), (7, 0), (5, 0), (0, 3), (3, 1), (3, 2), (1, 3), (3, 3), (4, 1), (7, 0), (5, 1), (7, 0), (7, 0), (7, 0), (7, 0), (7, 0), (6, 1), (4, 2), (7, 0), (5, 2), (7, 0), (7, 0), (7, 0), (6, 2), (2, 3), (7, 0), (7, 0), (7, 0), (7, 0), (7, 0), (4, 3), (5, 3), (6, 3)),
    ((0, 0), (0, 2), (3, 2), (1, 0), (3, 0), (7, 0), (0, 1), (0, 3), (1, 1), (2, 0), (1, 2), (3, 1), (7, 0), (7, 0), (1, 3), (4, 0), (6, 0), (7, 0), (5, 0), (7, 0), (7, 0), (3, 3), (2, 1), (7, 0), (2, 2), (7, 0), (7, 0), (4, 1), (6, 1), (5, 1), (4, 2), (5, 2), (7, 0), (7, 0), (7, 0), (6, 2), (7, 0), (7, 0), (7, 0), (2, 3), (7, 0), (4, 3), (5, 3), (6, 3)),
)
SCATTER_OPS_EARLY = (
    ((0, 0), (0, 1), (1, 0), (3, 0), (2, 0), (0, 2), (1, 1), (2, 1), (1, 2), (2, 2), (0, 3), (4, 0), (6, 0), (7, 0), (7, 0), (7, 0), (5, 0), (7, 0), (3, 1), (1, 3), (7, 0), (7, 0), (7, 0), (4, 1), (7, 0), (7, 0), (7, 0), (6, 1), (7, 0), (5, 1), (7, 0), (7, 0), (7, 0), (7, 0), (7, 0), (3, 2), (3, 3), (2, 3), (4, 2), (5, 2), (6, 2), (8, 0), (8, 1), (8, 2), (8, 3), (4, 3), (5, 3), (6, 3)),
    ((0, 2), (7, 0), (0, 0), (0, 1), (1, 0), (7, 0), (7, 0), (0, 3), (7, 0), (3, 3), (3, 0), (7, 0), (1, 1), (2, 0), (3, 2), (1, 2), (7, 0), (2, 2), (7, 0), (7, 0), (3, 1), (1, 3), (4, 0), (6, 0), (7, 0), (2, 1), (7, 0), (7, 0), (7, 0), (5, 0), (7, 0), (7, 0), (7, 0), (7, 0), (2, 3), (4, 1), (6, 1), (5, 1), (4, 2), (5, 2), (6, 2), (8, 0), (8, 1), (8, 2), (8, 3), (4, 3), (5, 3), (6, 3)),
)
SPLIT = ((0, 208), (208, 48))


def nibble(entries, index):
    word = jnp.int32(0)
    for start in range(0, len(entries), 7):
        packed = sum(entry << (4 * place) for place, entry in enumerate(entries[start : start + 7]))
        word = jnp.where(index >= start, jnp.int32(packed), word)
    return lax.rem(lax.shift_right_logical(word, 4 * lax.rem(index, 7)), 16)


def scatter_events(partial, other_work, late_work, ops, scratch):
    total, give, take, side_take, line_take, other_take = scratch[:6]
    core_send, core_recv, side_send, side_recv, line_send, line_recv = scratch[6:12]
    other_send, other_recv = scratch[12:]
    ctx, place, twin, across, twin_across = neighbours()
    below, above = place - 1, place + 1
    has_below, has_above = place > 0, place < SIDE - 1
    at_end = (place == 0) | (place == SIDE - 1)

    def rows_of(part):
        return pl.ds(*SPLIT[part])

    def core_copy(step, store):
        return to_axis(
            give.at[step], take.at[store], core_send.at[store], core_recv.at[store], "ctx", twin
        )

    def side_copy(step, part):
        return to_axis(
            take.at[step, rows_of(part)],
            side_take.at[step, rows_of(part)],
            side_send.at[step, part],
            side_recv.at[step, part],
            "ctx",
            across,
        )

    def line_copy(step, line, slot, target, part):
        return to_axis(
            take.at[SIDE + step, rows_of(part)],
            line_take.at[slot, rows_of(part)],
            line_send.at[line, part],
            line_recv.at[slot, part],
            "fsdp",
            target,
        )

    def other_copy(step, line, slot, target):
        return to_axis(
            take.at[step, rows_of(1)],
            other_take.at[slot],
            other_send.at[line],
            other_recv.at[slot],
            "fsdp",
            target,
        )

    def from_above(line):
        return jnp.where(line == place, SIDE, line)

    def to_below(line):
        return jnp.where(line == place - 1, SIDE, line)

    def one(number, turn):
        def by_end(field):
            ends, middle = (tuple(entry[field] for entry in table) for table in ops)
            return jnp.where(at_end, nibble(ends, number), nibble(middle, number))

        what, step = by_end(0), by_end(1)
        line = digit_of_row(FAR, place, step)

        @pl.when((what <= 1) | (what == 3) | (what == 4))
        def _():
            owner = jnp.where(
                what == 0,
                twin_across,
                jnp.where(what == 1, across, jnp.where(what == 3, twin, ctx)),
            )
            total[...] = partial(owner * SIDE + line)

        @pl.when(what == 0)
        def _():
            give[step] = total[...].astype(jnp.bfloat16)
            core_copy(step, step).start()

        @pl.when(what == 1)
        def _():
            core_copy(step, step).wait_recv()
            take[step] = (total[...] + take[step].astype(jnp.float32)).astype(jnp.bfloat16)
            side_copy(step, 0).start()

        @pl.when(what == 2)
        def _():
            rows = rows_of(1)

            @pl.when((line >= place) & has_below)
            def _():
                other_copy(step, line, line, below).wait_recv()
                take[step, rows] = (
                    take[step, rows].astype(jnp.float32) + other_take[line].astype(jnp.float32)
                ).astype(jnp.bfloat16)

            @pl.when((line <= place) & has_above)
            def _():
                other_copy(step, line, from_above(line), above).wait_recv()
                take[step, rows] = (
                    take[step, rows].astype(jnp.float32)
                    + other_take[from_above(line)].astype(jnp.float32)
                ).astype(jnp.bfloat16)

            @pl.when(line > place)
            def _():
                other_copy(step, line, line, above).start()

            @pl.when(line < place)
            def _():
                other_copy(step, line, to_below(line), below).start()

            @pl.when(line == place)
            def _():
                side_copy(step, 1).start()

        @pl.when(what == 3)
        def _():
            core_copy(step, step).wait_send()
            give[step] = total[...].astype(jnp.bfloat16)
            core_copy(step, SIDE + step).start()

        @pl.when(what == 4)
        def _():
            core_copy(step, SIDE + step).wait_recv()
            total[...] += take[SIDE + step].astype(jnp.float32)

        for part in range(2):
            rows = rows_of(part)

            @pl.when(what == 5 + part)
            def _(rows=rows, part=part):
                crossed = line == place if part == 1 else line >= 0

                @pl.when(crossed)
                def _():
                    side_copy(step, part).wait_recv()
                    total[rows] += side_take[step, rows].astype(jnp.float32)

                @pl.when((line >= place) & has_below)
                def _():
                    line_copy(step, line, line, below, part).wait_recv()
                    total[rows] += line_take[line, rows].astype(jnp.float32)

                @pl.when((line <= place) & has_above)
                def _():
                    line_copy(step, line, from_above(line), above, part).wait_recv()
                    total[rows] += line_take[from_above(line), rows].astype(jnp.float32)

                @pl.when(line > place)
                def _():
                    take[SIDE + step, rows] = total[rows].astype(jnp.bfloat16)
                    line_copy(step, line, line, above, part).start()

                @pl.when(line < place)
                def _():
                    take[SIDE + step, rows] = total[rows].astype(jnp.bfloat16)
                    line_copy(step, line, to_below(line), below, part).start()

        if other_work is not None:

            @pl.when(what == 7)
            def _():
                other_work(turn)

        if late_work is not None:

            @pl.when(what == 8)
            def _():
                late_work(step)

        return turn + jnp.where(what == 7, 1, 0)

    lax.fori_loop(0, len(ops[0]), one, jnp.int32(0))

    def finish(step, carry):
        line = digit_of_row(FAR, place, step)
        core_copy(step, SIDE + step).wait_send()
        side_copy(step, 0).wait_send()

        @pl.when(line == place)
        def _():
            side_copy(step, 1).wait_send()

        @pl.when(line != place)
        def _():
            for part in range(2):
                line_copy(step, line, line, place, part).wait_send()
            other_copy(step, line, line, place).wait_send()

        return carry

    lax.fori_loop(0, SIDE, finish, 0)


def scatter_scratch(rows):
    return [
        pltpu.VMEM((rows, D), jnp.float32),
        pltpu.VMEM((SIDE, rows, D), jnp.bfloat16),
        pltpu.VMEM((2 * SIDE, rows, D), jnp.bfloat16),
        pltpu.VMEM((SIDE, rows, D), jnp.bfloat16),
        pltpu.VMEM((SIDE + 1, rows, D), jnp.bfloat16),
        pltpu.VMEM((SIDE + 1, SPLIT[1][1], D), jnp.bfloat16),
        pltpu.SemaphoreType.DMA((2 * SIDE,)),
        pltpu.SemaphoreType.DMA((2 * SIDE,)),
        pltpu.SemaphoreType.DMA((SIDE, 2)),
        pltpu.SemaphoreType.DMA((SIDE, 2)),
        pltpu.SemaphoreType.DMA((SIDE, 2)),
        pltpu.SemaphoreType.DMA((SIDE + 1, 2)),
        pltpu.SemaphoreType.DMA((SIDE,)),
        pltpu.SemaphoreType.DMA((SIDE + 1,)),
    ]


def forward_scatter(hidden, bias, mixed, active, out_weight, down_weight, layer):
    rows = hidden.shape[0]

    def kernel(hidden, bias, mixed, active, out_weight, down_weight, out, *refs):
        hidden_part, mixed_part, active_part, out_part, down_part, load_sem = refs[:6]
        scratch = refs[6:]
        loads = load_all(
            (
                (mixed, mixed_part),
                (active, active_part),
                (out_weight, out_part),
                (down_weight, down_part),
                (hidden, hidden_part),
            ),
            load_sem,
        )
        greet_neighbours()
        wait_all(loads[:4])

        def partial(slot):
            return dot(mixed_part[slot], out_part[...]) + dot(active_part[slot], down_part[...])

        scatter_events(partial, None, None, SCATTER_OPS, scratch)
        loads[4].wait()
        out[...] = hidden_part[...].astype(jnp.float32) + (scratch[0][...] + bias[...])

    return pl.pallas_call(
        kernel,
        out_shape=jax.ShapeDtypeStruct((rows, D), jnp.float32),
        in_specs=[HBM, VMEM] + [HBM] * 4,
        out_specs=VMEM,
        scratch_shapes=[
            pltpu.VMEM(array.shape, array.dtype)
            for array in (hidden, mixed, active, out_weight, down_weight)
        ]
        + [pltpu.SemaphoreType.DMA((5,))]
        + scatter_scratch(rows),
        compiler_params=pltpu.CompilerParams(
            collective_id=10 + layer, has_side_effects=True, vmem_limit_bytes=ROOM
        ),
    )(hidden, bias, mixed, active, out_weight, down_weight)


SMALL_ROWS = 16


def backward_scatter(hidden, grad, gain, grad_joint, grad_inner, columns, every, layer, up=None):
    rows = hidden.shape[0]
    half = SHARE // 2
    collects = up is not None
    made = JOINT_COLS if collects else COLS
    tokens = GROUP * rows

    def kernel(*refs):
        inputs, refs = refs[: 8 if collects else 7], refs[8 if collects else 7 :]
        gain, every = inputs[2], inputs[6]
        out, small_out, refs = refs[0], refs[1], refs[2:]
        if collects:
            outputs, refs = refs[:2], refs[2:]
        else:
            mine, refs = refs[0], refs[1:]
        hidden, grad, grad_joint, grad_inner, columns, load_sem, strips, load = refs[:8]
        shares, small_land, small_mine, small_other = refs[8:12]
        small_send, small_recv, swap_send, swap_recv = refs[12:16]
        refs = refs[16:]
        if collects:
            mine, other, summed, arrived, arrived_up = refs[:5]
            cross_send, cross_recv, plane_send, plane_recv = refs[5:9]
            back_send, back_recv, keep = refs[9:12]
            up_send, up_recv, up_own = refs[12:15]
            refs = refs[15:]
        scratch = refs
        total = scratch[0]
        ctx, place, seq = lax.axis_index("ctx"), lax.axis_index("fsdp"), lax.axis_index("seq")
        me = ctx * SIDE + place
        part_rows = pl.ds(pl.multiple_of(seq * half, half), half)
        other_rows = pl.ds(pl.multiple_of((1 - seq) * half, half), half)

        def block_of(turn):
            return lax.rem(me + 1 + turn, GROUP)

        def load_strip(turn):
            start = pl.multiple_of(block_of(turn) * SHARE, SHARE)
            buffer = lax.rem(turn, 2)
            return pltpu.make_async_copy(
                every.at[:, :, pl.ds(start, SHARE)], strips.at[buffer], load.at[buffer]
            )

        loads = load_all(
            (
                (inputs[3], grad_joint),
                (inputs[4], grad_inner),
                (inputs[5], columns),
                (inputs[0], hidden),
                (inputs[1], grad),
            ),
            load_sem,
        )
        load_strip(jnp.int32(0)).start()
        greet_plane(GROUP)

        def partial(slot):
            return dot(grad_joint[slot], columns[:, :JOINT_COLS], 1, 1) + dot(
                grad_inner[slot], columns[:, JOINT_COLS:], 1, 1
            )

        def product(turn):
            block = block_of(turn)
            load_strip(turn).wait()

            @pl.when(turn + 1 < GROUP)
            def _():
                load_strip(turn + 1).start()

            strip = strips[lax.rem(turn, 2)].reshape(tokens, SHARE)
            mine[block, :, :JOINT_COLS] = dot(
                strip, grad_joint[...].reshape(tokens, JOINT_COLS), 0, 0
            ).astype(jnp.bfloat16)
            if not collects:
                mine[block, :, JOINT_COLS:] = dot(
                    strip, grad_inner[...].reshape(tokens, FEED_COLS), 0, 0
                ).astype(jnp.bfloat16)

        def cross_copy(block):
            return to_axis(
                mine.at[block, other_rows],
                other.at[block],
                cross_send.at[block],
                cross_recv.at[block],
                "seq",
                1 - seq,
            )

        def plane_copy(block):
            return to_peer(
                summed.at[block], arrived.at[me], plane_send.at[block], plane_recv.at[me], block
            )

        def up_copy(step):
            peer = lax.rem(me + step, GROUP)
            return to_peer(inputs[7].at[peer], arrived_up.at[me], up_send.at[step], up_recv.at[me], peer)

        def final_pieces(source):
            pieces = []
            for number, (which, start, at, width) in enumerate(column_places(source)):
                piece = arrived_up.at[source] if which else arrived.at[source, :, pl.ds(at, width)]
                pieces.append((number, piece, outputs[which].at[part_rows, pl.ds(start, width)]))
            return pieces

        def back_copy(number, piece, target, source):
            return to_axis(
                piece,
                target,
                back_send.at[source, number],
                back_recv.at[source, number],
                "seq",
                1 - seq,
            )

        def keep_copy(number, piece, target, source):
            return pltpu.make_async_copy(piece, target, keep.at[source, number])

        def pass_on(source, which):
            for number, piece, target in final_pieces(source):
                if (number == PLACES - 1) == (which == 1):
                    back_copy(number, piece, target, source).start()
                    keep_copy(number, piece, target, source).start()

        def add(turn):
            block = block_of(turn)
            cross_copy(block).wait_recv()
            summed[block] = (
                mine[block, part_rows].astype(jnp.float32) + other[block].astype(jnp.float32)
            ).astype(jnp.bfloat16)

            @pl.when(turn < GROUP - 1)
            def _():
                plane_copy(block).start()

        def other_work(turn):
            product(turn)
            if collects:
                cross_copy(block_of(turn)).start()

                @pl.when(turn >= SIDE)
                def _():
                    add(turn - SIDE)

        def late_work(step):
            def pass_up(more, carry):
                number = SIDE * step + more
                source = lax.rem(me + GROUP - number, GROUP)

                @pl.when(number == 0)
                def _():
                    own_up.wait()

                @pl.when(number > 0)
                def _():
                    block = arrived_up.at[source]
                    to_peer(block, block, up_send.at[number], up_recv.at[source], source).wait_recv()

                pass_on(source, 1)
                return carry

            lax.fori_loop(0, SIDE, pass_up, 0)

        def last_adds(turn, carry):
            add(turn)
            return carry

        def send_up(step, carry):
            up_copy(step).start()
            return carry

        wait_all(loads[:3])
        if collects:
            own_up = pltpu.make_async_copy(inputs[7].at[me], arrived_up.at[me], up_own)
            own_up.start()
            lax.fori_loop(1, GROUP, send_up, 0)
        scatter_events(
            partial,
            other_work,
            late_work if collects else None,
            SCATTER_OPS_EARLY if collects else SCATTER_OPS_WORK,
            scratch,
        )
        if collects:
            lax.fori_loop(GROUP - SIDE, GROUP, last_adds, 0)
            arrived[me] = summed[me]
        wait_all(loads[3:])

        def norm_back(part, sums):
            values = hidden[part].astype(jnp.float32)
            centred = values - jnp.mean(values, axis=1, keepdims=True)
            spread = jnp.mean(centred * centred, axis=1, keepdims=True)
            root = lax.rsqrt(spread + EPS)
            normed = centred * root
            above = total[part]
            scaled = above * gain[...]
            down = jnp.mean(scaled, axis=1, keepdims=True)
            along = jnp.mean(scaled * normed, axis=1, keepdims=True)
            passing = grad[part]
            out[part] = passing + root * (scaled - down - normed * along)
            low = passing.astype(jnp.bfloat16).astype(jnp.float32)

            def fold(values):
                return jnp.sum(values.reshape(STRIP // 8, 8, D), axis=0)

            return (sums[0] + fold(above * normed), sums[1] + fold(above), sums[2] + fold(low))

        zeros = jnp.zeros((8, D), jnp.float32)
        sums = each_strip(rows, norm_back, (zeros, zeros, zeros))
        shares[...] = jnp.zeros_like(shares)
        for number, folded in enumerate(sums):
            row = jnp.sum(folded, axis=0, keepdims=True)
            for block in range(GROUP):
                shares[block, number : number + 1] = row[:, block * SHARE : (block + 1) * SHARE]
        ones = jnp.ones((16, tokens), jnp.bfloat16)
        joint_bias = dot(ones, grad_joint[...].reshape(tokens, JOINT_COLS))[:1]
        upper_bias = dot(ones, grad_inner[...].reshape(tokens, FEED_COLS))[:1]
        for part in range(3):
            at = part * GROUP + me
            shares[at // 3, pl.ds(3 + lax.rem(at, 3), 1)] = joint_bias[
                :, part * HEAD_COLS : (part + 1) * HEAD_COLS
            ]
        for part in range(FEED_COLS // SHARE):
            shares[me, 6 + part : 7 + part] = upper_bias[:, part * SHARE : (part + 1) * SHARE]

        def small_copy(step):
            peer = lax.rem(me + step, GROUP)
            return to_peer(
                shares.at[peer], small_land.at[me], small_send.at[step], small_recv.at[me], peer
            )

        def small_begin(step, carry):
            small_copy(step).start()
            return carry

        lax.fori_loop(1, GROUP, small_begin, 0)
        small_land[me] = shares[me]

        def pass_joint(step, carry):
            source = lax.rem(me + GROUP - step, GROUP)

            @pl.when(step > 0)
            def _():
                to_peer(
                    summed.at[source],
                    arrived.at[source],
                    plane_send.at[source],
                    plane_recv.at[source],
                    source,
                ).wait_recv()

            pass_on(source, 0)
            return carry

        if collects:
            lax.fori_loop(0, GROUP, pass_joint, 0)

        def small_end(step, carry):
            source = lax.rem(me + GROUP - step, GROUP)
            to_peer(
                shares.at[source],
                small_land.at[source],
                small_send.at[step],
                small_recv.at[source],
                source,
            ).wait_recv()
            small_copy(step).wait_send()
            return carry

        lax.fori_loop(1, GROUP, small_end, 0)
        small_mine[...] = jnp.sum(small_land[...], axis=0)
        swap = to_axis(small_mine, small_other, swap_send, swap_recv, "seq", 1 - seq)
        swap.start()
        swap.wait()
        small_out[...] = small_mine[...] + small_other[...]

        def end(block, carry):
            cross_copy(block).wait_send()

            @pl.when(block != me)
            def _():
                plane_copy(block).wait_send()

            @pl.when(block > 0)
            def _():
                up_copy(block).wait_send()

            for number, piece, target in final_pieces(block):
                back_copy(number, piece, target, block).wait()
                keep_copy(number, piece, target, block).wait()
            return carry

        if collects:
            lax.fori_loop(0, GROUP, end, 0)

    def part(width, height=half):
        return pltpu.VMEM((GROUP, height, width), jnp.bfloat16)

    small = (SMALL_ROWS, SHARE)
    sixteen, places = pltpu.SemaphoreType.DMA((GROUP,)), pltpu.SemaphoreType.DMA((GROUP, PLACES))
    return pl.pallas_call(
        kernel,
        out_shape=(
            jax.ShapeDtypeStruct((rows, D), jnp.float32),
            jax.ShapeDtypeStruct(small, jnp.float32),
        )
        + (
            (
                jax.ShapeDtypeStruct((SHARE, 3 * D), jnp.bfloat16),
                jax.ShapeDtypeStruct((SHARE, FF), jnp.bfloat16),
            )
            if collects
            else (jax.ShapeDtypeStruct((GROUP, SHARE, COLS), jnp.bfloat16),)
        ),
        in_specs=[HBM, HBM, VMEM] + [HBM] * (5 if collects else 4),
        out_specs=(VMEM, VMEM) + ((HBM, HBM) if collects else (VMEM,)),
        scratch_shapes=[
            pltpu.VMEM(array.shape, array.dtype)
            for array in (hidden, grad, grad_joint, grad_inner, columns)
        ]
        + [
            pltpu.SemaphoreType.DMA((5,)),
            pltpu.VMEM((2, GROUP, rows, SHARE), jnp.bfloat16),
            pltpu.SemaphoreType.DMA((2,)),
            pltpu.VMEM((GROUP,) + small, jnp.float32),
            pltpu.VMEM((GROUP,) + small, jnp.float32),
            pltpu.VMEM(small, jnp.float32),
            pltpu.VMEM(small, jnp.float32),
            sixteen,
            sixteen,
            pltpu.SemaphoreType.DMA,
            pltpu.SemaphoreType.DMA,
        ]
        + (
            [part(JOINT_COLS, SHARE)]
            + [part(JOINT_COLS)] * 3
            + [part(FEED_COLS)]
            + [sixteen] * 4
            + [places] * 3
            + [sixteen] * 2
            + [pltpu.SemaphoreType.DMA]
            if collects
            else []
        )
        + scatter_scratch(rows),
        compiler_params=pltpu.CompilerParams(
            collective_id=20 + layer, has_side_effects=True, vmem_limit_bytes=ROOM
        ),
    )(hidden, grad, gain, grad_joint, grad_inner, columns, every, *((up,) if collects else ()))


def gather_small(packed):
    def kernel(packed, out, send, recv):
        ctx, place = lax.axis_index("ctx"), lax.axis_index("fsdp")
        me = ctx * SIDE + place
        greet_plane(GROUP, False)
        out[me] = packed[...]

        def copy(step):
            return to_peer(
                packed, out.at[me], send.at[step], recv.at[me], lax.rem(me + step, GROUP)
            )

        def begin(step, carry):
            copy(step).start()
            return carry

        lax.fori_loop(1, GROUP, begin, 0)

        def end(step, carry):
            source = lax.rem(me + GROUP - step, GROUP)
            to_peer(packed, out.at[source], send.at[step], recv.at[source], source).wait_recv()
            copy(step).wait_send()
            return carry

        lax.fori_loop(1, GROUP, end, 0)

    return pl.pallas_call(
        kernel,
        out_shape=jax.ShapeDtypeStruct((GROUP,) + packed.shape, packed.dtype),
        in_specs=[VMEM],
        out_specs=VMEM,
        scratch_shapes=[pltpu.SemaphoreType.DMA((GROUP,))] * 2,
        compiler_params=pltpu.CompilerParams(
            collective_id=6, has_side_effects=True, vmem_limit_bytes=ROOM
        ),
    )(packed)


def mask_rest(rows, begin, spot, first, lead):
    if lead:
        old = jnp.where(spot[:lead] >= begin, rows[:lead], NEG)
    key_at = lax.broadcasted_iota(jnp.int32, (first, first), 0) + lead
    query_at = lax.broadcasted_iota(jnp.int32, (first, first), 1) + lead
    near = spot[lead:]
    seen = ((near >= begin) & (near <= query_at)) | (key_at == query_at)
    new = jnp.where(seen, rows[lead:], NEG)
    return jnp.concatenate([old, new], axis=0) if lead else new


def head_lanes(head, rows):
    lane = lax.broadcasted_iota(jnp.int32, (rows, HEAD_COLS), 1)
    return (lane >= head * HEAD_DIM) & (lane < (head + 1) * HEAD_DIM)


def column_exchange(sources, land, sems, layer):
    plane_send, plane_recv, own_sem = sems
    ctx, place, seq = lax.axis_index("ctx"), lax.axis_index("fsdp"), lax.axis_index("seq")
    me = ctx * SIDE + place
    half = SHARE // 2
    part_rows = pl.ds(pl.multiple_of(seq * half, half), half)

    def piece(peer, number):
        which, start, at, width = column_places(peer)[number]
        return (
            sources[which].at[layer, part_rows, pl.ds(start, width)],
            land.at[me, :, pl.ds(at, width)],
        )

    def send_piece(step, number):
        peer = lax.rem(me + step, GROUP)
        source, target = piece(peer, number)
        return to_peer(source, target, plane_send.at[step, number], plane_recv.at[me, number], peer)

    def own_piece(number):
        return pltpu.make_async_copy(*piece(me, number), own_sem.at[number])

    def begin():
        greet_plane(GROUP, False)

        def send(step, carry):
            for number in range(PLACES):
                send_piece(step, number).start()
            return carry

        lax.fori_loop(1, GROUP, send, 0)
        for number in range(PLACES):
            own_piece(number).start()

    def end():
        def arrive(step, carry):
            source = lax.rem(me + GROUP - step, GROUP)
            for number in range(PLACES):
                _, _, at, width = column_places(0)[number]
                target = land.at[source, :, pl.ds(at, width)]
                to_peer(
                    target, target, plane_send.at[0, number], plane_recv.at[source, number], source
                ).wait_recv()
                send_piece(step, number).wait_send()
            return carry

        lax.fori_loop(1, GROUP, arrive, 0)
        for number in range(PLACES):
            own_piece(number).wait()

    return begin, end


def up_products(every, feed, out, scratch):
    feed_part, strips, mine, other, feed_sem, load, cross_send, cross_recv = scratch
    rows = feed.shape[1]
    tokens = GROUP * rows
    half = SHARE // 2
    seq = lax.axis_index("seq")
    me = lax.axis_index("ctx") * SIDE + lax.axis_index("fsdp")
    part_rows = pl.ds(pl.multiple_of(seq * half, half), half)
    other_rows = pl.ds(pl.multiple_of((1 - seq) * half, half), half)

    def load_strip(turn):
        start = pl.multiple_of(lax.rem(me + 1 + turn, GROUP) * SHARE, SHARE)
        buffer = lax.rem(turn, 2)
        return pltpu.make_async_copy(
            every.at[:, :, pl.ds(start, SHARE)], strips.at[buffer], load.at[buffer]
        )

    def cross_copy(block):
        return to_axis(
            mine.at[block, other_rows],
            other.at[block],
            cross_send.at[block],
            cross_recv.at[block],
            "seq",
            1 - seq,
        )

    def feed_copy():
        return pltpu.make_async_copy(feed, feed_part, feed_sem)

    def begin():
        feed_copy().start()
        load_strip(jnp.int32(0)).start()

    def product(turn, carry):
        block = lax.rem(me + 1 + turn, GROUP)
        load_strip(turn).wait()

        @pl.when(turn == 0)
        def _():
            feed_copy().wait()

        @pl.when(turn + 1 < GROUP)
        def _():
            load_strip(turn + 1).start()

        strip = strips[lax.rem(turn, 2)].reshape(tokens, SHARE)
        mine[block] = dot(strip, feed_part[...].reshape(tokens, FEED_COLS), 0, 0).astype(
            jnp.bfloat16
        )
        cross_copy(block).start()
        return carry

    def add(turn, carry):
        block = lax.rem(me + 1 + turn, GROUP)
        cross_copy(block).wait()
        out[block] = (
            mine[block, part_rows].astype(jnp.float32) + other[block].astype(jnp.float32)
        ).astype(jnp.bfloat16)
        return carry

    def make(step):
        lax.fori_loop(SIDE * step, SIDE * step + SIDE, product, 0)
        lax.fori_loop(SIDE * jnp.maximum(step - 1, 0), SIDE * step, add, 0)

    def end():
        lax.fori_loop(GROUP - SIDE, GROUP, add, 0)

    return begin, make, end


def row_exchange(summed, outputs, sems):
    plane_send, plane_recv, own_sem = sems
    me = lax.axis_index("ctx") * SIDE + lax.axis_index("fsdp")

    def piece(peer, number):
        which, start, at, width = column_places(me)[number]
        return summed.at[peer, :, pl.ds(at, width)], outputs[which].at[:, pl.ds(start, width)]

    def send_piece(step, number):
        peer = lax.rem(me + step, GROUP)
        source, target = piece(peer, number)
        return to_peer(source, target, plane_send.at[step, number], plane_recv.at[me, number], peer)

    def own_piece(number):
        return pltpu.make_async_copy(*piece(me, number), own_sem.at[number])

    def begin():
        greet_plane(GROUP)

        def send(step, carry):
            for number in range(PLACES):
                send_piece(step, number).start()
            return carry

        lax.fori_loop(1, GROUP, send, 0)
        for number in range(PLACES):
            own_piece(number).start()

    def end():
        def arrive(step, carry):
            source = lax.rem(me + GROUP - step, GROUP)
            for number in range(PLACES):
                which, start, _, width = column_places(source)[number]
                target = outputs[which].at[:, pl.ds(start, width)]
                to_peer(
                    target, target, plane_send.at[0, number], plane_recv.at[source, number], source
                ).wait_recv()
                send_piece(step, number).wait_send()
            return carry

        lax.fori_loop(1, GROUP, arrive, 0)
        for number in range(PLACES):
            own_piece(number).wait()

    return begin, end


EXCHANGE_SEMS = [
    pltpu.SemaphoreType.DMA((GROUP, PLACES)),
    pltpu.SemaphoreType.DMA((GROUP, PLACES)),
    pltpu.SemaphoreType.DMA((PLACES,)),
]


def attend_plane(query, key, value, begin, spot, weights=None, layer=0):
    rows = query.shape[1]
    length = SIDE * rows
    scale = 1.0 / math.sqrt(HEAD_DIM)

    def kernel(query, key, value, begin, spot, *refs):
        if weights is None:
            mixed, turned, stats = refs
        else:
            mixed, turned, stats, land = refs[2:6]
            begin_exchange, end_exchange = column_exchange(refs[:2], land, refs[6:], layer)
            pl.when(pl.program_id(0) == 0)(begin_exchange)
        keys = key[:, 0].reshape(length, HEAD_COLS)
        values = value[:, 0].reshape(length, HEAD_COLS)
        for chunk in range(SIDE):
            lead = chunk * rows
            seen = lead + rows
            scaled = query[chunk, 0] * jnp.bfloat16(scale)
            start = begin[0, :, lead:seen]
            outs = []
            for head in range(OWN):
                own = jnp.where(head_lanes(head, rows), scaled, jnp.bfloat16(0))
                scores = mask_rest(
                    dot(keys[:seen], own, 1, 1), start, spot[0, :seen], rows, lead
                )
                peak = jnp.max(scores, axis=0, keepdims=True)
                probs = jnp.exp(scores - peak)
                norm = jnp.sum(probs, axis=0, keepdims=True)
                stats[0, head : head + 1, lead:seen] = peak
                stats[0, OWN + head : OWN + head + 1, lead:seen] = norm
                whole = dot(values[:seen], probs.astype(jnp.bfloat16), 0, 0)
                outs.append(whole[head * HEAD_DIM : (head + 1) * HEAD_DIM] / norm)
            joined = jnp.concatenate(outs, axis=0)
            turned[chunk, 0] = joined
            mixed[chunk, 0] = joined.T.astype(jnp.bfloat16)
        if weights is not None:
            pl.when(pl.program_id(0) == SIDE - 1)(end_exchange)

    def spec(height, width):
        return pl.BlockSpec((SIDE, 1, height, width), lambda step: (0, step, 0, 0))

    def shape(height, width, dtype):
        return jax.ShapeDtypeStruct((SIDE, SIDE, height, width), dtype)

    extra = weights is not None
    land = (jax.ShapeDtypeStruct((GROUP, SHARE // 2, COLS), jnp.bfloat16),) if extra else ()
    mixed, turned, stats, *land = pl.pallas_call(
        kernel,
        grid=(SIDE,),
        out_shape=(
            shape(rows, HEAD_COLS, jnp.bfloat16),
            shape(HEAD_COLS, rows, jnp.float32),
            jax.ShapeDtypeStruct((SIDE, 2 * OWN, length), jnp.float32),
        )
        + land,
        in_specs=[spec(rows, HEAD_COLS)] * 3
        + [
            pl.BlockSpec((1, 1, length), lambda step: (step, 0, 0)),
            pl.BlockSpec((1, length, 1), lambda step: (step, 0, 0)),
        ]
        + [HBM] * (2 if extra else 0),
        out_specs=(
            spec(rows, HEAD_COLS),
            spec(HEAD_COLS, rows),
            pl.BlockSpec((1, 2 * OWN, length), lambda step: (step, 0, 0)),
        )
        + ((HBM,) if extra else ()),
        scratch_shapes=EXCHANGE_SEMS if extra else [],
        compiler_params=pltpu.CompilerParams(
            collective_id=40, has_side_effects=True, vmem_limit_bytes=ROOM
        )
        if extra
        else pltpu.CompilerParams(vmem_limit_bytes=ROOM),
    )(
        *(array.reshape(SIDE, SIDE, rows, HEAD_COLS) for array in (query, key, value)),
        begin,
        spot,
        *(weights or ()),
    )
    return mixed.reshape(GROUP, rows, HEAD_COLS), turned, stats, *land


def attend_plane_back(
    query, key, value, begin, spot, turned, stats, grad, tables, summed=None, every=None, feed=None
):
    rows = query.shape[1]
    length = SIDE * rows
    scale = 1.0 / math.sqrt(HEAD_DIM)

    extra = summed is not None

    def kernel(query, key, value, grad, cosine, sine, begin, spot, turned, stats, *refs):
        if extra:
            summed, every, feed, out = refs[:4]
            up_out, grad_k, grad_v = refs[6], refs[7], refs[8]
            begin_exchange, end_exchange = row_exchange(summed, refs[4:6], refs[9:12])
            begin_up, make_up, end_up = up_products(every, feed, up_out, refs[12:])

            @pl.when(pl.program_id(0) == 0)
            def _():
                begin_up()
                begin_exchange()

        else:
            out, grad_k, grad_v = refs
        keys = key[:, 0].reshape(length, HEAD_COLS)
        values = value[:, 0].reshape(length, HEAD_COLS)
        for chunk in range(SIDE):
            lead = chunk * rows
            seen = lead + rows
            if chunk == 0:
                grad_k[...] = jnp.zeros_like(grad_k)
                grad_v[...] = jnp.zeros_like(grad_v)
            scaled = query[chunk, 0] * jnp.bfloat16(scale)
            start = begin[0, :, lead:seen]
            flipped = grad[chunk, 0].T
            grad_q, drifts, numers = [], [], []
            for head in range(OWN):
                part = slice(head * HEAD_DIM, (head + 1) * HEAD_DIM)
                norm = stats[0, OWN + head : OWN + head + 1, lead:seen]
                drifts.append(
                    jnp.sum(flipped[part] * turned[chunk, 0, part], axis=0, keepdims=True) / norm
                )
                numers.append(flipped[part] / norm)
            numer = jnp.concatenate(numers, axis=0).T.astype(jnp.bfloat16)
            for head in range(OWN):
                part = slice(head * HEAD_DIM, (head + 1) * HEAD_DIM)
                lanes = head_lanes(head, rows)
                own = jnp.where(lanes, scaled, jnp.bfloat16(0))
                own_numer = jnp.where(lanes, numer, jnp.bfloat16(0))
                scores = mask_rest(
                    dot(keys[:seen], own, 1, 1), start, spot[0, :seen], rows, lead
                )
                probs = jnp.exp(scores - stats[0, head : head + 1, lead:seen])
                grad_probs = dot(values[:seen], own_numer, 1, 1)
                grad_scores = (probs * (grad_probs - drifts[head])).astype(jnp.bfloat16)
                grad_q.append(dot(keys[:seen], grad_scores, 0, 0)[part])
                grad_k[:seen] += dot(grad_scores, own)
                grad_v[:seen] += dot(probs.astype(jnp.bfloat16), own_numer)
            turns = (cosine[chunk, 0], sine[chunk, 0])
            whole = jnp.concatenate(grad_q, axis=0).T * scale
            out[chunk, 0, :, :HEAD_COLS] = spin(whole, *turns, -1.0).astype(jnp.bfloat16)
        for chunk in range(SIDE):
            place = slice(chunk * rows, (chunk + 1) * rows)
            turns = (cosine[chunk, 0], sine[chunk, 0])
            out[chunk, 0, :, HEAD_COLS : 2 * HEAD_COLS] = spin(grad_k[place], *turns, -1.0).astype(
                jnp.bfloat16
            )
            out[chunk, 0, :, 2 * HEAD_COLS :] = grad_v[place].astype(jnp.bfloat16)
        if extra:
            make_up(pl.program_id(0))

            @pl.when(pl.program_id(0) == SIDE - 1)
            def _():
                end_up()
                end_exchange()


    def spec(height, width):
        return pl.BlockSpec((SIDE, 1, height, width), lambda step: (0, step, 0, 0))

    half = SHARE // 2
    halves = (
        jax.ShapeDtypeStruct((half, 3 * D), jnp.bfloat16),
        jax.ShapeDtypeStruct((half, FF), jnp.bfloat16),
        jax.ShapeDtypeStruct((GROUP, half, FEED_COLS), jnp.bfloat16),
    )
    out, *halves = pl.pallas_call(
        kernel,
        grid=(SIDE,),
        out_shape=(jax.ShapeDtypeStruct((SIDE, SIDE, rows, JOINT_COLS), jnp.bfloat16),)
        + (halves if extra else ()),
        in_specs=[spec(rows, HEAD_COLS)] * 6
        + [
            pl.BlockSpec((1, 1, length), lambda step: (step, 0, 0)),
            pl.BlockSpec((1, length, 1), lambda step: (step, 0, 0)),
            spec(HEAD_COLS, rows),
            pl.BlockSpec((1, 2 * OWN, length), lambda step: (step, 0, 0)),
        ]
        + [HBM] * (3 if extra else 0),
        out_specs=(spec(rows, JOINT_COLS),)
        + (
            (HBM, HBM, pl.BlockSpec((GROUP, half, FEED_COLS), lambda step: (0, 0, 0)))
            if extra
            else ()
        ),
        scratch_shapes=[pltpu.VMEM((length, HEAD_COLS), jnp.float32)] * 2
        + (
            EXCHANGE_SEMS
            + [
                pltpu.VMEM((GROUP, rows, FEED_COLS), jnp.bfloat16),
                pltpu.VMEM((2, GROUP, rows, SHARE), jnp.bfloat16),
                pltpu.VMEM((GROUP, SHARE, FEED_COLS), jnp.bfloat16),
                pltpu.VMEM((GROUP, half, FEED_COLS), jnp.bfloat16),
                pltpu.SemaphoreType.DMA,
                pltpu.SemaphoreType.DMA((2,)),
                pltpu.SemaphoreType.DMA((GROUP,)),
                pltpu.SemaphoreType.DMA((GROUP,)),
            ]
            if extra
            else []
        ),
        compiler_params=pltpu.CompilerParams(
            collective_id=41, has_side_effects=True, vmem_limit_bytes=ROOM
        )
        if extra
        else pltpu.CompilerParams(vmem_limit_bytes=ROOM),
    )(
        *(
            array.reshape(SIDE, SIDE, rows, HEAD_COLS)
            for array in (query, key, value, grad) + tuple(tables)
        ),
        begin,
        spot,
        turned,
        stats,
        *((summed, every, feed) if extra else ()),
    )
    return out.reshape(GROUP, rows, JOINT_COLS), *halves


def on_device_split(
    tokens,
    doc_lengths,
    keep_mask,
    ln_gain,
    ln_bias,
    qkv_weight,
    qkv_bias,
    out_weight,
    out_bias,
    up_weight,
    up_bias,
    down_weight,
    down_bias,
    cotangent,
):
    rows = tokens.shape[1]
    length = SIDE * rows
    docs = doc_lengths.shape[1]
    me = lax.axis_index("ctx") * SIDE + lax.axis_index("fsdp")

    high = (doc_lengths[0] // 32).astype(jnp.bfloat16)
    low = (doc_lengths[0] % 32).astype(jnp.bfloat16)
    fields = [ln_gain, ln_bias, qkv_bias, out_bias, down_bias]
    packed = jnp.concatenate(
        [field.reshape(-1) for field in fields]
        + [keep_mask[0].astype(jnp.bfloat16), high, low]
    )
    tile = 16 * 128
    packed = jnp.pad(packed, (0, -packed.shape[0] % tile)).reshape(-1, 128)
    everyone = gather_small(packed).reshape(GROUP, -1)
    at = 0
    whole = []
    for field in fields:
        width = field.shape[1]
        part = everyone[:, at : at + LAYERS * width].reshape(GROUP, LAYERS, width)
        whole.append(part.transpose(1, 0, 2).reshape(LAYERS, 1, GROUP * width).astype(jnp.float32))
        at += LAYERS * width
    gain, shift, joint_bias, output_bias, lower_bias = whole
    keep = everyone[:, at : at + rows].reshape(SIDE, SIDE, rows)
    keep = keep.transpose(1, 0, 2).reshape(SIDE, length)
    at += rows
    lengths = (
        everyone[:SIDE, at : at + docs].astype(jnp.int32) * 32
        + everyone[:SIDE, at + docs : at + 2 * docs].astype(jnp.int32)
    )
    own_bias = lax.dynamic_slice_in_dim(
        joint_bias.reshape(LAYERS, 3, GROUP, HEAD_COLS), me, 1, axis=2
    ).reshape(LAYERS, JOINT_COLS)
    column_bias = jnp.concatenate([own_bias, up_bias.astype(jnp.float32)], axis=1)

    index = jnp.arange(length, dtype=jnp.int32)
    ends = jnp.cumsum(lengths, axis=1)
    passed = jnp.where(index[None, None, :] >= ends[:, :, None], ends[:, :, None], 0)
    begin = jnp.max(passed, axis=1)[:, None, :]
    spot = jnp.where(keep > 0, index[None, :], -1)[:, :, None]
    position = (index[None, None, :] - begin).astype(jnp.float32)
    position = position.reshape(SIDE, SIDE, rows).transpose(1, 0, 2).reshape(GROUP, rows, 1)
    lane = np.arange(HEAD_COLS) % HEAD_DIM
    inverse = 1.0 / 10000.0 ** (np.arange(0, ROT, 2, dtype=np.float32) / np.float32(ROT))
    inverse = np.where(lane < ROT, inverse[lane % (ROT // 2)], 0.0).astype(np.float32)
    inverse = jnp.asarray(inverse)[None, :]

    seq = lax.axis_index("seq")
    half = SHARE // 2
    swap = [(0, 1), (1, 0)]

    def swapped(values):
        return lax.ppermute(values, "seq", swap)

    hidden = tokens[0]
    saved, tables = [], None
    sources = (qkv_weight, up_weight)
    for layer in range(LAYERS):
        out = forward_gather(
            hidden,
            gain[layer],
            shift[layer],
            column_bias[layer][None, :],
            tables or (position, inverse),
            sources,
            layer,
        )
        every, columns, query, key, value, inner, active = out[:7]
        tables = tables or tuple(out[7:])
        if layer + 1 < LAYERS:
            mixed, turned, stats, arrived = attend_plane(
                query, key, value, begin, spot, (qkv_weight, up_weight), layer + 1
            )
            sources = (arrived, swapped(arrived))
        else:
            mixed, turned, stats = attend_plane(query, key, value, begin, spot)
        saved.append(
            (hidden, every, columns, query, key, value, inner, active, mixed, turned, stats)
        )
        hidden = forward_scatter(
            hidden,
            output_bias[layer] + lower_bias[layer],
            mixed,
            active,
            out_weight[layer],
            down_weight[layer],
            layer,
        )
    result = hidden.astype(jnp.bfloat16)[None]

    grad_hidden = cotangent[0].astype(jnp.float32) * keep_mask[0].astype(jnp.float32)[:, None]
    joint_grads, upper_grads, branch_grads, small_grads = [], [], [], []
    summed = None
    for layer in reversed(range(LAYERS)):
        before, every, columns, query, key, value, inner, active, mixed, turned, stats = saved[layer]
        grad_mixed, grad_inner, branch = backward_gather(
            grad_hidden.astype(jnp.bfloat16),
            out_weight[layer],
            down_weight[layer],
            inner,
            mixed,
            active,
        )
        branch_grads.insert(
            0, branch.astype(jnp.float32) + swapped(branch).astype(jnp.float32)
        )
        grad_joint, *rest = attend_plane_back(
            query,
            key,
            value,
            begin,
            spot,
            turned,
            stats,
            grad_mixed,
            tables,
            summed,
            every,
            grad_inner,
        )
        for grads, own in zip((joint_grads, upper_grads), rest[:2]):
            other = swapped(own)
            grads.insert(
                0,
                jnp.concatenate(
                    [jnp.where(seq == 0, own, other), jnp.where(seq == 0, other, own)], axis=0
                ),
            )
        grad_hidden, small, *grads = backward_scatter(
            before,
            grad_hidden,
            gain[layer],
            grad_joint,
            grad_inner,
            columns.reshape(D, COLS),
            every,
            layer,
            rest[2] if rest else None,
        )
        small_grads.insert(0, small)
        if layer > 0:
            own = lax.dynamic_slice_in_dim(grads[0], seq * half, half, axis=1)
            other = swapped(lax.dynamic_slice_in_dim(grads[0], (1 - seq) * half, half, axis=1))
            summed = (own.astype(jnp.float32) + other.astype(jnp.float32)).astype(jnp.bfloat16)
        else:
            joint_grads.insert(0, grads[0])
            upper_grads.insert(0, grads[1])
    branch_grad = jnp.stack(branch_grads)
    small = jnp.stack(small_grads)
    return (
        result,
        grad_hidden[None],
        small[:, 0],
        small[:, 1],
        jnp.stack(joint_grads).astype(jnp.float32),
        small[:, 3:6].reshape(LAYERS, JOINT_COLS),
        branch_grad[:, :HEAD_COLS],
        small[:, 2],
        jnp.stack(upper_grads).astype(jnp.float32),
        small[:, 6:10].reshape(LAYERS, FEED_COLS),
        branch_grad[:, HEAD_COLS:],
        small[:, 2],
    )


def solution(mesh):
    small = mesh.shape["ctx"] == SIDE and mesh.shape["fsdp"] == SIDE and mesh.shape["seq"] == 2
    on_device = on_device_split if small else on_device_gathered
    return jax.shard_map(
        on_device,
        mesh=mesh,
        in_specs=(
            P(("seq", "fsdp"), "ctx", None),
            P(("seq", "fsdp"), None),
            P(("seq", "fsdp"), "ctx"),
            P(None, ("ctx", "fsdp")),
            P(None, ("ctx", "fsdp")),
            P(None, ("ctx", "fsdp"), None),
            P(None, ("ctx", "fsdp")),
            P(None, ("ctx", "fsdp"), None),
            P(None, ("ctx", "fsdp")),
            P(None, ("ctx", "fsdp"), None),
            P(None, ("ctx", "fsdp")),
            P(None, ("ctx", "fsdp"), None),
            P(None, ("ctx", "fsdp")),
            P(("seq", "fsdp"), "ctx", None),
        ),
        out_specs=(
            P(("seq", "fsdp"), "ctx", None),
            P(("seq", "fsdp"), "ctx", None),
            P(None, ("ctx", "fsdp")),
            P(None, ("ctx", "fsdp")),
            P(None, ("ctx", "fsdp"), None),
            P(None, ("ctx", "fsdp")),
            P(None, ("ctx", "fsdp"), None),
            P(None, ("ctx", "fsdp")),
            P(None, ("ctx", "fsdp"), None),
            P(None, ("ctx", "fsdp")),
            P(None, ("ctx", "fsdp"), None),
            P(None, ("ctx", "fsdp")),
        ),
        check_vma=False,
    )
```

```python
import functools
import math

import jax
import jax.numpy as jnp
import numpy as np
from jax import lax
from jax.experimental import pallas as pl
from jax.experimental.pallas import tpu as pltpu
from jax.sharding import PartitionSpec as P

D = 2048
HEADS = 32
HEAD_DIM = 64
ROT = 32
FF = 8192
LAYERS = 2


EPS = 1e-05
NEG = -1e30


def place_tokens(token_index, lengths):
    bounds = jnp.cumsum(lengths)
    starts = bounds - lengths
    segment = jnp.sum((token_index[:, None] >= bounds[None, :]).astype(jnp.int32), axis=1)
    chosen = segment[:, None] == jnp.arange(lengths.shape[0], dtype=jnp.int32)[None, :]
    position = token_index - jnp.sum(jnp.where(chosen, starts[None, :], 0), axis=1)
    return (segment, position)


def angles(position):
    indices = jnp.arange(0, ROT, 2, dtype=jnp.float32) / ROT
    inverse = 1.0 / 10000.0**indices
    turned = position.astype(jnp.float32)[:, None] * inverse[None, :]
    turned = jnp.concatenate([turned, turned], axis=1)
    return (jnp.cos(turned), jnp.sin(turned))


def rotate(values, cosine, sine):
    rotary = values[..., :ROT]
    middle = ROT // 2
    turned = jnp.concatenate([-rotary[..., middle:], rotary[..., :middle]], axis=-1)
    mixed = rotary * cosine[:, None, :] + turned * sine[:, None, :]
    return jnp.concatenate([mixed, values[..., ROT:]], axis=-1)


def normalize(hidden, gain_row, shift_row):
    average = jnp.mean(hidden, axis=1, keepdims=True)
    centred = hidden - average
    spread = jnp.mean(centred * centred, axis=1, keepdims=True)
    return centred * lax.rsqrt(spread + EPS) * gain_row + shift_row


def block_scores(queries, travelling, start, query_index, query_segment, lengths):
    key_flat, value_flat, key_keep = travelling
    count = key_flat.shape[0]
    key_index = start + jnp.arange(count, dtype=jnp.int32)
    key_segment = place_tokens(key_index, lengths)[0]
    allowed = (
        (query_segment[:, None] == key_segment[None, :])
        & (key_index[None, :] <= query_index[:, None])
        & ((key_keep[None, :] > 0) | (key_index[None, :] == query_index[:, None]))
    )
    key_rows = key_flat.reshape(count, HEADS, HEAD_DIM)
    value_rows = value_flat.reshape(count, HEADS, HEAD_DIM)
    scores = jnp.einsum("qhd,khd->hqk", queries, key_rows, preferred_element_type=jnp.float32) * (
        1.0 / math.sqrt(HEAD_DIM)
    )
    return (scores, allowed, key_rows, value_rows)


def attend(running, travelling, start, queries, query_index, query_segment, lengths):
    maxima, totals, weighted = running
    scores, allowed, key_rows, value_rows = block_scores(
        queries, travelling, start, query_index, query_segment, lengths
    )
    masked = jnp.where(allowed[None], scores, NEG)
    new_max = jnp.maximum(maxima, jnp.max(masked, axis=2))
    probs = jnp.where(allowed[None], jnp.exp(masked - new_max[:, :, None]), 0.0)
    totals = jnp.sum(probs, axis=2)
    weighted = jnp.einsum(
        "hqk,khd->hqd", probs.astype(jnp.bfloat16), value_rows, preferred_element_type=jnp.float32
    )
    return (new_max, totals, weighted)


def attend_back(
    travelling, start, queries, maxima, grad_numer, drift, query_index, query_segment, lengths
):
    scores, allowed, key_rows, value_rows = block_scores(
        queries, travelling, start, query_index, query_segment, lengths
    )
    count = key_rows.shape[0]
    scale = 1.0 / math.sqrt(HEAD_DIM)
    probs = jnp.where(allowed[None], jnp.exp(scores - maxima[:, :, None]), 0.0)
    grad_probs = jnp.einsum(
        "hqd,khd->hqk", grad_numer, value_rows, preferred_element_type=jnp.float32
    )
    grad_scores = (probs * (grad_probs - drift[:, :, None])).astype(jnp.bfloat16)
    grad_query = (
        jnp.einsum("hqk,khd->qhd", grad_scores, key_rows, preferred_element_type=jnp.float32)
        * scale
    )
    grad_key = (
        jnp.einsum("hqk,qhd->khd", grad_scores, queries, preferred_element_type=jnp.float32) * scale
    )
    grad_value = jnp.einsum(
        "hqk,hqd->khd", probs.astype(jnp.bfloat16), grad_numer, preferred_element_type=jnp.float32
    )
    return (
        grad_query,
        grad_key.reshape(count, HEADS * HEAD_DIM),
        grad_value.reshape(count, HEADS * HEAD_DIM),
    )


def attention_forward(queries, key_flat, value_flat, key_keep, query_index, query_segment, lengths):
    row_count = key_flat.shape[0]
    initial = (
        jnp.full((HEADS, row_count), NEG, jnp.float32),
        jnp.zeros((HEADS, row_count), jnp.float32),
        jnp.zeros((HEADS, row_count, HEAD_DIM), jnp.float32),
    )
    return attend(
        initial,
        (
            lax.all_gather(key_flat, "ctx", axis=0, tiled=True),
            lax.all_gather(value_flat, "ctx", axis=0, tiled=True),
            lax.all_gather(key_keep, "ctx", axis=0, tiled=True),
        ),
        jnp.int32(0),
        queries,
        query_index,
        query_segment,
        lengths,
    )


def attention_backward(
    queries,
    key_flat,
    value_flat,
    key_keep,
    maxima,
    grad_numer,
    drift,
    query_index,
    query_segment,
    lengths,
):
    whole = (
        lax.all_gather(key_flat, "ctx", axis=0, tiled=True),
        lax.all_gather(value_flat, "ctx", axis=0, tiled=True),
        lax.all_gather(key_keep, "ctx", axis=0, tiled=True),
    )
    grad_query, every_key, every_value = attend_back(
        whole, 0, queries, maxima, grad_numer, drift, query_index, query_segment, lengths
    )
    grad_key, grad_value = (
        lax.psum_scatter(
            every_key.astype(jnp.bfloat16), "ctx", scatter_dimension=0, tiled=True
        ).astype(jnp.float32),
        lax.psum_scatter(
            every_value.astype(jnp.bfloat16), "ctx", scatter_dimension=0, tiled=True
        ).astype(jnp.float32),
    )
    return (grad_query, grad_key, grad_value)


def layer_forward(hidden, weights, cosine, sine, key_keep, query_index, query_segment, lengths):
    (
        norm_gain,
        norm_shift,
        joint_weight,
        joint_bias,
        output_weight,
        output_bias,
        upper_weight,
        upper_bias,
        lower_weight,
        lower_bias,
    ) = weights
    row_count = hidden.shape[0]
    width = HEADS * HEAD_DIM
    normed = normalize(
        hidden, norm_gain.astype(jnp.float32), norm_shift.astype(jnp.float32)
    ).astype(jnp.bfloat16)
    joint = jnp.dot(normed, joint_weight, preferred_element_type=jnp.float32) + joint_bias.astype(
        jnp.float32
    )
    queries = rotate(joint[:, :width].reshape(row_count, HEADS, HEAD_DIM), cosine, sine).astype(
        jnp.bfloat16
    )
    key_flat = (
        rotate(joint[:, width : 2 * width].reshape(row_count, HEADS, HEAD_DIM), cosine, sine)
        .astype(jnp.bfloat16)
        .reshape(row_count, width)
    )
    value_flat = joint[:, 2 * width :].astype(jnp.bfloat16)
    maxima, totals, weighted = attention_forward(
        queries, key_flat, value_flat, key_keep, query_index, query_segment, lengths
    )
    mixed = (weighted / totals[:, :, None]).transpose(1, 0, 2).reshape(row_count, width)
    attention_out = jnp.dot(
        mixed.astype(jnp.bfloat16), output_weight, preferred_element_type=jnp.float32
    ) + output_bias.astype(jnp.float32)
    inner = jnp.dot(normed, upper_weight, preferred_element_type=jnp.float32) + upper_bias.astype(
        jnp.float32
    )
    activated = jax.nn.gelu(inner, approximate=True).astype(jnp.bfloat16)
    feed_out = jnp.dot(
        activated, lower_weight, preferred_element_type=jnp.float32
    ) + lower_bias.astype(jnp.float32)
    saved = (hidden, normed, queries, key_flat, value_flat, maxima, totals, mixed, inner, activated)
    return (hidden + (attention_out + feed_out), saved)


def layer_backward(
    grad_out, saved, weights, cosine, sine, key_keep, query_index, query_segment, lengths
):
    hidden, normed, queries, key_flat, value_flat, maxima, totals, mixed, inner, activated = saved
    (
        norm_gain,
        norm_shift,
        joint_weight,
        joint_bias,
        output_weight,
        output_bias,
        upper_weight,
        upper_bias,
        lower_weight,
        lower_bias,
    ) = weights
    row_count = hidden.shape[0]
    width = HEADS * HEAD_DIM
    ratio = FF // D
    grad_branch = grad_out.astype(jnp.bfloat16)
    mixed_low = mixed.astype(jnp.bfloat16)
    branch_bias = jnp.sum(grad_branch, axis=0, dtype=jnp.float32)
    grad_activated = jnp.einsum(
        "td,fd->tf", grad_branch, lower_weight, preferred_element_type=jnp.float32
    )
    gelu_pull = jax.vjp(functools.partial(jax.nn.gelu, approximate=True), inner)[1]
    grad_inner = gelu_pull(grad_activated)[0].astype(jnp.bfloat16)
    upper_bias_grad = jnp.sum(grad_inner, axis=0, dtype=jnp.float32)
    grad_normed = jnp.einsum(
        "tf,df->td", grad_inner, upper_weight, preferred_element_type=jnp.float32
    )
    upper_bias_rows = upper_bias_grad.reshape(D, ratio)
    normed_cols = normed
    upper_part = jnp.einsum(
        "tc,tf->cf", normed_cols, grad_inner, preferred_element_type=jnp.float32
    )
    lower_part = jnp.einsum(
        "tc,td->cd", activated, grad_branch, preferred_element_type=jnp.float32
    ).reshape(lax.axis_size(("ctx", "fsdp")) * (D // lax.axis_size(("ctx", "fsdp"))), ratio * width)
    bias_part = upper_bias_rows
    branch_part = branch_bias[:, None]
    feed_share = lax.psum_scatter(
        jnp.concatenate([upper_part, lower_part, bias_part, branch_part], axis=1),
        ("ctx", "fsdp"),
        scatter_dimension=0,
        tiled=True,
    )
    share_rows = feed_share.shape[0]
    upper_share = feed_share[:, :FF]
    lower_share = feed_share[:, FF : FF + ratio * width].reshape(share_rows * ratio, width)
    upper_bias_share = feed_share[:, FF + ratio * width : FF + ratio * width + ratio].reshape(
        share_rows * ratio
    )
    branch_share = feed_share[:, FF + ratio * width + ratio]
    feed_parts = (upper_share, upper_bias_share, lower_share, branch_share)
    output_share = None
    grad_mixed = jnp.einsum(
        "te,de->td", grad_branch, output_weight, preferred_element_type=jnp.float32
    )
    head_mixed = mixed.reshape(row_count, HEADS, HEAD_DIM).transpose(1, 0, 2)
    head_grad = grad_mixed.reshape(row_count, HEADS, HEAD_DIM).transpose(1, 0, 2)
    drift = jnp.sum(head_grad * head_mixed, axis=2) / totals
    grad_numer = (head_grad / totals[:, :, None]).astype(jnp.bfloat16)
    grad_query, grad_key, grad_value = attention_backward(
        queries,
        key_flat,
        value_flat,
        key_keep,
        maxima,
        grad_numer,
        drift,
        query_index,
        query_segment,
        lengths,
    )
    grad_query = rotate(grad_query, cosine, -sine).reshape(row_count, width)
    grad_key = rotate(grad_key.reshape(row_count, HEADS, HEAD_DIM), cosine, -sine).reshape(
        row_count, width
    )
    grad_joint = jnp.concatenate([grad_query, grad_key, grad_value], axis=1).astype(jnp.bfloat16)
    joint_bias_grad = jnp.sum(grad_joint, axis=0, dtype=jnp.float32)
    grad_normed = grad_normed + jnp.einsum(
        "te,de->td", grad_joint, joint_weight, preferred_element_type=jnp.float32
    )
    norm_pull = jax.vjp(
        normalize, hidden, norm_gain.astype(jnp.float32), norm_shift.astype(jnp.float32)
    )[1]
    grad_hidden, gain_grad, shift_grad = norm_pull(grad_normed)
    joint_bias_rows = joint_bias_grad.reshape(D, 3)
    normed_cols = normed
    joint_part = jnp.einsum(
        "tc,te->ce", normed_cols, grad_joint, preferred_element_type=jnp.float32
    )
    output_part = jnp.einsum(
        "tc,te->ce", mixed_low, grad_branch, preferred_element_type=jnp.float32
    )
    bias_part = joint_bias_rows
    gain_part = gain_grad[:, None]
    shift_part = shift_grad[:, None]
    attn_share = lax.psum_scatter(
        jnp.concatenate([joint_part, output_part, bias_part, gain_part, shift_part], axis=1),
        ("ctx", "fsdp"),
        scatter_dimension=0,
        tiled=True,
    )
    share_rows = attn_share.shape[0]
    joint_share = attn_share[:, : 3 * width]
    output_share = attn_share[:, 3 * width : 4 * width]
    joint_bias_share = attn_share[:, 4 * width : 4 * width + 3].reshape(share_rows * 3)
    gain_share = attn_share[:, 4 * width + 3]
    shift_share = attn_share[:, 4 * width + 4]
    attention_parts = (gain_share, shift_share, joint_share, joint_bias_share, output_share)
    return (grad_out + grad_hidden, attention_parts, feed_parts)


def on_device_gathered(
    tokens,
    doc_lengths,
    keep_mask,
    ln_gain,
    ln_bias,
    qkv_weight,
    qkv_bias,
    out_weight,
    out_bias,
    up_weight,
    up_bias,
    down_weight,
    down_bias,
    cotangent,
):
    row_count = tokens.shape[1]
    position = lax.axis_index("ctx")
    query_index = position * row_count + jnp.arange(row_count, dtype=jnp.int32)
    lengths = doc_lengths[0]
    query_segment, query_position = place_tokens(query_index, lengths)
    cosine, sine = angles(query_position)
    key_keep = keep_mask[0].astype(jnp.bfloat16)
    shards = (
        ln_gain,
        ln_bias,
        qkv_weight,
        qkv_bias,
        out_weight,
        out_bias,
        up_weight,
        up_bias,
        down_weight,
        down_bias,
    )

    def fetch(layer_index):
        return (
            lax.all_gather(shards[0][layer_index], ("ctx", "fsdp"), axis=0, tiled=True),
            lax.all_gather(shards[1][layer_index], ("ctx", "fsdp"), axis=0, tiled=True),
            lax.all_gather(shards[2][layer_index], ("ctx", "fsdp"), axis=0, tiled=True),
            lax.all_gather(shards[3][layer_index], ("ctx", "fsdp"), axis=0, tiled=True),
            lax.all_gather(shards[4][layer_index], ("ctx", "fsdp"), axis=0, tiled=True),
            lax.all_gather(shards[5][layer_index], ("ctx", "fsdp"), axis=0, tiled=True),
            lax.all_gather(shards[6][layer_index], ("ctx", "fsdp"), axis=0, tiled=True),
            lax.all_gather(shards[7][layer_index], ("ctx", "fsdp"), axis=0, tiled=True),
            lax.all_gather(shards[8][layer_index], ("ctx", "fsdp"), axis=0, tiled=True),
            lax.all_gather(shards[9][layer_index], ("ctx", "fsdp"), axis=0, tiled=True),
        )

    hidden = tokens[0].astype(jnp.float32)
    saved_layers = []
    weights = None
    for layer_index in range(LAYERS):
        weights = fetch(layer_index)
        hidden, saved = layer_forward(
            hidden, weights, cosine, sine, key_keep, query_index, query_segment, lengths
        )
        saved_layers.append(saved)
    result = hidden.astype(jnp.bfloat16)[None]
    grad_hidden = cotangent[0].astype(jnp.float32) * keep_mask[0].astype(jnp.float32)[:, None]
    attention_list = [None] * LAYERS
    feed_list = [None] * LAYERS
    for layer_index in reversed(range(LAYERS)):
        weights = weights if layer_index == LAYERS - 1 else fetch(layer_index)
        grad_hidden, attention_parts, feed_parts = layer_backward(
            grad_hidden,
            saved_layers[layer_index],
            weights,
            cosine,
            sine,
            key_keep,
            query_index,
            query_segment,
            lengths,
        )
        attention_list[layer_index] = attention_parts
        feed_list[layer_index] = feed_parts
    gain_stack = jnp.stack([attention_list[layer_index][0] for layer_index in range(LAYERS)])
    shift_stack = jnp.stack([attention_list[layer_index][1] for layer_index in range(LAYERS)])
    joint_stack = jnp.stack([attention_list[layer_index][2] for layer_index in range(LAYERS)])
    joint_bias_stack = jnp.stack([attention_list[layer_index][3] for layer_index in range(LAYERS)])
    output_stack = jnp.stack([attention_list[layer_index][4] for layer_index in range(LAYERS)])
    upper_stack = jnp.stack([feed_list[layer_index][0] for layer_index in range(LAYERS)])
    upper_bias_stack = jnp.stack([feed_list[layer_index][1] for layer_index in range(LAYERS)])
    lower_stack = jnp.stack([feed_list[layer_index][2] for layer_index in range(LAYERS)])
    branch_stack = jnp.stack([feed_list[layer_index][3] for layer_index in range(LAYERS)])
    summed = (
        lax.psum(gain_stack.astype(jnp.bfloat16), "seq").astype(jnp.float32),
        lax.psum(shift_stack.astype(jnp.bfloat16), "seq").astype(jnp.float32),
        lax.psum(joint_stack.astype(jnp.bfloat16), "seq").astype(jnp.float32),
        lax.psum(joint_bias_stack.astype(jnp.bfloat16), "seq").astype(jnp.float32),
        lax.psum(output_stack.astype(jnp.bfloat16), "seq").astype(jnp.float32),
        lax.psum(upper_stack.astype(jnp.bfloat16), "seq").astype(jnp.float32),
        lax.psum(upper_bias_stack.astype(jnp.bfloat16), "seq").astype(jnp.float32),
        lax.psum(lower_stack.astype(jnp.bfloat16), "seq").astype(jnp.float32),
        lax.psum(branch_stack.astype(jnp.bfloat16), "seq").astype(jnp.float32),
    )
    return (
        result,
        grad_hidden[None],
        summed[0],
        summed[1],
        summed[2],
        summed[3],
        summed[4],
        summed[8],
        summed[5],
        summed[6],
        summed[7],
        summed[8],
    )


SIDE = 4
GROUP = SIDE * SIDE
OWN = HEADS // GROUP
HEAD_COLS = OWN * HEAD_DIM
JOINT_COLS = 3 * HEAD_COLS
FEED_COLS = FF // GROUP
COLS = JOINT_COLS + FEED_COLS
BACK_COLS = HEAD_COLS + FEED_COLS
SHARE = D // GROUP
VMEM = pl.BlockSpec(memory_space=pltpu.VMEM)
HBM = pl.BlockSpec(memory_space=pl.ANY)
MESH = pl.DeviceIdType.MESH
ROOM = 60 * 2**20


def dot(left, right, left_dim=1, right_dim=0):
    return lax.dot_general(
        left, right, (((left_dim,), (right_dim,)), ((), ())), preferred_element_type=jnp.float32
    )


def digit(entries, index):
    words = [
        sum(entry << (2 * place) for place, entry in enumerate(entries[start : start + 8]))
        for start in range(0, len(entries), 8)
    ]
    word = jnp.int32(words[0])
    for number in range(1, len(words)):
        word = jnp.where(index >= 8 * number, jnp.int32(words[number]), word)
    return lax.rem(lax.shift_right_logical(word, 2 * lax.rem(index, 8)), 4)


def nibble(entries, index):
    word = jnp.int32(0)
    for start in range(0, len(entries), 7):
        packed = sum(entry << (4 * place) for place, entry in enumerate(entries[start : start + 7]))
        word = jnp.where(index >= start, jnp.int32(packed), word)
    return lax.rem(lax.shift_right_logical(word, 4 * lax.rem(index, 7)), 16)


def digit_of_row(table, row, index):
    value = digit(table[0], index)
    for number in range(1, len(table)):
        value = jnp.where(row == number, digit(table[number], index), value)
    return value


NEAR = ((0, 1, 2, 3), (1, 0, 2, 3), (2, 3, 1, 0), (3, 2, 1, 0))
FAR = ((3, 2, 1, 0), (3, 0, 2, 1), (0, 3, 1, 2), (0, 1, 2, 3))


def neighbours():
    ctx, place = lax.axis_index("ctx"), lax.axis_index("fsdp")
    twin = ctx + 1 - 2 * lax.rem(ctx, 2)
    across = lax.rem(ctx + 2, 4)
    return ctx, place, twin, across, lax.rem(twin + 2, 4)


def greet_neighbours():
    ctx, place, twin, across, _ = neighbours()
    barrier = pltpu.get_barrier_semaphore()
    pl.semaphore_signal(barrier, inc=1, device_id={"ctx": twin}, device_id_type=MESH)
    pl.semaphore_signal(barrier, inc=1, device_id={"ctx": across}, device_id_type=MESH)

    @pl.when(place > 0)
    def _():
        pl.semaphore_signal(barrier, inc=1, device_id={"fsdp": place - 1}, device_id_type=MESH)

    @pl.when(place < SIDE - 1)
    def _():
        pl.semaphore_signal(barrier, inc=1, device_id={"fsdp": place + 1}, device_id_type=MESH)

    inner = jnp.int32(2) + jnp.where(place > 0, 1, 0) + jnp.where(place < SIDE - 1, 1, 0)
    pl.semaphore_wait(barrier, inner)


def greet_plane(steps, cross=True):
    ctx, place = lax.axis_index("ctx"), lax.axis_index("fsdp")
    me = ctx * SIDE + place
    barrier = pltpu.get_barrier_semaphore()
    for step in range(1, steps):
        peer = lax.rem(me + step, GROUP)
        pl.semaphore_signal(
            barrier,
            inc=1,
            device_id={"ctx": peer // SIDE, "fsdp": lax.rem(peer, SIDE)},
            device_id_type=MESH,
        )
    if cross:
        pl.semaphore_signal(
            barrier, inc=1, device_id={"seq": 1 - lax.axis_index("seq")}, device_id_type=MESH
        )
    pl.semaphore_wait(barrier, steps if cross else steps - 1)


def to_peer(source, target, send, recv, peer):
    return pltpu.make_async_remote_copy(
        src_ref=source,
        dst_ref=target,
        send_sem=send,
        recv_sem=recv,
        device_id={"ctx": peer // SIDE, "fsdp": lax.rem(peer, SIDE)},
        device_id_type=MESH,
    )


def to_axis(source, target, send, recv, axis, index):
    return pltpu.make_async_remote_copy(
        src_ref=source,
        dst_ref=target,
        send_sem=send,
        recv_sem=recv,
        device_id={axis: index},
        device_id_type=MESH,
    )


PARTS = ((0, 112), (112, 96), (208, 48))
LAST = len(PARTS) - 1
GATHER_KIND = (
    (0, 0, 0, 0, 0, 1, 0, 0, 1, 0, 2, 0, 1, 1, 1, 2, 0, 0, 1, 0, 1, 3, 2, 1, 0, 3, 1, 1, 1, 1, 0, 3, 0, 0, 1, 1, 1, 1, 2, 3),
    (0, 0, 0, 1, 0, 0, 0, 0, 0, 0, 0, 0, 1, 0, 2, 1, 2, 1, 0, 1, 1, 2, 0, 3, 1, 1, 0, 1, 1, 1, 3, 1, 1, 0, 1, 3, 1, 1, 2, 3),
)
GATHER_STEP = (
    (0, 0, 1, 0, 0, 0, 1, 1, 0, 1, 0, 2, 0, 0, 1, 1, 2, 2, 1, 2, 1, 0, 2, 1, 3, 1, 2, 2, 2, 2, 3, 2, 3, 3, 3, 3, 3, 3, 3, 3),
    (0, 0, 0, 0, 2, 2, 1, 0, 1, 2, 1, 1, 0, 2, 0, 0, 2, 0, 3, 2, 2, 1, 3, 0, 2, 1, 3, 1, 2, 1, 2, 3, 1, 3, 3, 1, 3, 3, 3, 3),
)
GATHER_PART = (
    (1, 0, 1, 2, 3, 1, 2, 0, 0, 3, 3, 2, 2, 3, 0, 3, 1, 0, 1, 3, 2, 3, 3, 3, 0, 3, 1, 2, 0, 3, 1, 3, 2, 3, 1, 0, 2, 3, 3, 3),
    (1, 0, 2, 0, 2, 0, 2, 3, 1, 1, 0, 3, 2, 3, 3, 1, 3, 3, 0, 0, 2, 3, 1, 3, 1, 1, 2, 2, 3, 0, 3, 2, 3, 3, 0, 3, 1, 3, 3, 3),
)
FIRST_KIND = (
    (0, 0, 0, 0, 0, 0, 0, 1, 0, 0, 0, 1, 0, 1, 0, 0, 0, 1, 0, 1, 1, 2, 0, 1, 0, 0, 0, 0, 1, 3, 0, 2, 3, 0, 2, 0, 2, 0, 3, 1, 0, 0, 3, 1, 1, 2, 2, 0, 1, 1, 0, 1, 1, 0, 1, 0, 1, 3, 3, 2, 1, 1, 1, 2, 3, 3),
    (0, 0, 0, 0, 0, 1, 0, 0, 0, 0, 1, 0, 0, 0, 0, 2, 1, 0, 1, 0, 1, 0, 0, 0, 0, 0, 0, 2, 1, 0, 0, 1, 0, 2, 1, 0, 3, 1, 3, 0, 1, 2, 0, 0, 0, 1, 1, 1, 2, 3, 1, 1, 1, 1, 3, 3, 1, 3, 1, 0, 2, 2, 3, 1, 2, 3),
)
FIRST_STEP = (
    (0, 0, 0, 1, 2, 0, 3, 0, 0, 0, 1, 0, 1, 0, 1, 2, 1, 1, 0, 1, 1, 0, 1, 1, 2, 3, 2, 2, 0, 1, 2, 1, 0, 0, 0, 1, 2, 0, 1, 2, 3, 2, 0, 0, 1, 1, 2, 3, 2, 2, 3, 2, 2, 3, 3, 3, 3, 2, 2, 3, 3, 3, 3, 3, 3, 3),
    (0, 1, 2, 0, 0, 0, 0, 0, 0, 2, 0, 3, 0, 2, 1, 0, 0, 1, 0, 1, 1, 1, 2, 1, 2, 2, 3, 1, 1, 0, 3, 1, 3, 0, 1, 1, 1, 2, 1, 3, 2, 1, 3, 3, 0, 2, 2, 3, 3, 0, 2, 3, 3, 3, 0, 2, 3, 3, 0, 2, 2, 3, 3, 1, 2, 2),
)
FIRST_WHAT = (
    (4, 5, 2, 4, 4, 0, 4, 0, 1, 6, 1, 1, 6, 2, 0, 6, 2, 2, 3, 0, 1, 3, 3, 3, 2, 6, 0, 1, 3, 3, 3, 3, 3, 7, 8, 8, 3, 8, 8, 0, 0, 8, 8, 8, 8, 8, 8, 1, 2, 1, 2, 3, 8, 3, 2, 8, 0, 3, 8, 3, 1, 3, 8, 8, 3, 8),
    (4, 4, 4, 5, 0, 0, 1, 2, 3, 1, 1, 4, 6, 2, 0, 3, 2, 2, 3, 6, 0, 1, 0, 3, 3, 6, 6, 3, 1, 7, 0, 2, 2, 8, 3, 8, 3, 0, 8, 1, 2, 8, 3, 8, 8, 1, 3, 2, 3, 3, 8, 1, 0, 3, 8, 3, 8, 3, 8, 8, 3, 8, 8, 8, 8, 8),
)
OPS = len(GATHER_KIND[0])
WORKS = tuple(
    tuple(
        number for number in range(OPS) if parts[number] == 3
    )
    for parts in GATHER_PART
)


def by_place(tables, index):
    place = lax.axis_index("fsdp")
    at_end = (place == 0) | (place == SIDE - 1)
    return jnp.where(at_end, digit(tables[0], index), digit(tables[1], index))


def gather_slot(kind, step):
    ctx, place, twin, across, twin_across = neighbours()
    line = digit_of_row(NEAR, place, step)
    owner = jnp.where(
        kind == 0, ctx, jnp.where(kind == 1, across, jnp.where(kind == 2, twin, twin_across))
    )
    return line, owner * SIDE + line


def work_slot(number):
    kind = by_place(
        tuple(tuple(row[at] for at in places) for row, places in zip(GATHER_KIND, WORKS)), number
    )
    step = by_place(
        tuple(tuple(row[at] for at in places) for row, places in zip(GATHER_STEP, WORKS)), number
    )
    return gather_slot(kind, step)[1]


def gather_blocks(
    land, every, up, down, side, core, arrived, core_arrived, kept, work, tables=None, more=()
):
    ctx, place, twin, across, _ = neighbours()
    kinds, steps, parts = tables or (GATHER_KIND, GATHER_STEP, GATHER_PART)
    at_end = (place == 0) | (place == SIDE - 1)

    def copies(kind, line, slot, part):
        start, size = PARTS[part]
        block = land.at[slot, pl.ds(start, size)]
        row, met = kind * SIDE + line, arrived.at[slot, part]
        return (
            lambda: to_axis(block, block, up.at[row, part], met, "fsdp", place + 1),
            lambda: to_axis(block, block, down.at[row, part], met, "fsdp", place - 1),
            lambda: to_axis(block, block, side.at[line, part], met, "ctx", across),
        )

    def routes(kind, line, part):
        goes_up = (line <= place) & (place < SIDE - 1)
        goes_down = (line >= place) & (place > 0)
        if part == LAST:
            return goes_up, goes_down, (kind == 0) & (line == place)
        return goes_up & (kind == 0), goes_down & (kind == 0), kind == 0

    def core_copy(kind, line, slot):
        block = land.at[slot]
        return to_axis(
            block, block, core.at[kind * SIDE + line], core_arrived.at[slot], "ctx", twin
        )

    def step_op(number, counts):
        worked, made = counts
        kind, step = by_place(kinds, number), by_place(steps, number)
        part = jnp.where(at_end, nibble(parts[0], number), nibble(parts[1], number))
        line, slot = gather_slot(kind, step)
        for which in range(len(PARTS)):

            @pl.when(part == which)
            def _(which=which):
                @pl.when((kind == 1) | (line != place))
                def _():
                    copies(kind, line, slot, which)[2]().wait_recv()

                for copy, goes in zip(
                    copies(kind, line, slot, which), routes(kind, line, which)
                ):

                    @pl.when(goes)
                    def _(copy=copy):
                        copy().start()

        @pl.when(part == 3)
        def _():
            @pl.when(kind <= 1)
            def _():
                core_copy(kind, line, slot).start()

            @pl.when(kind >= 2)
            def _():
                core_copy(kind - 2, line, slot).wait_recv()

            if every is not None:
                pltpu.make_async_copy(land.at[slot], every.at[slot], kept.at[slot]).start()
            work(worked, slot)

        for which, further in enumerate(more):

            @pl.when(part == 4 + which)
            def _(further=further):
                further(step, slot, made)

        return worked + jnp.where(part == 3, 1, 0), made + jnp.where(part == 8, 1, 0)

    lax.fori_loop(0, len(kinds[0]), step_op, (jnp.int32(0), jnp.int32(0)))

    def finish(number, carry):
        kind, line = number // SIDE, lax.rem(number, SIDE)
        slot = jnp.where(kind == 0, ctx, across) * SIDE + line
        for which in range(len(PARTS)):
            for copy, goes in zip(copies(kind, line, slot, which), routes(kind, line, which)):

                @pl.when(goes)
                def _(copy=copy):
                    copy().wait_send()

        core_copy(kind, line, slot).wait_send()
        return carry

    lax.fori_loop(0, 2 * SIDE, finish, 0)

    def finish_kept(slot, carry):
        pltpu.make_async_copy(land.at[slot], every.at[slot], kept.at[slot]).wait()
        return carry

    if every is not None:
        lax.fori_loop(0, GROUP, finish_kept, 0)


def gather_scratch(rows):
    parts = len(PARTS)
    return [
        pltpu.VMEM((GROUP, rows, D), jnp.bfloat16),
        pltpu.SemaphoreType.DMA((2 * SIDE, parts)),
        pltpu.SemaphoreType.DMA((2 * SIDE, parts)),
        pltpu.SemaphoreType.DMA((SIDE, parts)),
        pltpu.SemaphoreType.DMA((2 * SIDE,)),
        pltpu.SemaphoreType.DMA((GROUP, parts)),
        pltpu.SemaphoreType.DMA((GROUP,)),
        pltpu.SemaphoreType.DMA((GROUP,)),
    ]


def spin(values, cosine, sine, sign):
    lane = lax.rem(lax.broadcasted_iota(jnp.int32, values.shape, 1), HEAD_DIM)
    partner = jnp.where(
        lane < ROT // 2,
        -pltpu.roll(values, HEAD_COLS - ROT // 2, 1),
        pltpu.roll(values, ROT // 2, 1),
    )
    return values * cosine + sign * (partner * sine)


STRIP = 32


def each_strip(rows, body, start):
    def step(number, carry):
        return body(pl.ds(pl.multiple_of(number * STRIP, STRIP), STRIP), carry)

    return lax.fori_loop(0, rows // STRIP, step, start)


def column_places(block):
    return [
        (0, pl.multiple_of(part * D + block * HEAD_COLS, HEAD_COLS), part * HEAD_COLS, HEAD_COLS)
        for part in range(3)
    ] + [(1, pl.multiple_of(block * FEED_COLS, FEED_COLS), JOINT_COLS, FEED_COLS)]


PLACES = 4


def load_all(pairs, sems):
    copies = [
        pltpu.make_async_copy(source, target, sems.at[number])
        for number, (source, target) in enumerate(pairs)
    ]
    for copy in copies:
        copy.start()
    return copies


def wait_all(copies):
    for copy in copies:
        copy.wait()


def ring_scratch(rows):
    return [
        pltpu.VMEM((2, rows, HEAD_COLS), jnp.bfloat16),
        pltpu.VMEM((2, rows, HEAD_COLS), jnp.bfloat16),
        pltpu.VMEM((2, rows, HEAD_COLS), jnp.bfloat16),
        pltpu.VMEM((2, rows, FEED_COLS), jnp.float32),
        pltpu.VMEM((2, rows, FEED_COLS), jnp.bfloat16),
        pltpu.SemaphoreType.DMA((2, 5)),
    ]


def ring_shapes(rows):
    return [
        jax.ShapeDtypeStruct((GROUP, rows, width), dtype)
        for width, dtype in (
            (HEAD_COLS, jnp.bfloat16),
            (HEAD_COLS, jnp.bfloat16),
            (HEAD_COLS, jnp.bfloat16),
            (FEED_COLS, jnp.float32),
            (FEED_COLS, jnp.bfloat16),
        )
    ]


def ring_product(rings, sems, results, land, columns, bias, cosine, sine):
    query, key, value, inner, active = rings

    def leave(at, slot):
        return [
            pltpu.make_async_copy(ring.at[at], result.at[slot], sems.at[at, which])
            for which, (ring, result) in enumerate(zip(rings, results))
        ]

    def product(number, slot):
        whole = dot(land[slot], columns[...].reshape(D, COLS)) + bias[...]
        one, two = HEAD_COLS, 2 * HEAD_COLS
        at = lax.rem(number, 2)

        @pl.when(number >= 2)
        def _():
            wait_all(leave(at, 0))

        query[at] = spin(whole[:, :one], cosine[slot], sine[slot], 1.0).astype(jnp.bfloat16)
        key[at] = spin(whole[:, one:two], cosine[slot], sine[slot], 1.0).astype(jnp.bfloat16)
        value[at] = whole[:, two:JOINT_COLS].astype(jnp.bfloat16)
        units = whole[:, JOINT_COLS:]
        inner[at] = units
        active[at] = jax.nn.gelu(units, approximate=True).astype(jnp.bfloat16)
        for copy in leave(at, slot):
            copy.start()

    def finish():
        for at in range(2):
            wait_all(leave(at, 0))

    return product, finish


def norm_block(hidden, gain, shift, land, me):
    def strip(part, carry):
        values = hidden[part].astype(jnp.float32)
        centred = values - jnp.mean(values, axis=1, keepdims=True)
        spread = jnp.mean(centred * centred, axis=1, keepdims=True)
        normed = centred * lax.rsqrt(spread + EPS) * gain[...] + shift[...]
        land[me, part] = normed.astype(jnp.bfloat16)
        return carry

    each_strip(hidden.shape[0], strip, 0)


def forward_gather(hidden, gain, shift, bias, tables, halves, layer):
    rows = hidden.shape[0]
    half = SHARE // 2

    def kernel(hidden, gain, shift, bias, turn_a, turn_b, own_half, other_half, *refs):
        every, columns_out, results, refs = refs[0], refs[1], refs[2:7], refs[7:]
        cosine, sine, columns, load_sem, saved = refs[:5]
        rings, ring_sem, refs = refs[5:10], refs[10], refs[11:]
        land, sems = refs[0], refs[1:]
        ctx, place, seq = lax.axis_index("ctx"), lax.axis_index("fsdp"), lax.axis_index("seq")
        part_rows = pl.ds(pl.multiple_of(seq * half, half), half)
        other_rows = pl.ds(pl.multiple_of((1 - seq) * half, half), half)
        loads = load_all(
            (
                (own_half, columns.at[:, part_rows]),
                (other_half, columns.at[:, other_rows]),
                (turn_a, cosine),
                (turn_b, sine),
            ),
            load_sem,
        )
        greet_neighbours()
        norm_block(hidden, gain, shift, land, ctx * SIDE + place)
        save = pltpu.make_async_copy(columns, columns_out, saved)
        product, finish = ring_product(rings, ring_sem, results, land, columns, bias, cosine, sine)

        def work(number, slot):
            @pl.when(number == 0)
            def _():
                wait_all(loads)
                save.start()

            product(number, slot)

        gather_blocks(land, every, *sems, work)
        save.wait()
        finish()

    return pl.pallas_call(
        kernel,
        out_shape=[
            jax.ShapeDtypeStruct((GROUP, rows, D), jnp.bfloat16),
            jax.ShapeDtypeStruct((GROUP, SHARE, COLS), jnp.bfloat16),
        ]
        + ring_shapes(rows),
        in_specs=[VMEM] * 4 + [HBM] * 4,
        out_specs=[HBM] * 7,
        scratch_shapes=[pltpu.VMEM((GROUP, rows, HEAD_COLS), jnp.float32)] * 2
        + [
            pltpu.VMEM((GROUP, SHARE, COLS), jnp.bfloat16),
            pltpu.SemaphoreType.DMA((4,)),
            pltpu.SemaphoreType.DMA,
        ]
        + ring_scratch(rows)
        + gather_scratch(rows),
        compiler_params=pltpu.CompilerParams(
            collective_id=30 + layer, has_side_effects=True, vmem_limit_bytes=ROOM
        ),
    )(hidden, gain, shift, bias, *tables, *halves)


GAIN_ROW, SHIFT_ROW, JOINT_BIAS_ROW, OUT_BIAS_ROW, DOWN_BIAS_ROW, LAYER_ROWS = 0, 1, 2, 5, 6, 7
BEGIN_ROW = LAYERS * LAYER_ROWS


def first_gather(hidden, packed, up_bias, frequency, qkv_weight, up_weight):
    rows = hidden.shape[0]
    half = SHARE // 2

    def kernel(hidden, packed, up_bias, frequency, qkv_weight, up_weight, *refs):
        every, columns_out, results, small, cosine, sine = refs[0], refs[1], refs[2:7], *refs[7:10]
        refs = refs[10:]
        columns, plane_send, plane_recv, cross_send, cross_recv, own_sem, saved = refs[:7]
        small_send, small_recv, gain, shift, bias = refs[7:12]
        rings, ring_sem, refs = refs[12:17], refs[17], refs[18:]
        land, sems = refs[0], refs[1:]
        ctx, place, seq = lax.axis_index("ctx"), lax.axis_index("fsdp"), lax.axis_index("seq")
        me = ctx * SIDE + place
        part_rows = pl.ds(pl.multiple_of(seq * half, half), half)
        sources = (qkv_weight, up_weight)
        greet_plane(GROUP)

        def small_copy(step):
            return to_peer(
                packed,
                small.at[me],
                small_send.at[step],
                small_recv.at[me],
                lax.rem(me + step, GROUP),
            )

        def small_begin(step, carry):
            small_copy(step).start()
            return carry

        lax.fori_loop(1, GROUP, small_begin, 0)
        small[me] = packed[...]

        def piece(step, number):
            peer = lax.rem(me + step, GROUP)
            which, start, at, width = column_places(peer)[number]
            return (
                peer,
                sources[which].at[0, part_rows, pl.ds(start, width)],
                columns.at[me, part_rows, pl.ds(at, width)],
            )

        def send_piece(step, number):
            peer, source, target = piece(step, number)
            return to_peer(
                source, target, plane_send.at[step, number], plane_recv.at[me, number], peer
            )

        def own_piece(number):
            _, source, target = piece(0, number)
            return pltpu.make_async_copy(source, target, own_sem.at[number])

        def cross(source):
            block = columns.at[source, part_rows]
            return to_axis(
                block, block, cross_send.at[source], cross_recv.at[source], "seq", 1 - seq
            )

        for number in range(PLACES):
            own_piece(number).start()

        def send_columns(group, slot, made):
            def send(more, carry):
                step = SIDE * group + more

                @pl.when(step > 0)
                def _():
                    for number in range(PLACES):
                        send_piece(step, number).start()

                return carry

            lax.fori_loop(0, SIDE, send, 0)

        def norm_own(group, slot, made):
            def arrive(step, carry):
                source = lax.rem(me + GROUP - step, GROUP)
                to_peer(
                    packed, small.at[source], small_send.at[step], small_recv.at[source], source
                ).wait_recv()
                return carry

            lax.fori_loop(1, GROUP, arrive, 0)

            def whole_row(row):
                return jnp.concatenate(
                    [small[block, row : row + 1] for block in range(GROUP)], axis=1
                )

            gain[...] = whole_row(GAIN_ROW)
            shift[...] = whole_row(SHIFT_ROW)
            for part in range(3):
                at = part * GROUP + me
                bias[:, part * HEAD_COLS : (part + 1) * HEAD_COLS] = small[
                    at // 3, pl.ds(JOINT_BIAS_ROW + lax.rem(at, 3), 1)
                ]
            bias[:, JOINT_COLS:] = up_bias[...]
            norm_block(hidden, gain, shift, land, me)

        def pass_columns(group, slot, made):
            def pass_on(more, carry):
                step = SIDE * group + more
                source = lax.rem(me + GROUP - step, GROUP)

                @pl.when(step == 0)
                def _():
                    for number in range(PLACES):
                        own_piece(number).wait()

                @pl.when(step > 0)
                def _():
                    for number in range(PLACES):
                        _, _, at, width = column_places(0)[number]
                        target = columns.at[source, part_rows, pl.ds(at, width)]
                        to_peer(
                            target,
                            target,
                            plane_send.at[0, number],
                            plane_recv.at[source, number],
                            source,
                        ).wait_recv()

                cross(source).start()
                return carry

            lax.fori_loop(0, SIDE, pass_on, 0)

        save = pltpu.make_async_copy(columns, columns_out, saved)

        def wait_columns(group, slot, made):
            def arrive(source, carry):
                cross(source).wait_recv()
                return carry

            lax.fori_loop(0, GROUP, arrive, 0)
            save.start()

        product, finish = ring_product(rings, ring_sem, results, land, columns, bias, cosine, sine)

        def next_product(group, slot, made):
            product(made, slot)

        def work(number, slot):
            begin = jnp.concatenate(
                [small[slot, BEGIN_ROW + part : BEGIN_ROW + part + 1] for part in range(rows // SHARE)],
                axis=1,
            )
            begin = jnp.broadcast_to(begin, (8, rows)).T[:, :1]
            first = (slot // SIDE) * rows
            token = lax.broadcasted_iota(jnp.int32, (rows, 1), 0) + first
            angle = (token.astype(jnp.float32) - begin) * frequency[...]
            cosine[slot] = jnp.cos(angle)
            sine[slot] = jnp.sin(angle)

        gather_blocks(
            land,
            every,
            *sems,
            work,
            (FIRST_KIND, FIRST_STEP, FIRST_WHAT),
            (send_columns, norm_own, pass_columns, wait_columns, next_product),
        )
        save.wait()
        finish()

        def end(step, carry):
            cross(step).wait_send()

            @pl.when(step > 0)
            def _():
                small_copy(step).wait_send()
                for number in range(PLACES):
                    send_piece(step, number).wait_send()

            return carry

        lax.fori_loop(0, GROUP, end, 0)

    return pl.pallas_call(
        kernel,
        out_shape=[
            jax.ShapeDtypeStruct((GROUP, rows, D), jnp.bfloat16),
            jax.ShapeDtypeStruct((GROUP, SHARE, COLS), jnp.bfloat16),
        ]
        + ring_shapes(rows)
        + [jax.ShapeDtypeStruct((GROUP,) + packed.shape, packed.dtype)]
        + [jax.ShapeDtypeStruct((GROUP, rows, HEAD_COLS), jnp.float32)] * 2,
        in_specs=[VMEM] * 4 + [HBM] * 2,
        out_specs=[HBM] * 7 + [VMEM] * 3,
        scratch_shapes=[
            pltpu.VMEM((GROUP, SHARE, COLS), jnp.bfloat16),
            pltpu.SemaphoreType.DMA((GROUP, PLACES)),
            pltpu.SemaphoreType.DMA((GROUP, PLACES)),
            pltpu.SemaphoreType.DMA((GROUP,)),
            pltpu.SemaphoreType.DMA((GROUP,)),
            pltpu.SemaphoreType.DMA((PLACES,)),
            pltpu.SemaphoreType.DMA,
            pltpu.SemaphoreType.DMA((GROUP,)),
            pltpu.SemaphoreType.DMA((GROUP,)),
            pltpu.VMEM((1, D), jnp.float32),
            pltpu.VMEM((1, D), jnp.float32),
            pltpu.VMEM((1, COLS), jnp.float32),
        ]
        + ring_scratch(rows)
        + gather_scratch(rows),
        compiler_params=pltpu.CompilerParams(
            collective_id=30, has_side_effects=True, vmem_limit_bytes=ROOM
        ),
    )(hidden, packed, up_bias, frequency, qkv_weight, up_weight)


def backward_gather(grad, out_weight, down_weight, inner, mixed, active):
    rows = grad.shape[0]

    def kernel(own, out_weight, down_weight, inner, mixed, active, grad_mixed, grad_inner, branch, *refs):
        out_part, down_part, weight_sem, total = refs[:4]
        fetched, fetch_sem, rings, ring_sem = refs[4:7], refs[7], refs[8:10], refs[10]
        land, sems = refs[11], refs[12:]
        inner_part, mixed_part, active_part = fetched
        ctx, place, _, _, _ = neighbours()

        def fetch(number):
            at, slot = lax.rem(number, 2), work_slot(number)
            return [
                pltpu.make_async_copy(source.at[slot], target.at[at], fetch_sem.at[at, which])
                for which, (source, target) in enumerate(zip((inner, mixed, active), fetched))
            ]

        def leave(number):
            at, slot = lax.rem(number, 2), work_slot(number)
            return [
                pltpu.make_async_copy(ring.at[at], result.at[slot], ring_sem.at[at, which])
                for which, (ring, result) in enumerate(zip(rings, (grad_mixed, grad_inner)))
            ]

        weights = load_all(((out_weight, out_part), (down_weight, down_part)), weight_sem)
        for copy in fetch(jnp.int32(0)):
            copy.start()
        greet_neighbours()
        land[ctx * SIDE + place] = own[...]
        total[...] = jnp.zeros_like(total)

        def work(number, slot):
            at = lax.rem(number, 2)

            @pl.when(number == 0)
            def _():
                wait_all(weights)

            @pl.when(number + 1 < GROUP)
            def _():
                for copy in fetch(number + 1):
                    copy.start()

            @pl.when(number >= 2)
            def _():
                wait_all(leave(number - 2))

            wait_all(fetch(number))
            block = land[slot]
            rings[0][at] = dot(block, out_part[...], 1, 1)
            value = inner_part[at]
            factor = math.sqrt(2.0 / math.pi)
            square = value * value
            bend = jnp.tanh(factor * value * (1.0 + 0.044715 * square))
            slope = 0.5 * (1.0 + bend) + 0.5 * value * (1.0 - bend * bend) * (
                factor * (1.0 + 3 * 0.044715 * square)
            )
            rings[1][at] = (dot(block, down_part[...], 1, 1) * slope).astype(jnp.bfloat16)
            for copy in leave(number):
                copy.start()
            total[:HEAD_COLS] += dot(mixed_part[at], block, 0, 0)
            total[HEAD_COLS:] += dot(active_part[at], block, 0, 0)

        gather_blocks(land, None, *sems, work)
        branch[...] = total[...].astype(jnp.bfloat16)
        for number in (GROUP - 2, GROUP - 1):
            wait_all(leave(jnp.int32(number)))

    return pl.pallas_call(
        kernel,
        out_shape=(
            jax.ShapeDtypeStruct((GROUP, rows, HEAD_COLS), jnp.float32),
            jax.ShapeDtypeStruct((GROUP, rows, FEED_COLS), jnp.bfloat16),
            jax.ShapeDtypeStruct((BACK_COLS, D), jnp.bfloat16),
        ),
        in_specs=[VMEM] + [HBM] * 5,
        out_specs=(HBM, HBM, VMEM),
        scratch_shapes=[
            pltpu.VMEM(out_weight.shape, jnp.bfloat16),
            pltpu.VMEM(down_weight.shape, jnp.bfloat16),
            pltpu.SemaphoreType.DMA((2,)),
            pltpu.VMEM((BACK_COLS, D), jnp.float32),
            pltpu.VMEM((2, rows, FEED_COLS), jnp.float32),
            pltpu.VMEM((2, rows, HEAD_COLS), jnp.bfloat16),
            pltpu.VMEM((2, rows, FEED_COLS), jnp.bfloat16),
            pltpu.SemaphoreType.DMA((2, 3)),
            pltpu.VMEM((2, rows, HEAD_COLS), jnp.float32),
            pltpu.VMEM((2, rows, FEED_COLS), jnp.bfloat16),
            pltpu.SemaphoreType.DMA((2, 2)),
        ]
        + gather_scratch(rows),
        compiler_params=pltpu.CompilerParams(
            collective_id=4, has_side_effects=True, vmem_limit_bytes=ROOM
        ),
    )(grad, out_weight, down_weight, inner, mixed, active)


SCATTER_OPS = (
    ((0, 0), (0, 1), (1, 0), (2, 0), (1, 1), (0, 2), (2, 1), (3, 0), (1, 2), (2, 2), (4, 0), (6, 0), (5, 0), (0, 3), (3, 1), (3, 2), (1, 3), (3, 3), (4, 1), (5, 1), (6, 1), (4, 2), (5, 2), (6, 2), (2, 3), (4, 3), (5, 3), (6, 3)),
    ((0, 0), (0, 2), (3, 2), (1, 0), (3, 0), (0, 1), (0, 3), (1, 1), (2, 0), (1, 2), (3, 1), (1, 3), (4, 0), (6, 0), (5, 0), (3, 3), (2, 1), (2, 2), (4, 1), (6, 1), (5, 1), (4, 2), (5, 2), (6, 2), (2, 3), (4, 3), (5, 3), (6, 3)),
)
SCATTER_OPS_WORK = (
    ((0, 0), (0, 1), (1, 0), (2, 0), (1, 1), (0, 2), (2, 1), (3, 0), (1, 2), (2, 2), (4, 0), (6, 0), (7, 0), (5, 0), (0, 3), (3, 1), (3, 2), (1, 3), (3, 3), (4, 1), (7, 0), (5, 1), (7, 0), (7, 0), (7, 0), (7, 0), (7, 0), (6, 1), (4, 2), (7, 0), (5, 2), (7, 0), (7, 0), (7, 0), (6, 2), (2, 3), (7, 0), (7, 0), (7, 0), (7, 0), (7, 0), (4, 3), (5, 3), (6, 3)),
    ((0, 0), (0, 2), (3, 2), (1, 0), (3, 0), (7, 0), (0, 1), (0, 3), (1, 1), (2, 0), (1, 2), (3, 1), (7, 0), (7, 0), (1, 3), (4, 0), (6, 0), (7, 0), (5, 0), (7, 0), (7, 0), (3, 3), (2, 1), (7, 0), (2, 2), (7, 0), (7, 0), (4, 1), (6, 1), (5, 1), (4, 2), (5, 2), (7, 0), (7, 0), (7, 0), (6, 2), (7, 0), (7, 0), (7, 0), (2, 3), (7, 0), (4, 3), (5, 3), (6, 3)),
)
SCATTER_OPS_EARLY = (
    ((0, 0), (0, 1), (1, 0), (3, 0), (2, 0), (0, 2), (1, 1), (2, 1), (1, 2), (2, 2), (0, 3), (4, 0), (6, 0), (7, 0), (7, 0), (7, 0), (5, 0), (7, 0), (3, 1), (1, 3), (7, 0), (7, 0), (7, 0), (4, 1), (7, 0), (7, 0), (7, 0), (6, 1), (7, 0), (5, 1), (7, 0), (7, 0), (7, 0), (7, 0), (7, 0), (3, 2), (3, 3), (2, 3), (4, 2), (5, 2), (6, 2), (8, 0), (8, 1), (8, 2), (8, 3), (4, 3), (5, 3), (6, 3)),
    ((0, 2), (7, 0), (0, 0), (0, 1), (1, 0), (7, 0), (7, 0), (0, 3), (7, 0), (3, 3), (3, 0), (7, 0), (1, 1), (2, 0), (3, 2), (1, 2), (7, 0), (2, 2), (7, 0), (7, 0), (3, 1), (1, 3), (4, 0), (6, 0), (7, 0), (2, 1), (7, 0), (7, 0), (7, 0), (5, 0), (7, 0), (7, 0), (7, 0), (7, 0), (2, 3), (4, 1), (6, 1), (5, 1), (4, 2), (5, 2), (6, 2), (8, 0), (8, 1), (8, 2), (8, 3), (4, 3), (5, 3), (6, 3)),
)
SPLIT = ((0, 208), (208, 48))


def scatter_events(partial, other_work, late_work, ops, scratch):
    total, give, take, side_take, line_take, other_take = scratch[:6]
    core_send, core_recv, side_send, side_recv, line_send, line_recv = scratch[6:12]
    other_send, other_recv = scratch[12:]
    ctx, place, twin, across, twin_across = neighbours()
    below, above = place - 1, place + 1
    has_below, has_above = place > 0, place < SIDE - 1
    at_end = (place == 0) | (place == SIDE - 1)

    def rows_of(part):
        return pl.ds(*SPLIT[part])

    def core_copy(step, store):
        return to_axis(
            give.at[step], take.at[store], core_send.at[store], core_recv.at[store], "ctx", twin
        )

    def side_copy(step, part):
        return to_axis(
            take.at[step, rows_of(part)],
            side_take.at[step, rows_of(part)],
            side_send.at[step, part],
            side_recv.at[step, part],
            "ctx",
            across,
        )

    def line_copy(step, line, slot, target, part):
        return to_axis(
            take.at[SIDE + step, rows_of(part)],
            line_take.at[slot, rows_of(part)],
            line_send.at[line, part],
            line_recv.at[slot, part],
            "fsdp",
            target,
        )

    def other_copy(step, line, slot, target):
        return to_axis(
            take.at[step, rows_of(1)],
            other_take.at[slot],
            other_send.at[line],
            other_recv.at[slot],
            "fsdp",
            target,
        )

    def from_above(line):
        return jnp.where(line == place, SIDE, line)

    def to_below(line):
        return jnp.where(line == place - 1, SIDE, line)

    def one(number, turn):
        def by_end(field):
            ends, middle = (tuple(entry[field] for entry in table) for table in ops)
            return jnp.where(at_end, nibble(ends, number), nibble(middle, number))

        what, step = by_end(0), by_end(1)
        line = digit_of_row(FAR, place, step)

        @pl.when((what <= 1) | (what == 3) | (what == 4))
        def _():
            owner = jnp.where(
                what == 0,
                twin_across,
                jnp.where(what == 1, across, jnp.where(what == 3, twin, ctx)),
            )
            total[...] = partial(owner * SIDE + line)

        @pl.when(what == 0)
        def _():
            give[step] = total[...].astype(jnp.bfloat16)
            core_copy(step, step).start()

        @pl.when(what == 1)
        def _():
            core_copy(step, step).wait_recv()
            take[step] = (total[...] + take[step].astype(jnp.float32)).astype(jnp.bfloat16)
            side_copy(step, 0).start()

        @pl.when(what == 2)
        def _():
            rows = rows_of(1)

            @pl.when((line >= place) & has_below)
            def _():
                other_copy(step, line, line, below).wait_recv()
                take[step, rows] = (
                    take[step, rows].astype(jnp.float32) + other_take[line].astype(jnp.float32)
                ).astype(jnp.bfloat16)

            @pl.when((line <= place) & has_above)
            def _():
                other_copy(step, line, from_above(line), above).wait_recv()
                take[step, rows] = (
                    take[step, rows].astype(jnp.float32)
                    + other_take[from_above(line)].astype(jnp.float32)
                ).astype(jnp.bfloat16)

            @pl.when(line > place)
            def _():
                other_copy(step, line, line, above).start()

            @pl.when(line < place)
            def _():
                other_copy(step, line, to_below(line), below).start()

            @pl.when(line == place)
            def _():
                side_copy(step, 1).start()

        @pl.when(what == 3)
        def _():
            core_copy(step, step).wait_send()
            give[step] = total[...].astype(jnp.bfloat16)
            core_copy(step, SIDE + step).start()

        @pl.when(what == 4)
        def _():
            core_copy(step, SIDE + step).wait_recv()
            total[...] += take[SIDE + step].astype(jnp.float32)

        for part in range(2):
            rows = rows_of(part)

            @pl.when(what == 5 + part)
            def _(rows=rows, part=part):
                crossed = line == place if part == 1 else line >= 0

                @pl.when(crossed)
                def _():
                    side_copy(step, part).wait_recv()
                    total[rows] += side_take[step, rows].astype(jnp.float32)

                @pl.when((line >= place) & has_below)
                def _():
                    line_copy(step, line, line, below, part).wait_recv()
                    total[rows] += line_take[line, rows].astype(jnp.float32)

                @pl.when((line <= place) & has_above)
                def _():
                    line_copy(step, line, from_above(line), above, part).wait_recv()
                    total[rows] += line_take[from_above(line), rows].astype(jnp.float32)

                @pl.when(line > place)
                def _():
                    take[SIDE + step, rows] = total[rows].astype(jnp.bfloat16)
                    line_copy(step, line, line, above, part).start()

                @pl.when(line < place)
                def _():
                    take[SIDE + step, rows] = total[rows].astype(jnp.bfloat16)
                    line_copy(step, line, to_below(line), below, part).start()

        if other_work is not None:

            @pl.when(what == 7)
            def _():
                other_work(turn)

        if late_work is not None:

            @pl.when(what == 8)
            def _():
                late_work(step)

        return turn + jnp.where(what == 7, 1, 0)

    lax.fori_loop(0, len(ops[0]), one, jnp.int32(0))

    def finish(step, carry):
        line = digit_of_row(FAR, place, step)
        core_copy(step, SIDE + step).wait_send()
        side_copy(step, 0).wait_send()

        @pl.when(line == place)
        def _():
            side_copy(step, 1).wait_send()

        @pl.when(line != place)
        def _():
            for part in range(2):
                line_copy(step, line, line, place, part).wait_send()
            other_copy(step, line, line, place).wait_send()

        return carry

    lax.fori_loop(0, SIDE, finish, 0)


def scatter_scratch(rows):
    return [
        pltpu.VMEM((rows, D), jnp.float32),
        pltpu.VMEM((SIDE, rows, D), jnp.bfloat16),
        pltpu.VMEM((2 * SIDE, rows, D), jnp.bfloat16),
        pltpu.VMEM((SIDE, rows, D), jnp.bfloat16),
        pltpu.VMEM((SIDE + 1, rows, D), jnp.bfloat16),
        pltpu.VMEM((SIDE + 1, SPLIT[1][1], D), jnp.bfloat16),
        pltpu.SemaphoreType.DMA((2 * SIDE,)),
        pltpu.SemaphoreType.DMA((2 * SIDE,)),
        pltpu.SemaphoreType.DMA((SIDE, 2)),
        pltpu.SemaphoreType.DMA((SIDE, 2)),
        pltpu.SemaphoreType.DMA((SIDE, 2)),
        pltpu.SemaphoreType.DMA((SIDE + 1, 2)),
        pltpu.SemaphoreType.DMA((SIDE,)),
        pltpu.SemaphoreType.DMA((SIDE + 1,)),
    ]


def forward_scatter(hidden, bias, mixed, active, out_weight, down_weight, layer):
    rows = hidden.shape[0]

    def kernel(hidden, bias, mixed, active, out_weight, down_weight, out, *refs):
        hidden_part, mixed_part, active_part, out_part, down_part, load_sem = refs[:6]
        scratch = refs[6:]
        loads = load_all(
            (
                (mixed, mixed_part),
                (active, active_part),
                (out_weight, out_part),
                (down_weight, down_part),
                (hidden, hidden_part),
            ),
            load_sem,
        )
        greet_neighbours()
        wait_all(loads[:4])

        def partial(slot):
            return dot(mixed_part[slot], out_part[...]) + dot(active_part[slot], down_part[...])

        scatter_events(partial, None, None, SCATTER_OPS, scratch)
        loads[4].wait()
        out[...] = hidden_part[...].astype(jnp.float32) + (scratch[0][...] + bias[...])

    return pl.pallas_call(
        kernel,
        out_shape=jax.ShapeDtypeStruct((rows, D), jnp.float32),
        in_specs=[HBM, VMEM] + [HBM] * 4,
        out_specs=VMEM,
        scratch_shapes=[
            pltpu.VMEM(array.shape, array.dtype)
            for array in (hidden, mixed, active, out_weight, down_weight)
        ]
        + [pltpu.SemaphoreType.DMA((5,))]
        + scatter_scratch(rows),
        compiler_params=pltpu.CompilerParams(
            collective_id=10 + layer, has_side_effects=True, vmem_limit_bytes=ROOM
        ),
    )(hidden, bias, mixed, active, out_weight, down_weight)


SMALL_ROWS = 16
PAIRS = GROUP // 2


def backward_scatter(
    hidden, grad, gain, grad_joint, grad_inner, columns, every, layer, up=None, halves=()
):
    rows = hidden.shape[0]
    half = SHARE // 2
    collects = up is not None
    made = JOINT_COLS if collects else COLS
    tokens = GROUP * rows

    def kernel(*refs):
        inputs, refs = refs[: 10 if collects else 7], refs[10 if collects else 7 :]
        gain, every = inputs[2], inputs[6]
        out, small_out, refs = refs[0], refs[1], refs[2:]
        if collects:
            outputs, others, refs = refs[:2], refs[2:4], refs[4:]
        else:
            mine, refs = refs[0], refs[1:]
        hidden, grad, grad_joint, grad_inner, columns, load_sem, strips, load = refs[:8]
        shares, small_land, small_mine, small_other = refs[8:12]
        small_send, small_recv, swap_send, swap_recv = refs[12:16]
        refs = refs[16:]
        if collects:
            mine, other, summed, arrived, arrived_up = refs[:5]
            cross_send, cross_recv, plane_send, plane_recv = refs[5:9]
            back_send, back_recv, keep = refs[9:12]
            up_send, up_recv, up_own, half_send, half_recv = refs[12:17]
            refs = refs[17:]
        scratch = refs
        total = scratch[0]
        ctx, place, seq = lax.axis_index("ctx"), lax.axis_index("fsdp"), lax.axis_index("seq")
        me = ctx * SIDE + place
        part_rows = pl.ds(pl.multiple_of(seq * half, half), half)
        other_rows = pl.ds(pl.multiple_of((1 - seq) * half, half), half)

        def pair_of(turn):
            return lax.rem(me // 2 + 1 + turn, PAIRS)

        def load_strip(turn):
            start = pl.multiple_of(pair_of(turn) * 2 * SHARE, 2 * SHARE)
            buffer = lax.rem(turn, 2)
            return pltpu.make_async_copy(
                every.at[:, :, pl.ds(start, 2 * SHARE)], strips.at[buffer], load.at[buffer]
            )

        loads = load_all(
            (
                (inputs[3], grad_joint),
                (inputs[4], grad_inner),
                (inputs[5], columns),
                (inputs[0], hidden),
                (inputs[1], grad),
            ),
            load_sem,
        )
        load_strip(jnp.int32(0)).start()
        greet_plane(GROUP)

        def partial(slot):
            return dot(grad_joint[slot], columns[:, :JOINT_COLS], 1, 1) + dot(
                grad_inner[slot], columns[:, JOINT_COLS:], 1, 1
            )

        def product(turn):
            pair = pair_of(turn)
            load_strip(turn).wait()

            @pl.when(turn + 1 < PAIRS)
            def _():
                load_strip(turn + 1).start()

            strip = strips[lax.rem(turn, 2)].reshape(tokens, 2 * SHARE)
            made = dot(strip, grad_joint[...].reshape(tokens, JOINT_COLS), 0, 0).astype(jnp.bfloat16)
            for which in range(2):
                mine[2 * pair + which, :, :JOINT_COLS] = made[which * SHARE : (which + 1) * SHARE]
            if not collects:
                made = dot(strip, grad_inner[...].reshape(tokens, FEED_COLS), 0, 0).astype(
                    jnp.bfloat16
                )
                for which in range(2):
                    mine[2 * pair + which, :, JOINT_COLS:] = made[which * SHARE : (which + 1) * SHARE]

        def cross_copy(block):
            return to_axis(
                mine.at[block, other_rows],
                other.at[block],
                cross_send.at[block],
                cross_recv.at[block],
                "seq",
                1 - seq,
            )

        def plane_copy(block):
            return to_peer(
                summed.at[block], arrived.at[me], plane_send.at[block], plane_recv.at[me], block
            )

        def up_copy(step):
            peer = lax.rem(me + step, GROUP)
            return to_peer(inputs[7].at[peer], arrived_up.at[me], up_send.at[step], up_recv.at[me], peer)

        def half_copies(pieces):
            return [
                to_axis(
                    own.at[pl.ds(piece * (half // 4), half // 4)],
                    there.at[pl.ds(piece * (half // 4), half // 4)],
                    half_send.at[at, piece],
                    half_recv.at[at, piece],
                    "seq",
                    1 - seq,
                )
                for at, (own, there) in enumerate(zip(inputs[8:10], others))
                for piece in pieces
            ]

        def final_pieces(source):
            pieces = []
            for number, (which, start, at, width) in enumerate(column_places(source)):
                piece = arrived_up.at[source] if which else arrived.at[source, :, pl.ds(at, width)]
                pieces.append((number, piece, outputs[which].at[part_rows, pl.ds(start, width)]))
            return pieces

        def back_copy(number, piece, target, source):
            return to_axis(
                piece,
                target,
                back_send.at[source, number],
                back_recv.at[source, number],
                "seq",
                1 - seq,
            )

        def keep_copy(number, piece, target, source):
            return pltpu.make_async_copy(piece, target, keep.at[source, number])

        def pass_on(source, which):
            for number, piece, target in final_pieces(source):
                if (number == PLACES - 1) == (which == 1):
                    back_copy(number, piece, target, source).start()
                    keep_copy(number, piece, target, source).start()

        def add(turn):
            for which in range(2):
                block = 2 * pair_of(turn) + which
                cross_copy(block).wait_recv()
                summed[block] = (
                    mine[block, part_rows].astype(jnp.float32) + other[block].astype(jnp.float32)
                ).astype(jnp.bfloat16)

                @pl.when(block != me)
                def _(block=block):
                    plane_copy(block).start()

        def other_work(turn):
            @pl.when(lax.rem(turn, 2) == 0)
            def _():
                product(turn // 2)
                if collects:
                    for which in range(2):
                        cross_copy(2 * pair_of(turn // 2) + which).start()

            if collects:

                @pl.when((lax.rem(turn, 2) == 1) & (turn > 4))
                def _():
                    add((turn - 5) // 2)

                @pl.when(turn == GROUP - 1)
                def _():
                    for copy in half_copies((2, 3)):
                        copy.start()

        def late_work(step):
            def pass_up(more, carry):
                number = SIDE * step + more
                source = lax.rem(me + GROUP - number, GROUP)

                @pl.when(number == 0)
                def _():
                    own_up.wait()

                @pl.when(number > 0)
                def _():
                    block = arrived_up.at[source]
                    to_peer(block, block, up_send.at[number], up_recv.at[source], source).wait_recv()

                pass_on(source, 1)
                return carry

            lax.fori_loop(0, SIDE, pass_up, 0)

        def last_adds(turn, carry):
            add(turn)
            return carry

        def send_up(step, carry):
            up_copy(step).start()
            return carry

        wait_all(loads[:3])
        if collects:
            own_up = pltpu.make_async_copy(inputs[7].at[me], arrived_up.at[me], up_own)
            own_up.start()
            lax.fori_loop(1, GROUP, send_up, 0)
            for copy in half_copies((0, 1)):
                copy.start()
        scatter_events(
            partial,
            other_work,
            late_work if collects else None,
            SCATTER_OPS_EARLY if collects else SCATTER_OPS_WORK,
            scratch,
        )
        if collects:
            lax.fori_loop(PAIRS - 2, PAIRS, last_adds, 0)
            arrived[me] = summed[me]
        wait_all(loads[3:])

        def norm_back(part, sums):
            values = hidden[part].astype(jnp.float32)
            centred = values - jnp.mean(values, axis=1, keepdims=True)
            spread = jnp.mean(centred * centred, axis=1, keepdims=True)
            root = lax.rsqrt(spread + EPS)
            normed = centred * root
            above = total[part]
            scaled = above * gain[...]
            down = jnp.mean(scaled, axis=1, keepdims=True)
            along = jnp.mean(scaled * normed, axis=1, keepdims=True)
            passing = grad[part]
            out[part] = passing + root * (scaled - down - normed * along)
            low = passing.astype(jnp.bfloat16).astype(jnp.float32)

            def fold(values):
                return jnp.sum(values.reshape(STRIP // 8, 8, D), axis=0)

            return (sums[0] + fold(above * normed), sums[1] + fold(above), sums[2] + fold(low))

        zeros = jnp.zeros((8, D), jnp.float32)
        sums = each_strip(rows, norm_back, (zeros, zeros, zeros))
        shares[...] = jnp.zeros_like(shares)
        for number, folded in enumerate(sums):
            row = jnp.sum(folded, axis=0, keepdims=True)
            for block in range(GROUP):
                shares[block, number : number + 1] = row[:, block * SHARE : (block + 1) * SHARE]
        ones = jnp.ones((16, tokens), jnp.bfloat16)
        joint_bias = dot(ones, grad_joint[...].reshape(tokens, JOINT_COLS))[:1]
        upper_bias = dot(ones, grad_inner[...].reshape(tokens, FEED_COLS))[:1]
        for part in range(3):
            at = part * GROUP + me
            shares[at // 3, pl.ds(3 + lax.rem(at, 3), 1)] = joint_bias[
                :, part * HEAD_COLS : (part + 1) * HEAD_COLS
            ]
        for part in range(FEED_COLS // SHARE):
            shares[me, 6 + part : 7 + part] = upper_bias[:, part * SHARE : (part + 1) * SHARE]

        def small_copy(step):
            peer = lax.rem(me + step, GROUP)
            return to_peer(
                shares.at[peer], small_land.at[me], small_send.at[step], small_recv.at[me], peer
            )

        def small_begin(step, carry):
            small_copy(step).start()
            return carry

        lax.fori_loop(1, GROUP, small_begin, 0)
        small_land[me] = shares[me]

        def pass_joint(step, carry):
            source = lax.rem(me + GROUP - step, GROUP)

            @pl.when(step > 0)
            def _():
                to_peer(
                    summed.at[source],
                    arrived.at[source],
                    plane_send.at[source],
                    plane_recv.at[source],
                    source,
                ).wait_recv()

            pass_on(source, 0)
            return carry

        if collects:
            lax.fori_loop(0, GROUP, pass_joint, 0)

        def small_end(step, carry):
            source = lax.rem(me + GROUP - step, GROUP)
            to_peer(
                shares.at[source],
                small_land.at[source],
                small_send.at[step],
                small_recv.at[source],
                source,
            ).wait_recv()
            small_copy(step).wait_send()
            return carry

        lax.fori_loop(1, GROUP, small_end, 0)
        small_mine[...] = jnp.sum(small_land[...], axis=0)
        swap = to_axis(small_mine, small_other, swap_send, swap_recv, "seq", 1 - seq)
        swap.start()
        swap.wait()
        small_out[...] = small_mine[...] + small_other[...]

        def end(block, carry):
            cross_copy(block).wait_send()

            @pl.when(block != me)
            def _():
                plane_copy(block).wait_send()

            @pl.when(block > 0)
            def _():
                up_copy(block).wait_send()

            for number, piece, target in final_pieces(block):
                back_copy(number, piece, target, block).wait()
                keep_copy(number, piece, target, block).wait()
            return carry

        if collects:
            lax.fori_loop(0, GROUP, end, 0)
            wait_all(half_copies((0, 1, 2, 3)))

    def part(width, height=half):
        return pltpu.VMEM((GROUP, height, width), jnp.bfloat16)

    small = (SMALL_ROWS, SHARE)
    sixteen, places = pltpu.SemaphoreType.DMA((GROUP,)), pltpu.SemaphoreType.DMA((GROUP, PLACES))
    return pl.pallas_call(
        kernel,
        out_shape=(
            jax.ShapeDtypeStruct((rows, D), jnp.float32),
            jax.ShapeDtypeStruct(small, jnp.float32),
        )
        + (
            (
                jax.ShapeDtypeStruct((SHARE, 3 * D), jnp.bfloat16),
                jax.ShapeDtypeStruct((SHARE, FF), jnp.bfloat16),
                jax.ShapeDtypeStruct((half, 3 * D), jnp.bfloat16),
                jax.ShapeDtypeStruct((half, FF), jnp.bfloat16),
            )
            if collects
            else (jax.ShapeDtypeStruct((GROUP, SHARE, COLS), jnp.bfloat16),)
        ),
        in_specs=[HBM, HBM, VMEM] + [HBM] * (7 if collects else 4),
        out_specs=(VMEM, VMEM) + ((HBM,) * 4 if collects else (VMEM,)),
        scratch_shapes=[
            pltpu.VMEM(array.shape, array.dtype)
            for array in (hidden, grad, grad_joint, grad_inner, columns)
        ]
        + [
            pltpu.SemaphoreType.DMA((5,)),
            pltpu.VMEM((2, GROUP, rows, 2 * SHARE), jnp.bfloat16),
            pltpu.SemaphoreType.DMA((2,)),
            pltpu.VMEM((GROUP,) + small, jnp.float32),
            pltpu.VMEM((GROUP,) + small, jnp.float32),
            pltpu.VMEM(small, jnp.float32),
            pltpu.VMEM(small, jnp.float32),
            sixteen,
            sixteen,
            pltpu.SemaphoreType.DMA,
            pltpu.SemaphoreType.DMA,
        ]
        + (
            [part(JOINT_COLS, SHARE)]
            + [part(JOINT_COLS)] * 3
            + [part(FEED_COLS)]
            + [sixteen] * 4
            + [places] * 3
            + [sixteen] * 2
            + [pltpu.SemaphoreType.DMA]
            + [pltpu.SemaphoreType.DMA((2, 4))] * 2
            if collects
            else []
        )
        + scatter_scratch(rows),
        compiler_params=pltpu.CompilerParams(
            collective_id=20 + layer, has_side_effects=True, vmem_limit_bytes=ROOM
        ),
    )(hidden, grad, gain, grad_joint, grad_inner, columns, every, *((up, *halves) if collects else ()))


def mask_rest(rows, begin, spot, first, lead):
    if lead:
        old = jnp.where(spot[:lead] >= begin, rows[:lead], NEG)
    key_at = lax.broadcasted_iota(jnp.int32, (first, first), 0) + lead
    query_at = lax.broadcasted_iota(jnp.int32, (first, first), 1) + lead
    near = spot[lead:]
    seen = ((near >= begin) & (near <= query_at)) | (key_at == query_at)
    new = jnp.where(seen, rows[lead:], NEG)
    return jnp.concatenate([old, new], axis=0) if lead else new


def head_lanes(head, rows):
    lane = lax.broadcasted_iota(jnp.int32, (rows, HEAD_COLS), 1)
    return (lane >= head * HEAD_DIM) & (lane < (head + 1) * HEAD_DIM)


def column_exchange(sources, land, sems, layer):
    plane_send, plane_recv, own_sem = sems
    ctx, place, seq = lax.axis_index("ctx"), lax.axis_index("fsdp"), lax.axis_index("seq")
    me = ctx * SIDE + place
    half = SHARE // 2
    part_rows = pl.ds(pl.multiple_of(seq * half, half), half)

    def piece(peer, number):
        which, start, at, width = column_places(peer)[number]
        return (
            sources[which].at[layer, part_rows, pl.ds(start, width)],
            land.at[me, :, pl.ds(at, width)],
        )

    def send_piece(step, number):
        peer = lax.rem(me + step, GROUP)
        source, target = piece(peer, number)
        return to_peer(source, target, plane_send.at[step, number], plane_recv.at[me, number], peer)

    def own_piece(number):
        return pltpu.make_async_copy(*piece(me, number), own_sem.at[number])

    def begin():
        greet_plane(GROUP, False)

        def send(step, carry):
            for number in range(PLACES):
                send_piece(step, number).start()
            return carry

        lax.fori_loop(1, GROUP, send, 0)
        for number in range(PLACES):
            own_piece(number).start()

    def end():
        def arrive(step, carry):
            source = lax.rem(me + GROUP - step, GROUP)
            for number in range(PLACES):
                _, _, at, width = column_places(0)[number]
                target = land.at[source, :, pl.ds(at, width)]
                to_peer(
                    target, target, plane_send.at[0, number], plane_recv.at[source, number], source
                ).wait_recv()
                send_piece(step, number).wait_send()
            return carry

        lax.fori_loop(1, GROUP, arrive, 0)
        for number in range(PLACES):
            own_piece(number).wait()

    return begin, end


def up_products(every, feed, out, scratch):
    feed_part, strips, mine, other, feed_sem, load, cross_send, cross_recv = scratch
    rows = feed.shape[1]
    tokens = GROUP * rows
    half = SHARE // 2
    seq = lax.axis_index("seq")
    me = lax.axis_index("ctx") * SIDE + lax.axis_index("fsdp")
    part_rows = pl.ds(pl.multiple_of(seq * half, half), half)
    other_rows = pl.ds(pl.multiple_of((1 - seq) * half, half), half)

    def pair_of(turn):
        return lax.rem(me // 2 + 1 + turn, PAIRS)

    def load_strip(turn):
        start = pl.multiple_of(pair_of(turn) * 2 * SHARE, 2 * SHARE)
        buffer = lax.rem(turn, 2)
        return pltpu.make_async_copy(
            every.at[:, :, pl.ds(start, 2 * SHARE)], strips.at[buffer], load.at[buffer]
        )

    def cross_copy(block):
        return to_axis(
            mine.at[block, other_rows],
            other.at[block],
            cross_send.at[block],
            cross_recv.at[block],
            "seq",
            1 - seq,
        )

    def feed_copy():
        return pltpu.make_async_copy(feed, feed_part, feed_sem)

    def begin():
        feed_copy().start()
        load_strip(jnp.int32(0)).start()

    def product(turn, carry):
        pair = pair_of(turn)
        load_strip(turn).wait()

        @pl.when(turn == 0)
        def _():
            feed_copy().wait()

        @pl.when(turn + 1 < PAIRS)
        def _():
            load_strip(turn + 1).start()

        strip = strips[lax.rem(turn, 2)].reshape(tokens, 2 * SHARE)
        made = dot(strip, feed_part[...].reshape(tokens, FEED_COLS), 0, 0).astype(jnp.bfloat16)
        for which in range(2):
            mine[2 * pair + which] = made[which * SHARE : (which + 1) * SHARE]
            cross_copy(2 * pair + which).start()
        return carry

    def add(turn, carry):
        for which in range(2):
            block = 2 * pair_of(turn) + which
            cross_copy(block).wait()
            out[block] = (
                mine[block, part_rows].astype(jnp.float32) + other[block].astype(jnp.float32)
            ).astype(jnp.bfloat16)
        return carry

    each = PAIRS // SIDE

    def make(step):
        lax.fori_loop(each * step, each * step + each, product, 0)
        lax.fori_loop(each * jnp.maximum(step - 1, 0), each * step, add, 0)

    def end():
        lax.fori_loop(PAIRS - each, PAIRS, add, 0)

    return begin, make, end


def row_exchange(summed, outputs, sems):
    plane_send, plane_recv, own_sem = sems
    me = lax.axis_index("ctx") * SIDE + lax.axis_index("fsdp")

    def piece(peer, number):
        which, start, at, width = column_places(me)[number]
        return summed.at[peer, :, pl.ds(at, width)], outputs[which].at[:, pl.ds(start, width)]

    def send_piece(step, number):
        peer = lax.rem(me + step, GROUP)
        source, target = piece(peer, number)
        return to_peer(source, target, plane_send.at[step, number], plane_recv.at[me, number], peer)

    def own_piece(number):
        return pltpu.make_async_copy(*piece(me, number), own_sem.at[number])

    def begin():
        greet_plane(GROUP)

        def send(step, carry):
            for number in range(PLACES):
                send_piece(step, number).start()
            return carry

        lax.fori_loop(1, GROUP, send, 0)
        for number in range(PLACES):
            own_piece(number).start()

    def end():
        def arrive(step, carry):
            source = lax.rem(me + GROUP - step, GROUP)
            for number in range(PLACES):
                which, start, _, width = column_places(source)[number]
                target = outputs[which].at[:, pl.ds(start, width)]
                to_peer(
                    target, target, plane_send.at[0, number], plane_recv.at[source, number], source
                ).wait_recv()
                send_piece(step, number).wait_send()
            return carry

        lax.fori_loop(1, GROUP, arrive, 0)
        for number in range(PLACES):
            own_piece(number).wait()

    return begin, end


EXCHANGE_SEMS = [
    pltpu.SemaphoreType.DMA((GROUP, PLACES)),
    pltpu.SemaphoreType.DMA((GROUP, PLACES)),
    pltpu.SemaphoreType.DMA((PLACES,)),
]


def attend_plane(query, key, value, begin, spot, weights=None, layer=0):
    rows = query.shape[1]
    length = SIDE * rows
    scale = 1.0 / math.sqrt(HEAD_DIM)

    def kernel(query, key, value, begin, spot, *refs):
        if weights is None:
            mixed, turned, stats = refs
        else:
            mixed, turned, stats, land = refs[2:6]
            begin_exchange, end_exchange = column_exchange(refs[:2], land, refs[6:], layer)
            pl.when(pl.program_id(0) == 0)(begin_exchange)
        keys = key[:, 0].reshape(length, HEAD_COLS)
        values = value[:, 0].reshape(length, HEAD_COLS)
        for chunk in range(SIDE):
            lead = chunk * rows
            seen = lead + rows
            scaled = query[chunk, 0] * jnp.bfloat16(scale)
            start = begin[0, :, lead:seen]
            outs = []
            for head in range(OWN):
                own = jnp.where(head_lanes(head, rows), scaled, jnp.bfloat16(0))
                scores = mask_rest(
                    dot(keys[:seen], own, 1, 1), start, spot[0, :seen], rows, lead
                )
                peak = jnp.max(scores, axis=0, keepdims=True)
                probs = jnp.exp(scores - peak)
                norm = jnp.sum(probs, axis=0, keepdims=True)
                stats[0, head : head + 1, lead:seen] = peak
                stats[0, OWN + head : OWN + head + 1, lead:seen] = norm
                whole = dot(values[:seen], probs.astype(jnp.bfloat16), 0, 0)
                outs.append(whole[head * HEAD_DIM : (head + 1) * HEAD_DIM] / norm)
            joined = jnp.concatenate(outs, axis=0)
            turned[chunk, 0] = joined
            mixed[chunk, 0] = joined.T.astype(jnp.bfloat16)
        if weights is not None:
            pl.when(pl.program_id(0) == SIDE - 1)(end_exchange)

    def spec(height, width):
        return pl.BlockSpec((SIDE, 1, height, width), lambda step: (0, step, 0, 0))

    def shape(height, width, dtype):
        return jax.ShapeDtypeStruct((SIDE, SIDE, height, width), dtype)

    extra = weights is not None
    land = (jax.ShapeDtypeStruct((GROUP, SHARE // 2, COLS), jnp.bfloat16),) if extra else ()
    mixed, turned, stats, *land = pl.pallas_call(
        kernel,
        grid=(SIDE,),
        out_shape=(
            shape(rows, HEAD_COLS, jnp.bfloat16),
            shape(HEAD_COLS, rows, jnp.float32),
            jax.ShapeDtypeStruct((SIDE, 2 * OWN, length), jnp.float32),
        )
        + land,
        in_specs=[spec(rows, HEAD_COLS)] * 3
        + [
            pl.BlockSpec((1, 1, length), lambda step: (step, 0, 0)),
            pl.BlockSpec((1, length, 1), lambda step: (step, 0, 0)),
        ]
        + [HBM] * (2 if extra else 0),
        out_specs=(
            spec(rows, HEAD_COLS),
            spec(HEAD_COLS, rows),
            pl.BlockSpec((1, 2 * OWN, length), lambda step: (step, 0, 0)),
        )
        + ((HBM,) if extra else ()),
        scratch_shapes=EXCHANGE_SEMS if extra else [],
        compiler_params=pltpu.CompilerParams(
            collective_id=40, has_side_effects=True, vmem_limit_bytes=ROOM
        )
        if extra
        else pltpu.CompilerParams(vmem_limit_bytes=ROOM),
    )(
        *(array.reshape(SIDE, SIDE, rows, HEAD_COLS) for array in (query, key, value)),
        begin,
        spot,
        *(weights or ()),
    )
    return mixed.reshape(GROUP, rows, HEAD_COLS), turned, stats, *land


def attend_plane_back(
    query, key, value, begin, spot, turned, stats, grad, tables, summed=None, every=None, feed=None
):
    rows = query.shape[1]
    length = SIDE * rows
    scale = 1.0 / math.sqrt(HEAD_DIM)

    extra = summed is not None

    def kernel(query, key, value, grad, cosine, sine, begin, spot, turned, stats, *refs):
        if extra:
            summed, every, feed, out = refs[:4]
            up_out, grad_k, grad_v = refs[6], refs[7], refs[8]
            begin_exchange, end_exchange = row_exchange(summed, refs[4:6], refs[9:12])
            begin_up, make_up, end_up = up_products(every, feed, up_out, refs[12:])

            @pl.when(pl.program_id(0) == 0)
            def _():
                begin_up()
                begin_exchange()

        else:
            out, grad_k, grad_v = refs
        keys = key[:, 0].reshape(length, HEAD_COLS)
        values = value[:, 0].reshape(length, HEAD_COLS)
        for chunk in range(SIDE):
            lead = chunk * rows
            seen = lead + rows
            if chunk == 0:
                grad_k[...] = jnp.zeros_like(grad_k)
                grad_v[...] = jnp.zeros_like(grad_v)
            scaled = query[chunk, 0] * jnp.bfloat16(scale)
            start = begin[0, :, lead:seen]
            flipped = grad[chunk, 0].T
            grad_q, drifts, numers = [], [], []
            for head in range(OWN):
                part = slice(head * HEAD_DIM, (head + 1) * HEAD_DIM)
                norm = stats[0, OWN + head : OWN + head + 1, lead:seen]
                drifts.append(
                    jnp.sum(flipped[part] * turned[chunk, 0, part], axis=0, keepdims=True) / norm
                )
                numers.append(flipped[part] / norm)
            numer = jnp.concatenate(numers, axis=0).T.astype(jnp.bfloat16)
            for head in range(OWN):
                part = slice(head * HEAD_DIM, (head + 1) * HEAD_DIM)
                lanes = head_lanes(head, rows)
                own = jnp.where(lanes, scaled, jnp.bfloat16(0))
                own_numer = jnp.where(lanes, numer, jnp.bfloat16(0))
                scores = mask_rest(
                    dot(keys[:seen], own, 1, 1), start, spot[0, :seen], rows, lead
                )
                probs = jnp.exp(scores - stats[0, head : head + 1, lead:seen])
                grad_probs = dot(values[:seen], own_numer, 1, 1)
                grad_scores = (probs * (grad_probs - drifts[head])).astype(jnp.bfloat16)
                grad_q.append(dot(keys[:seen], grad_scores, 0, 0)[part])
                grad_k[:seen] += dot(grad_scores, own)
                grad_v[:seen] += dot(probs.astype(jnp.bfloat16), own_numer)
            turns = (cosine[chunk, 0], sine[chunk, 0])
            whole = jnp.concatenate(grad_q, axis=0).T * scale
            out[chunk, 0, :, :HEAD_COLS] = spin(whole, *turns, -1.0).astype(jnp.bfloat16)
        for chunk in range(SIDE):
            place = slice(chunk * rows, (chunk + 1) * rows)
            turns = (cosine[chunk, 0], sine[chunk, 0])
            out[chunk, 0, :, HEAD_COLS : 2 * HEAD_COLS] = spin(grad_k[place], *turns, -1.0).astype(
                jnp.bfloat16
            )
            out[chunk, 0, :, 2 * HEAD_COLS :] = grad_v[place].astype(jnp.bfloat16)
        if extra:
            make_up(pl.program_id(0))

            @pl.when(pl.program_id(0) == SIDE - 1)
            def _():
                end_up()
                end_exchange()


    def spec(height, width):
        return pl.BlockSpec((SIDE, 1, height, width), lambda step: (0, step, 0, 0))

    half = SHARE // 2
    halves = (
        jax.ShapeDtypeStruct((half, 3 * D), jnp.bfloat16),
        jax.ShapeDtypeStruct((half, FF), jnp.bfloat16),
        jax.ShapeDtypeStruct((GROUP, half, FEED_COLS), jnp.bfloat16),
    )
    out, *halves = pl.pallas_call(
        kernel,
        grid=(SIDE,),
        out_shape=(jax.ShapeDtypeStruct((SIDE, SIDE, rows, JOINT_COLS), jnp.bfloat16),)
        + (halves if extra else ()),
        in_specs=[spec(rows, HEAD_COLS)] * 6
        + [
            pl.BlockSpec((1, 1, length), lambda step: (step, 0, 0)),
            pl.BlockSpec((1, length, 1), lambda step: (step, 0, 0)),
            spec(HEAD_COLS, rows),
            pl.BlockSpec((1, 2 * OWN, length), lambda step: (step, 0, 0)),
        ]
        + [HBM] * (3 if extra else 0),
        out_specs=(spec(rows, JOINT_COLS),)
        + (
            (HBM, HBM, pl.BlockSpec((GROUP, half, FEED_COLS), lambda step: (0, 0, 0)))
            if extra
            else ()
        ),
        scratch_shapes=[pltpu.VMEM((length, HEAD_COLS), jnp.float32)] * 2
        + (
            EXCHANGE_SEMS
            + [
                pltpu.VMEM((GROUP, rows, FEED_COLS), jnp.bfloat16),
                pltpu.VMEM((2, GROUP, rows, 2 * SHARE), jnp.bfloat16),
                pltpu.VMEM((GROUP, SHARE, FEED_COLS), jnp.bfloat16),
                pltpu.VMEM((GROUP, half, FEED_COLS), jnp.bfloat16),
                pltpu.SemaphoreType.DMA,
                pltpu.SemaphoreType.DMA((2,)),
                pltpu.SemaphoreType.DMA((GROUP,)),
                pltpu.SemaphoreType.DMA((GROUP,)),
            ]
            if extra
            else []
        ),
        compiler_params=pltpu.CompilerParams(
            collective_id=41, has_side_effects=True, vmem_limit_bytes=ROOM
        )
        if extra
        else pltpu.CompilerParams(vmem_limit_bytes=ROOM),
    )(
        *(
            array.reshape(SIDE, SIDE, rows, HEAD_COLS)
            for array in (query, key, value, grad) + tuple(tables)
        ),
        begin,
        spot,
        turned,
        stats,
        *((summed, every, feed) if extra else ()),
    )
    return out.reshape(GROUP, rows, JOINT_COLS), *halves


def on_device_split(
    tokens,
    doc_lengths,
    keep_mask,
    ln_gain,
    ln_bias,
    qkv_weight,
    qkv_bias,
    out_weight,
    out_bias,
    up_weight,
    up_bias,
    down_weight,
    down_bias,
    cotangent,
):
    rows = tokens.shape[1]
    length = SIDE * rows
    me = lax.axis_index("ctx") * SIDE + lax.axis_index("fsdp")

    index = lax.axis_index("ctx") * rows + jnp.arange(rows, dtype=jnp.int32)
    ends = jnp.cumsum(doc_lengths[0])
    begin = jnp.max(jnp.where(index[:, None] >= ends[None, :], ends[None, :], 0), axis=1)
    fields = [ln_gain, ln_bias, qkv_bias, out_bias, down_bias]
    packed = jnp.concatenate(
        [field[layer].astype(jnp.float32) for layer in range(LAYERS) for field in fields]
        + [begin.astype(jnp.float32), keep_mask[0].astype(jnp.float32)]
    )
    packed = jnp.pad(packed, (0, -packed.shape[0] % (8 * SHARE))).reshape(-1, SHARE)
    lane = np.arange(HEAD_COLS) % HEAD_DIM
    inverse = 1.0 / 10000.0 ** (np.arange(0, ROT, 2, dtype=np.float32) / np.float32(ROT))
    inverse = np.where(lane < ROT, inverse[lane % (ROT // 2)], 0.0).astype(np.float32)
    up_bias = up_bias.astype(jnp.float32)

    seq = lax.axis_index("seq")
    half = SHARE // 2
    swap = [(0, 1), (1, 0)]

    def swapped(values):
        return lax.ppermute(values, "seq", swap)

    hidden = tokens[0]
    saved, gains, joint_grads, upper_grads, branch_grads, small_grads = [], [], [], [], [], []
    for layer in range(LAYERS):
        if layer == 0:
            *out, small, cosine, sine = first_gather(
                hidden, packed, up_bias[:1], jnp.asarray(inverse)[None, :], qkv_weight, up_weight
            )
            tables = (cosine, sine)
            length_rows = rows // SHARE

            def by_sequence(row):
                values = small[:, row : row + length_rows].reshape(SIDE, SIDE, rows)
                return values.transpose(1, 0, 2).reshape(SIDE, length).astype(jnp.int32)

            begin = by_sequence(BEGIN_ROW)[:, None, :]
            keep = by_sequence(BEGIN_ROW + length_rows)
            spot = jnp.where(keep > 0, jnp.arange(length, dtype=jnp.int32)[None, :], -1)[:, :, None]
        else:
            out = forward_gather(
                hidden,
                gain_row,
                row_of(layer, SHIFT_ROW),
                jnp.concatenate([own_bias, up_bias[layer : layer + 1]], axis=1),
                tables,
                halves,
                layer,
            )

        def row_of(layer, row):
            return small[:, layer * LAYER_ROWS + row].reshape(1, D)

        every, columns, query, key, value, inner, active = out
        gains.append(row_of(layer, GAIN_ROW))
        if layer + 1 < LAYERS:
            mixed, turned, stats, arrived = attend_plane(
                query, key, value, begin, spot, (qkv_weight, up_weight), layer + 1
            )
            halves = (arrived, swapped(arrived))
            gain_row = row_of(layer + 1, GAIN_ROW)
            at = (layer + 1) * LAYER_ROWS + JOINT_BIAS_ROW
            own_bias = lax.dynamic_slice_in_dim(
                small[:, at : at + 3].reshape(3, GROUP, HEAD_COLS), me, 1, axis=1
            ).reshape(1, JOINT_COLS)
        else:
            mixed, turned, stats = attend_plane(query, key, value, begin, spot)
        saved.append(
            (hidden, every, columns, query, key, value, inner, active, mixed, turned, stats)
        )
        hidden = forward_scatter(
            hidden,
            row_of(layer, OUT_BIAS_ROW) + row_of(layer, DOWN_BIAS_ROW),
            mixed,
            active,
            out_weight[layer],
            down_weight[layer],
            layer,
        )
    result = hidden.astype(jnp.bfloat16)[None]

    grad_hidden = cotangent[0].astype(jnp.float32) * keep_mask[0].astype(jnp.float32)[:, None]
    summed = None
    for layer in reversed(range(LAYERS)):
        before, every, columns, query, key, value, inner, active, mixed, turned, stats = saved[layer]
        grad_mixed, grad_inner, branch = backward_gather(
            grad_hidden.astype(jnp.bfloat16),
            out_weight[layer],
            down_weight[layer],
            inner,
            mixed,
            active,
        )
        branch_grads.insert(
            0, branch.astype(jnp.float32) + swapped(branch).astype(jnp.float32)
        )
        grad_joint, *rest = attend_plane_back(
            query,
            key,
            value,
            begin,
            spot,
            turned,
            stats,
            grad_mixed,
            tables,
            summed,
            every,
            grad_inner,
        )
        grad_hidden, small, *grads = backward_scatter(
            before,
            grad_hidden,
            gains[layer],
            grad_joint,
            grad_inner,
            columns.reshape(D, COLS),
            every,
            layer,
            rest[2] if rest else None,
            rest[:2],
        )
        small_grads.insert(0, small)
        if layer > 0:
            own = lax.dynamic_slice_in_dim(grads[0], seq * half, half, axis=1)
            other = swapped(lax.dynamic_slice_in_dim(grads[0], (1 - seq) * half, half, axis=1))
            summed = (own.astype(jnp.float32) + other.astype(jnp.float32)).astype(jnp.bfloat16)
        else:
            for total, whole, own, other in zip(
                (joint_grads, upper_grads), grads[:2], rest[:2], grads[2:]
            ):
                first, second = jnp.where(seq == 0, own, other), jnp.where(seq == 0, other, own)
                total.extend([whole, jnp.concatenate([first, second], axis=0)])
    branch_grad = jnp.stack(branch_grads)
    small = jnp.stack(small_grads)
    return (
        result,
        grad_hidden[None],
        small[:, 0],
        small[:, 1],
        jnp.stack(joint_grads).astype(jnp.float32),
        small[:, 3:6].reshape(LAYERS, JOINT_COLS),
        branch_grad[:, :HEAD_COLS],
        small[:, 2],
        jnp.stack(upper_grads).astype(jnp.float32),
        small[:, 6:10].reshape(LAYERS, FEED_COLS),
        branch_grad[:, HEAD_COLS:],
        small[:, 2],
    )


def solution(mesh):
    small = mesh.shape["ctx"] == SIDE and mesh.shape["fsdp"] == SIDE and mesh.shape["seq"] == 2
    on_device = on_device_split if small else on_device_gathered
    return jax.shard_map(
        on_device,
        mesh=mesh,
        in_specs=(
            P(("seq", "fsdp"), "ctx", None),
            P(("seq", "fsdp"), None),
            P(("seq", "fsdp"), "ctx"),
            P(None, ("ctx", "fsdp")),
            P(None, ("ctx", "fsdp")),
            P(None, ("ctx", "fsdp"), None),
            P(None, ("ctx", "fsdp")),
            P(None, ("ctx", "fsdp"), None),
            P(None, ("ctx", "fsdp")),
            P(None, ("ctx", "fsdp"), None),
            P(None, ("ctx", "fsdp")),
            P(None, ("ctx", "fsdp"), None),
            P(None, ("ctx", "fsdp")),
            P(("seq", "fsdp"), "ctx", None),
        ),
        out_specs=(
            P(("seq", "fsdp"), "ctx", None),
            P(("seq", "fsdp"), "ctx", None),
            P(None, ("ctx", "fsdp")),
            P(None, ("ctx", "fsdp")),
            P(None, ("ctx", "fsdp"), None),
            P(None, ("ctx", "fsdp")),
            P(None, ("ctx", "fsdp"), None),
            P(None, ("ctx", "fsdp")),
            P(None, ("ctx", "fsdp"), None),
            P(None, ("ctx", "fsdp")),
            P(None, ("ctx", "fsdp"), None),
            P(None, ("ctx", "fsdp")),
        ),
        check_vma=False,
    )
```

```python
import functools
import math

import jax
import jax.numpy as jnp
import numpy as np
from jax import lax
from jax.experimental import pallas as pl
from jax.experimental.pallas import tpu as pltpu
from jax.sharding import PartitionSpec as P

D = 2048
HEADS = 32
HEAD_DIM = 64
ROT = 32
FF = 8192
LAYERS = 2


EPS = 1e-05
NEG = -1e30


def place_tokens(token_index, lengths):
    bounds = jnp.cumsum(lengths)
    starts = bounds - lengths
    segment = jnp.sum((token_index[:, None] >= bounds[None, :]).astype(jnp.int32), axis=1)
    chosen = segment[:, None] == jnp.arange(lengths.shape[0], dtype=jnp.int32)[None, :]
    position = token_index - jnp.sum(jnp.where(chosen, starts[None, :], 0), axis=1)
    return (segment, position)


def angles(position):
    indices = jnp.arange(0, ROT, 2, dtype=jnp.float32) / ROT
    inverse = 1.0 / 10000.0**indices
    turned = position.astype(jnp.float32)[:, None] * inverse[None, :]
    turned = jnp.concatenate([turned, turned], axis=1)
    return (jnp.cos(turned), jnp.sin(turned))


def rotate(values, cosine, sine):
    rotary = values[..., :ROT]
    middle = ROT // 2
    turned = jnp.concatenate([-rotary[..., middle:], rotary[..., :middle]], axis=-1)
    mixed = rotary * cosine[:, None, :] + turned * sine[:, None, :]
    return jnp.concatenate([mixed, values[..., ROT:]], axis=-1)


def normalize(hidden, gain_row, shift_row):
    average = jnp.mean(hidden, axis=1, keepdims=True)
    centred = hidden - average
    spread = jnp.mean(centred * centred, axis=1, keepdims=True)
    return centred * lax.rsqrt(spread + EPS) * gain_row + shift_row


def block_scores(queries, travelling, start, query_index, query_segment, lengths):
    key_flat, value_flat, key_keep = travelling
    count = key_flat.shape[0]
    key_index = start + jnp.arange(count, dtype=jnp.int32)
    key_segment = place_tokens(key_index, lengths)[0]
    allowed = (
        (query_segment[:, None] == key_segment[None, :])
        & (key_index[None, :] <= query_index[:, None])
        & ((key_keep[None, :] > 0) | (key_index[None, :] == query_index[:, None]))
    )
    key_rows = key_flat.reshape(count, HEADS, HEAD_DIM)
    value_rows = value_flat.reshape(count, HEADS, HEAD_DIM)
    scores = jnp.einsum("qhd,khd->hqk", queries, key_rows, preferred_element_type=jnp.float32) * (
        1.0 / math.sqrt(HEAD_DIM)
    )
    return (scores, allowed, key_rows, value_rows)


def attend(running, travelling, start, queries, query_index, query_segment, lengths):
    maxima, totals, weighted = running
    scores, allowed, key_rows, value_rows = block_scores(
        queries, travelling, start, query_index, query_segment, lengths
    )
    masked = jnp.where(allowed[None], scores, NEG)
    new_max = jnp.maximum(maxima, jnp.max(masked, axis=2))
    probs = jnp.where(allowed[None], jnp.exp(masked - new_max[:, :, None]), 0.0)
    totals = jnp.sum(probs, axis=2)
    weighted = jnp.einsum(
        "hqk,khd->hqd", probs.astype(jnp.bfloat16), value_rows, preferred_element_type=jnp.float32
    )
    return (new_max, totals, weighted)


def attend_back(
    travelling, start, queries, maxima, grad_numer, drift, query_index, query_segment, lengths
):
    scores, allowed, key_rows, value_rows = block_scores(
        queries, travelling, start, query_index, query_segment, lengths
    )
    count = key_rows.shape[0]
    scale = 1.0 / math.sqrt(HEAD_DIM)
    probs = jnp.where(allowed[None], jnp.exp(scores - maxima[:, :, None]), 0.0)
    grad_probs = jnp.einsum(
        "hqd,khd->hqk", grad_numer, value_rows, preferred_element_type=jnp.float32
    )
    grad_scores = (probs * (grad_probs - drift[:, :, None])).astype(jnp.bfloat16)
    grad_query = (
        jnp.einsum("hqk,khd->qhd", grad_scores, key_rows, preferred_element_type=jnp.float32)
        * scale
    )
    grad_key = (
        jnp.einsum("hqk,qhd->khd", grad_scores, queries, preferred_element_type=jnp.float32) * scale
    )
    grad_value = jnp.einsum(
        "hqk,hqd->khd", probs.astype(jnp.bfloat16), grad_numer, preferred_element_type=jnp.float32
    )
    return (
        grad_query,
        grad_key.reshape(count, HEADS * HEAD_DIM),
        grad_value.reshape(count, HEADS * HEAD_DIM),
    )


def attention_forward(queries, key_flat, value_flat, key_keep, query_index, query_segment, lengths):
    row_count = key_flat.shape[0]
    initial = (
        jnp.full((HEADS, row_count), NEG, jnp.float32),
        jnp.zeros((HEADS, row_count), jnp.float32),
        jnp.zeros((HEADS, row_count, HEAD_DIM), jnp.float32),
    )
    return attend(
        initial,
        (
            lax.all_gather(key_flat, "ctx", axis=0, tiled=True),
            lax.all_gather(value_flat, "ctx", axis=0, tiled=True),
            lax.all_gather(key_keep, "ctx", axis=0, tiled=True),
        ),
        jnp.int32(0),
        queries,
        query_index,
        query_segment,
        lengths,
    )


def attention_backward(
    queries,
    key_flat,
    value_flat,
    key_keep,
    maxima,
    grad_numer,
    drift,
    query_index,
    query_segment,
    lengths,
):
    whole = (
        lax.all_gather(key_flat, "ctx", axis=0, tiled=True),
        lax.all_gather(value_flat, "ctx", axis=0, tiled=True),
        lax.all_gather(key_keep, "ctx", axis=0, tiled=True),
    )
    grad_query, every_key, every_value = attend_back(
        whole, 0, queries, maxima, grad_numer, drift, query_index, query_segment, lengths
    )
    grad_key, grad_value = (
        lax.psum_scatter(
            every_key.astype(jnp.bfloat16), "ctx", scatter_dimension=0, tiled=True
        ).astype(jnp.float32),
        lax.psum_scatter(
            every_value.astype(jnp.bfloat16), "ctx", scatter_dimension=0, tiled=True
        ).astype(jnp.float32),
    )
    return (grad_query, grad_key, grad_value)


def layer_forward(hidden, weights, cosine, sine, key_keep, query_index, query_segment, lengths):
    (
        norm_gain,
        norm_shift,
        joint_weight,
        joint_bias,
        output_weight,
        output_bias,
        upper_weight,
        upper_bias,
        lower_weight,
        lower_bias,
    ) = weights
    row_count = hidden.shape[0]
    width = HEADS * HEAD_DIM
    normed = normalize(
        hidden, norm_gain.astype(jnp.float32), norm_shift.astype(jnp.float32)
    ).astype(jnp.bfloat16)
    joint = jnp.dot(normed, joint_weight, preferred_element_type=jnp.float32) + joint_bias.astype(
        jnp.float32
    )
    queries = rotate(joint[:, :width].reshape(row_count, HEADS, HEAD_DIM), cosine, sine).astype(
        jnp.bfloat16
    )
    key_flat = (
        rotate(joint[:, width : 2 * width].reshape(row_count, HEADS, HEAD_DIM), cosine, sine)
        .astype(jnp.bfloat16)
        .reshape(row_count, width)
    )
    value_flat = joint[:, 2 * width :].astype(jnp.bfloat16)
    maxima, totals, weighted = attention_forward(
        queries, key_flat, value_flat, key_keep, query_index, query_segment, lengths
    )
    mixed = (weighted / totals[:, :, None]).transpose(1, 0, 2).reshape(row_count, width)
    attention_out = jnp.dot(
        mixed.astype(jnp.bfloat16), output_weight, preferred_element_type=jnp.float32
    ) + output_bias.astype(jnp.float32)
    inner = jnp.dot(normed, upper_weight, preferred_element_type=jnp.float32) + upper_bias.astype(
        jnp.float32
    )
    activated = jax.nn.gelu(inner, approximate=True).astype(jnp.bfloat16)
    feed_out = jnp.dot(
        activated, lower_weight, preferred_element_type=jnp.float32
    ) + lower_bias.astype(jnp.float32)
    saved = (hidden, normed, queries, key_flat, value_flat, maxima, totals, mixed, inner, activated)
    return (hidden + (attention_out + feed_out), saved)


def layer_backward(
    grad_out, saved, weights, cosine, sine, key_keep, query_index, query_segment, lengths
):
    hidden, normed, queries, key_flat, value_flat, maxima, totals, mixed, inner, activated = saved
    (
        norm_gain,
        norm_shift,
        joint_weight,
        joint_bias,
        output_weight,
        output_bias,
        upper_weight,
        upper_bias,
        lower_weight,
        lower_bias,
    ) = weights
    row_count = hidden.shape[0]
    width = HEADS * HEAD_DIM
    ratio = FF // D
    grad_branch = grad_out.astype(jnp.bfloat16)
    mixed_low = mixed.astype(jnp.bfloat16)
    branch_bias = jnp.sum(grad_branch, axis=0, dtype=jnp.float32)
    grad_activated = jnp.einsum(
        "td,fd->tf", grad_branch, lower_weight, preferred_element_type=jnp.float32
    )
    gelu_pull = jax.vjp(functools.partial(jax.nn.gelu, approximate=True), inner)[1]
    grad_inner = gelu_pull(grad_activated)[0].astype(jnp.bfloat16)
    upper_bias_grad = jnp.sum(grad_inner, axis=0, dtype=jnp.float32)
    grad_normed = jnp.einsum(
        "tf,df->td", grad_inner, upper_weight, preferred_element_type=jnp.float32
    )
    upper_bias_rows = upper_bias_grad.reshape(D, ratio)
    normed_cols = normed
    upper_part = jnp.einsum(
        "tc,tf->cf", normed_cols, grad_inner, preferred_element_type=jnp.float32
    )
    lower_part = jnp.einsum(
        "tc,td->cd", activated, grad_branch, preferred_element_type=jnp.float32
    ).reshape(lax.axis_size(("ctx", "fsdp")) * (D // lax.axis_size(("ctx", "fsdp"))), ratio * width)
    bias_part = upper_bias_rows
    branch_part = branch_bias[:, None]
    feed_share = lax.psum_scatter(
        jnp.concatenate([upper_part, lower_part, bias_part, branch_part], axis=1),
        ("ctx", "fsdp"),
        scatter_dimension=0,
        tiled=True,
    )
    share_rows = feed_share.shape[0]
    upper_share = feed_share[:, :FF]
    lower_share = feed_share[:, FF : FF + ratio * width].reshape(share_rows * ratio, width)
    upper_bias_share = feed_share[:, FF + ratio * width : FF + ratio * width + ratio].reshape(
        share_rows * ratio
    )
    branch_share = feed_share[:, FF + ratio * width + ratio]
    feed_parts = (upper_share, upper_bias_share, lower_share, branch_share)
    output_share = None
    grad_mixed = jnp.einsum(
        "te,de->td", grad_branch, output_weight, preferred_element_type=jnp.float32
    )
    head_mixed = mixed.reshape(row_count, HEADS, HEAD_DIM).transpose(1, 0, 2)
    head_grad = grad_mixed.reshape(row_count, HEADS, HEAD_DIM).transpose(1, 0, 2)
    drift = jnp.sum(head_grad * head_mixed, axis=2) / totals
    grad_numer = (head_grad / totals[:, :, None]).astype(jnp.bfloat16)
    grad_query, grad_key, grad_value = attention_backward(
        queries,
        key_flat,
        value_flat,
        key_keep,
        maxima,
        grad_numer,
        drift,
        query_index,
        query_segment,
        lengths,
    )
    grad_query = rotate(grad_query, cosine, -sine).reshape(row_count, width)
    grad_key = rotate(grad_key.reshape(row_count, HEADS, HEAD_DIM), cosine, -sine).reshape(
        row_count, width
    )
    grad_joint = jnp.concatenate([grad_query, grad_key, grad_value], axis=1).astype(jnp.bfloat16)
    joint_bias_grad = jnp.sum(grad_joint, axis=0, dtype=jnp.float32)
    grad_normed = grad_normed + jnp.einsum(
        "te,de->td", grad_joint, joint_weight, preferred_element_type=jnp.float32
    )
    norm_pull = jax.vjp(
        normalize, hidden, norm_gain.astype(jnp.float32), norm_shift.astype(jnp.float32)
    )[1]
    grad_hidden, gain_grad, shift_grad = norm_pull(grad_normed)
    joint_bias_rows = joint_bias_grad.reshape(D, 3)
    normed_cols = normed
    joint_part = jnp.einsum(
        "tc,te->ce", normed_cols, grad_joint, preferred_element_type=jnp.float32
    )
    output_part = jnp.einsum(
        "tc,te->ce", mixed_low, grad_branch, preferred_element_type=jnp.float32
    )
    bias_part = joint_bias_rows
    gain_part = gain_grad[:, None]
    shift_part = shift_grad[:, None]
    attn_share = lax.psum_scatter(
        jnp.concatenate([joint_part, output_part, bias_part, gain_part, shift_part], axis=1),
        ("ctx", "fsdp"),
        scatter_dimension=0,
        tiled=True,
    )
    share_rows = attn_share.shape[0]
    joint_share = attn_share[:, : 3 * width]
    output_share = attn_share[:, 3 * width : 4 * width]
    joint_bias_share = attn_share[:, 4 * width : 4 * width + 3].reshape(share_rows * 3)
    gain_share = attn_share[:, 4 * width + 3]
    shift_share = attn_share[:, 4 * width + 4]
    attention_parts = (gain_share, shift_share, joint_share, joint_bias_share, output_share)
    return (grad_out + grad_hidden, attention_parts, feed_parts)


def on_device_gathered(
    tokens,
    doc_lengths,
    keep_mask,
    ln_gain,
    ln_bias,
    qkv_weight,
    qkv_bias,
    out_weight,
    out_bias,
    up_weight,
    up_bias,
    down_weight,
    down_bias,
    cotangent,
):
    row_count = tokens.shape[1]
    position = lax.axis_index("ctx")
    query_index = position * row_count + jnp.arange(row_count, dtype=jnp.int32)
    lengths = doc_lengths[0]
    query_segment, query_position = place_tokens(query_index, lengths)
    cosine, sine = angles(query_position)
    key_keep = keep_mask[0].astype(jnp.bfloat16)
    shards = (
        ln_gain,
        ln_bias,
        qkv_weight,
        qkv_bias,
        out_weight,
        out_bias,
        up_weight,
        up_bias,
        down_weight,
        down_bias,
    )

    def fetch(layer_index):
        return (
            lax.all_gather(shards[0][layer_index], ("ctx", "fsdp"), axis=0, tiled=True),
            lax.all_gather(shards[1][layer_index], ("ctx", "fsdp"), axis=0, tiled=True),
            lax.all_gather(shards[2][layer_index], ("ctx", "fsdp"), axis=0, tiled=True),
            lax.all_gather(shards[3][layer_index], ("ctx", "fsdp"), axis=0, tiled=True),
            lax.all_gather(shards[4][layer_index], ("ctx", "fsdp"), axis=0, tiled=True),
            lax.all_gather(shards[5][layer_index], ("ctx", "fsdp"), axis=0, tiled=True),
            lax.all_gather(shards[6][layer_index], ("ctx", "fsdp"), axis=0, tiled=True),
            lax.all_gather(shards[7][layer_index], ("ctx", "fsdp"), axis=0, tiled=True),
            lax.all_gather(shards[8][layer_index], ("ctx", "fsdp"), axis=0, tiled=True),
            lax.all_gather(shards[9][layer_index], ("ctx", "fsdp"), axis=0, tiled=True),
        )

    hidden = tokens[0].astype(jnp.float32)
    saved_layers = []
    weights = None
    for layer_index in range(LAYERS):
        weights = fetch(layer_index)
        hidden, saved = layer_forward(
            hidden, weights, cosine, sine, key_keep, query_index, query_segment, lengths
        )
        saved_layers.append(saved)
    result = hidden.astype(jnp.bfloat16)[None]
    grad_hidden = cotangent[0].astype(jnp.float32) * keep_mask[0].astype(jnp.float32)[:, None]
    attention_list = [None] * LAYERS
    feed_list = [None] * LAYERS
    for layer_index in reversed(range(LAYERS)):
        weights = weights if layer_index == LAYERS - 1 else fetch(layer_index)
        grad_hidden, attention_parts, feed_parts = layer_backward(
            grad_hidden,
            saved_layers[layer_index],
            weights,
            cosine,
            sine,
            key_keep,
            query_index,
            query_segment,
            lengths,
        )
        attention_list[layer_index] = attention_parts
        feed_list[layer_index] = feed_parts
    gain_stack = jnp.stack([attention_list[layer_index][0] for layer_index in range(LAYERS)])
    shift_stack = jnp.stack([attention_list[layer_index][1] for layer_index in range(LAYERS)])
    joint_stack = jnp.stack([attention_list[layer_index][2] for layer_index in range(LAYERS)])
    joint_bias_stack = jnp.stack([attention_list[layer_index][3] for layer_index in range(LAYERS)])
    output_stack = jnp.stack([attention_list[layer_index][4] for layer_index in range(LAYERS)])
    upper_stack = jnp.stack([feed_list[layer_index][0] for layer_index in range(LAYERS)])
    upper_bias_stack = jnp.stack([feed_list[layer_index][1] for layer_index in range(LAYERS)])
    lower_stack = jnp.stack([feed_list[layer_index][2] for layer_index in range(LAYERS)])
    branch_stack = jnp.stack([feed_list[layer_index][3] for layer_index in range(LAYERS)])
    summed = (
        lax.psum(gain_stack.astype(jnp.bfloat16), "seq").astype(jnp.float32),
        lax.psum(shift_stack.astype(jnp.bfloat16), "seq").astype(jnp.float32),
        lax.psum(joint_stack.astype(jnp.bfloat16), "seq").astype(jnp.float32),
        lax.psum(joint_bias_stack.astype(jnp.bfloat16), "seq").astype(jnp.float32),
        lax.psum(output_stack.astype(jnp.bfloat16), "seq").astype(jnp.float32),
        lax.psum(upper_stack.astype(jnp.bfloat16), "seq").astype(jnp.float32),
        lax.psum(upper_bias_stack.astype(jnp.bfloat16), "seq").astype(jnp.float32),
        lax.psum(lower_stack.astype(jnp.bfloat16), "seq").astype(jnp.float32),
        lax.psum(branch_stack.astype(jnp.bfloat16), "seq").astype(jnp.float32),
    )
    return (
        result,
        grad_hidden[None],
        summed[0],
        summed[1],
        summed[2],
        summed[3],
        summed[4],
        summed[8],
        summed[5],
        summed[6],
        summed[7],
        summed[8],
    )


SIDE = 4
GROUP = SIDE * SIDE
OWN = HEADS // GROUP
HEAD_COLS = OWN * HEAD_DIM
JOINT_COLS = 3 * HEAD_COLS
FEED_COLS = FF // GROUP
COLS = JOINT_COLS + FEED_COLS
BACK_COLS = HEAD_COLS + FEED_COLS
SHARE = D // GROUP
VMEM = pl.BlockSpec(memory_space=pltpu.VMEM)
HBM = pl.BlockSpec(memory_space=pl.ANY)
MESH = pl.DeviceIdType.MESH
ROOM = 60 * 2**20


def dot(left, right, left_dim=1, right_dim=0):
    return lax.dot_general(
        left, right, (((left_dim,), (right_dim,)), ((), ())), preferred_element_type=jnp.float32
    )


def digit(entries, index):
    words = [
        sum(entry << (2 * place) for place, entry in enumerate(entries[start : start + 8]))
        for start in range(0, len(entries), 8)
    ]
    word = jnp.int32(words[0])
    for number in range(1, len(words)):
        word = jnp.where(index >= 8 * number, jnp.int32(words[number]), word)
    return lax.rem(lax.shift_right_logical(word, 2 * lax.rem(index, 8)), 4)


def nibble(entries, index):
    word = jnp.int32(0)
    for start in range(0, len(entries), 7):
        packed = sum(entry << (4 * place) for place, entry in enumerate(entries[start : start + 7]))
        word = jnp.where(index >= start, jnp.int32(packed), word)
    return lax.rem(lax.shift_right_logical(word, 4 * lax.rem(index, 7)), 16)


def digit_of_row(table, row, index):
    value = digit(table[0], index)
    for number in range(1, len(table)):
        value = jnp.where(row == number, digit(table[number], index), value)
    return value


NEAR = ((0, 1, 2, 3), (1, 0, 2, 3), (2, 3, 1, 0), (3, 2, 1, 0))
FAR = ((3, 2, 1, 0), (3, 0, 2, 1), (0, 3, 1, 2), (0, 1, 2, 3))


def neighbours():
    ctx, place = lax.axis_index("ctx"), lax.axis_index("fsdp")
    twin = ctx + 1 - 2 * lax.rem(ctx, 2)
    across = lax.rem(ctx + 2, 4)
    return ctx, place, twin, across, lax.rem(twin + 2, 4)


def greet_neighbours(cross=False):
    ctx, place, twin, across, _ = neighbours()
    barrier = pltpu.get_barrier_semaphore()
    pl.semaphore_signal(barrier, inc=1, device_id={"ctx": twin}, device_id_type=MESH)
    pl.semaphore_signal(barrier, inc=1, device_id={"ctx": across}, device_id_type=MESH)

    @pl.when(place > 0)
    def _():
        pl.semaphore_signal(barrier, inc=1, device_id={"fsdp": place - 1}, device_id_type=MESH)

    @pl.when(place < SIDE - 1)
    def _():
        pl.semaphore_signal(barrier, inc=1, device_id={"fsdp": place + 1}, device_id_type=MESH)

    if cross:
        pl.semaphore_signal(
            barrier, inc=1, device_id={"seq": 1 - lax.axis_index("seq")}, device_id_type=MESH
        )
    inner = jnp.int32(3 if cross else 2) + jnp.where(place > 0, 1, 0) + jnp.where(place < SIDE - 1, 1, 0)
    pl.semaphore_wait(barrier, inner)


def greet_plane(steps, cross=True):
    ctx, place = lax.axis_index("ctx"), lax.axis_index("fsdp")
    me = ctx * SIDE + place
    barrier = pltpu.get_barrier_semaphore()
    for step in range(1, steps):
        peer = lax.rem(me + step, GROUP)
        pl.semaphore_signal(
            barrier,
            inc=1,
            device_id={"ctx": peer // SIDE, "fsdp": lax.rem(peer, SIDE)},
            device_id_type=MESH,
        )
    if cross:
        pl.semaphore_signal(
            barrier, inc=1, device_id={"seq": 1 - lax.axis_index("seq")}, device_id_type=MESH
        )
    pl.semaphore_wait(barrier, steps if cross else steps - 1)


def to_peer(source, target, send, recv, peer):
    return pltpu.make_async_remote_copy(
        src_ref=source,
        dst_ref=target,
        send_sem=send,
        recv_sem=recv,
        device_id={"ctx": peer // SIDE, "fsdp": lax.rem(peer, SIDE)},
        device_id_type=MESH,
    )


def to_axis(source, target, send, recv, axis, index):
    return pltpu.make_async_remote_copy(
        src_ref=source,
        dst_ref=target,
        send_sem=send,
        recv_sem=recv,
        device_id={axis: index},
        device_id_type=MESH,
    )


PARTS = ((0, 112), (112, 96), (208, 48))
LAST = len(PARTS) - 1
GATHER_KIND = (
    (0, 0, 0, 0, 0, 1, 0, 0, 1, 0, 2, 0, 1, 1, 1, 2, 0, 0, 1, 0, 1, 3, 2, 1, 0, 3, 1, 1, 1, 1, 0, 3, 0, 0, 1, 1, 1, 1, 2, 3),
    (0, 0, 0, 1, 0, 0, 0, 0, 0, 0, 0, 0, 1, 0, 2, 1, 2, 1, 0, 1, 1, 2, 0, 3, 1, 1, 0, 1, 1, 1, 3, 1, 1, 0, 1, 3, 1, 1, 2, 3),
)
GATHER_STEP = (
    (0, 0, 1, 0, 0, 0, 1, 1, 0, 1, 0, 2, 0, 0, 1, 1, 2, 2, 1, 2, 1, 0, 2, 1, 3, 1, 2, 2, 2, 2, 3, 2, 3, 3, 3, 3, 3, 3, 3, 3),
    (0, 0, 0, 0, 2, 2, 1, 0, 1, 2, 1, 1, 0, 2, 0, 0, 2, 0, 3, 2, 2, 1, 3, 0, 2, 1, 3, 1, 2, 1, 2, 3, 1, 3, 3, 1, 3, 3, 3, 3),
)
GATHER_PART = (
    (1, 0, 1, 2, 3, 1, 2, 0, 0, 3, 3, 2, 2, 3, 0, 3, 1, 0, 1, 3, 2, 3, 3, 3, 0, 3, 1, 2, 0, 3, 1, 3, 2, 3, 1, 0, 2, 3, 3, 3),
    (1, 0, 2, 0, 2, 0, 2, 3, 1, 1, 0, 3, 2, 3, 3, 1, 3, 3, 0, 0, 2, 3, 1, 3, 1, 1, 2, 2, 3, 0, 3, 2, 3, 3, 0, 3, 1, 3, 3, 3),
)
FIRST_KIND = (
    (0, 0, 0, 0, 0, 0, 0, 0, 0, 1, 3, 2, 3, 2, 0, 1, 3, 1, 0, 1, 0, 0, 0, 1, 1, 0, 0, 3, 0, 0, 2, 2, 0, 1, 0, 0, 1, 1, 1, 0, 0, 1, 1, 2, 2, 3, 3, 0, 1, 0, 0, 0, 0, 1, 1, 3, 2, 1, 0, 1, 1, 2, 0, 2, 2, 0, 1, 3, 0, 1, 0, 0, 3, 3, 2, 1, 1, 1, 2, 1, 3, 3),
    (0, 0, 0, 0, 0, 2, 0, 0, 0, 1, 0, 0, 2, 1, 3, 1, 1, 0, 2, 0, 3, 3, 0, 0, 0, 0, 0, 0, 1, 1, 0, 1, 0, 0, 2, 3, 1, 2, 0, 1, 0, 0, 0, 1, 0, 1, 0, 2, 0, 1, 1, 1, 3, 2, 2, 3, 0, 3, 1, 0, 0, 0, 1, 2, 0, 0, 1, 1, 1, 1, 1, 3, 2, 3, 1, 2, 1, 1, 3, 3, 2, 3),
)
FIRST_STEP = (
    (0, 0, 1, 2, 3, 3, 0, 0, 0, 3, 0, 0, 2, 1, 0, 0, 1, 1, 0, 0, 0, 1, 1, 0, 0, 2, 2, 3, 1, 1, 2, 3, 3, 2, 1, 2, 0, 1, 1, 2, 1, 1, 1, 0, 1, 0, 1, 0, 1, 2, 1, 0, 2, 2, 0, 0, 1, 2, 3, 2, 2, 2, 2, 2, 0, 3, 2, 1, 3, 3, 3, 3, 2, 2, 3, 3, 3, 3, 3, 3, 3, 3),
    (0, 1, 2, 0, 0, 0, 2, 1, 3, 0, 0, 0, 3, 3, 1, 2, 0, 3, 1, 0, 2, 0, 0, 1, 2, 0, 2, 1, 1, 0, 1, 0, 3, 2, 0, 3, 1, 2, 1, 0, 2, 0, 1, 0, 3, 1, 2, 0, 0, 1, 1, 2, 0, 1, 1, 1, 3, 1, 2, 3, 2, 1, 2, 2, 3, 3, 2, 3, 1, 2, 3, 0, 2, 2, 3, 3, 3, 3, 3, 3, 3, 2),
)
FIRST_WHAT = (
    (5, 4, 4, 4, 9, 4, 0, 9, 2, 9, 9, 9, 9, 9, 1, 2, 9, 9, 6, 0, 3, 1, 6, 1, 3, 9, 6, 9, 0, 9, 9, 9, 6, 9, 2, 1, 9, 1, 2, 2, 3, 0, 3, 3, 3, 3, 3, 7, 8, 0, 8, 8, 3, 1, 8, 8, 8, 0, 0, 2, 3, 3, 8, 8, 8, 1, 8, 8, 2, 0, 3, 8, 3, 8, 3, 2, 1, 3, 8, 8, 3, 8),
    (4, 4, 4, 5, 0, 9, 9, 9, 9, 0, 9, 1, 9, 9, 9, 9, 9, 4, 9, 6, 9, 9, 2, 6, 1, 3, 6, 0, 9, 2, 1, 1, 6, 2, 3, 9, 0, 9, 2, 3, 0, 7, 3, 8, 0, 2, 3, 8, 8, 1, 3, 2, 3, 3, 8, 3, 1, 8, 0, 2, 8, 8, 1, 3, 3, 8, 3, 2, 8, 8, 1, 8, 8, 3, 0, 3, 3, 8, 3, 8, 8, 8),
)
OPS = len(GATHER_KIND[0])
WORKS = tuple(
    tuple(
        number for number in range(OPS) if parts[number] == 3
    )
    for parts in GATHER_PART
)


def by_place(tables, index):
    place = lax.axis_index("fsdp")
    at_end = (place == 0) | (place == SIDE - 1)
    return jnp.where(at_end, digit(tables[0], index), digit(tables[1], index))


def gather_slot(kind, step):
    ctx, place, twin, across, twin_across = neighbours()
    line = digit_of_row(NEAR, place, step)
    owner = jnp.where(
        kind == 0, ctx, jnp.where(kind == 1, across, jnp.where(kind == 2, twin, twin_across))
    )
    return line, owner * SIDE + line


def work_slot(number):
    kind = by_place(
        tuple(tuple(row[at] for at in places) for row, places in zip(GATHER_KIND, WORKS)), number
    )
    step = by_place(
        tuple(tuple(row[at] for at in places) for row, places in zip(GATHER_STEP, WORKS)), number
    )
    return gather_slot(kind, step)[1]


def gather_blocks(
    land, every, up, down, side, core, arrived, core_arrived, kept, work, tables=None, more=()
):
    ctx, place, twin, across, _ = neighbours()
    kinds, steps, parts = tables or (GATHER_KIND, GATHER_STEP, GATHER_PART)
    at_end = (place == 0) | (place == SIDE - 1)

    def copies(kind, line, slot, part):
        start, size = PARTS[part]
        block = land.at[slot, pl.ds(start, size)]
        row, met = kind * SIDE + line, arrived.at[slot, part]
        return (
            lambda: to_axis(block, block, up.at[row, part], met, "fsdp", place + 1),
            lambda: to_axis(block, block, down.at[row, part], met, "fsdp", place - 1),
            lambda: to_axis(block, block, side.at[line, part], met, "ctx", across),
        )

    def routes(kind, line, part):
        goes_up = (line <= place) & (place < SIDE - 1)
        goes_down = (line >= place) & (place > 0)
        if part == LAST:
            return goes_up, goes_down, (kind == 0) & (line == place)
        return goes_up & (kind == 0), goes_down & (kind == 0), kind == 0

    def core_copy(kind, line, slot):
        block = land.at[slot]
        return to_axis(
            block, block, core.at[kind * SIDE + line], core_arrived.at[slot], "ctx", twin
        )

    def step_op(number, counts):
        worked, made = counts
        kind, step = by_place(kinds, number), by_place(steps, number)
        part = jnp.where(at_end, nibble(parts[0], number), nibble(parts[1], number))
        line, slot = gather_slot(kind, step)
        for which in range(len(PARTS)):

            @pl.when(part == which)
            def _(which=which):
                @pl.when((kind == 1) | (line != place))
                def _():
                    copies(kind, line, slot, which)[2]().wait_recv()

                for copy, goes in zip(
                    copies(kind, line, slot, which), routes(kind, line, which)
                ):

                    @pl.when(goes)
                    def _(copy=copy):
                        copy().start()

        @pl.when(part == 3)
        def _():
            @pl.when(kind <= 1)
            def _():
                core_copy(kind, line, slot).start()

            @pl.when(kind >= 2)
            def _():
                core_copy(kind - 2, line, slot).wait_recv()

            if every is not None:
                pltpu.make_async_copy(land.at[slot], every.at[slot], kept.at[slot]).start()
            work(worked, slot)

        for which, further in enumerate(more):

            @pl.when(part == 4 + which)
            def _(further=further):
                further(step, slot, made)

        return worked + jnp.where(part == 3, 1, 0), made + jnp.where(part == 8, 1, 0)

    lax.fori_loop(0, len(kinds[0]), step_op, (jnp.int32(0), jnp.int32(0)))

    def finish(number, carry):
        kind, line = number // SIDE, lax.rem(number, SIDE)
        slot = jnp.where(kind == 0, ctx, across) * SIDE + line
        for which in range(len(PARTS)):
            for copy, goes in zip(copies(kind, line, slot, which), routes(kind, line, which)):

                @pl.when(goes)
                def _(copy=copy):
                    copy().wait_send()

        core_copy(kind, line, slot).wait_send()
        return carry

    lax.fori_loop(0, 2 * SIDE, finish, 0)

    def finish_kept(slot, carry):
        pltpu.make_async_copy(land.at[slot], every.at[slot], kept.at[slot]).wait()
        return carry

    if every is not None:
        lax.fori_loop(0, GROUP, finish_kept, 0)


def gather_scratch(rows):
    parts = len(PARTS)
    return [
        pltpu.VMEM((GROUP, rows, D), jnp.bfloat16),
        pltpu.SemaphoreType.DMA((2 * SIDE, parts)),
        pltpu.SemaphoreType.DMA((2 * SIDE, parts)),
        pltpu.SemaphoreType.DMA((SIDE, parts)),
        pltpu.SemaphoreType.DMA((2 * SIDE,)),
        pltpu.SemaphoreType.DMA((GROUP, parts)),
        pltpu.SemaphoreType.DMA((GROUP,)),
        pltpu.SemaphoreType.DMA((GROUP,)),
    ]


def spin(values, cosine, sine, sign):
    lane = lax.rem(lax.broadcasted_iota(jnp.int32, values.shape, 1), HEAD_DIM)
    partner = jnp.where(
        lane < ROT // 2,
        -pltpu.roll(values, HEAD_COLS - ROT // 2, 1),
        pltpu.roll(values, ROT // 2, 1),
    )
    return values * cosine + sign * (partner * sine)


STRIP = 32


def each_strip(rows, body, start):
    def step(number, carry):
        return body(pl.ds(pl.multiple_of(number * STRIP, STRIP), STRIP), carry)

    return lax.fori_loop(0, rows // STRIP, step, start)


def column_places(block):
    return [
        (0, pl.multiple_of(part * D + block * HEAD_COLS, HEAD_COLS), part * HEAD_COLS, HEAD_COLS)
        for part in range(3)
    ] + [(1, pl.multiple_of(block * FEED_COLS, FEED_COLS), JOINT_COLS, FEED_COLS)]


PLACES = 4


def plane_swap(swap, sems):
    source, target = swap
    return to_axis(source, target, sems.at[0], sems.at[1], "seq", 1 - lax.axis_index("seq"))


def load_all(pairs, sems):
    copies = [
        pltpu.make_async_copy(source, target, sems.at[number])
        for number, (source, target) in enumerate(pairs)
    ]
    for copy in copies:
        copy.start()
    return copies


def wait_all(copies):
    for copy in copies:
        copy.wait()


def ring_scratch(rows):
    return [
        pltpu.VMEM((2, rows, HEAD_COLS), jnp.bfloat16),
        pltpu.VMEM((2, rows, HEAD_COLS), jnp.bfloat16),
        pltpu.VMEM((2, rows, HEAD_COLS), jnp.bfloat16),
        pltpu.VMEM((2, rows, FEED_COLS), jnp.float32),
        pltpu.VMEM((2, rows, FEED_COLS), jnp.bfloat16),
        pltpu.SemaphoreType.DMA((2, 5)),
    ]


def ring_shapes(rows):
    return [
        jax.ShapeDtypeStruct((GROUP, rows, width), dtype)
        for width, dtype in (
            (HEAD_COLS, jnp.bfloat16),
            (HEAD_COLS, jnp.bfloat16),
            (HEAD_COLS, jnp.bfloat16),
            (FEED_COLS, jnp.float32),
            (FEED_COLS, jnp.bfloat16),
        )
    ]


def ring_product(rings, sems, results, land, columns, bias, cosine, sine):
    query, key, value, inner, active = rings

    def leave(at, slot):
        return [
            pltpu.make_async_copy(ring.at[at], result.at[slot], sems.at[at, which])
            for which, (ring, result) in enumerate(zip(rings, results))
        ]

    def product(number, slot):
        whole = dot(land[slot], columns[...].reshape(D, COLS)) + bias[...]
        one, two = HEAD_COLS, 2 * HEAD_COLS
        at = lax.rem(number, 2)

        @pl.when(number >= 2)
        def _():
            wait_all(leave(at, 0))

        query[at] = spin(whole[:, :one], cosine[slot], sine[slot], 1.0).astype(jnp.bfloat16)
        key[at] = spin(whole[:, one:two], cosine[slot], sine[slot], 1.0).astype(jnp.bfloat16)
        value[at] = whole[:, two:JOINT_COLS].astype(jnp.bfloat16)
        units = whole[:, JOINT_COLS:]
        inner[at] = units
        active[at] = jax.nn.gelu(units, approximate=True).astype(jnp.bfloat16)
        for copy in leave(at, slot):
            copy.start()

    def finish():
        for at in range(2):
            wait_all(leave(at, 0))

    return product, finish


def norm_block(hidden, gain, shift, land, me):
    def strip(part, carry):
        values = hidden[part].astype(jnp.float32)
        centred = values - jnp.mean(values, axis=1, keepdims=True)
        spread = jnp.mean(centred * centred, axis=1, keepdims=True)
        normed = centred * lax.rsqrt(spread + EPS) * gain[...] + shift[...]
        land[me, part] = normed.astype(jnp.bfloat16)
        return carry

    each_strip(hidden.shape[0], strip, 0)


def forward_gather(hidden, gain, shift, bias, tables, halves, layer):
    rows = hidden.shape[0]
    half = SHARE // 2

    def kernel(hidden, gain, shift, bias, turn_a, turn_b, own_half, other_half, *refs):
        every, columns_out, results, refs = refs[0], refs[1], refs[2:7], refs[7:]
        cosine, sine, columns, load_sem, saved = refs[:5]
        rings, ring_sem, refs = refs[5:10], refs[10], refs[11:]
        land, sems = refs[0], refs[1:]
        ctx, place, seq = lax.axis_index("ctx"), lax.axis_index("fsdp"), lax.axis_index("seq")
        part_rows = pl.ds(pl.multiple_of(seq * half, half), half)
        other_rows = pl.ds(pl.multiple_of((1 - seq) * half, half), half)
        loads = load_all(
            (
                (own_half, columns.at[:, part_rows]),
                (other_half, columns.at[:, other_rows]),
                (turn_a, cosine),
                (turn_b, sine),
            ),
            load_sem,
        )
        greet_neighbours()
        norm_block(hidden, gain, shift, land, ctx * SIDE + place)
        save = pltpu.make_async_copy(columns, columns_out, saved)
        product, finish = ring_product(rings, ring_sem, results, land, columns, bias, cosine, sine)

        def work(number, slot):
            @pl.when(number == 0)
            def _():
                wait_all(loads)
                save.start()

            product(number, slot)

        gather_blocks(land, every, *sems, work)
        save.wait()
        finish()

    return pl.pallas_call(
        kernel,
        out_shape=[
            jax.ShapeDtypeStruct((GROUP, rows, D), jnp.bfloat16),
            jax.ShapeDtypeStruct((GROUP, SHARE, COLS), jnp.bfloat16),
        ]
        + ring_shapes(rows),
        in_specs=[VMEM] * 4 + [HBM] * 4,
        out_specs=[HBM] * 7,
        scratch_shapes=[pltpu.VMEM((GROUP, rows, HEAD_COLS), jnp.float32)] * 2
        + [
            pltpu.VMEM((GROUP, SHARE, COLS), jnp.bfloat16),
            pltpu.SemaphoreType.DMA((4,)),
            pltpu.SemaphoreType.DMA,
        ]
        + ring_scratch(rows)
        + gather_scratch(rows),
        compiler_params=pltpu.CompilerParams(
            collective_id=30 + layer, has_side_effects=True, vmem_limit_bytes=ROOM
        ),
    )(hidden, gain, shift, bias, *tables, *halves)


GAIN_ROW, SHIFT_ROW, JOINT_BIAS_ROW, OUT_BIAS_ROW, DOWN_BIAS_ROW, LAYER_ROWS = 0, 1, 2, 5, 6, 7
BEGIN_ROW = LAYERS * LAYER_ROWS


def first_gather(hidden, packed, up_bias, frequency, qkv_weight, up_weight):
    rows = hidden.shape[0]
    half = SHARE // 2

    def kernel(hidden, packed, up_bias, frequency, qkv_weight, up_weight, *refs):
        every, columns_out, results, small, cosine, sine = refs[0], refs[1], refs[2:7], *refs[7:10]
        refs = refs[10:]
        columns, plane_send, plane_recv, cross_send, cross_recv, own_sem, saved = refs[:7]
        small_send, small_recv, gain, shift, bias = refs[7:12]
        rings, ring_sem, refs = refs[12:17], refs[17], refs[18:]
        land, sems = refs[0], refs[1:]
        ctx, place, seq = lax.axis_index("ctx"), lax.axis_index("fsdp"), lax.axis_index("seq")
        me = ctx * SIDE + place
        part_rows = pl.ds(pl.multiple_of(seq * half, half), half)
        sources = (qkv_weight, up_weight)
        greet_plane(GROUP)

        def small_copy(step):
            return to_peer(
                packed,
                small.at[me],
                small_send.at[step],
                small_recv.at[me],
                lax.rem(me + step, GROUP),
            )

        def small_begin(step, carry):
            small_copy(step).start()
            return carry

        lax.fori_loop(1, GROUP, small_begin, 0)
        small[me] = packed[...]

        def piece(step, number):
            peer = lax.rem(me + step, GROUP)
            which, start, at, width = column_places(peer)[number]
            return (
                peer,
                sources[which].at[0, part_rows, pl.ds(start, width)],
                columns.at[me, part_rows, pl.ds(at, width)],
            )

        def send_piece(step, number):
            peer, source, target = piece(step, number)
            return to_peer(
                source, target, plane_send.at[step, number], plane_recv.at[me, number], peer
            )

        def own_piece(number):
            _, source, target = piece(0, number)
            return pltpu.make_async_copy(source, target, own_sem.at[number])

        def cross(source):
            block = columns.at[source, part_rows]
            return to_axis(
                block, block, cross_send.at[source], cross_recv.at[source], "seq", 1 - seq
            )

        for number in range(PLACES):
            own_piece(number).start()

        def send_columns(group, slot, made):
            def send(more, carry):
                step = SIDE * group + more

                @pl.when(step > 0)
                def _():
                    for number in range(PLACES):
                        send_piece(step, number).start()

                return carry

            lax.fori_loop(0, SIDE, send, 0)

        def norm_own(group, slot, made):
            def arrive(step, carry):
                source = lax.rem(me + GROUP - step, GROUP)
                to_peer(
                    packed, small.at[source], small_send.at[step], small_recv.at[source], source
                ).wait_recv()
                return carry

            lax.fori_loop(1, GROUP, arrive, 0)

            def whole_row(row):
                return jnp.concatenate(
                    [small[block, row : row + 1] for block in range(GROUP)], axis=1
                )

            gain[...] = whole_row(GAIN_ROW)
            shift[...] = whole_row(SHIFT_ROW)
            for part in range(3):
                at = part * GROUP + me
                bias[:, part * HEAD_COLS : (part + 1) * HEAD_COLS] = small[
                    at // 3, pl.ds(JOINT_BIAS_ROW + lax.rem(at, 3), 1)
                ]
            bias[:, JOINT_COLS:] = up_bias[...]
            norm_block(hidden, gain, shift, land, me)

        def pass_columns(group, slot, made):
            def pass_on(more, carry):
                step = SIDE * group + more
                source = lax.rem(me + GROUP - step, GROUP)

                @pl.when(step == 0)
                def _():
                    for number in range(PLACES):
                        own_piece(number).wait()

                @pl.when(step > 0)
                def _():
                    for number in range(PLACES):
                        _, _, at, width = column_places(0)[number]
                        target = columns.at[source, part_rows, pl.ds(at, width)]
                        to_peer(
                            target,
                            target,
                            plane_send.at[0, number],
                            plane_recv.at[source, number],
                            source,
                        ).wait_recv()

                cross(source).start()
                return carry

            lax.fori_loop(0, SIDE, pass_on, 0)

        save = pltpu.make_async_copy(columns, columns_out, saved)

        def wait_columns(group, slot, made):
            def arrive(source, carry):
                cross(source).wait_recv()
                return carry

            lax.fori_loop(0, GROUP, arrive, 0)
            save.start()

        product, finish = ring_product(rings, ring_sem, results, land, columns, bias, cosine, sine)

        def next_product(group, slot, made):
            product(made, slot)

        def turn_block(group, slot, made):
            begin = jnp.concatenate(
                [small[slot, BEGIN_ROW + part : BEGIN_ROW + part + 1] for part in range(rows // SHARE)],
                axis=1,
            )
            begin = jnp.broadcast_to(begin, (8, rows)).T[:, :1]
            first = (slot // SIDE) * rows
            token = lax.broadcasted_iota(jnp.int32, (rows, 1), 0) + first
            angle = (token.astype(jnp.float32) - begin) * frequency[...]
            cosine[slot] = jnp.cos(angle)
            sine[slot] = jnp.sin(angle)

        gather_blocks(
            land,
            every,
            *sems,
            lambda number, slot: None,
            (FIRST_KIND, FIRST_STEP, FIRST_WHAT),
            (send_columns, norm_own, pass_columns, wait_columns, next_product, turn_block),
        )
        save.wait()
        finish()

        def end(step, carry):
            cross(step).wait_send()

            @pl.when(step > 0)
            def _():
                small_copy(step).wait_send()
                for number in range(PLACES):
                    send_piece(step, number).wait_send()

            return carry

        lax.fori_loop(0, GROUP, end, 0)

    return pl.pallas_call(
        kernel,
        out_shape=[
            jax.ShapeDtypeStruct((GROUP, rows, D), jnp.bfloat16),
            jax.ShapeDtypeStruct((GROUP, SHARE, COLS), jnp.bfloat16),
        ]
        + ring_shapes(rows)
        + [jax.ShapeDtypeStruct((GROUP,) + packed.shape, packed.dtype)]
        + [jax.ShapeDtypeStruct((GROUP, rows, HEAD_COLS), jnp.float32)] * 2,
        in_specs=[VMEM] * 4 + [HBM] * 2,
        out_specs=[HBM] * 7 + [VMEM] * 3,
        scratch_shapes=[
            pltpu.VMEM((GROUP, SHARE, COLS), jnp.bfloat16),
            pltpu.SemaphoreType.DMA((GROUP, PLACES)),
            pltpu.SemaphoreType.DMA((GROUP, PLACES)),
            pltpu.SemaphoreType.DMA((GROUP,)),
            pltpu.SemaphoreType.DMA((GROUP,)),
            pltpu.SemaphoreType.DMA((PLACES,)),
            pltpu.SemaphoreType.DMA,
            pltpu.SemaphoreType.DMA((GROUP,)),
            pltpu.SemaphoreType.DMA((GROUP,)),
            pltpu.VMEM((1, D), jnp.float32),
            pltpu.VMEM((1, D), jnp.float32),
            pltpu.VMEM((1, COLS), jnp.float32),
        ]
        + ring_scratch(rows)
        + gather_scratch(rows),
        compiler_params=pltpu.CompilerParams(
            collective_id=30, has_side_effects=True, vmem_limit_bytes=ROOM
        ),
    )(hidden, packed, up_bias, frequency, qkv_weight, up_weight)


def backward_gather(grad, out_weight, down_weight, inner, mixed, active, layer, swap=()):
    rows = grad.shape[0]

    def kernel(own, out_weight, down_weight, inner, mixed, active, *refs):
        if swap:
            source, grad_mixed, grad_inner, branch, target, swap_sem = refs[:6]
            refs = refs[6:]
        else:
            grad_mixed, grad_inner, branch = refs[:3]
            refs = refs[3:]
        out_part, down_part, weight_sem, total = refs[:4]
        fetched, fetch_sem, rings, ring_sem = refs[4:7], refs[7], refs[8:10], refs[10]
        land, sems = refs[11], refs[12:]
        inner_part, mixed_part, active_part = fetched
        ctx, place, _, _, _ = neighbours()

        def fetch(number):
            at, slot = lax.rem(number, 2), work_slot(number)
            return [
                pltpu.make_async_copy(source.at[slot], target.at[at], fetch_sem.at[at, which])
                for which, (source, target) in enumerate(zip((inner, mixed, active), fetched))
            ]

        def leave(number):
            at, slot = lax.rem(number, 2), work_slot(number)
            return [
                pltpu.make_async_copy(ring.at[at], result.at[slot], ring_sem.at[at, which])
                for which, (ring, result) in enumerate(zip(rings, (grad_mixed, grad_inner)))
            ]

        weights = load_all(
            ((out_weight.at[layer], out_part), (down_weight.at[layer], down_part)), weight_sem
        )
        for copy in fetch(jnp.int32(0)):
            copy.start()
        greet_neighbours(bool(swap))
        if swap:
            plane_swap((source, target), swap_sem).start()
        land[ctx * SIDE + place] = own[...]
        total[...] = jnp.zeros_like(total)

        def work(number, slot):
            at = lax.rem(number, 2)

            @pl.when(number == 0)
            def _():
                wait_all(weights)

            @pl.when(number + 1 < GROUP)
            def _():
                for copy in fetch(number + 1):
                    copy.start()

            @pl.when(number >= 2)
            def _():
                wait_all(leave(number - 2))

            wait_all(fetch(number))
            block = land[slot]
            rings[0][at] = dot(block, out_part[...], 1, 1)
            value = inner_part[at]
            factor = math.sqrt(2.0 / math.pi)
            square = value * value
            bend = jnp.tanh(factor * value * (1.0 + 0.044715 * square))
            slope = 0.5 * (1.0 + bend) + 0.5 * value * (1.0 - bend * bend) * (
                factor * (1.0 + 3 * 0.044715 * square)
            )
            rings[1][at] = (dot(block, down_part[...], 1, 1) * slope).astype(jnp.bfloat16)
            for copy in leave(number):
                copy.start()
            total[:HEAD_COLS] += dot(mixed_part[at], block, 0, 0)
            total[HEAD_COLS:] += dot(active_part[at], block, 0, 0)

        gather_blocks(land, None, *sems, work)
        branch[...] = total[...].astype(jnp.bfloat16)
        if swap:
            plane_swap((source, target), swap_sem).wait()
        for number in (GROUP - 2, GROUP - 1):
            wait_all(leave(jnp.int32(number)))

    return pl.pallas_call(
        kernel,
        out_shape=(
            jax.ShapeDtypeStruct((GROUP, rows, HEAD_COLS), jnp.float32),
            jax.ShapeDtypeStruct((GROUP, rows, FEED_COLS), jnp.bfloat16),
            jax.ShapeDtypeStruct((BACK_COLS, D), jnp.bfloat16),
        )
        + tuple(jax.ShapeDtypeStruct(array.shape, array.dtype) for array in swap),
        in_specs=[VMEM] + [HBM] * (5 + len(swap)),
        out_specs=(HBM, HBM, VMEM) + (HBM,) * len(swap),
        scratch_shapes=[pltpu.SemaphoreType.DMA((2,))] * len(swap)
        + [
            pltpu.VMEM(out_weight.shape[1:], jnp.bfloat16),
            pltpu.VMEM(down_weight.shape[1:], jnp.bfloat16),
            pltpu.SemaphoreType.DMA((2,)),
            pltpu.VMEM((BACK_COLS, D), jnp.float32),
            pltpu.VMEM((2, rows, FEED_COLS), jnp.float32),
            pltpu.VMEM((2, rows, HEAD_COLS), jnp.bfloat16),
            pltpu.VMEM((2, rows, FEED_COLS), jnp.bfloat16),
            pltpu.SemaphoreType.DMA((2, 3)),
            pltpu.VMEM((2, rows, HEAD_COLS), jnp.float32),
            pltpu.VMEM((2, rows, FEED_COLS), jnp.bfloat16),
            pltpu.SemaphoreType.DMA((2, 2)),
        ]
        + gather_scratch(rows),
        compiler_params=pltpu.CompilerParams(
            collective_id=50 + layer, has_side_effects=True, vmem_limit_bytes=ROOM
        ),
    )(grad, out_weight, down_weight, inner, mixed, active, *swap)


SCATTER_OPS = (
    ((0, 0), (0, 1), (1, 0), (2, 0), (1, 1), (0, 2), (2, 1), (3, 0), (1, 2), (2, 2), (4, 0), (6, 0), (5, 0), (0, 3), (3, 1), (3, 2), (1, 3), (3, 3), (4, 1), (5, 1), (6, 1), (4, 2), (5, 2), (6, 2), (2, 3), (4, 3), (5, 3), (6, 3)),
    ((0, 0), (0, 2), (3, 2), (1, 0), (3, 0), (0, 1), (0, 3), (1, 1), (2, 0), (1, 2), (3, 1), (1, 3), (4, 0), (6, 0), (5, 0), (3, 3), (2, 1), (2, 2), (4, 1), (6, 1), (5, 1), (4, 2), (5, 2), (6, 2), (2, 3), (4, 3), (5, 3), (6, 3)),
)
SCATTER_OPS_WORK = (
    ((0, 0), (0, 1), (1, 0), (2, 0), (1, 1), (0, 2), (2, 1), (3, 0), (1, 2), (2, 2), (4, 0), (6, 0), (7, 0), (5, 0), (0, 3), (3, 1), (3, 2), (1, 3), (3, 3), (4, 1), (7, 0), (5, 1), (7, 0), (7, 0), (7, 0), (7, 0), (7, 0), (6, 1), (4, 2), (7, 0), (5, 2), (7, 0), (7, 0), (7, 0), (6, 2), (2, 3), (7, 0), (7, 0), (7, 0), (7, 0), (7, 0), (4, 3), (5, 3), (6, 3)),
    ((0, 0), (0, 2), (3, 2), (1, 0), (3, 0), (7, 0), (0, 1), (0, 3), (1, 1), (2, 0), (1, 2), (3, 1), (7, 0), (7, 0), (1, 3), (4, 0), (6, 0), (7, 0), (5, 0), (7, 0), (7, 0), (3, 3), (2, 1), (7, 0), (2, 2), (7, 0), (7, 0), (4, 1), (6, 1), (5, 1), (4, 2), (5, 2), (7, 0), (7, 0), (7, 0), (6, 2), (7, 0), (7, 0), (7, 0), (2, 3), (7, 0), (4, 3), (5, 3), (6, 3)),
)
SCATTER_OPS_EARLY = (
    ((0, 0), (0, 1), (1, 0), (3, 0), (2, 0), (0, 2), (1, 1), (2, 1), (1, 2), (2, 2), (0, 3), (4, 0), (6, 0), (7, 0), (7, 0), (7, 0), (5, 0), (7, 0), (3, 1), (1, 3), (7, 0), (7, 0), (7, 0), (4, 1), (7, 0), (7, 0), (7, 0), (6, 1), (7, 0), (5, 1), (7, 0), (7, 0), (7, 0), (7, 0), (7, 0), (3, 2), (3, 3), (2, 3), (4, 2), (5, 2), (6, 2), (8, 0), (8, 1), (8, 2), (8, 3), (4, 3), (5, 3), (6, 3)),
    ((0, 2), (7, 0), (0, 0), (0, 1), (1, 0), (7, 0), (7, 0), (0, 3), (7, 0), (3, 3), (3, 0), (7, 0), (1, 1), (2, 0), (3, 2), (1, 2), (7, 0), (2, 2), (7, 0), (7, 0), (3, 1), (1, 3), (4, 0), (6, 0), (7, 0), (2, 1), (7, 0), (7, 0), (7, 0), (5, 0), (7, 0), (7, 0), (7, 0), (7, 0), (2, 3), (4, 1), (6, 1), (5, 1), (4, 2), (5, 2), (6, 2), (8, 0), (8, 1), (8, 2), (8, 3), (4, 3), (5, 3), (6, 3)),
)
SPLIT = ((0, 208), (208, 48))


def scatter_events(partial, other_work, late_work, ops, scratch):
    total, give, take, side_take, line_take, other_take = scratch[:6]
    core_send, core_recv, side_send, side_recv, line_send, line_recv = scratch[6:12]
    other_send, other_recv = scratch[12:]
    ctx, place, twin, across, twin_across = neighbours()
    below, above = place - 1, place + 1
    has_below, has_above = place > 0, place < SIDE - 1
    at_end = (place == 0) | (place == SIDE - 1)

    def rows_of(part):
        return pl.ds(*SPLIT[part])

    def core_copy(step, store):
        return to_axis(
            give.at[step], take.at[store], core_send.at[store], core_recv.at[store], "ctx", twin
        )

    def side_copy(step, part):
        return to_axis(
            take.at[step, rows_of(part)],
            side_take.at[step, rows_of(part)],
            side_send.at[step, part],
            side_recv.at[step, part],
            "ctx",
            across,
        )

    def line_copy(step, line, slot, target, part):
        return to_axis(
            take.at[SIDE + step, rows_of(part)],
            line_take.at[slot, rows_of(part)],
            line_send.at[line, part],
            line_recv.at[slot, part],
            "fsdp",
            target,
        )

    def other_copy(step, line, slot, target):
        return to_axis(
            take.at[step, rows_of(1)],
            other_take.at[slot],
            other_send.at[line],
            other_recv.at[slot],
            "fsdp",
            target,
        )

    def from_above(line):
        return jnp.where(line == place, SIDE, line)

    def to_below(line):
        return jnp.where(line == place - 1, SIDE, line)

    def one(number, turn):
        def by_end(field):
            ends, middle = (tuple(entry[field] for entry in table) for table in ops)
            return jnp.where(at_end, nibble(ends, number), nibble(middle, number))

        what, step = by_end(0), by_end(1)
        line = digit_of_row(FAR, place, step)

        @pl.when((what <= 1) | (what == 3) | (what == 4))
        def _():
            owner = jnp.where(
                what == 0,
                twin_across,
                jnp.where(what == 1, across, jnp.where(what == 3, twin, ctx)),
            )
            total[...] = partial(owner * SIDE + line)

        @pl.when(what == 0)
        def _():
            give[step] = total[...].astype(jnp.bfloat16)
            core_copy(step, step).start()

        @pl.when(what == 1)
        def _():
            core_copy(step, step).wait_recv()
            take[step] = (total[...] + take[step].astype(jnp.float32)).astype(jnp.bfloat16)
            side_copy(step, 0).start()

        @pl.when(what == 2)
        def _():
            rows = rows_of(1)

            @pl.when((line >= place) & has_below)
            def _():
                other_copy(step, line, line, below).wait_recv()
                take[step, rows] = (
                    take[step, rows].astype(jnp.float32) + other_take[line].astype(jnp.float32)
                ).astype(jnp.bfloat16)

            @pl.when((line <= place) & has_above)
            def _():
                other_copy(step, line, from_above(line), above).wait_recv()
                take[step, rows] = (
                    take[step, rows].astype(jnp.float32)
                    + other_take[from_above(line)].astype(jnp.float32)
                ).astype(jnp.bfloat16)

            @pl.when(line > place)
            def _():
                other_copy(step, line, line, above).start()

            @pl.when(line < place)
            def _():
                other_copy(step, line, to_below(line), below).start()

            @pl.when(line == place)
            def _():
                side_copy(step, 1).start()

        @pl.when(what == 3)
        def _():
            core_copy(step, step).wait_send()
            give[step] = total[...].astype(jnp.bfloat16)
            core_copy(step, SIDE + step).start()

        @pl.when(what == 4)
        def _():
            core_copy(step, SIDE + step).wait_recv()
            total[...] += take[SIDE + step].astype(jnp.float32)

        for part in range(2):
            rows = rows_of(part)

            @pl.when(what == 5 + part)
            def _(rows=rows, part=part):
                crossed = line == place if part == 1 else line >= 0

                @pl.when(crossed)
                def _():
                    side_copy(step, part).wait_recv()
                    total[rows] += side_take[step, rows].astype(jnp.float32)

                @pl.when((line >= place) & has_below)
                def _():
                    line_copy(step, line, line, below, part).wait_recv()
                    total[rows] += line_take[line, rows].astype(jnp.float32)

                @pl.when((line <= place) & has_above)
                def _():
                    line_copy(step, line, from_above(line), above, part).wait_recv()
                    total[rows] += line_take[from_above(line), rows].astype(jnp.float32)

                @pl.when(line > place)
                def _():
                    take[SIDE + step, rows] = total[rows].astype(jnp.bfloat16)
                    line_copy(step, line, line, above, part).start()

                @pl.when(line < place)
                def _():
                    take[SIDE + step, rows] = total[rows].astype(jnp.bfloat16)
                    line_copy(step, line, to_below(line), below, part).start()

        if other_work is not None:

            @pl.when(what == 7)
            def _():
                other_work(turn)

        if late_work is not None:

            @pl.when(what == 8)
            def _():
                late_work(step)

        return turn + jnp.where(what == 7, 1, 0)

    lax.fori_loop(0, len(ops[0]), one, jnp.int32(0))

    def finish(step, carry):
        line = digit_of_row(FAR, place, step)
        core_copy(step, SIDE + step).wait_send()
        side_copy(step, 0).wait_send()

        @pl.when(line == place)
        def _():
            side_copy(step, 1).wait_send()

        @pl.when(line != place)
        def _():
            for part in range(2):
                line_copy(step, line, line, place, part).wait_send()
            other_copy(step, line, line, place).wait_send()

        return carry

    lax.fori_loop(0, SIDE, finish, 0)


def scatter_scratch(rows):
    return [
        pltpu.VMEM((rows, D), jnp.float32),
        pltpu.VMEM((SIDE, rows, D), jnp.bfloat16),
        pltpu.VMEM((2 * SIDE, rows, D), jnp.bfloat16),
        pltpu.VMEM((SIDE, rows, D), jnp.bfloat16),
        pltpu.VMEM((SIDE + 1, rows, D), jnp.bfloat16),
        pltpu.VMEM((SIDE + 1, SPLIT[1][1], D), jnp.bfloat16),
        pltpu.SemaphoreType.DMA((2 * SIDE,)),
        pltpu.SemaphoreType.DMA((2 * SIDE,)),
        pltpu.SemaphoreType.DMA((SIDE, 2)),
        pltpu.SemaphoreType.DMA((SIDE, 2)),
        pltpu.SemaphoreType.DMA((SIDE, 2)),
        pltpu.SemaphoreType.DMA((SIDE + 1, 2)),
        pltpu.SemaphoreType.DMA((SIDE,)),
        pltpu.SemaphoreType.DMA((SIDE + 1,)),
    ]


def forward_scatter(hidden, bias, mixed, active, out_weight, down_weight, layer, swap=()):
    rows = hidden.shape[0]

    def kernel(hidden, bias, mixed, active, out_weight, down_weight, *refs):
        if swap:
            source, out, target, swap_sem = refs[:4]
            refs = refs[4:]
        else:
            out, refs = refs[0], refs[1:]
        hidden_part, mixed_part, active_part, out_part, down_part, load_sem = refs[:6]
        scratch = refs[6:]
        loads = load_all(
            (
                (mixed, mixed_part),
                (active, active_part),
                (out_weight.at[layer], out_part),
                (down_weight.at[layer], down_part),
                (hidden, hidden_part),
            ),
            load_sem,
        )
        greet_neighbours(bool(swap))
        if swap:
            plane_swap((source, target), swap_sem).start()
        wait_all(loads[:4])

        def partial(slot):
            return dot(mixed_part[slot], out_part[...]) + dot(active_part[slot], down_part[...])

        scatter_events(partial, None, None, SCATTER_OPS, scratch)
        loads[4].wait()
        out[...] = hidden_part[...].astype(jnp.float32) + (scratch[0][...] + bias[...])
        if swap:
            plane_swap((source, target), swap_sem).wait()

    return pl.pallas_call(
        kernel,
        out_shape=(jax.ShapeDtypeStruct((rows, D), jnp.float32),)
        + tuple(jax.ShapeDtypeStruct(array.shape, array.dtype) for array in swap),
        in_specs=[HBM, VMEM] + [HBM] * (4 + len(swap)),
        out_specs=(VMEM,) + (HBM,) * len(swap),
        scratch_shapes=[pltpu.SemaphoreType.DMA((2,))] * len(swap)
        + [pltpu.VMEM(array.shape, array.dtype) for array in (hidden, mixed, active)]
        + [
            pltpu.VMEM(out_weight.shape[1:], jnp.bfloat16),
            pltpu.VMEM(down_weight.shape[1:], jnp.bfloat16),
        ]
        + [pltpu.SemaphoreType.DMA((5,))]
        + scatter_scratch(rows),
        compiler_params=pltpu.CompilerParams(
            collective_id=10 + layer, has_side_effects=True, vmem_limit_bytes=ROOM
        ),
    )(hidden, bias, mixed, active, out_weight, down_weight, *swap)


SMALL_ROWS = 16
PAIRS = GROUP // 2


def backward_scatter(
    hidden, grad, gain, grad_joint, grad_inner, columns, every, layer, up=None, halves=()
):
    rows = hidden.shape[0]
    half = SHARE // 2
    collects = up is not None
    made = JOINT_COLS if collects else COLS
    tokens = GROUP * rows

    def kernel(*refs):
        inputs, refs = refs[: 10 if collects else 7], refs[10 if collects else 7 :]
        gain, every = inputs[2], inputs[6]
        out, small_out, refs = refs[0], refs[1], refs[2:]
        if collects:
            outputs, others, refs = refs[:2], refs[2:4], refs[4:]
        else:
            summed, refs = refs[0], refs[1:]
        hidden, grad, grad_joint, grad_inner, columns, load_sem, strips, load = refs[:8]
        shares, small_land, small_mine, small_other = refs[8:12]
        small_send, small_recv, swap_send, swap_recv = refs[12:16]
        mine, other, cross_send, cross_recv = refs[16:20]
        refs = refs[20:]
        if collects:
            summed, arrived, arrived_up, plane_send, plane_recv = refs[:5]
            back_send, back_recv, keep = refs[5:8]
            up_send, up_recv, up_own, half_send, half_recv, half_own = refs[8:14]
            refs = refs[14:]
        scratch = refs
        total = scratch[0]
        ctx, place, seq = lax.axis_index("ctx"), lax.axis_index("fsdp"), lax.axis_index("seq")
        me = ctx * SIDE + place
        part_rows = pl.ds(pl.multiple_of(seq * half, half), half)
        other_rows = pl.ds(pl.multiple_of((1 - seq) * half, half), half)

        def pair_of(turn):
            return lax.rem(me // 2 + 1 + turn, PAIRS)

        def load_strip(turn):
            start = pl.multiple_of(pair_of(turn) * 2 * SHARE, 2 * SHARE)
            buffer = lax.rem(turn, 2)
            return pltpu.make_async_copy(
                every.at[:, :, pl.ds(start, 2 * SHARE)], strips.at[buffer], load.at[buffer]
            )

        loads = load_all(
            (
                (inputs[3], grad_joint),
                (inputs[4], grad_inner),
                (inputs[5], columns),
                (inputs[0], hidden),
                (inputs[1], grad),
            ),
            load_sem,
        )
        load_strip(jnp.int32(0)).start()
        shares[...] = jnp.zeros_like(shares)
        greet_plane(GROUP)

        def partial(slot):
            return dot(grad_joint[slot], columns[:, :JOINT_COLS], 1, 1) + dot(
                grad_inner[slot], columns[:, JOINT_COLS:], 1, 1
            )

        def product(turn):
            pair = pair_of(turn)
            load_strip(turn).wait()

            @pl.when(turn + 1 < PAIRS)
            def _():
                load_strip(turn + 1).start()

            strip = strips[lax.rem(turn, 2)].reshape(tokens, 2 * SHARE)
            result = dot(strip, grad_joint[...].reshape(tokens, JOINT_COLS), 0, 0).astype(jnp.bfloat16)
            for which in range(2):
                mine[2 * pair + which, :, :JOINT_COLS] = result[which * SHARE : (which + 1) * SHARE]
            if not collects:
                result = dot(strip, grad_inner[...].reshape(tokens, FEED_COLS), 0, 0).astype(
                    jnp.bfloat16
                )
                for which in range(2):
                    mine[2 * pair + which, :, JOINT_COLS:] = result[which * SHARE : (which + 1) * SHARE]

        def cross_copy(block):
            return to_axis(
                mine.at[block, other_rows],
                other.at[block],
                cross_send.at[block],
                cross_recv.at[block],
                "seq",
                1 - seq,
            )

        def plane_copy(block):
            return to_peer(
                summed.at[block], arrived.at[me], plane_send.at[block], plane_recv.at[me], block
            )

        def up_copy(step):
            peer = lax.rem(me + step, GROUP)
            return to_peer(inputs[7].at[peer], arrived_up.at[me], up_send.at[step], up_recv.at[me], peer)

        def half_copies(pieces):
            return [
                to_axis(
                    own.at[pl.ds(piece * (half // 4), half // 4)],
                    there.at[pl.ds(pl.multiple_of(seq * half + piece * (half // 4), half // 4), half // 4)],
                    half_send.at[at, piece],
                    half_recv.at[at, piece],
                    "seq",
                    1 - seq,
                )
                for at, (own, there) in enumerate(zip(inputs[8:10], others))
                for piece in pieces
            ]

        def half_kept():
            return [
                pltpu.make_async_copy(own, there.at[part_rows], half_own.at[at])
                for at, (own, there) in enumerate(zip(inputs[8:10], others))
            ]

        def final_pieces(source):
            pieces = []
            for number, (which, start, at, width) in enumerate(column_places(source)):
                piece = arrived_up.at[source] if which else arrived.at[source, :, pl.ds(at, width)]
                pieces.append((number, piece, outputs[which].at[part_rows, pl.ds(start, width)]))
            return pieces

        def back_copy(number, piece, target, source):
            return to_axis(
                piece,
                target,
                back_send.at[source, number],
                back_recv.at[source, number],
                "seq",
                1 - seq,
            )

        def keep_copy(number, piece, target, source):
            return pltpu.make_async_copy(piece, target, keep.at[source, number])

        def pass_on(source, which):
            for number, piece, target in final_pieces(source):
                if (number == PLACES - 1) == (which == 1):
                    back_copy(number, piece, target, source).start()
                    keep_copy(number, piece, target, source).start()

        def add(turn):
            for which in range(2):
                block = 2 * pair_of(turn) + which
                cross_copy(block).wait_recv()
                summed[block] = (
                    mine[block, part_rows].astype(jnp.float32) + other[block].astype(jnp.float32)
                ).astype(jnp.bfloat16)

                if collects:

                    @pl.when(block != me)
                    def _(block=block):
                        plane_copy(block).start()

        def bias_sums():
            ones = jnp.ones((16, tokens), jnp.bfloat16)
            joint_bias = dot(ones, grad_joint[...].reshape(tokens, JOINT_COLS))[:1]
            upper_bias = dot(ones, grad_inner[...].reshape(tokens, FEED_COLS))[:1]
            for part in range(3):
                at = part * GROUP + me
                shares[at // 3, pl.ds(3 + lax.rem(at, 3), 1)] = joint_bias[
                    :, part * HEAD_COLS : (part + 1) * HEAD_COLS
                ]
            for part in range(FEED_COLS // SHARE):
                shares[me, 6 + part : 7 + part] = upper_bias[:, part * SHARE : (part + 1) * SHARE]

        def other_work(turn):
            pl.when(turn == 1)(bias_sums)

            @pl.when(lax.rem(turn, 2) == 0)
            def _():
                product(turn // 2)
                for which in range(2):
                    cross_copy(2 * pair_of(turn // 2) + which).start()

            @pl.when((lax.rem(turn, 2) == 1) & (turn > 4))
            def _():
                add((turn - 5) // 2)

            if collects:

                @pl.when(turn == GROUP - 1)
                def _():
                    for copy in half_copies((2, 3)):
                        copy.start()

        def late_work(step):
            @pl.when(step == 0)
            def _():
                lax.fori_loop(PAIRS - 2, PAIRS, last_adds, 0)
                arrived[me] = summed[me]

            def pass_up(more, carry):
                number = SIDE * step + more
                source = lax.rem(me + GROUP - number, GROUP)

                @pl.when(number == 0)
                def _():
                    own_up.wait()

                @pl.when(number > 0)
                def _():
                    block = arrived_up.at[source]
                    to_peer(block, block, up_send.at[number], up_recv.at[source], source).wait_recv()

                pass_on(source, 1)
                return carry

            lax.fori_loop(0, SIDE, pass_up, 0)

        def pass_joint(step, carry):
            source = lax.rem(me + GROUP - step, GROUP)

            @pl.when(step > 0)
            def _():
                to_peer(
                    summed.at[source],
                    arrived.at[source],
                    plane_send.at[source],
                    plane_recv.at[source],
                    source,
                ).wait_recv()

            pass_on(source, 0)
            return carry

        def last_adds(turn, carry):
            add(turn)
            return carry

        def send_up(step, carry):
            up_copy(step).start()
            return carry

        wait_all(loads[:3])
        if collects:
            own_up = pltpu.make_async_copy(inputs[7].at[me], arrived_up.at[me], up_own)
            own_up.start()
            lax.fori_loop(1, GROUP, send_up, 0)
            for copy in half_copies((0, 1)) + half_kept():
                copy.start()
        scatter_events(
            partial,
            other_work,
            late_work if collects else None,
            SCATTER_OPS_EARLY if collects else SCATTER_OPS_WORK,
            scratch,
        )
        if collects:
            lax.fori_loop(0, GROUP, pass_joint, 0)
        else:
            lax.fori_loop(PAIRS - 2, PAIRS, last_adds, 0)
        wait_all(loads[3:])

        def norm_back(part, sums):
            values = hidden[part].astype(jnp.float32)
            centred = values - jnp.mean(values, axis=1, keepdims=True)
            spread = jnp.mean(centred * centred, axis=1, keepdims=True)
            root = lax.rsqrt(spread + EPS)
            normed = centred * root
            above = total[part]
            scaled = above * gain[...]
            down = jnp.mean(scaled, axis=1, keepdims=True)
            along = jnp.mean(scaled * normed, axis=1, keepdims=True)
            passing = grad[part]
            out[part] = passing + root * (scaled - down - normed * along)
            low = passing.astype(jnp.bfloat16).astype(jnp.float32)

            def fold(values):
                return jnp.sum(values.reshape(STRIP // 8, 8, D), axis=0)

            return (sums[0] + fold(above * normed), sums[1] + fold(above), sums[2] + fold(low))

        zeros = jnp.zeros((8, D), jnp.float32)
        sums = each_strip(rows, norm_back, (zeros, zeros, zeros))
        for number, folded in enumerate(sums):
            row = jnp.sum(folded, axis=0, keepdims=True)
            for block in range(GROUP):
                shares[block, number : number + 1] = row[:, block * SHARE : (block + 1) * SHARE]
        def small_copy(step):
            peer = lax.rem(me + step, GROUP)
            return to_peer(
                shares.at[peer], small_land.at[me], small_send.at[step], small_recv.at[me], peer
            )

        def small_begin(step, carry):
            small_copy(step).start()
            return carry

        lax.fori_loop(1, GROUP, small_begin, 0)
        small_land[me] = shares[me]

        def small_end(step, carry):
            source = lax.rem(me + GROUP - step, GROUP)
            to_peer(
                shares.at[source],
                small_land.at[source],
                small_send.at[step],
                small_recv.at[source],
                source,
            ).wait_recv()
            small_copy(step).wait_send()
            return carry

        lax.fori_loop(1, GROUP, small_end, 0)
        small_mine[...] = jnp.sum(small_land[...], axis=0)
        swap = to_axis(small_mine, small_other, swap_send, swap_recv, "seq", 1 - seq)
        swap.start()
        swap.wait()
        small_out[...] = small_mine[...] + small_other[...]

        def end_cross(block, carry):
            cross_copy(block).wait_send()
            return carry

        lax.fori_loop(0, GROUP, end_cross, 0)

        def end(block, carry):
            @pl.when(block != me)
            def _():
                plane_copy(block).wait_send()

            @pl.when(block > 0)
            def _():
                up_copy(block).wait_send()

            for number, piece, target in final_pieces(block):
                back_copy(number, piece, target, block).wait()
                keep_copy(number, piece, target, block).wait()
            return carry

        if collects:
            lax.fori_loop(0, GROUP, end, 0)
            wait_all(half_copies((0, 1, 2, 3)) + half_kept())

    def part(width, height=half):
        return pltpu.VMEM((GROUP, height, width), jnp.bfloat16)

    small = (SMALL_ROWS, SHARE)
    sixteen, places = pltpu.SemaphoreType.DMA((GROUP,)), pltpu.SemaphoreType.DMA((GROUP, PLACES))
    return pl.pallas_call(
        kernel,
        out_shape=(
            jax.ShapeDtypeStruct((rows, D), jnp.float32),
            jax.ShapeDtypeStruct(small, jnp.float32),
        )
        + (
            (
                jax.ShapeDtypeStruct((SHARE, 3 * D), jnp.bfloat16),
                jax.ShapeDtypeStruct((SHARE, FF), jnp.bfloat16),
            )
            * 2
            if collects
            else (jax.ShapeDtypeStruct((GROUP, half, COLS), jnp.bfloat16),)
        ),
        in_specs=[HBM, HBM, VMEM] + [HBM] * (7 if collects else 4),
        out_specs=(VMEM, VMEM) + ((HBM,) * 4 if collects else (VMEM,)),
        scratch_shapes=[
            pltpu.VMEM(array.shape, array.dtype)
            for array in (hidden, grad, grad_joint, grad_inner, columns)
        ]
        + [
            pltpu.SemaphoreType.DMA((5,)),
            pltpu.VMEM((2, GROUP, rows, 2 * SHARE), jnp.bfloat16),
            pltpu.SemaphoreType.DMA((2,)),
            pltpu.VMEM((GROUP,) + small, jnp.float32),
            pltpu.VMEM((GROUP,) + small, jnp.float32),
            pltpu.VMEM(small, jnp.float32),
            pltpu.VMEM(small, jnp.float32),
            sixteen,
            sixteen,
            pltpu.SemaphoreType.DMA,
            pltpu.SemaphoreType.DMA,
            part(made, SHARE),
            part(made),
            sixteen,
            sixteen,
        ]
        + (
            [part(JOINT_COLS)] * 2
            + [part(FEED_COLS)]
            + [sixteen] * 2
            + [places] * 3
            + [sixteen] * 2
            + [pltpu.SemaphoreType.DMA]
            + [pltpu.SemaphoreType.DMA((2, 4))] * 2
            + [pltpu.SemaphoreType.DMA((2,))]
            if collects
            else []
        )
        + scatter_scratch(rows),
        compiler_params=pltpu.CompilerParams(
            collective_id=20 + layer, has_side_effects=True, vmem_limit_bytes=ROOM
        ),
    )(hidden, grad, gain, grad_joint, grad_inner, columns, every, *((up, *halves) if collects else ()))


def mask_rest(rows, begin, spot, first, lead):
    if lead:
        old = jnp.where(spot[:lead] >= begin, rows[:lead], NEG)
    key_at = lax.broadcasted_iota(jnp.int32, (first, first), 0) + lead
    query_at = lax.broadcasted_iota(jnp.int32, (first, first), 1) + lead
    near = spot[lead:]
    seen = ((near >= begin) & (near <= query_at)) | (key_at == query_at)
    new = jnp.where(seen, rows[lead:], NEG)
    return jnp.concatenate([old, new], axis=0) if lead else new


def head_lanes(head, rows):
    lane = lax.broadcasted_iota(jnp.int32, (rows, HEAD_COLS), 1)
    return (lane >= head * HEAD_DIM) & (lane < (head + 1) * HEAD_DIM)


def column_exchange(sources, land, sems, layer):
    plane_send, plane_recv, own_sem = sems
    ctx, place, seq = lax.axis_index("ctx"), lax.axis_index("fsdp"), lax.axis_index("seq")
    me = ctx * SIDE + place
    half = SHARE // 2
    part_rows = pl.ds(pl.multiple_of(seq * half, half), half)

    def piece(peer, number):
        which, start, at, width = column_places(peer)[number]
        return (
            sources[which].at[layer, part_rows, pl.ds(start, width)],
            land.at[me, :, pl.ds(at, width)],
        )

    def send_piece(step, number):
        peer = lax.rem(me + step, GROUP)
        source, target = piece(peer, number)
        return to_peer(source, target, plane_send.at[step, number], plane_recv.at[me, number], peer)

    def own_piece(number):
        return pltpu.make_async_copy(*piece(me, number), own_sem.at[number])

    def begin():
        greet_plane(GROUP, False)

        def send(step, carry):
            for number in range(PLACES):
                send_piece(step, number).start()
            return carry

        lax.fori_loop(1, GROUP, send, 0)
        for number in range(PLACES):
            own_piece(number).start()

    def end():
        def arrive(step, carry):
            source = lax.rem(me + GROUP - step, GROUP)
            for number in range(PLACES):
                _, _, at, width = column_places(0)[number]
                target = land.at[source, :, pl.ds(at, width)]
                to_peer(
                    target, target, plane_send.at[0, number], plane_recv.at[source, number], source
                ).wait_recv()
                send_piece(step, number).wait_send()
            return carry

        lax.fori_loop(1, GROUP, arrive, 0)
        for number in range(PLACES):
            own_piece(number).wait()

    return begin, end


def up_products(every, feed, out, scratch):
    feed_part, strips, mine, other, feed_sem, load, cross_send, cross_recv = scratch
    rows = feed.shape[1]
    tokens = GROUP * rows
    half = SHARE // 2
    seq = lax.axis_index("seq")
    me = lax.axis_index("ctx") * SIDE + lax.axis_index("fsdp")
    part_rows = pl.ds(pl.multiple_of(seq * half, half), half)
    other_rows = pl.ds(pl.multiple_of((1 - seq) * half, half), half)

    def pair_of(turn):
        return lax.rem(me // 2 + 1 + turn, PAIRS)

    def load_strip(turn):
        start = pl.multiple_of(pair_of(turn) * 2 * SHARE, 2 * SHARE)
        buffer = lax.rem(turn, 2)
        return pltpu.make_async_copy(
            every.at[:, :, pl.ds(start, 2 * SHARE)], strips.at[buffer], load.at[buffer]
        )

    def cross_copy(block):
        return to_axis(
            mine.at[block, other_rows],
            other.at[block],
            cross_send.at[block],
            cross_recv.at[block],
            "seq",
            1 - seq,
        )

    def feed_copy():
        return pltpu.make_async_copy(feed, feed_part, feed_sem)

    def begin():
        feed_copy().start()
        load_strip(jnp.int32(0)).start()

    def product(turn, carry):
        pair = pair_of(turn)
        load_strip(turn).wait()

        @pl.when(turn == 0)
        def _():
            feed_copy().wait()

        @pl.when(turn + 1 < PAIRS)
        def _():
            load_strip(turn + 1).start()

        strip = strips[lax.rem(turn, 2)].reshape(tokens, 2 * SHARE)
        made = dot(strip, feed_part[...].reshape(tokens, FEED_COLS), 0, 0).astype(jnp.bfloat16)
        for which in range(2):
            mine[2 * pair + which] = made[which * SHARE : (which + 1) * SHARE]
            cross_copy(2 * pair + which).start()
        return carry

    def add(turn, carry):
        for which in range(2):
            block = 2 * pair_of(turn) + which
            cross_copy(block).wait()
            out[block] = (
                mine[block, part_rows].astype(jnp.float32) + other[block].astype(jnp.float32)
            ).astype(jnp.bfloat16)
        return carry

    each = PAIRS // SIDE

    def make(step):
        lax.fori_loop(each * step, each * step + each, product, 0)
        lax.fori_loop(each * jnp.maximum(step - 1, 0), each * step, add, 0)

    def end():
        lax.fori_loop(PAIRS - each, PAIRS, add, 0)

    return begin, make, end


def row_exchange(summed, outputs, sems):
    plane_send, plane_recv, own_sem = sems
    me = lax.axis_index("ctx") * SIDE + lax.axis_index("fsdp")

    def piece(peer, number):
        which, start, at, width = column_places(me)[number]
        return summed.at[peer, :, pl.ds(at, width)], outputs[which].at[:, pl.ds(start, width)]

    def send_piece(step, number):
        peer = lax.rem(me + step, GROUP)
        source, target = piece(peer, number)
        return to_peer(source, target, plane_send.at[step, number], plane_recv.at[me, number], peer)

    def own_piece(number):
        return pltpu.make_async_copy(*piece(me, number), own_sem.at[number])

    def begin():
        greet_plane(GROUP)

        def send(step, carry):
            for number in range(PLACES):
                send_piece(step, number).start()
            return carry

        lax.fori_loop(1, GROUP, send, 0)
        for number in range(PLACES):
            own_piece(number).start()

    def end():
        def arrive(step, carry):
            source = lax.rem(me + GROUP - step, GROUP)
            for number in range(PLACES):
                which, start, _, width = column_places(source)[number]
                target = outputs[which].at[:, pl.ds(start, width)]
                to_peer(
                    target, target, plane_send.at[0, number], plane_recv.at[source, number], source
                ).wait_recv()
                send_piece(step, number).wait_send()
            return carry

        lax.fori_loop(1, GROUP, arrive, 0)
        for number in range(PLACES):
            own_piece(number).wait()

    return begin, end


EXCHANGE_SEMS = [
    pltpu.SemaphoreType.DMA((GROUP, PLACES)),
    pltpu.SemaphoreType.DMA((GROUP, PLACES)),
    pltpu.SemaphoreType.DMA((PLACES,)),
]


def attend_plane(query, key, value, begin, spot, weights=None, layer=0):
    rows = query.shape[1]
    length = SIDE * rows
    scale = 1.0 / math.sqrt(HEAD_DIM)

    def kernel(query, key, value, begin, spot, *refs):
        if weights is None:
            mixed, turned, stats = refs
        else:
            mixed, turned, stats, land = refs[2:6]
            begin_exchange, end_exchange = column_exchange(refs[:2], land, refs[6:], layer)
            pl.when(pl.program_id(0) == 0)(begin_exchange)
        keys = key[:, 0].reshape(length, HEAD_COLS)
        values = value[:, 0].reshape(length, HEAD_COLS)
        for chunk in range(SIDE):
            lead = chunk * rows
            seen = lead + rows
            scaled = query[chunk, 0] * jnp.bfloat16(scale)
            start = begin[0, :, lead:seen]
            outs = []
            for head in range(OWN):
                own = jnp.where(head_lanes(head, rows), scaled, jnp.bfloat16(0))
                scores = mask_rest(
                    dot(keys[:seen], own, 1, 1), start, spot[0, :seen], rows, lead
                )
                peak = jnp.max(scores, axis=0, keepdims=True)
                probs = jnp.exp(scores - peak)
                norm = jnp.sum(probs, axis=0, keepdims=True)
                stats[0, head : head + 1, lead:seen] = peak
                stats[0, OWN + head : OWN + head + 1, lead:seen] = norm
                whole = dot(values[:seen], probs.astype(jnp.bfloat16), 0, 0)
                outs.append(whole[head * HEAD_DIM : (head + 1) * HEAD_DIM] / norm)
            joined = jnp.concatenate(outs, axis=0)
            turned[chunk, 0] = joined
            mixed[chunk, 0] = joined.T.astype(jnp.bfloat16)
        if weights is not None:
            pl.when(pl.program_id(0) == SIDE - 1)(end_exchange)

    def spec(height, width):
        return pl.BlockSpec((SIDE, 1, height, width), lambda step: (0, step, 0, 0))

    def shape(height, width, dtype):
        return jax.ShapeDtypeStruct((SIDE, SIDE, height, width), dtype)

    extra = weights is not None
    land = (jax.ShapeDtypeStruct((GROUP, SHARE // 2, COLS), jnp.bfloat16),) if extra else ()
    mixed, turned, stats, *land = pl.pallas_call(
        kernel,
        grid=(SIDE,),
        out_shape=(
            shape(rows, HEAD_COLS, jnp.bfloat16),
            shape(HEAD_COLS, rows, jnp.float32),
            jax.ShapeDtypeStruct((SIDE, 2 * OWN, length), jnp.float32),
        )
        + land,
        in_specs=[spec(rows, HEAD_COLS)] * 3
        + [
            pl.BlockSpec((1, 1, length), lambda step: (step, 0, 0)),
            pl.BlockSpec((1, length, 1), lambda step: (step, 0, 0)),
        ]
        + [HBM] * (2 if extra else 0),
        out_specs=(
            spec(rows, HEAD_COLS),
            spec(HEAD_COLS, rows),
            pl.BlockSpec((1, 2 * OWN, length), lambda step: (step, 0, 0)),
        )
        + ((HBM,) if extra else ()),
        scratch_shapes=EXCHANGE_SEMS if extra else [],
        compiler_params=pltpu.CompilerParams(
            collective_id=40, has_side_effects=True, vmem_limit_bytes=ROOM
        )
        if extra
        else pltpu.CompilerParams(vmem_limit_bytes=ROOM),
    )(
        *(array.reshape(SIDE, SIDE, rows, HEAD_COLS) for array in (query, key, value)),
        begin,
        spot,
        *(weights or ()),
    )
    return mixed.reshape(GROUP, rows, HEAD_COLS), turned, stats, *land


def attend_plane_back(
    query, key, value, begin, spot, turned, stats, grad, tables, summed=None, every=None, feed=None
):
    rows = query.shape[1]
    length = SIDE * rows
    scale = 1.0 / math.sqrt(HEAD_DIM)

    extra = summed is not None

    def kernel(query, key, value, grad, cosine, sine, begin, spot, turned, stats, *refs):
        if extra:
            summed, every, feed, out = refs[:4]
            up_out, grad_k, grad_v = refs[6], refs[7], refs[8]
            begin_exchange, end_exchange = row_exchange(summed, refs[4:6], refs[9:12])
            begin_up, make_up, end_up = up_products(every, feed, up_out, refs[12:])

            @pl.when(pl.program_id(0) == 0)
            def _():
                begin_up()
                begin_exchange()

        else:
            out, grad_k, grad_v = refs
        keys = key[:, 0].reshape(length, HEAD_COLS)
        values = value[:, 0].reshape(length, HEAD_COLS)
        for chunk in range(SIDE):
            lead = chunk * rows
            seen = lead + rows
            if chunk == 0:
                grad_k[...] = jnp.zeros_like(grad_k)
                grad_v[...] = jnp.zeros_like(grad_v)
            scaled = query[chunk, 0] * jnp.bfloat16(scale)
            start = begin[0, :, lead:seen]
            flipped = grad[chunk, 0].T
            grad_q, drifts, numers = [], [], []
            for head in range(OWN):
                part = slice(head * HEAD_DIM, (head + 1) * HEAD_DIM)
                norm = stats[0, OWN + head : OWN + head + 1, lead:seen]
                drifts.append(
                    jnp.sum(flipped[part] * turned[chunk, 0, part], axis=0, keepdims=True) / norm
                )
                numers.append(flipped[part] / norm)
            numer = jnp.concatenate(numers, axis=0).T.astype(jnp.bfloat16)
            for head in range(OWN):
                part = slice(head * HEAD_DIM, (head + 1) * HEAD_DIM)
                lanes = head_lanes(head, rows)
                own = jnp.where(lanes, scaled, jnp.bfloat16(0))
                own_numer = jnp.where(lanes, numer, jnp.bfloat16(0))
                scores = mask_rest(
                    dot(keys[:seen], own, 1, 1), start, spot[0, :seen], rows, lead
                )
                probs = jnp.exp(scores - stats[0, head : head + 1, lead:seen])
                grad_probs = dot(values[:seen], own_numer, 1, 1)
                grad_scores = (probs * (grad_probs - drifts[head])).astype(jnp.bfloat16)
                grad_q.append(dot(keys[:seen], grad_scores, 0, 0)[part])
                grad_k[:seen] += dot(grad_scores, own)
                grad_v[:seen] += dot(probs.astype(jnp.bfloat16), own_numer)
            turns = (cosine[chunk, 0], sine[chunk, 0])
            whole = jnp.concatenate(grad_q, axis=0).T * scale
            out[chunk, 0, :, :HEAD_COLS] = spin(whole, *turns, -1.0).astype(jnp.bfloat16)
        for chunk in range(SIDE):
            place = slice(chunk * rows, (chunk + 1) * rows)
            turns = (cosine[chunk, 0], sine[chunk, 0])
            out[chunk, 0, :, HEAD_COLS : 2 * HEAD_COLS] = spin(grad_k[place], *turns, -1.0).astype(
                jnp.bfloat16
            )
            out[chunk, 0, :, 2 * HEAD_COLS :] = grad_v[place].astype(jnp.bfloat16)
        if extra:
            make_up(pl.program_id(0))

            @pl.when(pl.program_id(0) == SIDE - 1)
            def _():
                end_up()
                end_exchange()


    def spec(height, width):
        return pl.BlockSpec((SIDE, 1, height, width), lambda step: (0, step, 0, 0))

    half = SHARE // 2
    halves = (
        jax.ShapeDtypeStruct((half, 3 * D), jnp.bfloat16),
        jax.ShapeDtypeStruct((half, FF), jnp.bfloat16),
        jax.ShapeDtypeStruct((GROUP, half, FEED_COLS), jnp.bfloat16),
    )
    out, *halves = pl.pallas_call(
        kernel,
        grid=(SIDE,),
        out_shape=(jax.ShapeDtypeStruct((SIDE, SIDE, rows, JOINT_COLS), jnp.bfloat16),)
        + (halves if extra else ()),
        in_specs=[spec(rows, HEAD_COLS)] * 6
        + [
            pl.BlockSpec((1, 1, length), lambda step: (step, 0, 0)),
            pl.BlockSpec((1, length, 1), lambda step: (step, 0, 0)),
            spec(HEAD_COLS, rows),
            pl.BlockSpec((1, 2 * OWN, length), lambda step: (step, 0, 0)),
        ]
        + [HBM] * (3 if extra else 0),
        out_specs=(spec(rows, JOINT_COLS),)
        + (
            (HBM, HBM, pl.BlockSpec((GROUP, half, FEED_COLS), lambda step: (0, 0, 0)))
            if extra
            else ()
        ),
        scratch_shapes=[pltpu.VMEM((length, HEAD_COLS), jnp.float32)] * 2
        + (
            EXCHANGE_SEMS
            + [
                pltpu.VMEM((GROUP, rows, FEED_COLS), jnp.bfloat16),
                pltpu.VMEM((2, GROUP, rows, 2 * SHARE), jnp.bfloat16),
                pltpu.VMEM((GROUP, SHARE, FEED_COLS), jnp.bfloat16),
                pltpu.VMEM((GROUP, half, FEED_COLS), jnp.bfloat16),
                pltpu.SemaphoreType.DMA,
                pltpu.SemaphoreType.DMA((2,)),
                pltpu.SemaphoreType.DMA((GROUP,)),
                pltpu.SemaphoreType.DMA((GROUP,)),
            ]
            if extra
            else []
        ),
        compiler_params=pltpu.CompilerParams(
            collective_id=41, has_side_effects=True, vmem_limit_bytes=ROOM
        )
        if extra
        else pltpu.CompilerParams(vmem_limit_bytes=ROOM),
    )(
        *(
            array.reshape(SIDE, SIDE, rows, HEAD_COLS)
            for array in (query, key, value, grad) + tuple(tables)
        ),
        begin,
        spot,
        turned,
        stats,
        *((summed, every, feed) if extra else ()),
    )
    return out.reshape(GROUP, rows, JOINT_COLS), *halves


def on_device_split(
    tokens,
    doc_lengths,
    keep_mask,
    ln_gain,
    ln_bias,
    qkv_weight,
    qkv_bias,
    out_weight,
    out_bias,
    up_weight,
    up_bias,
    down_weight,
    down_bias,
    cotangent,
):
    rows = tokens.shape[1]
    length = SIDE * rows
    me = lax.axis_index("ctx") * SIDE + lax.axis_index("fsdp")

    index = lax.axis_index("ctx") * rows + jnp.arange(rows, dtype=jnp.int32)
    ends = jnp.cumsum(doc_lengths[0])
    begin = jnp.max(jnp.where(index[:, None] >= ends[None, :], ends[None, :], 0), axis=1)
    fields = [ln_gain, ln_bias, qkv_bias, out_bias, down_bias]
    packed = jnp.concatenate(
        [field[layer].astype(jnp.float32) for layer in range(LAYERS) for field in fields]
        + [begin.astype(jnp.float32), keep_mask[0].astype(jnp.float32)]
    )
    packed = jnp.pad(packed, (0, -packed.shape[0] % (8 * SHARE))).reshape(-1, SHARE)
    lane = np.arange(HEAD_COLS) % HEAD_DIM
    inverse = 1.0 / 10000.0 ** (np.arange(0, ROT, 2, dtype=np.float32) / np.float32(ROT))
    inverse = np.where(lane < ROT, inverse[lane % (ROT // 2)], 0.0).astype(np.float32)
    up_bias = up_bias.astype(jnp.float32)

    seq = lax.axis_index("seq")
    half = SHARE // 2
    swap = [(0, 1), (1, 0)]

    def swapped(values):
        return lax.ppermute(values, "seq", swap)

    hidden = tokens[0]
    saved, gains, joint_grads, upper_grads, small_grads = [], [], [], [], []
    for layer in range(LAYERS):
        if layer == 0:
            *out, small, cosine, sine = first_gather(
                hidden, packed, up_bias[:1], jnp.asarray(inverse)[None, :], qkv_weight, up_weight
            )
            tables = (cosine, sine)
            length_rows = rows // SHARE

            def by_sequence(row):
                values = small[:, row : row + length_rows].reshape(SIDE, SIDE, rows)
                return values.transpose(1, 0, 2).reshape(SIDE, length).astype(jnp.int32)

            begin = by_sequence(BEGIN_ROW)[:, None, :]
            keep = by_sequence(BEGIN_ROW + length_rows)
            spot = jnp.where(keep > 0, jnp.arange(length, dtype=jnp.int32)[None, :], -1)[:, :, None]
        else:
            out = forward_gather(
                hidden,
                gain_row,
                row_of(layer, SHIFT_ROW),
                jnp.concatenate([own_bias, up_bias[layer : layer + 1]], axis=1),
                tables,
                halves,
                layer,
            )

        def row_of(layer, row):
            return small[:, layer * LAYER_ROWS + row].reshape(1, D)

        every, columns, query, key, value, inner, active = out
        gains.append(row_of(layer, GAIN_ROW))
        if layer + 1 < LAYERS:
            mixed, turned, stats, arrived = attend_plane(
                query, key, value, begin, spot, (qkv_weight, up_weight), layer + 1
            )
            halves = (arrived, swapped(arrived))
            gain_row = row_of(layer + 1, GAIN_ROW)
            at = (layer + 1) * LAYER_ROWS + JOINT_BIAS_ROW
            own_bias = lax.dynamic_slice_in_dim(
                small[:, at : at + 3].reshape(3, GROUP, HEAD_COLS), me, 1, axis=1
            ).reshape(1, JOINT_COLS)
        else:
            mixed, turned, stats = attend_plane(query, key, value, begin, spot)
        saved.append(
            (hidden, every, columns, query, key, value, inner, active, mixed, turned, stats)
        )
        branches = (
            hidden,
            row_of(layer, OUT_BIAS_ROW) + row_of(layer, DOWN_BIAS_ROW),
            mixed,
            active,
            out_weight,
            down_weight,
            layer,
        )
        if layer + 1 < LAYERS:
            hidden = forward_scatter(*branches)[0]

    grad_hidden = cotangent[0].astype(jnp.float32) * keep_mask[0].astype(jnp.float32)[:, None]
    summed = branch = None
    own_branches, other_branches = [], []
    for layer in reversed(range(LAYERS)):
        before, every, columns, query, key, value, inner, active, mixed, turned, stats = saved[layer]
        grad_mixed, grad_inner, branch, *other = backward_gather(
            grad_hidden.astype(jnp.bfloat16),
            out_weight,
            down_weight,
            inner,
            mixed,
            active,
            layer,
            () if layer + 1 == LAYERS else (branch,),
        )
        own_branches.insert(0, branch)
        other_branches = list(other) + other_branches
        if layer == 0:
            hidden, other = forward_scatter(*branches, (branch,))
            other_branches.insert(0, other)
        grad_joint, *rest = attend_plane_back(
            query,
            key,
            value,
            begin,
            spot,
            turned,
            stats,
            grad_mixed,
            tables,
            summed,
            every,
            grad_inner,
        )
        grad_hidden, small, *grads = backward_scatter(
            before,
            grad_hidden,
            gains[layer],
            grad_joint,
            grad_inner,
            columns.reshape(D, COLS),
            every,
            layer,
            rest[2] if rest else None,
            rest[:2],
        )
        small_grads.insert(0, small)
        if layer > 0:
            summed = grads[0]
        else:
            joint_grads.extend(grads[0::2])
            upper_grads.extend(grads[1::2])
    here, there = jnp.stack(own_branches), jnp.stack(other_branches)
    result = hidden.astype(jnp.bfloat16)[None]

    def branch_grad(part):
        return here[:, part].astype(jnp.float32) + there[:, part].astype(jnp.float32)

    small = jnp.stack(small_grads)
    return (
        result,
        grad_hidden[None],
        small[:, 0],
        small[:, 1],
        jnp.stack(joint_grads).astype(jnp.float32),
        small[:, 3:6].reshape(LAYERS, JOINT_COLS),
        branch_grad(slice(0, HEAD_COLS)),
        small[:, 2],
        jnp.stack(upper_grads).astype(jnp.float32),
        small[:, 6:10].reshape(LAYERS, FEED_COLS),
        branch_grad(slice(HEAD_COLS, None)),
        small[:, 2],
    )


def solution(mesh):
    small = mesh.shape["ctx"] == SIDE and mesh.shape["fsdp"] == SIDE and mesh.shape["seq"] == 2
    on_device = on_device_split if small else on_device_gathered
    return jax.shard_map(
        on_device,
        mesh=mesh,
        in_specs=(
            P(("seq", "fsdp"), "ctx", None),
            P(("seq", "fsdp"), None),
            P(("seq", "fsdp"), "ctx"),
            P(None, ("ctx", "fsdp")),
            P(None, ("ctx", "fsdp")),
            P(None, ("ctx", "fsdp"), None),
            P(None, ("ctx", "fsdp")),
            P(None, ("ctx", "fsdp"), None),
            P(None, ("ctx", "fsdp")),
            P(None, ("ctx", "fsdp"), None),
            P(None, ("ctx", "fsdp")),
            P(None, ("ctx", "fsdp"), None),
            P(None, ("ctx", "fsdp")),
            P(("seq", "fsdp"), "ctx", None),
        ),
        out_specs=(
            P(("seq", "fsdp"), "ctx", None),
            P(("seq", "fsdp"), "ctx", None),
            P(None, ("ctx", "fsdp")),
            P(None, ("ctx", "fsdp")),
            P(None, ("ctx", "fsdp"), None),
            P(None, ("ctx", "fsdp")),
            P(None, ("ctx", "fsdp"), None),
            P(None, ("ctx", "fsdp")),
            P(None, ("ctx", "fsdp"), None),
            P(None, ("ctx", "fsdp")),
            P(None, ("ctx", "fsdp"), None),
            P(None, ("ctx", "fsdp")),
        ),
        check_vma=False,
    )
```

```python
import functools
import math

import jax
import jax.numpy as jnp
import numpy as np
from jax import lax
from jax.experimental import pallas as pl
from jax.experimental.pallas import tpu as pltpu
from jax.sharding import PartitionSpec as P

D = 2048
HEADS = 32
HEAD_DIM = 64
ROT = 32
FF = 8192
LAYERS = 2


EPS = 1e-05
NEG = -1e30


def place_tokens(token_index, lengths):
    bounds = jnp.cumsum(lengths)
    starts = bounds - lengths
    segment = jnp.sum((token_index[:, None] >= bounds[None, :]).astype(jnp.int32), axis=1)
    chosen = segment[:, None] == jnp.arange(lengths.shape[0], dtype=jnp.int32)[None, :]
    position = token_index - jnp.sum(jnp.where(chosen, starts[None, :], 0), axis=1)
    return (segment, position)


def angles(position):
    indices = jnp.arange(0, ROT, 2, dtype=jnp.float32) / ROT
    inverse = 1.0 / 10000.0**indices
    turned = position.astype(jnp.float32)[:, None] * inverse[None, :]
    turned = jnp.concatenate([turned, turned], axis=1)
    return (jnp.cos(turned), jnp.sin(turned))


def rotate(values, cosine, sine):
    rotary = values[..., :ROT]
    middle = ROT // 2
    turned = jnp.concatenate([-rotary[..., middle:], rotary[..., :middle]], axis=-1)
    mixed = rotary * cosine[:, None, :] + turned * sine[:, None, :]
    return jnp.concatenate([mixed, values[..., ROT:]], axis=-1)


def normalize(hidden, gain_row, shift_row):
    average = jnp.mean(hidden, axis=1, keepdims=True)
    centred = hidden - average
    spread = jnp.mean(centred * centred, axis=1, keepdims=True)
    return centred * lax.rsqrt(spread + EPS) * gain_row + shift_row


def block_scores(queries, travelling, start, query_index, query_segment, lengths):
    key_flat, value_flat, key_keep = travelling
    count = key_flat.shape[0]
    key_index = start + jnp.arange(count, dtype=jnp.int32)
    key_segment = place_tokens(key_index, lengths)[0]
    allowed = (
        (query_segment[:, None] == key_segment[None, :])
        & (key_index[None, :] <= query_index[:, None])
        & ((key_keep[None, :] > 0) | (key_index[None, :] == query_index[:, None]))
    )
    key_rows = key_flat.reshape(count, HEADS, HEAD_DIM)
    value_rows = value_flat.reshape(count, HEADS, HEAD_DIM)
    scores = jnp.einsum("qhd,khd->hqk", queries, key_rows, preferred_element_type=jnp.float32) * (
        1.0 / math.sqrt(HEAD_DIM)
    )
    return (scores, allowed, key_rows, value_rows)


def attend(running, travelling, start, queries, query_index, query_segment, lengths):
    maxima, totals, weighted = running
    scores, allowed, key_rows, value_rows = block_scores(
        queries, travelling, start, query_index, query_segment, lengths
    )
    masked = jnp.where(allowed[None], scores, NEG)
    new_max = jnp.maximum(maxima, jnp.max(masked, axis=2))
    probs = jnp.where(allowed[None], jnp.exp(masked - new_max[:, :, None]), 0.0)
    totals = jnp.sum(probs, axis=2)
    weighted = jnp.einsum(
        "hqk,khd->hqd", probs.astype(jnp.bfloat16), value_rows, preferred_element_type=jnp.float32
    )
    return (new_max, totals, weighted)


def attend_back(
    travelling, start, queries, maxima, grad_numer, drift, query_index, query_segment, lengths
):
    scores, allowed, key_rows, value_rows = block_scores(
        queries, travelling, start, query_index, query_segment, lengths
    )
    count = key_rows.shape[0]
    scale = 1.0 / math.sqrt(HEAD_DIM)
    probs = jnp.where(allowed[None], jnp.exp(scores - maxima[:, :, None]), 0.0)
    grad_probs = jnp.einsum(
        "hqd,khd->hqk", grad_numer, value_rows, preferred_element_type=jnp.float32
    )
    grad_scores = (probs * (grad_probs - drift[:, :, None])).astype(jnp.bfloat16)
    grad_query = (
        jnp.einsum("hqk,khd->qhd", grad_scores, key_rows, preferred_element_type=jnp.float32)
        * scale
    )
    grad_key = (
        jnp.einsum("hqk,qhd->khd", grad_scores, queries, preferred_element_type=jnp.float32) * scale
    )
    grad_value = jnp.einsum(
        "hqk,hqd->khd", probs.astype(jnp.bfloat16), grad_numer, preferred_element_type=jnp.float32
    )
    return (
        grad_query,
        grad_key.reshape(count, HEADS * HEAD_DIM),
        grad_value.reshape(count, HEADS * HEAD_DIM),
    )


def attention_forward(queries, key_flat, value_flat, key_keep, query_index, query_segment, lengths):
    row_count = key_flat.shape[0]
    initial = (
        jnp.full((HEADS, row_count), NEG, jnp.float32),
        jnp.zeros((HEADS, row_count), jnp.float32),
        jnp.zeros((HEADS, row_count, HEAD_DIM), jnp.float32),
    )
    return attend(
        initial,
        (
            lax.all_gather(key_flat, "ctx", axis=0, tiled=True),
            lax.all_gather(value_flat, "ctx", axis=0, tiled=True),
            lax.all_gather(key_keep, "ctx", axis=0, tiled=True),
        ),
        jnp.int32(0),
        queries,
        query_index,
        query_segment,
        lengths,
    )


def attention_backward(
    queries,
    key_flat,
    value_flat,
    key_keep,
    maxima,
    grad_numer,
    drift,
    query_index,
    query_segment,
    lengths,
):
    whole = (
        lax.all_gather(key_flat, "ctx", axis=0, tiled=True),
        lax.all_gather(value_flat, "ctx", axis=0, tiled=True),
        lax.all_gather(key_keep, "ctx", axis=0, tiled=True),
    )
    grad_query, every_key, every_value = attend_back(
        whole, 0, queries, maxima, grad_numer, drift, query_index, query_segment, lengths
    )
    grad_key, grad_value = (
        lax.psum_scatter(
            every_key.astype(jnp.bfloat16), "ctx", scatter_dimension=0, tiled=True
        ).astype(jnp.float32),
        lax.psum_scatter(
            every_value.astype(jnp.bfloat16), "ctx", scatter_dimension=0, tiled=True
        ).astype(jnp.float32),
    )
    return (grad_query, grad_key, grad_value)


def layer_forward(hidden, weights, cosine, sine, key_keep, query_index, query_segment, lengths):
    (
        norm_gain,
        norm_shift,
        joint_weight,
        joint_bias,
        output_weight,
        output_bias,
        upper_weight,
        upper_bias,
        lower_weight,
        lower_bias,
    ) = weights
    row_count = hidden.shape[0]
    width = HEADS * HEAD_DIM
    normed = normalize(
        hidden, norm_gain.astype(jnp.float32), norm_shift.astype(jnp.float32)
    ).astype(jnp.bfloat16)
    joint = jnp.dot(normed, joint_weight, preferred_element_type=jnp.float32) + joint_bias.astype(
        jnp.float32
    )
    queries = rotate(joint[:, :width].reshape(row_count, HEADS, HEAD_DIM), cosine, sine).astype(
        jnp.bfloat16
    )
    key_flat = (
        rotate(joint[:, width : 2 * width].reshape(row_count, HEADS, HEAD_DIM), cosine, sine)
        .astype(jnp.bfloat16)
        .reshape(row_count, width)
    )
    value_flat = joint[:, 2 * width :].astype(jnp.bfloat16)
    maxima, totals, weighted = attention_forward(
        queries, key_flat, value_flat, key_keep, query_index, query_segment, lengths
    )
    mixed = (weighted / totals[:, :, None]).transpose(1, 0, 2).reshape(row_count, width)
    attention_out = jnp.dot(
        mixed.astype(jnp.bfloat16), output_weight, preferred_element_type=jnp.float32
    ) + output_bias.astype(jnp.float32)
    inner = jnp.dot(normed, upper_weight, preferred_element_type=jnp.float32) + upper_bias.astype(
        jnp.float32
    )
    activated = jax.nn.gelu(inner, approximate=True).astype(jnp.bfloat16)
    feed_out = jnp.dot(
        activated, lower_weight, preferred_element_type=jnp.float32
    ) + lower_bias.astype(jnp.float32)
    saved = (hidden, normed, queries, key_flat, value_flat, maxima, totals, mixed, inner, activated)
    return (hidden + (attention_out + feed_out), saved)


def layer_backward(
    grad_out, saved, weights, cosine, sine, key_keep, query_index, query_segment, lengths
):
    hidden, normed, queries, key_flat, value_flat, maxima, totals, mixed, inner, activated = saved
    (
        norm_gain,
        norm_shift,
        joint_weight,
        joint_bias,
        output_weight,
        output_bias,
        upper_weight,
        upper_bias,
        lower_weight,
        lower_bias,
    ) = weights
    row_count = hidden.shape[0]
    width = HEADS * HEAD_DIM
    ratio = FF // D
    grad_branch = grad_out.astype(jnp.bfloat16)
    mixed_low = mixed.astype(jnp.bfloat16)
    branch_bias = jnp.sum(grad_branch, axis=0, dtype=jnp.float32)
    grad_activated = jnp.einsum(
        "td,fd->tf", grad_branch, lower_weight, preferred_element_type=jnp.float32
    )
    gelu_pull = jax.vjp(functools.partial(jax.nn.gelu, approximate=True), inner)[1]
    grad_inner = gelu_pull(grad_activated)[0].astype(jnp.bfloat16)
    upper_bias_grad = jnp.sum(grad_inner, axis=0, dtype=jnp.float32)
    grad_normed = jnp.einsum(
        "tf,df->td", grad_inner, upper_weight, preferred_element_type=jnp.float32
    )
    upper_bias_rows = upper_bias_grad.reshape(D, ratio)
    normed_cols = normed
    upper_part = jnp.einsum(
        "tc,tf->cf", normed_cols, grad_inner, preferred_element_type=jnp.float32
    )
    lower_part = jnp.einsum(
        "tc,td->cd", activated, grad_branch, preferred_element_type=jnp.float32
    ).reshape(lax.axis_size(("ctx", "fsdp")) * (D // lax.axis_size(("ctx", "fsdp"))), ratio * width)
    bias_part = upper_bias_rows
    branch_part = branch_bias[:, None]
    feed_share = lax.psum_scatter(
        jnp.concatenate([upper_part, lower_part, bias_part, branch_part], axis=1),
        ("ctx", "fsdp"),
        scatter_dimension=0,
        tiled=True,
    )
    share_rows = feed_share.shape[0]
    upper_share = feed_share[:, :FF]
    lower_share = feed_share[:, FF : FF + ratio * width].reshape(share_rows * ratio, width)
    upper_bias_share = feed_share[:, FF + ratio * width : FF + ratio * width + ratio].reshape(
        share_rows * ratio
    )
    branch_share = feed_share[:, FF + ratio * width + ratio]
    feed_parts = (upper_share, upper_bias_share, lower_share, branch_share)
    output_share = None
    grad_mixed = jnp.einsum(
        "te,de->td", grad_branch, output_weight, preferred_element_type=jnp.float32
    )
    head_mixed = mixed.reshape(row_count, HEADS, HEAD_DIM).transpose(1, 0, 2)
    head_grad = grad_mixed.reshape(row_count, HEADS, HEAD_DIM).transpose(1, 0, 2)
    drift = jnp.sum(head_grad * head_mixed, axis=2) / totals
    grad_numer = (head_grad / totals[:, :, None]).astype(jnp.bfloat16)
    grad_query, grad_key, grad_value = attention_backward(
        queries,
        key_flat,
        value_flat,
        key_keep,
        maxima,
        grad_numer,
        drift,
        query_index,
        query_segment,
        lengths,
    )
    grad_query = rotate(grad_query, cosine, -sine).reshape(row_count, width)
    grad_key = rotate(grad_key.reshape(row_count, HEADS, HEAD_DIM), cosine, -sine).reshape(
        row_count, width
    )
    grad_joint = jnp.concatenate([grad_query, grad_key, grad_value], axis=1).astype(jnp.bfloat16)
    joint_bias_grad = jnp.sum(grad_joint, axis=0, dtype=jnp.float32)
    grad_normed = grad_normed + jnp.einsum(
        "te,de->td", grad_joint, joint_weight, preferred_element_type=jnp.float32
    )
    norm_pull = jax.vjp(
        normalize, hidden, norm_gain.astype(jnp.float32), norm_shift.astype(jnp.float32)
    )[1]
    grad_hidden, gain_grad, shift_grad = norm_pull(grad_normed)
    joint_bias_rows = joint_bias_grad.reshape(D, 3)
    normed_cols = normed
    joint_part = jnp.einsum(
        "tc,te->ce", normed_cols, grad_joint, preferred_element_type=jnp.float32
    )
    output_part = jnp.einsum(
        "tc,te->ce", mixed_low, grad_branch, preferred_element_type=jnp.float32
    )
    bias_part = joint_bias_rows
    gain_part = gain_grad[:, None]
    shift_part = shift_grad[:, None]
    attn_share = lax.psum_scatter(
        jnp.concatenate([joint_part, output_part, bias_part, gain_part, shift_part], axis=1),
        ("ctx", "fsdp"),
        scatter_dimension=0,
        tiled=True,
    )
    share_rows = attn_share.shape[0]
    joint_share = attn_share[:, : 3 * width]
    output_share = attn_share[:, 3 * width : 4 * width]
    joint_bias_share = attn_share[:, 4 * width : 4 * width + 3].reshape(share_rows * 3)
    gain_share = attn_share[:, 4 * width + 3]
    shift_share = attn_share[:, 4 * width + 4]
    attention_parts = (gain_share, shift_share, joint_share, joint_bias_share, output_share)
    return (grad_out + grad_hidden, attention_parts, feed_parts)


def on_device_gathered(
    tokens,
    doc_lengths,
    keep_mask,
    ln_gain,
    ln_bias,
    qkv_weight,
    qkv_bias,
    out_weight,
    out_bias,
    up_weight,
    up_bias,
    down_weight,
    down_bias,
    cotangent,
):
    row_count = tokens.shape[1]
    position = lax.axis_index("ctx")
    query_index = position * row_count + jnp.arange(row_count, dtype=jnp.int32)
    lengths = doc_lengths[0]
    query_segment, query_position = place_tokens(query_index, lengths)
    cosine, sine = angles(query_position)
    key_keep = keep_mask[0].astype(jnp.bfloat16)
    shards = (
        ln_gain,
        ln_bias,
        qkv_weight,
        qkv_bias,
        out_weight,
        out_bias,
        up_weight,
        up_bias,
        down_weight,
        down_bias,
    )

    def fetch(layer_index):
        return (
            lax.all_gather(shards[0][layer_index], ("ctx", "fsdp"), axis=0, tiled=True),
            lax.all_gather(shards[1][layer_index], ("ctx", "fsdp"), axis=0, tiled=True),
            lax.all_gather(shards[2][layer_index], ("ctx", "fsdp"), axis=0, tiled=True),
            lax.all_gather(shards[3][layer_index], ("ctx", "fsdp"), axis=0, tiled=True),
            lax.all_gather(shards[4][layer_index], ("ctx", "fsdp"), axis=0, tiled=True),
            lax.all_gather(shards[5][layer_index], ("ctx", "fsdp"), axis=0, tiled=True),
            lax.all_gather(shards[6][layer_index], ("ctx", "fsdp"), axis=0, tiled=True),
            lax.all_gather(shards[7][layer_index], ("ctx", "fsdp"), axis=0, tiled=True),
            lax.all_gather(shards[8][layer_index], ("ctx", "fsdp"), axis=0, tiled=True),
            lax.all_gather(shards[9][layer_index], ("ctx", "fsdp"), axis=0, tiled=True),
        )

    hidden = tokens[0].astype(jnp.float32)
    saved_layers = []
    weights = None
    for layer_index in range(LAYERS):
        weights = fetch(layer_index)
        hidden, saved = layer_forward(
            hidden, weights, cosine, sine, key_keep, query_index, query_segment, lengths
        )
        saved_layers.append(saved)
    result = hidden.astype(jnp.bfloat16)[None]
    grad_hidden = cotangent[0].astype(jnp.float32) * keep_mask[0].astype(jnp.float32)[:, None]
    attention_list = [None] * LAYERS
    feed_list = [None] * LAYERS
    for layer_index in reversed(range(LAYERS)):
        weights = weights if layer_index == LAYERS - 1 else fetch(layer_index)
        grad_hidden, attention_parts, feed_parts = layer_backward(
            grad_hidden,
            saved_layers[layer_index],
            weights,
            cosine,
            sine,
            key_keep,
            query_index,
            query_segment,
            lengths,
        )
        attention_list[layer_index] = attention_parts
        feed_list[layer_index] = feed_parts
    gain_stack = jnp.stack([attention_list[layer_index][0] for layer_index in range(LAYERS)])
    shift_stack = jnp.stack([attention_list[layer_index][1] for layer_index in range(LAYERS)])
    joint_stack = jnp.stack([attention_list[layer_index][2] for layer_index in range(LAYERS)])
    joint_bias_stack = jnp.stack([attention_list[layer_index][3] for layer_index in range(LAYERS)])
    output_stack = jnp.stack([attention_list[layer_index][4] for layer_index in range(LAYERS)])
    upper_stack = jnp.stack([feed_list[layer_index][0] for layer_index in range(LAYERS)])
    upper_bias_stack = jnp.stack([feed_list[layer_index][1] for layer_index in range(LAYERS)])
    lower_stack = jnp.stack([feed_list[layer_index][2] for layer_index in range(LAYERS)])
    branch_stack = jnp.stack([feed_list[layer_index][3] for layer_index in range(LAYERS)])
    summed = (
        lax.psum(gain_stack.astype(jnp.bfloat16), "seq").astype(jnp.float32),
        lax.psum(shift_stack.astype(jnp.bfloat16), "seq").astype(jnp.float32),
        lax.psum(joint_stack.astype(jnp.bfloat16), "seq").astype(jnp.float32),
        lax.psum(joint_bias_stack.astype(jnp.bfloat16), "seq").astype(jnp.float32),
        lax.psum(output_stack.astype(jnp.bfloat16), "seq").astype(jnp.float32),
        lax.psum(upper_stack.astype(jnp.bfloat16), "seq").astype(jnp.float32),
        lax.psum(upper_bias_stack.astype(jnp.bfloat16), "seq").astype(jnp.float32),
        lax.psum(lower_stack.astype(jnp.bfloat16), "seq").astype(jnp.float32),
        lax.psum(branch_stack.astype(jnp.bfloat16), "seq").astype(jnp.float32),
    )
    return (
        result,
        grad_hidden[None],
        summed[0],
        summed[1],
        summed[2],
        summed[3],
        summed[4],
        summed[8],
        summed[5],
        summed[6],
        summed[7],
        summed[8],
    )


SIDE = 4
GROUP = SIDE * SIDE
OWN = HEADS // GROUP
HEAD_COLS = OWN * HEAD_DIM
JOINT_COLS = 3 * HEAD_COLS
FEED_COLS = FF // GROUP
COLS = JOINT_COLS + FEED_COLS
BACK_COLS = HEAD_COLS + FEED_COLS
SHARE = D // GROUP
VMEM = pl.BlockSpec(memory_space=pltpu.VMEM)
HBM = pl.BlockSpec(memory_space=pl.ANY)
MESH = pl.DeviceIdType.MESH
ROOM = 60 * 2**20


def dot(left, right, left_dim=1, right_dim=0):
    return lax.dot_general(
        left, right, (((left_dim,), (right_dim,)), ((), ())), preferred_element_type=jnp.float32
    )


def digit(entries, index):
    words = [
        sum(entry << (2 * place) for place, entry in enumerate(entries[start : start + 8]))
        for start in range(0, len(entries), 8)
    ]
    word = jnp.int32(words[0])
    for number in range(1, len(words)):
        word = jnp.where(index >= 8 * number, jnp.int32(words[number]), word)
    return lax.rem(lax.shift_right_logical(word, 2 * lax.rem(index, 8)), 4)


def nibble(entries, index):
    word = jnp.int32(0)
    for start in range(0, len(entries), 7):
        packed = sum(entry << (4 * place) for place, entry in enumerate(entries[start : start + 7]))
        word = jnp.where(index >= start, jnp.int32(packed), word)
    return lax.rem(lax.shift_right_logical(word, 4 * lax.rem(index, 7)), 16)


def digit_of_row(table, row, index):
    value = digit(table[0], index)
    for number in range(1, len(table)):
        value = jnp.where(row == number, digit(table[number], index), value)
    return value


NEAR = ((0, 1, 2, 3), (1, 0, 2, 3), (2, 3, 1, 0), (3, 2, 1, 0))
FAR = ((3, 2, 1, 0), (3, 0, 2, 1), (0, 3, 1, 2), (0, 1, 2, 3))


def neighbours():
    ctx, place = lax.axis_index("ctx"), lax.axis_index("fsdp")
    twin = ctx + 1 - 2 * lax.rem(ctx, 2)
    across = lax.rem(ctx + 2, 4)
    return ctx, place, twin, across, lax.rem(twin + 2, 4)


def greet_neighbours(cross=False):
    ctx, place, twin, across, _ = neighbours()
    barrier = pltpu.get_barrier_semaphore()
    pl.semaphore_signal(barrier, inc=1, device_id={"ctx": twin}, device_id_type=MESH)
    pl.semaphore_signal(barrier, inc=1, device_id={"ctx": across}, device_id_type=MESH)

    @pl.when(place > 0)
    def _():
        pl.semaphore_signal(barrier, inc=1, device_id={"fsdp": place - 1}, device_id_type=MESH)

    @pl.when(place < SIDE - 1)
    def _():
        pl.semaphore_signal(barrier, inc=1, device_id={"fsdp": place + 1}, device_id_type=MESH)

    if cross:
        pl.semaphore_signal(
            barrier, inc=1, device_id={"seq": 1 - lax.axis_index("seq")}, device_id_type=MESH
        )
    inner = jnp.int32(3 if cross else 2) + jnp.where(place > 0, 1, 0) + jnp.where(place < SIDE - 1, 1, 0)
    pl.semaphore_wait(barrier, inner)


def greet_plane(steps, cross=True):
    ctx, place = lax.axis_index("ctx"), lax.axis_index("fsdp")
    me = ctx * SIDE + place
    barrier = pltpu.get_barrier_semaphore()
    for step in range(1, steps):
        peer = lax.rem(me + step, GROUP)
        pl.semaphore_signal(
            barrier,
            inc=1,
            device_id={"ctx": peer // SIDE, "fsdp": lax.rem(peer, SIDE)},
            device_id_type=MESH,
        )
    if cross:
        pl.semaphore_signal(
            barrier, inc=1, device_id={"seq": 1 - lax.axis_index("seq")}, device_id_type=MESH
        )
    pl.semaphore_wait(barrier, steps if cross else steps - 1)


def to_peer(source, target, send, recv, peer):
    return pltpu.make_async_remote_copy(
        src_ref=source,
        dst_ref=target,
        send_sem=send,
        recv_sem=recv,
        device_id={"ctx": peer // SIDE, "fsdp": lax.rem(peer, SIDE)},
        device_id_type=MESH,
    )


def to_axis(source, target, send, recv, axis, index):
    return pltpu.make_async_remote_copy(
        src_ref=source,
        dst_ref=target,
        send_sem=send,
        recv_sem=recv,
        device_id={axis: index},
        device_id_type=MESH,
    )


PARTS = ((0, 112), (112, 96), (208, 48))
LAST = len(PARTS) - 1
GATHER_KIND = (
    (0, 0, 0, 0, 0, 1, 0, 0, 1, 0, 2, 0, 1, 1, 1, 2, 0, 0, 1, 0, 1, 3, 2, 1, 0, 3, 1, 1, 1, 1, 0, 3, 0, 0, 1, 1, 1, 1, 2, 3),
    (0, 0, 0, 1, 0, 0, 0, 0, 0, 0, 0, 0, 1, 0, 2, 1, 2, 1, 0, 1, 1, 2, 0, 3, 1, 1, 0, 1, 1, 1, 3, 1, 1, 0, 1, 3, 1, 1, 2, 3),
)
GATHER_STEP = (
    (0, 0, 1, 0, 0, 0, 1, 1, 0, 1, 0, 2, 0, 0, 1, 1, 2, 2, 1, 2, 1, 0, 2, 1, 3, 1, 2, 2, 2, 2, 3, 2, 3, 3, 3, 3, 3, 3, 3, 3),
    (0, 0, 0, 0, 2, 2, 1, 0, 1, 2, 1, 1, 0, 2, 0, 0, 2, 0, 3, 2, 2, 1, 3, 0, 2, 1, 3, 1, 2, 1, 2, 3, 1, 3, 3, 1, 3, 3, 3, 3),
)
GATHER_PART = (
    (1, 0, 1, 2, 3, 1, 2, 0, 0, 3, 3, 2, 2, 3, 0, 3, 1, 0, 1, 3, 2, 3, 3, 3, 0, 3, 1, 2, 0, 3, 1, 3, 2, 3, 1, 0, 2, 3, 3, 3),
    (1, 0, 2, 0, 2, 0, 2, 3, 1, 1, 0, 3, 2, 3, 3, 1, 3, 3, 0, 0, 2, 3, 1, 3, 1, 1, 2, 2, 3, 0, 3, 2, 3, 3, 0, 3, 1, 3, 3, 3),
)
FIRST_KIND = (
    (0, 0, 0, 0, 0, 0, 0, 0, 0, 1, 3, 2, 3, 2, 0, 1, 3, 1, 0, 1, 0, 0, 0, 1, 1, 0, 0, 3, 0, 0, 2, 2, 0, 1, 0, 0, 1, 1, 1, 0, 0, 1, 1, 2, 2, 3, 3, 0, 1, 0, 0, 0, 0, 1, 1, 3, 2, 1, 0, 1, 1, 2, 0, 2, 2, 0, 1, 3, 0, 1, 0, 0, 3, 3, 2, 1, 1, 1, 2, 1, 3, 3),
    (0, 0, 0, 0, 0, 2, 0, 0, 0, 1, 0, 0, 2, 1, 3, 1, 1, 0, 2, 0, 3, 3, 0, 0, 0, 0, 0, 0, 1, 1, 0, 1, 0, 0, 2, 3, 1, 2, 0, 1, 0, 0, 0, 1, 0, 1, 0, 2, 0, 1, 1, 1, 3, 2, 2, 3, 0, 3, 1, 0, 0, 0, 1, 2, 0, 0, 1, 1, 1, 1, 1, 3, 2, 3, 1, 2, 1, 1, 3, 3, 2, 3),
)
FIRST_STEP = (
    (0, 0, 1, 2, 3, 3, 0, 0, 0, 3, 0, 0, 2, 1, 0, 0, 1, 1, 0, 0, 0, 1, 1, 0, 0, 2, 2, 3, 1, 1, 2, 3, 3, 2, 1, 2, 0, 1, 1, 2, 1, 1, 1, 0, 1, 0, 1, 0, 1, 2, 1, 0, 2, 2, 0, 0, 1, 2, 3, 2, 2, 2, 2, 2, 0, 3, 2, 1, 3, 3, 3, 3, 2, 2, 3, 3, 3, 3, 3, 3, 3, 3),
    (0, 1, 2, 0, 0, 0, 2, 1, 3, 0, 0, 0, 3, 3, 1, 2, 0, 3, 1, 0, 2, 0, 0, 1, 2, 0, 2, 1, 1, 0, 1, 0, 3, 2, 0, 3, 1, 2, 1, 0, 2, 0, 1, 0, 3, 1, 2, 0, 0, 1, 1, 2, 0, 1, 1, 1, 3, 1, 2, 3, 2, 1, 2, 2, 3, 3, 2, 3, 1, 2, 3, 0, 2, 2, 3, 3, 3, 3, 3, 3, 3, 2),
)
FIRST_WHAT = (
    (5, 4, 4, 4, 9, 4, 0, 9, 2, 9, 9, 9, 9, 9, 1, 2, 9, 9, 6, 0, 3, 1, 6, 1, 3, 9, 6, 9, 0, 9, 9, 9, 6, 9, 2, 1, 9, 1, 2, 2, 3, 0, 3, 3, 3, 3, 3, 7, 8, 0, 8, 8, 3, 1, 8, 8, 8, 0, 0, 2, 3, 3, 8, 8, 8, 1, 8, 8, 2, 0, 3, 8, 3, 8, 3, 2, 1, 3, 8, 8, 3, 8),
    (4, 4, 4, 5, 0, 9, 9, 9, 9, 0, 9, 1, 9, 9, 9, 9, 9, 4, 9, 6, 9, 9, 2, 6, 1, 3, 6, 0, 9, 2, 1, 1, 6, 2, 3, 9, 0, 9, 2, 3, 0, 7, 3, 8, 0, 2, 3, 8, 8, 1, 3, 2, 3, 3, 8, 3, 1, 8, 0, 2, 8, 8, 1, 3, 3, 8, 3, 2, 8, 8, 1, 8, 8, 3, 0, 3, 3, 8, 3, 8, 8, 8),
)
OPS = len(GATHER_KIND[0])
WORKS = tuple(
    tuple(
        number for number in range(OPS) if parts[number] == 3
    )
    for parts in GATHER_PART
)


def by_place(tables, index):
    place = lax.axis_index("fsdp")
    at_end = (place == 0) | (place == SIDE - 1)
    return jnp.where(at_end, digit(tables[0], index), digit(tables[1], index))


def gather_slot(kind, step):
    ctx, place, twin, across, twin_across = neighbours()
    line = digit_of_row(NEAR, place, step)
    owner = jnp.where(
        kind == 0, ctx, jnp.where(kind == 1, across, jnp.where(kind == 2, twin, twin_across))
    )
    return line, owner * SIDE + line


def work_slot(number):
    kind = by_place(
        tuple(tuple(row[at] for at in places) for row, places in zip(GATHER_KIND, WORKS)), number
    )
    step = by_place(
        tuple(tuple(row[at] for at in places) for row, places in zip(GATHER_STEP, WORKS)), number
    )
    return gather_slot(kind, step)[1]


def gather_blocks(
    land, every, up, down, side, core, arrived, core_arrived, kept, work, tables=None, more=()
):
    ctx, place, twin, across, _ = neighbours()
    kinds, steps, parts = tables or (GATHER_KIND, GATHER_STEP, GATHER_PART)
    at_end = (place == 0) | (place == SIDE - 1)

    def copies(kind, line, slot, part):
        start, size = PARTS[part]
        block = land.at[slot, pl.ds(start, size)]
        row, met = kind * SIDE + line, arrived.at[slot, part]
        return (
            lambda: to_axis(block, block, up.at[row, part], met, "fsdp", place + 1),
            lambda: to_axis(block, block, down.at[row, part], met, "fsdp", place - 1),
            lambda: to_axis(block, block, side.at[line, part], met, "ctx", across),
        )

    def routes(kind, line, part):
        goes_up = (line <= place) & (place < SIDE - 1)
        goes_down = (line >= place) & (place > 0)
        if part == LAST:
            return goes_up, goes_down, (kind == 0) & (line == place)
        return goes_up & (kind == 0), goes_down & (kind == 0), kind == 0

    def core_copy(kind, line, slot):
        block = land.at[slot]
        return to_axis(
            block, block, core.at[kind * SIDE + line], core_arrived.at[slot], "ctx", twin
        )

    def step_op(number, counts):
        worked, made = counts
        kind, step = by_place(kinds, number), by_place(steps, number)
        part = jnp.where(at_end, nibble(parts[0], number), nibble(parts[1], number))
        line, slot = gather_slot(kind, step)
        for which in range(len(PARTS)):

            @pl.when(part == which)
            def _(which=which):
                @pl.when((kind == 1) | (line != place))
                def _():
                    copies(kind, line, slot, which)[2]().wait_recv()

                for copy, goes in zip(
                    copies(kind, line, slot, which), routes(kind, line, which)
                ):

                    @pl.when(goes)
                    def _(copy=copy):
                        copy().start()

        @pl.when(part == 3)
        def _():
            @pl.when(kind <= 1)
            def _():
                core_copy(kind, line, slot).start()

            @pl.when(kind >= 2)
            def _():
                core_copy(kind - 2, line, slot).wait_recv()

            if every is not None:
                pltpu.make_async_copy(land.at[slot], every.at[slot], kept.at[slot]).start()
            work(worked, slot)

        for which, further in enumerate(more):

            @pl.when(part == 4 + which)
            def _(further=further):
                further(step, slot, made)

        return worked + jnp.where(part == 3, 1, 0), made + jnp.where(part == 8, 1, 0)

    lax.fori_loop(0, len(kinds[0]), step_op, (jnp.int32(0), jnp.int32(0)))

    def finish(number, carry):
        kind, line = number // SIDE, lax.rem(number, SIDE)
        slot = jnp.where(kind == 0, ctx, across) * SIDE + line
        for which in range(len(PARTS)):
            for copy, goes in zip(copies(kind, line, slot, which), routes(kind, line, which)):

                @pl.when(goes)
                def _(copy=copy):
                    copy().wait_send()

        core_copy(kind, line, slot).wait_send()
        return carry

    lax.fori_loop(0, 2 * SIDE, finish, 0)

    def finish_kept(slot, carry):
        pltpu.make_async_copy(land.at[slot], every.at[slot], kept.at[slot]).wait()
        return carry

    if every is not None:
        lax.fori_loop(0, GROUP, finish_kept, 0)


def gather_scratch(rows):
    parts = len(PARTS)
    return [
        pltpu.VMEM((GROUP, rows, D), jnp.bfloat16),
        pltpu.SemaphoreType.DMA((2 * SIDE, parts)),
        pltpu.SemaphoreType.DMA((2 * SIDE, parts)),
        pltpu.SemaphoreType.DMA((SIDE, parts)),
        pltpu.SemaphoreType.DMA((2 * SIDE,)),
        pltpu.SemaphoreType.DMA((GROUP, parts)),
        pltpu.SemaphoreType.DMA((GROUP,)),
        pltpu.SemaphoreType.DMA((GROUP,)),
    ]


def spin(values, cosine, sine, sign):
    lane = lax.rem(lax.broadcasted_iota(jnp.int32, values.shape, 1), HEAD_DIM)
    partner = jnp.where(
        lane < ROT // 2,
        -pltpu.roll(values, HEAD_COLS - ROT // 2, 1),
        pltpu.roll(values, ROT // 2, 1),
    )
    return values * cosine + sign * (partner * sine)


STRIP = 32


def each_strip(rows, body, start):
    def step(number, carry):
        return body(pl.ds(pl.multiple_of(number * STRIP, STRIP), STRIP), carry)

    return lax.fori_loop(0, rows // STRIP, step, start)


def column_places(block):
    return [
        (0, pl.multiple_of(part * D + block * HEAD_COLS, HEAD_COLS), part * HEAD_COLS, HEAD_COLS)
        for part in range(3)
    ] + [(1, pl.multiple_of(block * FEED_COLS, FEED_COLS), JOINT_COLS, FEED_COLS)]


PLACES = 4


def plane_swap(swap, sems):
    source, target = swap
    return to_axis(source, target, sems.at[0], sems.at[1], "seq", 1 - lax.axis_index("seq"))


def load_all(pairs, sems):
    copies = [
        pltpu.make_async_copy(source, target, sems.at[number])
        for number, (source, target) in enumerate(pairs)
    ]
    for copy in copies:
        copy.start()
    return copies


def wait_all(copies):
    for copy in copies:
        copy.wait()


def ring_scratch(rows):
    return [
        pltpu.VMEM((2, rows, HEAD_COLS), jnp.bfloat16),
        pltpu.VMEM((2, rows, HEAD_COLS), jnp.bfloat16),
        pltpu.VMEM((2, rows, HEAD_COLS), jnp.bfloat16),
        pltpu.VMEM((2, rows, FEED_COLS), jnp.float32),
        pltpu.VMEM((2, rows, FEED_COLS), jnp.bfloat16),
        pltpu.SemaphoreType.DMA((2, 5)),
    ]


def ring_shapes(rows):
    return [
        jax.ShapeDtypeStruct((GROUP, rows, width), dtype)
        for width, dtype in (
            (HEAD_COLS, jnp.bfloat16),
            (HEAD_COLS, jnp.bfloat16),
            (HEAD_COLS, jnp.bfloat16),
            (FEED_COLS, jnp.float32),
            (FEED_COLS, jnp.bfloat16),
        )
    ]


def ring_product(rings, sems, results, land, columns, bias, cosine, sine):
    query, key, value, inner, active = rings

    def leave(at, slot):
        return [
            pltpu.make_async_copy(ring.at[at], result.at[slot], sems.at[at, which])
            for which, (ring, result) in enumerate(zip(rings, results))
        ]

    def product(number, slot):
        whole = dot(land[slot], columns[...].reshape(D, COLS)) + bias[...]
        one, two = HEAD_COLS, 2 * HEAD_COLS
        at = lax.rem(number, 2)

        @pl.when(number >= 2)
        def _():
            wait_all(leave(at, 0))

        query[at] = spin(whole[:, :one], cosine[slot], sine[slot], 1.0).astype(jnp.bfloat16)
        key[at] = spin(whole[:, one:two], cosine[slot], sine[slot], 1.0).astype(jnp.bfloat16)
        value[at] = whole[:, two:JOINT_COLS].astype(jnp.bfloat16)
        units = whole[:, JOINT_COLS:]
        inner[at] = units
        active[at] = jax.nn.gelu(units, approximate=True).astype(jnp.bfloat16)
        for copy in leave(at, slot):
            copy.start()

    def finish():
        for at in range(2):
            wait_all(leave(at, 0))

    return product, finish


def norm_block(hidden, gain, shift, land, me):
    def strip(part, carry):
        values = hidden[part].astype(jnp.float32)
        centred = values - jnp.mean(values, axis=1, keepdims=True)
        spread = jnp.mean(centred * centred, axis=1, keepdims=True)
        normed = centred * lax.rsqrt(spread + EPS) * gain[...] + shift[...]
        land[me, part] = normed.astype(jnp.bfloat16)
        return carry

    each_strip(hidden.shape[0], strip, 0)


def forward_gather(hidden, gain, shift, bias, tables, halves, layer):
    rows = hidden.shape[0]
    half = SHARE // 2

    def kernel(hidden, gain, shift, bias, turn_a, turn_b, own_half, other_half, *refs):
        every, columns_out, results, refs = refs[0], refs[1], refs[2:7], refs[7:]
        cosine, sine, columns, load_sem, saved = refs[:5]
        rings, ring_sem, refs = refs[5:10], refs[10], refs[11:]
        land, sems = refs[0], refs[1:]
        ctx, place, seq = lax.axis_index("ctx"), lax.axis_index("fsdp"), lax.axis_index("seq")
        part_rows = pl.ds(pl.multiple_of(seq * half, half), half)
        other_rows = pl.ds(pl.multiple_of((1 - seq) * half, half), half)
        loads = load_all(
            (
                (own_half, columns.at[:, part_rows]),
                (other_half, columns.at[:, other_rows]),
                (turn_a, cosine),
                (turn_b, sine),
            ),
            load_sem,
        )
        greet_neighbours()
        norm_block(hidden, gain, shift, land, ctx * SIDE + place)
        save = pltpu.make_async_copy(columns, columns_out, saved)
        product, finish = ring_product(rings, ring_sem, results, land, columns, bias, cosine, sine)

        def work(number, slot):
            @pl.when(number == 0)
            def _():
                wait_all(loads)
                save.start()

            product(number, slot)

        gather_blocks(land, every, *sems, work)
        save.wait()
        finish()

    return pl.pallas_call(
        kernel,
        out_shape=[
            jax.ShapeDtypeStruct((GROUP, rows, D), jnp.bfloat16),
            jax.ShapeDtypeStruct((GROUP, SHARE, COLS), jnp.bfloat16),
        ]
        + ring_shapes(rows),
        in_specs=[VMEM] * 4 + [HBM] * 4,
        out_specs=[HBM] * 7,
        scratch_shapes=[pltpu.VMEM((GROUP, rows, HEAD_COLS), jnp.float32)] * 2
        + [
            pltpu.VMEM((GROUP, SHARE, COLS), jnp.bfloat16),
            pltpu.SemaphoreType.DMA((4,)),
            pltpu.SemaphoreType.DMA,
        ]
        + ring_scratch(rows)
        + gather_scratch(rows),
        compiler_params=pltpu.CompilerParams(
            collective_id=30 + layer, has_side_effects=True, vmem_limit_bytes=ROOM
        ),
    )(hidden, gain, shift, bias, *tables, *halves)


GAIN_ROW, SHIFT_ROW, JOINT_BIAS_ROW, OUT_BIAS_ROW, DOWN_BIAS_ROW, LAYER_ROWS = 0, 1, 2, 5, 6, 7
BEGIN_ROW = LAYERS * LAYER_ROWS


def first_gather(hidden, packed, up_bias, frequency, qkv_weight, up_weight):
    rows = hidden.shape[0]
    half = SHARE // 2

    def kernel(hidden, packed, up_bias, frequency, qkv_weight, up_weight, *refs):
        every, columns_out, results, small, cosine, sine = refs[0], refs[1], refs[2:7], *refs[7:10]
        refs = refs[10:]
        columns, plane_send, plane_recv, cross_send, cross_recv, own_sem, saved = refs[:7]
        small_send, small_recv, gain, shift, bias = refs[7:12]
        rings, ring_sem, refs = refs[12:17], refs[17], refs[18:]
        land, sems = refs[0], refs[1:]
        ctx, place, seq = lax.axis_index("ctx"), lax.axis_index("fsdp"), lax.axis_index("seq")
        me = ctx * SIDE + place
        part_rows = pl.ds(pl.multiple_of(seq * half, half), half)
        sources = (qkv_weight, up_weight)
        greet_plane(GROUP)

        def small_copy(step):
            return to_peer(
                packed,
                small.at[me],
                small_send.at[step],
                small_recv.at[me],
                lax.rem(me + step, GROUP),
            )

        def small_begin(step, carry):
            small_copy(step).start()
            return carry

        lax.fori_loop(1, GROUP, small_begin, 0)
        small[me] = packed[...]

        def piece(step, number):
            peer = lax.rem(me + step, GROUP)
            which, start, at, width = column_places(peer)[number]
            return (
                peer,
                sources[which].at[0, part_rows, pl.ds(start, width)],
                columns.at[me, part_rows, pl.ds(at, width)],
            )

        def send_piece(step, number):
            peer, source, target = piece(step, number)
            return to_peer(
                source, target, plane_send.at[step, number], plane_recv.at[me, number], peer
            )

        def own_piece(number):
            _, source, target = piece(0, number)
            return pltpu.make_async_copy(source, target, own_sem.at[number])

        def cross(source):
            block = columns.at[source, part_rows]
            return to_axis(
                block, block, cross_send.at[source], cross_recv.at[source], "seq", 1 - seq
            )

        for number in range(PLACES):
            own_piece(number).start()

        def send_columns(group, slot, made):
            def send(more, carry):
                step = SIDE * group + more

                @pl.when(step > 0)
                def _():
                    for number in range(PLACES):
                        send_piece(step, number).start()

                return carry

            lax.fori_loop(0, SIDE, send, 0)

        def norm_own(group, slot, made):
            def arrive(step, carry):
                source = lax.rem(me + GROUP - step, GROUP)
                to_peer(
                    packed, small.at[source], small_send.at[step], small_recv.at[source], source
                ).wait_recv()
                return carry

            lax.fori_loop(1, GROUP, arrive, 0)

            def whole_row(row):
                return jnp.concatenate(
                    [small[block, row : row + 1] for block in range(GROUP)], axis=1
                )

            gain[...] = whole_row(GAIN_ROW)
            shift[...] = whole_row(SHIFT_ROW)
            for part in range(3):
                at = part * GROUP + me
                bias[:, part * HEAD_COLS : (part + 1) * HEAD_COLS] = small[
                    at // 3, pl.ds(JOINT_BIAS_ROW + lax.rem(at, 3), 1)
                ]
            bias[:, JOINT_COLS:] = up_bias[...]
            norm_block(hidden, gain, shift, land, me)

        def pass_columns(group, slot, made):
            def pass_on(more, carry):
                step = SIDE * group + more
                source = lax.rem(me + GROUP - step, GROUP)

                @pl.when(step == 0)
                def _():
                    for number in range(PLACES):
                        own_piece(number).wait()

                @pl.when(step > 0)
                def _():
                    for number in range(PLACES):
                        _, _, at, width = column_places(0)[number]
                        target = columns.at[source, part_rows, pl.ds(at, width)]
                        to_peer(
                            target,
                            target,
                            plane_send.at[0, number],
                            plane_recv.at[source, number],
                            source,
                        ).wait_recv()

                cross(source).start()
                return carry

            lax.fori_loop(0, SIDE, pass_on, 0)

        save = pltpu.make_async_copy(columns, columns_out, saved)

        def wait_columns(group, slot, made):
            def arrive(source, carry):
                cross(source).wait_recv()
                return carry

            lax.fori_loop(0, GROUP, arrive, 0)
            save.start()

        product, finish = ring_product(rings, ring_sem, results, land, columns, bias, cosine, sine)

        def next_product(group, slot, made):
            product(made, slot)

        def turn_block(group, slot, made):
            begin = jnp.concatenate(
                [small[slot, BEGIN_ROW + part : BEGIN_ROW + part + 1] for part in range(rows // SHARE)],
                axis=1,
            )
            begin = jnp.broadcast_to(begin, (8, rows)).T[:, :1]
            first = (slot // SIDE) * rows
            token = lax.broadcasted_iota(jnp.int32, (rows, 1), 0) + first
            angle = (token.astype(jnp.float32) - begin) * frequency[...]
            cosine[slot] = jnp.cos(angle)
            sine[slot] = jnp.sin(angle)

        gather_blocks(
            land,
            every,
            *sems,
            lambda number, slot: None,
            (FIRST_KIND, FIRST_STEP, FIRST_WHAT),
            (send_columns, norm_own, pass_columns, wait_columns, next_product, turn_block),
        )
        save.wait()
        finish()

        def end(step, carry):
            cross(step).wait_send()

            @pl.when(step > 0)
            def _():
                small_copy(step).wait_send()
                for number in range(PLACES):
                    send_piece(step, number).wait_send()

            return carry

        lax.fori_loop(0, GROUP, end, 0)

    return pl.pallas_call(
        kernel,
        out_shape=[
            jax.ShapeDtypeStruct((GROUP, rows, D), jnp.bfloat16),
            jax.ShapeDtypeStruct((GROUP, SHARE, COLS), jnp.bfloat16),
        ]
        + ring_shapes(rows)
        + [jax.ShapeDtypeStruct((GROUP,) + packed.shape, packed.dtype)]
        + [jax.ShapeDtypeStruct((GROUP, rows, HEAD_COLS), jnp.float32)] * 2,
        in_specs=[VMEM] * 4 + [HBM] * 2,
        out_specs=[HBM] * 7 + [VMEM] * 3,
        scratch_shapes=[
            pltpu.VMEM((GROUP, SHARE, COLS), jnp.bfloat16),
            pltpu.SemaphoreType.DMA((GROUP, PLACES)),
            pltpu.SemaphoreType.DMA((GROUP, PLACES)),
            pltpu.SemaphoreType.DMA((GROUP,)),
            pltpu.SemaphoreType.DMA((GROUP,)),
            pltpu.SemaphoreType.DMA((PLACES,)),
            pltpu.SemaphoreType.DMA,
            pltpu.SemaphoreType.DMA((GROUP,)),
            pltpu.SemaphoreType.DMA((GROUP,)),
            pltpu.VMEM((1, D), jnp.float32),
            pltpu.VMEM((1, D), jnp.float32),
            pltpu.VMEM((1, COLS), jnp.float32),
        ]
        + ring_scratch(rows)
        + gather_scratch(rows),
        compiler_params=pltpu.CompilerParams(
            collective_id=30, has_side_effects=True, vmem_limit_bytes=ROOM
        ),
    )(hidden, packed, up_bias, frequency, qkv_weight, up_weight)


def backward_gather(grad, out_weight, down_weight, inner, mixed, active, layer, swap=()):
    rows = grad.shape[0]

    def kernel(own, out_weight, down_weight, inner, mixed, active, *refs):
        if swap:
            source, grad_mixed, grad_inner, branch, target, swap_sem = refs[:6]
            refs = refs[6:]
        else:
            grad_mixed, grad_inner, branch = refs[:3]
            refs = refs[3:]
        out_part, down_part, weight_sem, total = refs[:4]
        fetched, fetch_sem, rings, ring_sem = refs[4:7], refs[7], refs[8:10], refs[10]
        land, sems = refs[11], refs[12:]
        inner_part, mixed_part, active_part = fetched
        ctx, place, _, _, _ = neighbours()

        def fetch(number):
            at, slot = lax.rem(number, 2), work_slot(number)
            return [
                pltpu.make_async_copy(source.at[slot], target.at[at], fetch_sem.at[at, which])
                for which, (source, target) in enumerate(zip((inner, mixed, active), fetched))
            ]

        def leave(number):
            at, slot = lax.rem(number, 2), work_slot(number)
            return [
                pltpu.make_async_copy(ring.at[at], result.at[slot], ring_sem.at[at, which])
                for which, (ring, result) in enumerate(zip(rings, (grad_mixed, grad_inner)))
            ]

        weights = load_all(
            ((out_weight.at[layer], out_part), (down_weight.at[layer], down_part)), weight_sem
        )
        for copy in fetch(jnp.int32(0)):
            copy.start()
        greet_neighbours(bool(swap))
        if swap:
            plane_swap((source, target), swap_sem).start()
        land[ctx * SIDE + place] = own[...]
        total[...] = jnp.zeros_like(total)

        def work(number, slot):
            at = lax.rem(number, 2)

            @pl.when(number == 0)
            def _():
                wait_all(weights)

            @pl.when(number + 1 < GROUP)
            def _():
                for copy in fetch(number + 1):
                    copy.start()

            @pl.when(number >= 2)
            def _():
                wait_all(leave(number - 2))

            wait_all(fetch(number))
            block = land[slot]
            rings[0][at] = dot(block, out_part[...], 1, 1)
            value = inner_part[at]
            factor = math.sqrt(2.0 / math.pi)
            square = value * value
            bend = jnp.tanh(factor * value * (1.0 + 0.044715 * square))
            slope = 0.5 * (1.0 + bend) + 0.5 * value * (1.0 - bend * bend) * (
                factor * (1.0 + 3 * 0.044715 * square)
            )
            rings[1][at] = (dot(block, down_part[...], 1, 1) * slope).astype(jnp.bfloat16)
            for copy in leave(number):
                copy.start()
            total[:HEAD_COLS] += dot(mixed_part[at], block, 0, 0)
            total[HEAD_COLS:] += dot(active_part[at], block, 0, 0)

        gather_blocks(land, None, *sems, work)
        branch[...] = total[...].astype(jnp.bfloat16)
        if swap:
            plane_swap((source, target), swap_sem).wait()
        for number in (GROUP - 2, GROUP - 1):
            wait_all(leave(jnp.int32(number)))

    return pl.pallas_call(
        kernel,
        out_shape=(
            jax.ShapeDtypeStruct((GROUP, rows, HEAD_COLS), jnp.float32),
            jax.ShapeDtypeStruct((GROUP, rows, FEED_COLS), jnp.bfloat16),
            jax.ShapeDtypeStruct((BACK_COLS, D), jnp.bfloat16),
        )
        + tuple(jax.ShapeDtypeStruct(array.shape, array.dtype) for array in swap),
        in_specs=[VMEM] + [HBM] * (5 + len(swap)),
        out_specs=(HBM, HBM, VMEM) + (HBM,) * len(swap),
        scratch_shapes=[pltpu.SemaphoreType.DMA((2,))] * len(swap)
        + [
            pltpu.VMEM(out_weight.shape[1:], jnp.bfloat16),
            pltpu.VMEM(down_weight.shape[1:], jnp.bfloat16),
            pltpu.SemaphoreType.DMA((2,)),
            pltpu.VMEM((BACK_COLS, D), jnp.float32),
            pltpu.VMEM((2, rows, FEED_COLS), jnp.float32),
            pltpu.VMEM((2, rows, HEAD_COLS), jnp.bfloat16),
            pltpu.VMEM((2, rows, FEED_COLS), jnp.bfloat16),
            pltpu.SemaphoreType.DMA((2, 3)),
            pltpu.VMEM((2, rows, HEAD_COLS), jnp.float32),
            pltpu.VMEM((2, rows, FEED_COLS), jnp.bfloat16),
            pltpu.SemaphoreType.DMA((2, 2)),
        ]
        + gather_scratch(rows),
        compiler_params=pltpu.CompilerParams(
            collective_id=50 + layer, has_side_effects=True, vmem_limit_bytes=ROOM
        ),
    )(grad, out_weight, down_weight, inner, mixed, active, *swap)


SCATTER_OPS = (
    ((0, 0), (0, 1), (1, 0), (2, 0), (1, 1), (0, 2), (2, 1), (3, 0), (1, 2), (2, 2), (4, 0), (6, 0), (5, 0), (0, 3), (3, 1), (3, 2), (1, 3), (3, 3), (4, 1), (5, 1), (6, 1), (4, 2), (5, 2), (6, 2), (2, 3), (4, 3), (5, 3), (6, 3)),
    ((0, 0), (0, 2), (3, 2), (1, 0), (3, 0), (0, 1), (0, 3), (1, 1), (2, 0), (1, 2), (3, 1), (1, 3), (4, 0), (6, 0), (5, 0), (3, 3), (2, 1), (2, 2), (4, 1), (6, 1), (5, 1), (4, 2), (5, 2), (6, 2), (2, 3), (4, 3), (5, 3), (6, 3)),
)
SCATTER_OPS_WORK = (
    ((0, 0), (0, 1), (1, 0), (2, 0), (1, 1), (0, 2), (2, 1), (3, 0), (1, 2), (2, 2), (4, 0), (6, 0), (7, 0), (5, 0), (0, 3), (3, 1), (3, 2), (1, 3), (3, 3), (4, 1), (7, 0), (5, 1), (7, 0), (7, 0), (7, 0), (7, 0), (7, 0), (6, 1), (4, 2), (7, 0), (5, 2), (7, 0), (7, 0), (7, 0), (6, 2), (2, 3), (7, 0), (7, 0), (7, 0), (7, 0), (7, 0), (4, 3), (5, 3), (6, 3)),
    ((0, 0), (0, 2), (3, 2), (1, 0), (3, 0), (7, 0), (0, 1), (0, 3), (1, 1), (2, 0), (1, 2), (3, 1), (7, 0), (7, 0), (1, 3), (4, 0), (6, 0), (7, 0), (5, 0), (7, 0), (7, 0), (3, 3), (2, 1), (7, 0), (2, 2), (7, 0), (7, 0), (4, 1), (6, 1), (5, 1), (4, 2), (5, 2), (7, 0), (7, 0), (7, 0), (6, 2), (7, 0), (7, 0), (7, 0), (2, 3), (7, 0), (4, 3), (5, 3), (6, 3)),
)
SCATTER_OPS_EARLY = (
    ((0, 0), (0, 1), (1, 0), (3, 0), (2, 0), (0, 2), (1, 1), (2, 1), (1, 2), (2, 2), (0, 3), (4, 0), (6, 0), (7, 0), (7, 0), (7, 0), (5, 0), (7, 0), (3, 1), (1, 3), (7, 0), (7, 0), (7, 0), (4, 1), (7, 0), (7, 0), (7, 0), (6, 1), (7, 0), (5, 1), (7, 0), (7, 0), (7, 0), (7, 0), (7, 0), (3, 2), (3, 3), (2, 3), (4, 2), (5, 2), (6, 2), (8, 0), (8, 1), (8, 2), (8, 3), (4, 3), (5, 3), (6, 3)),
    ((0, 2), (7, 0), (0, 0), (0, 1), (1, 0), (7, 0), (7, 0), (0, 3), (7, 0), (3, 3), (3, 0), (7, 0), (1, 1), (2, 0), (3, 2), (1, 2), (7, 0), (2, 2), (7, 0), (7, 0), (3, 1), (1, 3), (4, 0), (6, 0), (7, 0), (2, 1), (7, 0), (7, 0), (7, 0), (5, 0), (7, 0), (7, 0), (7, 0), (7, 0), (2, 3), (4, 1), (6, 1), (5, 1), (4, 2), (5, 2), (6, 2), (8, 0), (8, 1), (8, 2), (8, 3), (4, 3), (5, 3), (6, 3)),
)
SPLIT = ((0, 208), (208, 48))


def scatter_events(partial, other_work, late_work, ops, scratch):
    total, give, take, side_take, line_take, other_take = scratch[:6]
    core_send, core_recv, side_send, side_recv, line_send, line_recv = scratch[6:12]
    other_send, other_recv = scratch[12:]
    ctx, place, twin, across, twin_across = neighbours()
    below, above = place - 1, place + 1
    has_below, has_above = place > 0, place < SIDE - 1
    at_end = (place == 0) | (place == SIDE - 1)

    def rows_of(part):
        return pl.ds(*SPLIT[part])

    def core_copy(step, store):
        return to_axis(
            give.at[step], take.at[store], core_send.at[store], core_recv.at[store], "ctx", twin
        )

    def side_copy(step, part):
        return to_axis(
            take.at[step, rows_of(part)],
            side_take.at[step, rows_of(part)],
            side_send.at[step, part],
            side_recv.at[step, part],
            "ctx",
            across,
        )

    def line_copy(step, line, slot, target, part):
        return to_axis(
            take.at[SIDE + step, rows_of(part)],
            line_take.at[slot, rows_of(part)],
            line_send.at[line, part],
            line_recv.at[slot, part],
            "fsdp",
            target,
        )

    def other_copy(step, line, slot, target):
        return to_axis(
            take.at[step, rows_of(1)],
            other_take.at[slot],
            other_send.at[line],
            other_recv.at[slot],
            "fsdp",
            target,
        )

    def from_above(line):
        return jnp.where(line == place, SIDE, line)

    def to_below(line):
        return jnp.where(line == place - 1, SIDE, line)

    def one(number, turn):
        def by_end(field):
            ends, middle = (tuple(entry[field] for entry in table) for table in ops)
            return jnp.where(at_end, nibble(ends, number), nibble(middle, number))

        what, step = by_end(0), by_end(1)
        line = digit_of_row(FAR, place, step)

        @pl.when((what <= 1) | (what == 3) | (what == 4))
        def _():
            owner = jnp.where(
                what == 0,
                twin_across,
                jnp.where(what == 1, across, jnp.where(what == 3, twin, ctx)),
            )
            total[...] = partial(owner * SIDE + line)

        @pl.when(what == 0)
        def _():
            give[step] = total[...].astype(jnp.bfloat16)
            core_copy(step, step).start()

        @pl.when(what == 1)
        def _():
            core_copy(step, step).wait_recv()
            take[step] = (total[...] + take[step].astype(jnp.float32)).astype(jnp.bfloat16)
            side_copy(step, 0).start()

        @pl.when(what == 2)
        def _():
            rows = rows_of(1)

            @pl.when((line >= place) & has_below)
            def _():
                other_copy(step, line, line, below).wait_recv()
                take[step, rows] = (
                    take[step, rows].astype(jnp.float32) + other_take[line].astype(jnp.float32)
                ).astype(jnp.bfloat16)

            @pl.when((line <= place) & has_above)
            def _():
                other_copy(step, line, from_above(line), above).wait_recv()
                take[step, rows] = (
                    take[step, rows].astype(jnp.float32)
                    + other_take[from_above(line)].astype(jnp.float32)
                ).astype(jnp.bfloat16)

            @pl.when(line > place)
            def _():
                other_copy(step, line, line, above).start()

            @pl.when(line < place)
            def _():
                other_copy(step, line, to_below(line), below).start()

            @pl.when(line == place)
            def _():
                side_copy(step, 1).start()

        @pl.when(what == 3)
        def _():
            core_copy(step, step).wait_send()
            give[step] = total[...].astype(jnp.bfloat16)
            core_copy(step, SIDE + step).start()

        @pl.when(what == 4)
        def _():
            core_copy(step, SIDE + step).wait_recv()
            total[...] += take[SIDE + step].astype(jnp.float32)

        for part in range(2):
            rows = rows_of(part)

            @pl.when(what == 5 + part)
            def _(rows=rows, part=part):
                crossed = line == place if part == 1 else line >= 0

                @pl.when(crossed)
                def _():
                    side_copy(step, part).wait_recv()
                    total[rows] += side_take[step, rows].astype(jnp.float32)

                @pl.when((line >= place) & has_below)
                def _():
                    line_copy(step, line, line, below, part).wait_recv()
                    total[rows] += line_take[line, rows].astype(jnp.float32)

                @pl.when((line <= place) & has_above)
                def _():
                    line_copy(step, line, from_above(line), above, part).wait_recv()
                    total[rows] += line_take[from_above(line), rows].astype(jnp.float32)

                @pl.when(line > place)
                def _():
                    take[SIDE + step, rows] = total[rows].astype(jnp.bfloat16)
                    line_copy(step, line, line, above, part).start()

                @pl.when(line < place)
                def _():
                    take[SIDE + step, rows] = total[rows].astype(jnp.bfloat16)
                    line_copy(step, line, to_below(line), below, part).start()

        if other_work is not None:

            @pl.when(what == 7)
            def _():
                other_work(turn)

        if late_work is not None:

            @pl.when(what == 8)
            def _():
                late_work(step)

        return turn + jnp.where(what == 7, 1, 0)

    lax.fori_loop(0, len(ops[0]), one, jnp.int32(0))

    def finish(step, carry):
        line = digit_of_row(FAR, place, step)
        core_copy(step, SIDE + step).wait_send()
        side_copy(step, 0).wait_send()

        @pl.when(line == place)
        def _():
            side_copy(step, 1).wait_send()

        @pl.when(line != place)
        def _():
            for part in range(2):
                line_copy(step, line, line, place, part).wait_send()
            other_copy(step, line, line, place).wait_send()

        return carry

    lax.fori_loop(0, SIDE, finish, 0)


def scatter_scratch(rows):
    return [
        pltpu.VMEM((rows, D), jnp.float32),
        pltpu.VMEM((SIDE, rows, D), jnp.bfloat16),
        pltpu.VMEM((2 * SIDE, rows, D), jnp.bfloat16),
        pltpu.VMEM((SIDE, rows, D), jnp.bfloat16),
        pltpu.VMEM((SIDE + 1, rows, D), jnp.bfloat16),
        pltpu.VMEM((SIDE + 1, SPLIT[1][1], D), jnp.bfloat16),
        pltpu.SemaphoreType.DMA((2 * SIDE,)),
        pltpu.SemaphoreType.DMA((2 * SIDE,)),
        pltpu.SemaphoreType.DMA((SIDE, 2)),
        pltpu.SemaphoreType.DMA((SIDE, 2)),
        pltpu.SemaphoreType.DMA((SIDE, 2)),
        pltpu.SemaphoreType.DMA((SIDE + 1, 2)),
        pltpu.SemaphoreType.DMA((SIDE,)),
        pltpu.SemaphoreType.DMA((SIDE + 1,)),
    ]


SMALL_ROWS = 16
PAIRS = GROUP // 2


def norm_back_strip(hidden, grad, total, gain, out, part):
    values = hidden[part].astype(jnp.float32)
    centred = values - jnp.mean(values, axis=1, keepdims=True)
    spread = jnp.mean(centred * centred, axis=1, keepdims=True)
    root = lax.rsqrt(spread + EPS)
    normed = centred * root
    above = total[part]
    scaled = above * gain[...]
    down = jnp.mean(scaled, axis=1, keepdims=True)
    along = jnp.mean(scaled * normed, axis=1, keepdims=True)
    passing = grad[part]
    out[part] = passing + root * (scaled - down - normed * along)
    low = passing.astype(jnp.bfloat16).astype(jnp.float32)
    return tuple(
        jnp.sum(sums.reshape(STRIP // 8, 8, D), axis=0) for sums in (above * normed, above, low)
    )


def small_exchange(shares, land, mine, other, out, sems):
    send, recv, swap_send, swap_recv = sems
    me = lax.axis_index("ctx") * SIDE + lax.axis_index("fsdp")

    def copy(step):
        peer = lax.rem(me + step, GROUP)
        return to_peer(shares.at[peer], land.at[me], send.at[step], recv.at[me], peer)

    def swap():
        return to_axis(mine, other, swap_send, swap_recv, "seq", 1 - lax.axis_index("seq"))

    def begin(sums):
        for number, folded in enumerate(sums):
            row = jnp.sum(folded, axis=0, keepdims=True)
            for block in range(GROUP):
                shares[block, number : number + 1] = row[:, block * SHARE : (block + 1) * SHARE]

        def start(step, carry):
            copy(step).start()
            return carry

        lax.fori_loop(1, GROUP, start, 0)
        land[me] = shares[me]

    def middle():
        def arrive(step, carry):
            source = lax.rem(me + GROUP - step, GROUP)
            to_peer(shares.at[source], land.at[source], send.at[step], recv.at[source], source).wait_recv()
            copy(step).wait_send()
            return carry

        lax.fori_loop(1, GROUP, arrive, 0)
        mine[...] = jnp.sum(land[...], axis=0)
        swap().start()

    def end():
        swap().wait()
        out[...] = mine[...] + other[...]

    return begin, middle, end


def small_scratch():
    small = (SMALL_ROWS, SHARE)
    return [
        pltpu.VMEM((GROUP,) + small, jnp.float32),
        pltpu.VMEM(small, jnp.float32),
        pltpu.VMEM(small, jnp.float32),
        pltpu.SemaphoreType.DMA((GROUP,)),
        pltpu.SemaphoreType.DMA((GROUP,)),
        pltpu.SemaphoreType.DMA,
        pltpu.SemaphoreType.DMA,
    ]


def half_swaps(halves, wholes, sems, pieces=4):
    send, recv, own = sems
    seq = lax.axis_index("seq")
    half = SHARE // 2
    size = half // pieces

    def copies(which):
        return [
            to_axis(
                source.at[pl.ds(piece * size, size)],
                target.at[pl.ds(pl.multiple_of(seq * half + piece * size, size), size)],
                send.at[at, piece],
                recv.at[at, piece],
                "seq",
                1 - seq,
            )
            for at, (source, target) in enumerate(zip(halves, wholes))
            for piece in which
        ]

    def kept():
        rows = pl.ds(pl.multiple_of(seq * half, half), half)
        return [
            pltpu.make_async_copy(source, target.at[rows], own.at[at])
            for at, (source, target) in enumerate(zip(halves, wholes))
        ]

    return copies, kept


def half_sems(pieces=4):
    return [
        pltpu.SemaphoreType.DMA((2, pieces)),
        pltpu.SemaphoreType.DMA((2, pieces)),
        pltpu.SemaphoreType.DMA((2,)),
    ]


WHOLES = (
    jax.ShapeDtypeStruct((SHARE, 3 * D), jnp.bfloat16),
    jax.ShapeDtypeStruct((SHARE, FF), jnp.bfloat16),
)
HALVES = (
    jax.ShapeDtypeStruct((SHARE // 2, 3 * D), jnp.bfloat16),
    jax.ShapeDtypeStruct((SHARE // 2, FF), jnp.bfloat16),
)


def forward_scatter(hidden, bias, mixed, active, out_weight, down_weight, layer, rest=None):
    rows = hidden.shape[0]
    last = rest is not None

    def kernel(hidden, bias, mixed, active, out_weight, down_weight, *refs):
        if last:
            (below_total, below_hidden, below_grad, gain, below_shares, joint, upper, branch), refs = (
                refs[:8],
                refs[8:],
            )
            out, grad_out, small_out, joint_out, upper_out, branch_out = refs[:6]
            refs = refs[6:]
        else:
            out, refs = refs[0], refs[1:]
        hidden_part, mixed_part, active_part, out_part, down_part, load_sem = refs[:6]
        refs = refs[6:]
        loads = load_all(
            (
                (mixed, mixed_part),
                (active, active_part),
                (out_weight.at[layer], out_part),
                (down_weight.at[layer], down_part),
                (hidden, hidden_part),
            ),
            load_sem,
        )
        other_work = None
        if last:
            parts, part_sem, sums, swap_sem = refs[:4], refs[4], refs[5], refs[6]
            shares, small, swap_sems, refs = parts[3], refs[7:14], refs[14:17], refs[17:]
            below = load_all(
                tuple(zip((below_total, below_hidden, below_grad, below_shares), parts)), part_sem
            )
            small_begin, small_middle, small_end = small_exchange(
                shares, small[0], small[1], small[2], small_out, small[3:]
            )
            copies, kept = half_swaps((joint, upper), (joint_out, upper_out), swap_sems)
            greet_plane(GROUP)
            for copy in copies((0, 1, 2, 3)) + kept():
                copy.start()
            sums[...] = jnp.zeros_like(sums)
            strips = rows // STRIP

            def other_work(turn):
                @pl.when(turn == 0)
                def _():
                    wait_all(below)

                @pl.when(turn < strips)
                def _():
                    part = pl.ds(pl.multiple_of(turn * STRIP, STRIP), STRIP)
                    found = norm_back_strip(parts[1], parts[2], parts[0], gain, grad_out, part)
                    for number, folded in enumerate(found):
                        sums[number] += folded

                @pl.when(turn == strips)
                def _():
                    small_begin([sums[number] for number in range(3)])

                @pl.when(turn == GROUP - 4)
                def _():
                    small_middle()
                    plane_swap((branch, branch_out), swap_sem).start()

        else:
            greet_neighbours()
        scratch = refs
        wait_all(loads[:4])

        def partial(slot):
            return dot(mixed_part[slot], out_part[...]) + dot(active_part[slot], down_part[...])

        scatter_events(
            partial, other_work, None, SCATTER_OPS_WORK if last else SCATTER_OPS, scratch
        )
        loads[4].wait()
        out[...] = hidden_part[...].astype(jnp.float32) + (scratch[0][...] + bias[...])
        if last:
            small_end()
            wait_all(copies((0, 1, 2, 3)) + kept())
            plane_swap((branch, branch_out), swap_sem).wait()

    out_shape = (jax.ShapeDtypeStruct((rows, D), jnp.float32),)
    out_specs = (VMEM,)
    extra_scratch = []
    if last:
        total, before, grad, _, shares, _, _, branch = rest
        out_shape += (
            (
                jax.ShapeDtypeStruct((rows, D), jnp.float32),
                jax.ShapeDtypeStruct((SMALL_ROWS, SHARE), jnp.float32),
            )
            + WHOLES
            + (jax.ShapeDtypeStruct(branch.shape, branch.dtype),)
        )
        out_specs += (VMEM, VMEM, HBM, HBM, HBM)
        extra_scratch = (
            [pltpu.VMEM(array.shape, array.dtype) for array in (total, before, grad, shares)]
            + [
                pltpu.SemaphoreType.DMA((4,)),
                pltpu.VMEM((3, 8, D), jnp.float32),
                pltpu.SemaphoreType.DMA((2,)),
            ]
            + small_scratch()
            + half_sems()
        )
    return pl.pallas_call(
        kernel,
        out_shape=out_shape,
        in_specs=[HBM, VMEM] + [HBM] * 4 + ([HBM] * 3 + [VMEM] + [HBM] * 4 if last else []),
        out_specs=out_specs,
        scratch_shapes=[pltpu.VMEM(array.shape, array.dtype) for array in (hidden, mixed, active)]
        + [
            pltpu.VMEM(out_weight.shape[1:], jnp.bfloat16),
            pltpu.VMEM(down_weight.shape[1:], jnp.bfloat16),
        ]
        + [pltpu.SemaphoreType.DMA((5,))]
        + extra_scratch
        + scatter_scratch(rows),
        compiler_params=pltpu.CompilerParams(
            collective_id=10 + layer, has_side_effects=True, vmem_limit_bytes=ROOM
        ),
    )(hidden, bias, mixed, active, out_weight, down_weight, *(rest or ()))


def backward_scatter(
    hidden, grad, gain, grad_joint, grad_inner, columns, every, layer, up=None, halves=()
):
    rows = grad.shape[0]
    half = SHARE // 2
    collects = up is not None
    made = JOINT_COLS if collects else COLS
    tokens = GROUP * rows

    def kernel(*refs):
        if collects:
            (joint_in, inner_in, columns_in, every, up, *halves), refs = refs[:7], refs[7:]
            out, shares, joint_half, up_half, *wholes = refs[:6]
            refs = refs[6:]
        else:
            (joint_in, inner_in, columns_in, every, hidden_in, grad_in, gain), refs = refs[:7], refs[7:]
            out, small_out, summed, refs = refs[0], refs[1], refs[2], refs[3:]
        grad_joint, grad_inner, columns, load_sem, strips, load = refs[:6]
        mine, other, cross_send, cross_recv = refs[6:10]
        refs = refs[10:]
        if collects:
            summed, plane_send, plane_recv, plane_own, up_send, up_recv, up_own = refs[:7]
            swap_sems, refs = refs[7:10], refs[10:]
            copies, kept = half_swaps(halves, wholes, swap_sems)
        else:
            hidden, grad, shares, small, refs = refs[0], refs[1], refs[2], refs[3:10], refs[10:]
            small_begin, small_middle, small_end = small_exchange(
                shares, small[0], small[1], small[2], small_out, small[3:]
            )
        scratch = refs
        total = scratch[0]
        ctx, place, seq = lax.axis_index("ctx"), lax.axis_index("fsdp"), lax.axis_index("seq")
        me = ctx * SIDE + place
        part_rows = pl.ds(pl.multiple_of(seq * half, half), half)
        other_rows = pl.ds(pl.multiple_of((1 - seq) * half, half), half)

        def pair_of(turn):
            return lax.rem(me // 2 + 1 + turn, PAIRS)

        def load_strip(turn):
            start = pl.multiple_of(pair_of(turn) * 2 * SHARE, 2 * SHARE)
            buffer = lax.rem(turn, 2)
            return pltpu.make_async_copy(
                every.at[:, :, pl.ds(start, 2 * SHARE)], strips.at[buffer], load.at[buffer]
            )

        pairs = [(joint_in, grad_joint), (inner_in, grad_inner), (columns_in, columns)]
        if not collects:
            pairs += [(hidden_in, hidden), (grad_in, grad)]
        loads = load_all(pairs, load_sem)
        load_strip(jnp.int32(0)).start()
        shares[...] = jnp.zeros_like(shares)
        greet_plane(GROUP)

        def partial(slot):
            return dot(grad_joint[slot], columns[:, :JOINT_COLS], 1, 1) + dot(
                grad_inner[slot], columns[:, JOINT_COLS:], 1, 1
            )

        def product(turn):
            pair = pair_of(turn)
            load_strip(turn).wait()

            @pl.when(turn + 1 < PAIRS)
            def _():
                load_strip(turn + 1).start()

            strip = strips[lax.rem(turn, 2)].reshape(tokens, 2 * SHARE)
            result = dot(strip, grad_joint[...].reshape(tokens, JOINT_COLS), 0, 0).astype(
                jnp.bfloat16
            )
            for which in range(2):
                mine[2 * pair + which, :, :JOINT_COLS] = result[which * SHARE : (which + 1) * SHARE]
            if not collects:
                result = dot(strip, grad_inner[...].reshape(tokens, FEED_COLS), 0, 0).astype(
                    jnp.bfloat16
                )
                for which in range(2):
                    mine[2 * pair + which, :, JOINT_COLS:] = result[
                        which * SHARE : (which + 1) * SHARE
                    ]

        def cross_copy(block):
            return to_axis(
                mine.at[block, other_rows],
                other.at[block],
                cross_send.at[block],
                cross_recv.at[block],
                "seq",
                1 - seq,
            )

        def joint_places():
            return [
                (at, joint_half.at[:, pl.ds(start, width)], pl.ds(at * HEAD_COLS, HEAD_COLS))
                for at, (_, start, _, width) in enumerate(column_places(me)[:3])
            ]

        def plane_copies(block):
            return [
                to_peer(
                    summed.at[block, :, piece],
                    target,
                    plane_send.at[block, at],
                    plane_recv.at[me, at],
                    block,
                )
                for at, target, piece in joint_places()
            ]

        def own_copies():
            return [
                pltpu.make_async_copy(summed.at[me, :, piece], target, plane_own.at[at])
                for at, target, piece in joint_places()
            ]

        def up_place(block):
            return up_half.at[:, pl.ds(pl.multiple_of(block * FEED_COLS, FEED_COLS), FEED_COLS)]

        def up_copy(step):
            peer = lax.rem(me + step, GROUP)
            return to_peer(up.at[peer], up_place(me), up_send.at[step], up_recv.at[me], peer)

        def own_up():
            return pltpu.make_async_copy(up.at[me], up_place(me), up_own)

        def add(turn):
            for which in range(2):
                block = 2 * pair_of(turn) + which
                cross_copy(block).wait_recv()
                summed[block] = (
                    mine[block, part_rows].astype(jnp.float32) + other[block].astype(jnp.float32)
                ).astype(jnp.bfloat16)
                if collects:

                    @pl.when(block != me)
                    def _(block=block):
                        for copy in plane_copies(block):
                            copy.start()

                    @pl.when(block == me)
                    def _(block=block):
                        for copy in own_copies():
                            copy.start()

        def bias_sums():
            ones = jnp.ones((16, tokens), jnp.bfloat16)
            joint_bias = dot(ones, grad_joint[...].reshape(tokens, JOINT_COLS))[:1]
            upper_bias = dot(ones, grad_inner[...].reshape(tokens, FEED_COLS))[:1]
            for part in range(3):
                at = part * GROUP + me
                shares[at // 3, pl.ds(3 + lax.rem(at, 3), 1)] = joint_bias[
                    :, part * HEAD_COLS : (part + 1) * HEAD_COLS
                ]
            for part in range(FEED_COLS // SHARE):
                shares[me, 6 + part : 7 + part] = upper_bias[:, part * SHARE : (part + 1) * SHARE]

        def other_work(turn):
            pl.when(turn == 1)(bias_sums)

            @pl.when(lax.rem(turn, 2) == 0)
            def _():
                product(turn // 2)
                for which in range(2):
                    cross_copy(2 * pair_of(turn // 2) + which).start()

            @pl.when((lax.rem(turn, 2) == 1) & (turn > 4))
            def _():
                add((turn - 5) // 2)

            if collects:

                @pl.when(turn == GROUP - 1)
                def _():
                    for copy in copies((2, 3)):
                        copy.start()

        def last_adds(turn, carry):
            add(turn)
            return carry

        def late_work(step):
            @pl.when(step == 0)
            def _():
                lax.fori_loop(PAIRS - 2, PAIRS, last_adds, 0)

        def send_up(step, carry):
            up_copy(step).start()
            return carry

        wait_all(loads[:3])
        if collects:
            own_up().start()
            lax.fori_loop(1, GROUP, send_up, 0)
            for copy in copies((0, 1)) + kept():
                copy.start()
        scatter_events(
            partial,
            other_work,
            late_work if collects else None,
            SCATTER_OPS_EARLY if collects else SCATTER_OPS_WORK,
            scratch,
        )

        def end_cross(block, carry):
            cross_copy(block).wait_send()
            return carry

        def end(step, carry):
            source = lax.rem(me + GROUP - step, GROUP)
            target = up_place(source)
            to_peer(target, target, up_send.at[step], up_recv.at[source], source).wait_recv()
            up_copy(step).wait_send()
            for at, (_, start, _, width) in enumerate(column_places(source)[:3]):
                target = joint_half.at[:, pl.ds(start, width)]
                to_peer(
                    target, target, plane_send.at[source, at], plane_recv.at[source, at], source
                ).wait_recv()
            for copy in plane_copies(lax.rem(me + step, GROUP)):
                copy.wait_send()
            return carry

        if collects:
            out[...] = total[...]
            lax.fori_loop(1, GROUP, end, 0)
            wait_all(own_copies() + [own_up()] + copies((0, 1, 2, 3)) + kept())
        else:
            lax.fori_loop(PAIRS - 2, PAIRS, last_adds, 0)
            wait_all(loads[3:])

            def norm_back(part, sums):
                found = norm_back_strip(hidden, grad, total, gain, out, part)
                return tuple(before + more for before, more in zip(sums, found))

            zeros = jnp.zeros((8, D), jnp.float32)
            small_begin(each_strip(rows, norm_back, (zeros, zeros, zeros)))
            small_middle()
            small_end()
        lax.fori_loop(0, GROUP, end_cross, 0)

    def part(width, height=half):
        return pltpu.VMEM((GROUP, height, width), jnp.bfloat16)

    def same(*arrays):
        return [pltpu.VMEM(array.shape, array.dtype) for array in arrays]

    small = (SMALL_ROWS, SHARE)
    shares = (GROUP,) + small
    sixteen = pltpu.SemaphoreType.DMA((GROUP,))
    row_shape = jax.ShapeDtypeStruct((rows, D), jnp.float32)
    common = (
        same(grad_joint, grad_inner, columns)
        + [
            pltpu.SemaphoreType.DMA((5,)),
            pltpu.VMEM((2, GROUP, rows, 2 * SHARE), jnp.bfloat16),
            pltpu.SemaphoreType.DMA((2,)),
            part(made, SHARE),
            part(made),
            sixteen,
            sixteen,
        ]
    )
    if collects:
        out_shape = (row_shape, jax.ShapeDtypeStruct(shares, jnp.float32)) + HALVES + WHOLES
        out_specs = (VMEM, VMEM) + (HBM,) * 4
        operands = (grad_joint, grad_inner, columns, every, up, *halves)
        in_specs = [HBM] * 7
        special = [
            part(JOINT_COLS),
            pltpu.SemaphoreType.DMA((GROUP, 3)),
            pltpu.SemaphoreType.DMA((GROUP, 3)),
            pltpu.SemaphoreType.DMA((3,)),
            sixteen,
            sixteen,
            pltpu.SemaphoreType.DMA,
        ] + half_sems()
    else:
        out_shape = (
            row_shape,
            jax.ShapeDtypeStruct(small, jnp.float32),
            jax.ShapeDtypeStruct((GROUP, half, COLS), jnp.bfloat16),
        )
        out_specs = (VMEM,) * 3
        operands = (grad_joint, grad_inner, columns, every, hidden, grad, gain)
        in_specs = [HBM] * 6 + [VMEM]
        special = same(hidden, grad) + [pltpu.VMEM(shares, jnp.float32)] + small_scratch()
    return pl.pallas_call(
        kernel,
        out_shape=out_shape,
        in_specs=in_specs,
        out_specs=out_specs,
        scratch_shapes=common + special + scatter_scratch(rows),
        compiler_params=pltpu.CompilerParams(
            collective_id=20 + layer, has_side_effects=True, vmem_limit_bytes=ROOM
        ),
    )(*operands)


def mask_rest(rows, begin, spot, first, lead):
    if lead:
        old = jnp.where(spot[:lead] >= begin, rows[:lead], NEG)
    key_at = lax.broadcasted_iota(jnp.int32, (first, first), 0) + lead
    query_at = lax.broadcasted_iota(jnp.int32, (first, first), 1) + lead
    near = spot[lead:]
    seen = ((near >= begin) & (near <= query_at)) | (key_at == query_at)
    new = jnp.where(seen, rows[lead:], NEG)
    return jnp.concatenate([old, new], axis=0) if lead else new


def head_lanes(head, rows):
    lane = lax.broadcasted_iota(jnp.int32, (rows, HEAD_COLS), 1)
    return (lane >= head * HEAD_DIM) & (lane < (head + 1) * HEAD_DIM)


def column_exchange(sources, land, sems, layer):
    plane_send, plane_recv, own_sem = sems
    ctx, place, seq = lax.axis_index("ctx"), lax.axis_index("fsdp"), lax.axis_index("seq")
    me = ctx * SIDE + place
    half = SHARE // 2
    part_rows = pl.ds(pl.multiple_of(seq * half, half), half)

    def piece(peer, number):
        which, start, at, width = column_places(peer)[number]
        return (
            sources[which].at[layer, part_rows, pl.ds(start, width)],
            land.at[me, :, pl.ds(at, width)],
        )

    def send_piece(step, number):
        peer = lax.rem(me + step, GROUP)
        source, target = piece(peer, number)
        return to_peer(source, target, plane_send.at[step, number], plane_recv.at[me, number], peer)

    def own_piece(number):
        return pltpu.make_async_copy(*piece(me, number), own_sem.at[number])

    def begin():
        greet_plane(GROUP, False)

        def send(step, carry):
            for number in range(PLACES):
                send_piece(step, number).start()
            return carry

        lax.fori_loop(1, GROUP, send, 0)
        for number in range(PLACES):
            own_piece(number).start()

    def end():
        def arrive(step, carry):
            source = lax.rem(me + GROUP - step, GROUP)
            for number in range(PLACES):
                _, _, at, width = column_places(0)[number]
                target = land.at[source, :, pl.ds(at, width)]
                to_peer(
                    target, target, plane_send.at[0, number], plane_recv.at[source, number], source
                ).wait_recv()
                send_piece(step, number).wait_send()
            return carry

        lax.fori_loop(1, GROUP, arrive, 0)
        for number in range(PLACES):
            own_piece(number).wait()

    return begin, end


def up_products(every, feed, out, scratch):
    feed_part, strips, mine, other, feed_sem, load, cross_send, cross_recv = scratch
    rows = feed.shape[1]
    tokens = GROUP * rows
    half = SHARE // 2
    seq = lax.axis_index("seq")
    me = lax.axis_index("ctx") * SIDE + lax.axis_index("fsdp")
    part_rows = pl.ds(pl.multiple_of(seq * half, half), half)
    other_rows = pl.ds(pl.multiple_of((1 - seq) * half, half), half)

    def pair_of(turn):
        return lax.rem(me // 2 + 1 + turn, PAIRS)

    def load_strip(turn):
        start = pl.multiple_of(pair_of(turn) * 2 * SHARE, 2 * SHARE)
        buffer = lax.rem(turn, 2)
        return pltpu.make_async_copy(
            every.at[:, :, pl.ds(start, 2 * SHARE)], strips.at[buffer], load.at[buffer]
        )

    def cross_copy(block):
        return to_axis(
            mine.at[block, other_rows],
            other.at[block],
            cross_send.at[block],
            cross_recv.at[block],
            "seq",
            1 - seq,
        )

    def feed_copy():
        return pltpu.make_async_copy(feed, feed_part, feed_sem)

    def begin():
        feed_copy().start()
        load_strip(jnp.int32(0)).start()

    def product(turn, carry):
        pair = pair_of(turn)
        load_strip(turn).wait()

        @pl.when(turn == 0)
        def _():
            feed_copy().wait()

        @pl.when(turn + 1 < PAIRS)
        def _():
            load_strip(turn + 1).start()

        strip = strips[lax.rem(turn, 2)].reshape(tokens, 2 * SHARE)
        made = dot(strip, feed_part[...].reshape(tokens, FEED_COLS), 0, 0).astype(jnp.bfloat16)
        for which in range(2):
            mine[2 * pair + which] = made[which * SHARE : (which + 1) * SHARE]
            cross_copy(2 * pair + which).start()
        return carry

    def add(turn, carry):
        for which in range(2):
            block = 2 * pair_of(turn) + which
            cross_copy(block).wait()
            out[block] = (
                mine[block, part_rows].astype(jnp.float32) + other[block].astype(jnp.float32)
            ).astype(jnp.bfloat16)
        return carry

    each = PAIRS // SIDE

    def make(step):
        lax.fori_loop(each * step, each * step + each, product, 0)
        lax.fori_loop(each * jnp.maximum(step - 1, 0), each * step, add, 0)

    def end():
        lax.fori_loop(PAIRS - each, PAIRS, add, 0)

    return begin, make, end


def row_exchange(summed, outputs, sems):
    plane_send, plane_recv, own_sem = sems
    me = lax.axis_index("ctx") * SIDE + lax.axis_index("fsdp")

    def piece(peer, number):
        which, start, at, width = column_places(me)[number]
        return summed.at[peer, :, pl.ds(at, width)], outputs[which].at[:, pl.ds(start, width)]

    def send_piece(step, number):
        peer = lax.rem(me + step, GROUP)
        source, target = piece(peer, number)
        return to_peer(source, target, plane_send.at[step, number], plane_recv.at[me, number], peer)

    def own_piece(number):
        return pltpu.make_async_copy(*piece(me, number), own_sem.at[number])

    def begin():
        greet_plane(GROUP)

        def send(step, carry):
            for number in range(PLACES):
                send_piece(step, number).start()
            return carry

        lax.fori_loop(1, GROUP, send, 0)
        for number in range(PLACES):
            own_piece(number).start()

    def end():
        def arrive(step, carry):
            source = lax.rem(me + GROUP - step, GROUP)
            for number in range(PLACES):
                which, start, _, width = column_places(source)[number]
                target = outputs[which].at[:, pl.ds(start, width)]
                to_peer(
                    target, target, plane_send.at[0, number], plane_recv.at[source, number], source
                ).wait_recv()
                send_piece(step, number).wait_send()
            return carry

        lax.fori_loop(1, GROUP, arrive, 0)
        for number in range(PLACES):
            own_piece(number).wait()

    return begin, end


EXCHANGE_SEMS = [
    pltpu.SemaphoreType.DMA((GROUP, PLACES)),
    pltpu.SemaphoreType.DMA((GROUP, PLACES)),
    pltpu.SemaphoreType.DMA((PLACES,)),
]


def attend_plane(query, key, value, begin, spot, weights=None, layer=0):
    rows = query.shape[1]
    length = SIDE * rows
    scale = 1.0 / math.sqrt(HEAD_DIM)

    def kernel(query, key, value, begin, spot, *refs):
        if weights is None:
            mixed, turned, stats = refs
        else:
            mixed, turned, stats, land = refs[2:6]
            begin_exchange, end_exchange = column_exchange(refs[:2], land, refs[6:], layer)
            pl.when(pl.program_id(0) == 0)(begin_exchange)
        keys = key[:, 0].reshape(length, HEAD_COLS)
        values = value[:, 0].reshape(length, HEAD_COLS)
        for chunk in range(SIDE):
            lead = chunk * rows
            seen = lead + rows
            scaled = query[chunk, 0] * jnp.bfloat16(scale)
            start = begin[0, :, lead:seen]
            outs = []
            for head in range(OWN):
                own = jnp.where(head_lanes(head, rows), scaled, jnp.bfloat16(0))
                scores = mask_rest(
                    dot(keys[:seen], own, 1, 1), start, spot[0, :seen], rows, lead
                )
                peak = jnp.max(scores, axis=0, keepdims=True)
                probs = jnp.exp(scores - peak)
                norm = jnp.sum(probs, axis=0, keepdims=True)
                stats[0, head : head + 1, lead:seen] = peak
                stats[0, OWN + head : OWN + head + 1, lead:seen] = norm
                whole = dot(values[:seen], probs.astype(jnp.bfloat16), 0, 0)
                outs.append(whole[head * HEAD_DIM : (head + 1) * HEAD_DIM] / norm)
            joined = jnp.concatenate(outs, axis=0)
            turned[chunk, 0] = joined
            mixed[chunk, 0] = joined.T.astype(jnp.bfloat16)
        if weights is not None:
            pl.when(pl.program_id(0) == SIDE - 1)(end_exchange)

    def spec(height, width):
        return pl.BlockSpec((SIDE, 1, height, width), lambda step: (0, step, 0, 0))

    def shape(height, width, dtype):
        return jax.ShapeDtypeStruct((SIDE, SIDE, height, width), dtype)

    extra = weights is not None
    land = (jax.ShapeDtypeStruct((GROUP, SHARE // 2, COLS), jnp.bfloat16),) if extra else ()
    mixed, turned, stats, *land = pl.pallas_call(
        kernel,
        grid=(SIDE,),
        out_shape=(
            shape(rows, HEAD_COLS, jnp.bfloat16),
            shape(HEAD_COLS, rows, jnp.float32),
            jax.ShapeDtypeStruct((SIDE, 2 * OWN, length), jnp.float32),
        )
        + land,
        in_specs=[spec(rows, HEAD_COLS)] * 3
        + [
            pl.BlockSpec((1, 1, length), lambda step: (step, 0, 0)),
            pl.BlockSpec((1, length, 1), lambda step: (step, 0, 0)),
        ]
        + [HBM] * (2 if extra else 0),
        out_specs=(
            spec(rows, HEAD_COLS),
            spec(HEAD_COLS, rows),
            pl.BlockSpec((1, 2 * OWN, length), lambda step: (step, 0, 0)),
        )
        + ((HBM,) if extra else ()),
        scratch_shapes=EXCHANGE_SEMS if extra else [],
        compiler_params=pltpu.CompilerParams(
            collective_id=40, has_side_effects=True, vmem_limit_bytes=ROOM
        )
        if extra
        else pltpu.CompilerParams(vmem_limit_bytes=ROOM),
    )(
        *(array.reshape(SIDE, SIDE, rows, HEAD_COLS) for array in (query, key, value)),
        begin,
        spot,
        *(weights or ()),
    )
    return mixed.reshape(GROUP, rows, HEAD_COLS), turned, stats, *land


def attend_plane_back(
    query, key, value, begin, spot, turned, stats, grad, tables, summed=None, every=None, feed=None
):
    rows = query.shape[1]
    length = SIDE * rows
    scale = 1.0 / math.sqrt(HEAD_DIM)

    extra = summed is not None

    def kernel(query, key, value, grad, cosine, sine, begin, spot, turned, stats, *refs):
        if extra:
            summed, every, feed, out = refs[:4]
            up_out, grad_k, grad_v = refs[6], refs[7], refs[8]
            begin_exchange, end_exchange = row_exchange(summed, refs[4:6], refs[9:12])
            begin_up, make_up, end_up = up_products(every, feed, up_out, refs[12:])

            @pl.when(pl.program_id(0) == 0)
            def _():
                begin_up()
                begin_exchange()

        else:
            out, grad_k, grad_v = refs
        keys = key[:, 0].reshape(length, HEAD_COLS)
        values = value[:, 0].reshape(length, HEAD_COLS)
        for chunk in range(SIDE):
            lead = chunk * rows
            seen = lead + rows
            if chunk == 0:
                grad_k[...] = jnp.zeros_like(grad_k)
                grad_v[...] = jnp.zeros_like(grad_v)
            scaled = query[chunk, 0] * jnp.bfloat16(scale)
            start = begin[0, :, lead:seen]
            flipped = grad[chunk, 0].T
            grad_q, drifts, numers = [], [], []
            for head in range(OWN):
                part = slice(head * HEAD_DIM, (head + 1) * HEAD_DIM)
                norm = stats[0, OWN + head : OWN + head + 1, lead:seen]
                drifts.append(
                    jnp.sum(flipped[part] * turned[chunk, 0, part], axis=0, keepdims=True) / norm
                )
                numers.append(flipped[part] / norm)
            numer = jnp.concatenate(numers, axis=0).T.astype(jnp.bfloat16)
            for head in range(OWN):
                part = slice(head * HEAD_DIM, (head + 1) * HEAD_DIM)
                lanes = head_lanes(head, rows)
                own = jnp.where(lanes, scaled, jnp.bfloat16(0))
                own_numer = jnp.where(lanes, numer, jnp.bfloat16(0))
                scores = mask_rest(
                    dot(keys[:seen], own, 1, 1), start, spot[0, :seen], rows, lead
                )
                probs = jnp.exp(scores - stats[0, head : head + 1, lead:seen])
                grad_probs = dot(values[:seen], own_numer, 1, 1)
                grad_scores = (probs * (grad_probs - drifts[head])).astype(jnp.bfloat16)
                grad_q.append(dot(keys[:seen], grad_scores, 0, 0)[part])
                grad_k[:seen] += dot(grad_scores, own)
                grad_v[:seen] += dot(probs.astype(jnp.bfloat16), own_numer)
            turns = (cosine[chunk, 0], sine[chunk, 0])
            whole = jnp.concatenate(grad_q, axis=0).T * scale
            out[chunk, 0, :, :HEAD_COLS] = spin(whole, *turns, -1.0).astype(jnp.bfloat16)
        for chunk in range(SIDE):
            place = slice(chunk * rows, (chunk + 1) * rows)
            turns = (cosine[chunk, 0], sine[chunk, 0])
            out[chunk, 0, :, HEAD_COLS : 2 * HEAD_COLS] = spin(grad_k[place], *turns, -1.0).astype(
                jnp.bfloat16
            )
            out[chunk, 0, :, 2 * HEAD_COLS :] = grad_v[place].astype(jnp.bfloat16)
        if extra:
            make_up(pl.program_id(0))

            @pl.when(pl.program_id(0) == SIDE - 1)
            def _():
                end_up()
                end_exchange()


    def spec(height, width):
        return pl.BlockSpec((SIDE, 1, height, width), lambda step: (0, step, 0, 0))

    half = SHARE // 2
    halves = (
        jax.ShapeDtypeStruct((half, 3 * D), jnp.bfloat16),
        jax.ShapeDtypeStruct((half, FF), jnp.bfloat16),
        jax.ShapeDtypeStruct((GROUP, half, FEED_COLS), jnp.bfloat16),
    )
    out, *halves = pl.pallas_call(
        kernel,
        grid=(SIDE,),
        out_shape=(jax.ShapeDtypeStruct((SIDE, SIDE, rows, JOINT_COLS), jnp.bfloat16),)
        + (halves if extra else ()),
        in_specs=[spec(rows, HEAD_COLS)] * 6
        + [
            pl.BlockSpec((1, 1, length), lambda step: (step, 0, 0)),
            pl.BlockSpec((1, length, 1), lambda step: (step, 0, 0)),
            spec(HEAD_COLS, rows),
            pl.BlockSpec((1, 2 * OWN, length), lambda step: (step, 0, 0)),
        ]
        + [HBM] * (3 if extra else 0),
        out_specs=(spec(rows, JOINT_COLS),)
        + (
            (HBM, HBM, pl.BlockSpec((GROUP, half, FEED_COLS), lambda step: (0, 0, 0)))
            if extra
            else ()
        ),
        scratch_shapes=[pltpu.VMEM((length, HEAD_COLS), jnp.float32)] * 2
        + (
            EXCHANGE_SEMS
            + [
                pltpu.VMEM((GROUP, rows, FEED_COLS), jnp.bfloat16),
                pltpu.VMEM((2, GROUP, rows, 2 * SHARE), jnp.bfloat16),
                pltpu.VMEM((GROUP, SHARE, FEED_COLS), jnp.bfloat16),
                pltpu.VMEM((GROUP, half, FEED_COLS), jnp.bfloat16),
                pltpu.SemaphoreType.DMA,
                pltpu.SemaphoreType.DMA((2,)),
                pltpu.SemaphoreType.DMA((GROUP,)),
                pltpu.SemaphoreType.DMA((GROUP,)),
            ]
            if extra
            else []
        ),
        compiler_params=pltpu.CompilerParams(
            collective_id=41, has_side_effects=True, vmem_limit_bytes=ROOM
        )
        if extra
        else pltpu.CompilerParams(vmem_limit_bytes=ROOM),
    )(
        *(
            array.reshape(SIDE, SIDE, rows, HEAD_COLS)
            for array in (query, key, value, grad) + tuple(tables)
        ),
        begin,
        spot,
        turned,
        stats,
        *((summed, every, feed) if extra else ()),
    )
    return out.reshape(GROUP, rows, JOINT_COLS), *halves


def on_device_split(
    tokens,
    doc_lengths,
    keep_mask,
    ln_gain,
    ln_bias,
    qkv_weight,
    qkv_bias,
    out_weight,
    out_bias,
    up_weight,
    up_bias,
    down_weight,
    down_bias,
    cotangent,
):
    rows = tokens.shape[1]
    length = SIDE * rows
    me = lax.axis_index("ctx") * SIDE + lax.axis_index("fsdp")

    index = lax.axis_index("ctx") * rows + jnp.arange(rows, dtype=jnp.int32)
    ends = jnp.cumsum(doc_lengths[0])
    begin = jnp.max(jnp.where(index[:, None] >= ends[None, :], ends[None, :], 0), axis=1)
    fields = [ln_gain, ln_bias, qkv_bias, out_bias, down_bias]
    packed = jnp.concatenate(
        [field[layer].astype(jnp.float32) for layer in range(LAYERS) for field in fields]
        + [begin.astype(jnp.float32), keep_mask[0].astype(jnp.float32)]
    )
    packed = jnp.pad(packed, (0, -packed.shape[0] % (8 * SHARE))).reshape(-1, SHARE)
    lane = np.arange(HEAD_COLS) % HEAD_DIM
    inverse = 1.0 / 10000.0 ** (np.arange(0, ROT, 2, dtype=np.float32) / np.float32(ROT))
    inverse = np.where(lane < ROT, inverse[lane % (ROT // 2)], 0.0).astype(np.float32)
    up_bias = up_bias.astype(jnp.float32)

    seq = lax.axis_index("seq")
    half = SHARE // 2
    swap = [(0, 1), (1, 0)]

    def swapped(values):
        return lax.ppermute(values, "seq", swap)

    hidden = tokens[0]
    saved, gains, joint_grads, upper_grads, small_grads = [], [], [], [], []
    for layer in range(LAYERS):
        if layer == 0:
            *out, small, cosine, sine = first_gather(
                hidden, packed, up_bias[:1], jnp.asarray(inverse)[None, :], qkv_weight, up_weight
            )
            tables = (cosine, sine)
            length_rows = rows // SHARE

            def by_sequence(row):
                values = small[:, row : row + length_rows].reshape(SIDE, SIDE, rows)
                return values.transpose(1, 0, 2).reshape(SIDE, length).astype(jnp.int32)

            begin = by_sequence(BEGIN_ROW)[:, None, :]
            keep = by_sequence(BEGIN_ROW + length_rows)
            spot = jnp.where(keep > 0, jnp.arange(length, dtype=jnp.int32)[None, :], -1)[:, :, None]
        else:
            out = forward_gather(
                hidden,
                gain_row,
                row_of(layer, SHIFT_ROW),
                jnp.concatenate([own_bias, up_bias[layer : layer + 1]], axis=1),
                tables,
                halves,
                layer,
            )

        def row_of(layer, row):
            return small[:, layer * LAYER_ROWS + row].reshape(1, D)

        every, columns, query, key, value, inner, active = out
        gains.append(row_of(layer, GAIN_ROW))
        if layer + 1 < LAYERS:
            mixed, turned, stats, arrived = attend_plane(
                query, key, value, begin, spot, (qkv_weight, up_weight), layer + 1
            )
            halves = (arrived, swapped(arrived))
            gain_row = row_of(layer + 1, GAIN_ROW)
            at = (layer + 1) * LAYER_ROWS + JOINT_BIAS_ROW
            own_bias = lax.dynamic_slice_in_dim(
                small[:, at : at + 3].reshape(3, GROUP, HEAD_COLS), me, 1, axis=1
            ).reshape(1, JOINT_COLS)
        else:
            mixed, turned, stats = attend_plane(query, key, value, begin, spot)
        saved.append(
            (hidden, every, columns, query, key, value, inner, active, mixed, turned, stats)
        )
        branches = (
            hidden,
            row_of(layer, OUT_BIAS_ROW) + row_of(layer, DOWN_BIAS_ROW),
            mixed,
            active,
            out_weight,
            down_weight,
            layer,
        )
        if layer + 1 < LAYERS:
            hidden = forward_scatter(*branches)[0]

    grad_hidden = cotangent[0].astype(jnp.float32) * keep_mask[0].astype(jnp.float32)[:, None]
    summed = branch = None
    own_branches, other_branches = [], []
    for layer in reversed(range(LAYERS)):
        before, every, columns, query, key, value, inner, active, mixed, turned, stats = saved[layer]
        grad_mixed, grad_inner, branch, *other = backward_gather(
            grad_hidden.astype(jnp.bfloat16),
            out_weight,
            down_weight,
            inner,
            mixed,
            active,
            layer,
            () if layer + 1 == LAYERS else (branch,),
        )
        own_branches.insert(0, branch)
        other_branches = list(other) + other_branches
        grad_joint, *rest = attend_plane_back(
            query,
            key,
            value,
            begin,
            spot,
            turned,
            stats,
            grad_mixed,
            tables,
            summed,
            every,
            grad_inner,
        )
        grad_above = grad_hidden
        out = backward_scatter(
            before,
            grad_hidden,
            gains[layer],
            grad_joint,
            grad_inner,
            columns.reshape(D, COLS),
            every,
            layer,
            *((rest[2], rest[:2]) if rest else ()),
        )
        if layer > 0:
            grad_hidden, small, summed = out
            small_grads.insert(0, small)
            continue
        total, shares, joint, upper, *wholes = out
        joint_grads.append(wholes[0])
        upper_grads.append(wholes[1])
        hidden, grad_hidden, small, joint, upper, other = forward_scatter(
            *branches, (total, before, grad_above, gains[layer], shares, joint, upper, branch)
        )
        small_grads.insert(0, small)
        joint_grads.insert(0, joint)
        upper_grads.insert(0, upper)
        other_branches.insert(0, other)
    here, there = jnp.stack(own_branches), jnp.stack(other_branches)
    result = hidden.astype(jnp.bfloat16)[None]

    def branch_grad(part):
        return here[:, part].astype(jnp.float32) + there[:, part].astype(jnp.float32)

    small = jnp.stack(small_grads)
    return (
        result,
        grad_hidden[None],
        small[:, 0],
        small[:, 1],
        jnp.stack(joint_grads).astype(jnp.float32),
        small[:, 3:6].reshape(LAYERS, JOINT_COLS),
        branch_grad(slice(0, HEAD_COLS)),
        small[:, 2],
        jnp.stack(upper_grads).astype(jnp.float32),
        small[:, 6:10].reshape(LAYERS, FEED_COLS),
        branch_grad(slice(HEAD_COLS, None)),
        small[:, 2],
    )


def solution(mesh):
    small = mesh.shape["ctx"] == SIDE and mesh.shape["fsdp"] == SIDE and mesh.shape["seq"] == 2
    on_device = on_device_split if small else on_device_gathered
    return jax.shard_map(
        on_device,
        mesh=mesh,
        in_specs=(
            P(("seq", "fsdp"), "ctx", None),
            P(("seq", "fsdp"), None),
            P(("seq", "fsdp"), "ctx"),
            P(None, ("ctx", "fsdp")),
            P(None, ("ctx", "fsdp")),
            P(None, ("ctx", "fsdp"), None),
            P(None, ("ctx", "fsdp")),
            P(None, ("ctx", "fsdp"), None),
            P(None, ("ctx", "fsdp")),
            P(None, ("ctx", "fsdp"), None),
            P(None, ("ctx", "fsdp")),
            P(None, ("ctx", "fsdp"), None),
            P(None, ("ctx", "fsdp")),
            P(("seq", "fsdp"), "ctx", None),
        ),
        out_specs=(
            P(("seq", "fsdp"), "ctx", None),
            P(("seq", "fsdp"), "ctx", None),
            P(None, ("ctx", "fsdp")),
            P(None, ("ctx", "fsdp")),
            P(None, ("ctx", "fsdp"), None),
            P(None, ("ctx", "fsdp")),
            P(None, ("ctx", "fsdp"), None),
            P(None, ("ctx", "fsdp")),
            P(None, ("ctx", "fsdp"), None),
            P(None, ("ctx", "fsdp")),
            P(None, ("ctx", "fsdp"), None),
            P(None, ("ctx", "fsdp")),
        ),
        check_vma=False,
    )
```

```python
import functools
import math

import jax
import jax.numpy as jnp
import numpy as np
from jax import lax
from jax.experimental import pallas as pl
from jax.experimental.pallas import tpu as pltpu
from jax.sharding import PartitionSpec as P

D = 2048
HEADS = 32
HEAD_DIM = 64
ROT = 32
FF = 8192
LAYERS = 2


EPS = 1e-05
NEG = -1e30


def place_tokens(token_index, lengths):
    bounds = jnp.cumsum(lengths)
    starts = bounds - lengths
    segment = jnp.sum((token_index[:, None] >= bounds[None, :]).astype(jnp.int32), axis=1)
    chosen = segment[:, None] == jnp.arange(lengths.shape[0], dtype=jnp.int32)[None, :]
    position = token_index - jnp.sum(jnp.where(chosen, starts[None, :], 0), axis=1)
    return (segment, position)


def angles(position):
    indices = jnp.arange(0, ROT, 2, dtype=jnp.float32) / ROT
    inverse = 1.0 / 10000.0**indices
    turned = position.astype(jnp.float32)[:, None] * inverse[None, :]
    turned = jnp.concatenate([turned, turned], axis=1)
    return (jnp.cos(turned), jnp.sin(turned))


def rotate(values, cosine, sine):
    rotary = values[..., :ROT]
    middle = ROT // 2
    turned = jnp.concatenate([-rotary[..., middle:], rotary[..., :middle]], axis=-1)
    mixed = rotary * cosine[:, None, :] + turned * sine[:, None, :]
    return jnp.concatenate([mixed, values[..., ROT:]], axis=-1)


def normalize(hidden, gain_row, shift_row):
    average = jnp.mean(hidden, axis=1, keepdims=True)
    centred = hidden - average
    spread = jnp.mean(centred * centred, axis=1, keepdims=True)
    return centred * lax.rsqrt(spread + EPS) * gain_row + shift_row


def block_scores(queries, travelling, start, query_index, query_segment, lengths):
    key_flat, value_flat, key_keep = travelling
    count = key_flat.shape[0]
    key_index = start + jnp.arange(count, dtype=jnp.int32)
    key_segment = place_tokens(key_index, lengths)[0]
    allowed = (
        (query_segment[:, None] == key_segment[None, :])
        & (key_index[None, :] <= query_index[:, None])
        & ((key_keep[None, :] > 0) | (key_index[None, :] == query_index[:, None]))
    )
    key_rows = key_flat.reshape(count, HEADS, HEAD_DIM)
    value_rows = value_flat.reshape(count, HEADS, HEAD_DIM)
    scores = jnp.einsum("qhd,khd->hqk", queries, key_rows, preferred_element_type=jnp.float32) * (
        1.0 / math.sqrt(HEAD_DIM)
    )
    return (scores, allowed, key_rows, value_rows)


def attend(running, travelling, start, queries, query_index, query_segment, lengths):
    maxima, totals, weighted = running
    scores, allowed, key_rows, value_rows = block_scores(
        queries, travelling, start, query_index, query_segment, lengths
    )
    masked = jnp.where(allowed[None], scores, NEG)
    new_max = jnp.maximum(maxima, jnp.max(masked, axis=2))
    probs = jnp.where(allowed[None], jnp.exp(masked - new_max[:, :, None]), 0.0)
    totals = jnp.sum(probs, axis=2)
    weighted = jnp.einsum(
        "hqk,khd->hqd", probs.astype(jnp.bfloat16), value_rows, preferred_element_type=jnp.float32
    )
    return (new_max, totals, weighted)


def attend_back(
    travelling, start, queries, maxima, grad_numer, drift, query_index, query_segment, lengths
):
    scores, allowed, key_rows, value_rows = block_scores(
        queries, travelling, start, query_index, query_segment, lengths
    )
    count = key_rows.shape[0]
    scale = 1.0 / math.sqrt(HEAD_DIM)
    probs = jnp.where(allowed[None], jnp.exp(scores - maxima[:, :, None]), 0.0)
    grad_probs = jnp.einsum(
        "hqd,khd->hqk", grad_numer, value_rows, preferred_element_type=jnp.float32
    )
    grad_scores = (probs * (grad_probs - drift[:, :, None])).astype(jnp.bfloat16)
    grad_query = (
        jnp.einsum("hqk,khd->qhd", grad_scores, key_rows, preferred_element_type=jnp.float32)
        * scale
    )
    grad_key = (
        jnp.einsum("hqk,qhd->khd", grad_scores, queries, preferred_element_type=jnp.float32) * scale
    )
    grad_value = jnp.einsum(
        "hqk,hqd->khd", probs.astype(jnp.bfloat16), grad_numer, preferred_element_type=jnp.float32
    )
    return (
        grad_query,
        grad_key.reshape(count, HEADS * HEAD_DIM),
        grad_value.reshape(count, HEADS * HEAD_DIM),
    )


def attention_forward(queries, key_flat, value_flat, key_keep, query_index, query_segment, lengths):
    row_count = key_flat.shape[0]
    initial = (
        jnp.full((HEADS, row_count), NEG, jnp.float32),
        jnp.zeros((HEADS, row_count), jnp.float32),
        jnp.zeros((HEADS, row_count, HEAD_DIM), jnp.float32),
    )
    return attend(
        initial,
        (
            lax.all_gather(key_flat, "ctx", axis=0, tiled=True),
            lax.all_gather(value_flat, "ctx", axis=0, tiled=True),
            lax.all_gather(key_keep, "ctx", axis=0, tiled=True),
        ),
        jnp.int32(0),
        queries,
        query_index,
        query_segment,
        lengths,
    )


def attention_backward(
    queries,
    key_flat,
    value_flat,
    key_keep,
    maxima,
    grad_numer,
    drift,
    query_index,
    query_segment,
    lengths,
):
    whole = (
        lax.all_gather(key_flat, "ctx", axis=0, tiled=True),
        lax.all_gather(value_flat, "ctx", axis=0, tiled=True),
        lax.all_gather(key_keep, "ctx", axis=0, tiled=True),
    )
    grad_query, every_key, every_value = attend_back(
        whole, 0, queries, maxima, grad_numer, drift, query_index, query_segment, lengths
    )
    grad_key, grad_value = (
        lax.psum_scatter(
            every_key.astype(jnp.bfloat16), "ctx", scatter_dimension=0, tiled=True
        ).astype(jnp.float32),
        lax.psum_scatter(
            every_value.astype(jnp.bfloat16), "ctx", scatter_dimension=0, tiled=True
        ).astype(jnp.float32),
    )
    return (grad_query, grad_key, grad_value)


def layer_forward(hidden, weights, cosine, sine, key_keep, query_index, query_segment, lengths):
    (
        norm_gain,
        norm_shift,
        joint_weight,
        joint_bias,
        output_weight,
        output_bias,
        upper_weight,
        upper_bias,
        lower_weight,
        lower_bias,
    ) = weights
    row_count = hidden.shape[0]
    width = HEADS * HEAD_DIM
    normed = normalize(
        hidden, norm_gain.astype(jnp.float32), norm_shift.astype(jnp.float32)
    ).astype(jnp.bfloat16)
    joint = jnp.dot(normed, joint_weight, preferred_element_type=jnp.float32) + joint_bias.astype(
        jnp.float32
    )
    queries = rotate(joint[:, :width].reshape(row_count, HEADS, HEAD_DIM), cosine, sine).astype(
        jnp.bfloat16
    )
    key_flat = (
        rotate(joint[:, width : 2 * width].reshape(row_count, HEADS, HEAD_DIM), cosine, sine)
        .astype(jnp.bfloat16)
        .reshape(row_count, width)
    )
    value_flat = joint[:, 2 * width :].astype(jnp.bfloat16)
    maxima, totals, weighted = attention_forward(
        queries, key_flat, value_flat, key_keep, query_index, query_segment, lengths
    )
    mixed = (weighted / totals[:, :, None]).transpose(1, 0, 2).reshape(row_count, width)
    attention_out = jnp.dot(
        mixed.astype(jnp.bfloat16), output_weight, preferred_element_type=jnp.float32
    ) + output_bias.astype(jnp.float32)
    inner = jnp.dot(normed, upper_weight, preferred_element_type=jnp.float32) + upper_bias.astype(
        jnp.float32
    )
    activated = jax.nn.gelu(inner, approximate=True).astype(jnp.bfloat16)
    feed_out = jnp.dot(
        activated, lower_weight, preferred_element_type=jnp.float32
    ) + lower_bias.astype(jnp.float32)
    saved = (hidden, normed, queries, key_flat, value_flat, maxima, totals, mixed, inner, activated)
    return (hidden + (attention_out + feed_out), saved)


def layer_backward(
    grad_out, saved, weights, cosine, sine, key_keep, query_index, query_segment, lengths
):
    hidden, normed, queries, key_flat, value_flat, maxima, totals, mixed, inner, activated = saved
    (
        norm_gain,
        norm_shift,
        joint_weight,
        joint_bias,
        output_weight,
        output_bias,
        upper_weight,
        upper_bias,
        lower_weight,
        lower_bias,
    ) = weights
    row_count = hidden.shape[0]
    width = HEADS * HEAD_DIM
    ratio = FF // D
    grad_branch = grad_out.astype(jnp.bfloat16)
    mixed_low = mixed.astype(jnp.bfloat16)
    branch_bias = jnp.sum(grad_branch, axis=0, dtype=jnp.float32)
    grad_activated = jnp.einsum(
        "td,fd->tf", grad_branch, lower_weight, preferred_element_type=jnp.float32
    )
    gelu_pull = jax.vjp(functools.partial(jax.nn.gelu, approximate=True), inner)[1]
    grad_inner = gelu_pull(grad_activated)[0].astype(jnp.bfloat16)
    upper_bias_grad = jnp.sum(grad_inner, axis=0, dtype=jnp.float32)
    grad_normed = jnp.einsum(
        "tf,df->td", grad_inner, upper_weight, preferred_element_type=jnp.float32
    )
    upper_bias_rows = upper_bias_grad.reshape(D, ratio)
    normed_cols = normed
    upper_part = jnp.einsum(
        "tc,tf->cf", normed_cols, grad_inner, preferred_element_type=jnp.float32
    )
    lower_part = jnp.einsum(
        "tc,td->cd", activated, grad_branch, preferred_element_type=jnp.float32
    ).reshape(lax.axis_size(("ctx", "fsdp")) * (D // lax.axis_size(("ctx", "fsdp"))), ratio * width)
    bias_part = upper_bias_rows
    branch_part = branch_bias[:, None]
    feed_share = lax.psum_scatter(
        jnp.concatenate([upper_part, lower_part, bias_part, branch_part], axis=1),
        ("ctx", "fsdp"),
        scatter_dimension=0,
        tiled=True,
    )
    share_rows = feed_share.shape[0]
    upper_share = feed_share[:, :FF]
    lower_share = feed_share[:, FF : FF + ratio * width].reshape(share_rows * ratio, width)
    upper_bias_share = feed_share[:, FF + ratio * width : FF + ratio * width + ratio].reshape(
        share_rows * ratio
    )
    branch_share = feed_share[:, FF + ratio * width + ratio]
    feed_parts = (upper_share, upper_bias_share, lower_share, branch_share)
    output_share = None
    grad_mixed = jnp.einsum(
        "te,de->td", grad_branch, output_weight, preferred_element_type=jnp.float32
    )
    head_mixed = mixed.reshape(row_count, HEADS, HEAD_DIM).transpose(1, 0, 2)
    head_grad = grad_mixed.reshape(row_count, HEADS, HEAD_DIM).transpose(1, 0, 2)
    drift = jnp.sum(head_grad * head_mixed, axis=2) / totals
    grad_numer = (head_grad / totals[:, :, None]).astype(jnp.bfloat16)
    grad_query, grad_key, grad_value = attention_backward(
        queries,
        key_flat,
        value_flat,
        key_keep,
        maxima,
        grad_numer,
        drift,
        query_index,
        query_segment,
        lengths,
    )
    grad_query = rotate(grad_query, cosine, -sine).reshape(row_count, width)
    grad_key = rotate(grad_key.reshape(row_count, HEADS, HEAD_DIM), cosine, -sine).reshape(
        row_count, width
    )
    grad_joint = jnp.concatenate([grad_query, grad_key, grad_value], axis=1).astype(jnp.bfloat16)
    joint_bias_grad = jnp.sum(grad_joint, axis=0, dtype=jnp.float32)
    grad_normed = grad_normed + jnp.einsum(
        "te,de->td", grad_joint, joint_weight, preferred_element_type=jnp.float32
    )
    norm_pull = jax.vjp(
        normalize, hidden, norm_gain.astype(jnp.float32), norm_shift.astype(jnp.float32)
    )[1]
    grad_hidden, gain_grad, shift_grad = norm_pull(grad_normed)
    joint_bias_rows = joint_bias_grad.reshape(D, 3)
    normed_cols = normed
    joint_part = jnp.einsum(
        "tc,te->ce", normed_cols, grad_joint, preferred_element_type=jnp.float32
    )
    output_part = jnp.einsum(
        "tc,te->ce", mixed_low, grad_branch, preferred_element_type=jnp.float32
    )
    bias_part = joint_bias_rows
    gain_part = gain_grad[:, None]
    shift_part = shift_grad[:, None]
    attn_share = lax.psum_scatter(
        jnp.concatenate([joint_part, output_part, bias_part, gain_part, shift_part], axis=1),
        ("ctx", "fsdp"),
        scatter_dimension=0,
        tiled=True,
    )
    share_rows = attn_share.shape[0]
    joint_share = attn_share[:, : 3 * width]
    output_share = attn_share[:, 3 * width : 4 * width]
    joint_bias_share = attn_share[:, 4 * width : 4 * width + 3].reshape(share_rows * 3)
    gain_share = attn_share[:, 4 * width + 3]
    shift_share = attn_share[:, 4 * width + 4]
    attention_parts = (gain_share, shift_share, joint_share, joint_bias_share, output_share)
    return (grad_out + grad_hidden, attention_parts, feed_parts)


def on_device_gathered(
    tokens,
    doc_lengths,
    keep_mask,
    ln_gain,
    ln_bias,
    qkv_weight,
    qkv_bias,
    out_weight,
    out_bias,
    up_weight,
    up_bias,
    down_weight,
    down_bias,
    cotangent,
):
    row_count = tokens.shape[1]
    position = lax.axis_index("ctx")
    query_index = position * row_count + jnp.arange(row_count, dtype=jnp.int32)
    lengths = doc_lengths[0]
    query_segment, query_position = place_tokens(query_index, lengths)
    cosine, sine = angles(query_position)
    key_keep = keep_mask[0].astype(jnp.bfloat16)
    shards = (
        ln_gain,
        ln_bias,
        qkv_weight,
        qkv_bias,
        out_weight,
        out_bias,
        up_weight,
        up_bias,
        down_weight,
        down_bias,
    )

    def fetch(layer_index):
        return (
            lax.all_gather(shards[0][layer_index], ("ctx", "fsdp"), axis=0, tiled=True),
            lax.all_gather(shards[1][layer_index], ("ctx", "fsdp"), axis=0, tiled=True),
            lax.all_gather(shards[2][layer_index], ("ctx", "fsdp"), axis=0, tiled=True),
            lax.all_gather(shards[3][layer_index], ("ctx", "fsdp"), axis=0, tiled=True),
            lax.all_gather(shards[4][layer_index], ("ctx", "fsdp"), axis=0, tiled=True),
            lax.all_gather(shards[5][layer_index], ("ctx", "fsdp"), axis=0, tiled=True),
            lax.all_gather(shards[6][layer_index], ("ctx", "fsdp"), axis=0, tiled=True),
            lax.all_gather(shards[7][layer_index], ("ctx", "fsdp"), axis=0, tiled=True),
            lax.all_gather(shards[8][layer_index], ("ctx", "fsdp"), axis=0, tiled=True),
            lax.all_gather(shards[9][layer_index], ("ctx", "fsdp"), axis=0, tiled=True),
        )

    hidden = tokens[0].astype(jnp.float32)
    saved_layers = []
    weights = None
    for layer_index in range(LAYERS):
        weights = fetch(layer_index)
        hidden, saved = layer_forward(
            hidden, weights, cosine, sine, key_keep, query_index, query_segment, lengths
        )
        saved_layers.append(saved)
    result = hidden.astype(jnp.bfloat16)[None]
    grad_hidden = cotangent[0].astype(jnp.float32) * keep_mask[0].astype(jnp.float32)[:, None]
    attention_list = [None] * LAYERS
    feed_list = [None] * LAYERS
    for layer_index in reversed(range(LAYERS)):
        weights = weights if layer_index == LAYERS - 1 else fetch(layer_index)
        grad_hidden, attention_parts, feed_parts = layer_backward(
            grad_hidden,
            saved_layers[layer_index],
            weights,
            cosine,
            sine,
            key_keep,
            query_index,
            query_segment,
            lengths,
        )
        attention_list[layer_index] = attention_parts
        feed_list[layer_index] = feed_parts
    gain_stack = jnp.stack([attention_list[layer_index][0] for layer_index in range(LAYERS)])
    shift_stack = jnp.stack([attention_list[layer_index][1] for layer_index in range(LAYERS)])
    joint_stack = jnp.stack([attention_list[layer_index][2] for layer_index in range(LAYERS)])
    joint_bias_stack = jnp.stack([attention_list[layer_index][3] for layer_index in range(LAYERS)])
    output_stack = jnp.stack([attention_list[layer_index][4] for layer_index in range(LAYERS)])
    upper_stack = jnp.stack([feed_list[layer_index][0] for layer_index in range(LAYERS)])
    upper_bias_stack = jnp.stack([feed_list[layer_index][1] for layer_index in range(LAYERS)])
    lower_stack = jnp.stack([feed_list[layer_index][2] for layer_index in range(LAYERS)])
    branch_stack = jnp.stack([feed_list[layer_index][3] for layer_index in range(LAYERS)])
    summed = (
        lax.psum(gain_stack.astype(jnp.bfloat16), "seq").astype(jnp.float32),
        lax.psum(shift_stack.astype(jnp.bfloat16), "seq").astype(jnp.float32),
        lax.psum(joint_stack.astype(jnp.bfloat16), "seq").astype(jnp.float32),
        lax.psum(joint_bias_stack.astype(jnp.bfloat16), "seq").astype(jnp.float32),
        lax.psum(output_stack.astype(jnp.bfloat16), "seq").astype(jnp.float32),
        lax.psum(upper_stack.astype(jnp.bfloat16), "seq").astype(jnp.float32),
        lax.psum(upper_bias_stack.astype(jnp.bfloat16), "seq").astype(jnp.float32),
        lax.psum(lower_stack.astype(jnp.bfloat16), "seq").astype(jnp.float32),
        lax.psum(branch_stack.astype(jnp.bfloat16), "seq").astype(jnp.float32),
    )
    return (
        result,
        grad_hidden[None],
        summed[0],
        summed[1],
        summed[2],
        summed[3],
        summed[4],
        summed[8],
        summed[5],
        summed[6],
        summed[7],
        summed[8],
    )


SIDE = 4
GROUP = SIDE * SIDE
OWN = HEADS // GROUP
HEAD_COLS = OWN * HEAD_DIM
JOINT_COLS = 3 * HEAD_COLS
FEED_COLS = FF // GROUP
COLS = JOINT_COLS + FEED_COLS
BACK_COLS = HEAD_COLS + FEED_COLS
SHARE = D // GROUP
VMEM = pl.BlockSpec(memory_space=pltpu.VMEM)
HBM = pl.BlockSpec(memory_space=pl.ANY)
MESH = pl.DeviceIdType.MESH
ROOM = 60 * 2**20


def dot(left, right, left_dim=1, right_dim=0):
    return lax.dot_general(
        left, right, (((left_dim,), (right_dim,)), ((), ())), preferred_element_type=jnp.float32
    )


def digit(entries, index):
    words = [
        sum(entry << (2 * place) for place, entry in enumerate(entries[start : start + 8]))
        for start in range(0, len(entries), 8)
    ]
    word = jnp.int32(words[0])
    for number in range(1, len(words)):
        word = jnp.where(index >= 8 * number, jnp.int32(words[number]), word)
    return lax.rem(lax.shift_right_logical(word, 2 * lax.rem(index, 8)), 4)


def nibble(entries, index):
    word = jnp.int32(0)
    for start in range(0, len(entries), 7):
        packed = sum(entry << (4 * place) for place, entry in enumerate(entries[start : start + 7]))
        word = jnp.where(index >= start, jnp.int32(packed), word)
    return lax.rem(lax.shift_right_logical(word, 4 * lax.rem(index, 7)), 16)


def digit_of_row(table, row, index):
    value = digit(table[0], index)
    for number in range(1, len(table)):
        value = jnp.where(row == number, digit(table[number], index), value)
    return value


NEAR = ((0, 1, 2, 3), (1, 0, 2, 3), (2, 3, 1, 0), (3, 2, 1, 0))
FAR = ((3, 2, 1, 0), (3, 0, 2, 1), (0, 3, 1, 2), (0, 1, 2, 3))


def neighbours():
    ctx, place = lax.axis_index("ctx"), lax.axis_index("fsdp")
    twin = ctx + 1 - 2 * lax.rem(ctx, 2)
    across = lax.rem(ctx + 2, 4)
    return ctx, place, twin, across, lax.rem(twin + 2, 4)


def greet_neighbours(cross=False):
    ctx, place, twin, across, _ = neighbours()
    barrier = pltpu.get_barrier_semaphore()
    pl.semaphore_signal(barrier, inc=1, device_id={"ctx": twin}, device_id_type=MESH)
    pl.semaphore_signal(barrier, inc=1, device_id={"ctx": across}, device_id_type=MESH)

    @pl.when(place > 0)
    def _():
        pl.semaphore_signal(barrier, inc=1, device_id={"fsdp": place - 1}, device_id_type=MESH)

    @pl.when(place < SIDE - 1)
    def _():
        pl.semaphore_signal(barrier, inc=1, device_id={"fsdp": place + 1}, device_id_type=MESH)

    if cross:
        pl.semaphore_signal(
            barrier, inc=1, device_id={"seq": 1 - lax.axis_index("seq")}, device_id_type=MESH
        )
    inner = jnp.int32(3 if cross else 2) + jnp.where(place > 0, 1, 0) + jnp.where(place < SIDE - 1, 1, 0)
    pl.semaphore_wait(barrier, inner)


def greet_plane(steps, cross=True):
    ctx, place = lax.axis_index("ctx"), lax.axis_index("fsdp")
    me = ctx * SIDE + place
    barrier = pltpu.get_barrier_semaphore()
    for step in range(1, steps):
        peer = lax.rem(me + step, GROUP)
        pl.semaphore_signal(
            barrier,
            inc=1,
            device_id={"ctx": peer // SIDE, "fsdp": lax.rem(peer, SIDE)},
            device_id_type=MESH,
        )
    if cross:
        pl.semaphore_signal(
            barrier, inc=1, device_id={"seq": 1 - lax.axis_index("seq")}, device_id_type=MESH
        )
    pl.semaphore_wait(barrier, steps if cross else steps - 1)


def to_peer(source, target, send, recv, peer):
    return pltpu.make_async_remote_copy(
        src_ref=source,
        dst_ref=target,
        send_sem=send,
        recv_sem=recv,
        device_id={"ctx": peer // SIDE, "fsdp": lax.rem(peer, SIDE)},
        device_id_type=MESH,
    )


def to_axis(source, target, send, recv, axis, index):
    return pltpu.make_async_remote_copy(
        src_ref=source,
        dst_ref=target,
        send_sem=send,
        recv_sem=recv,
        device_id={axis: index},
        device_id_type=MESH,
    )


PARTS = ((0, 112), (112, 96), (208, 48))
LAST = len(PARTS) - 1
GATHER_KIND = (
    (0, 0, 0, 0, 0, 1, 0, 0, 1, 0, 2, 0, 1, 1, 1, 2, 0, 0, 1, 0, 1, 3, 2, 1, 0, 3, 1, 1, 1, 1, 0, 3, 0, 0, 1, 1, 1, 1, 2, 3),
    (0, 0, 0, 1, 0, 0, 0, 0, 0, 0, 0, 0, 1, 0, 2, 1, 2, 1, 0, 1, 1, 2, 0, 3, 1, 1, 0, 1, 1, 1, 3, 1, 1, 0, 1, 3, 1, 1, 2, 3),
)
GATHER_STEP = (
    (0, 0, 1, 0, 0, 0, 1, 1, 0, 1, 0, 2, 0, 0, 1, 1, 2, 2, 1, 2, 1, 0, 2, 1, 3, 1, 2, 2, 2, 2, 3, 2, 3, 3, 3, 3, 3, 3, 3, 3),
    (0, 0, 0, 0, 2, 2, 1, 0, 1, 2, 1, 1, 0, 2, 0, 0, 2, 0, 3, 2, 2, 1, 3, 0, 2, 1, 3, 1, 2, 1, 2, 3, 1, 3, 3, 1, 3, 3, 3, 3),
)
GATHER_PART = (
    (1, 0, 1, 2, 3, 1, 2, 0, 0, 3, 3, 2, 2, 3, 0, 3, 1, 0, 1, 3, 2, 3, 3, 3, 0, 3, 1, 2, 0, 3, 1, 3, 2, 3, 1, 0, 2, 3, 3, 3),
    (1, 0, 2, 0, 2, 0, 2, 3, 1, 1, 0, 3, 2, 3, 3, 1, 3, 3, 0, 0, 2, 3, 1, 3, 1, 1, 2, 2, 3, 0, 3, 2, 3, 3, 0, 3, 1, 3, 3, 3),
)
FIRST_KIND = (
    (0, 0, 0, 0, 0, 0, 0, 0, 0, 1, 3, 2, 3, 2, 0, 1, 3, 1, 0, 1, 0, 0, 0, 1, 1, 0, 0, 3, 0, 0, 2, 2, 0, 1, 0, 0, 1, 1, 1, 0, 0, 1, 1, 2, 2, 3, 3, 0, 1, 0, 0, 0, 0, 1, 1, 3, 2, 1, 0, 1, 1, 2, 0, 2, 2, 0, 1, 3, 0, 1, 0, 0, 3, 3, 2, 1, 1, 1, 2, 1, 3, 3),
    (0, 0, 0, 0, 0, 2, 0, 0, 0, 1, 0, 0, 2, 1, 3, 1, 1, 0, 2, 0, 3, 3, 0, 0, 0, 0, 0, 0, 1, 1, 0, 1, 0, 0, 2, 3, 1, 2, 0, 1, 0, 0, 0, 1, 0, 1, 0, 2, 0, 1, 1, 1, 3, 2, 2, 3, 0, 3, 1, 0, 0, 0, 1, 2, 0, 0, 1, 1, 1, 1, 1, 3, 2, 3, 1, 2, 1, 1, 3, 3, 2, 3),
)
FIRST_STEP = (
    (0, 0, 1, 2, 3, 3, 0, 0, 0, 3, 0, 0, 2, 1, 0, 0, 1, 1, 0, 0, 0, 1, 1, 0, 0, 2, 2, 3, 1, 1, 2, 3, 3, 2, 1, 2, 0, 1, 1, 2, 1, 1, 1, 0, 1, 0, 1, 0, 1, 2, 1, 0, 2, 2, 0, 0, 1, 2, 3, 2, 2, 2, 2, 2, 0, 3, 2, 1, 3, 3, 3, 3, 2, 2, 3, 3, 3, 3, 3, 3, 3, 3),
    (0, 1, 2, 0, 0, 0, 2, 1, 3, 0, 0, 0, 3, 3, 1, 2, 0, 3, 1, 0, 2, 0, 0, 1, 2, 0, 2, 1, 1, 0, 1, 0, 3, 2, 0, 3, 1, 2, 1, 0, 2, 0, 1, 0, 3, 1, 2, 0, 0, 1, 1, 2, 0, 1, 1, 1, 3, 1, 2, 3, 2, 1, 2, 2, 3, 3, 2, 3, 1, 2, 3, 0, 2, 2, 3, 3, 3, 3, 3, 3, 3, 2),
)
FIRST_WHAT = (
    (5, 4, 4, 4, 9, 4, 0, 9, 2, 9, 9, 9, 9, 9, 1, 2, 9, 9, 6, 0, 3, 1, 6, 1, 3, 9, 6, 9, 0, 9, 9, 9, 6, 9, 2, 1, 9, 1, 2, 2, 3, 0, 3, 3, 3, 3, 3, 7, 8, 0, 8, 8, 3, 1, 8, 8, 8, 0, 0, 2, 3, 3, 8, 8, 8, 1, 8, 8, 2, 0, 3, 8, 3, 8, 3, 2, 1, 3, 8, 8, 3, 8),
    (4, 4, 4, 5, 0, 9, 9, 9, 9, 0, 9, 1, 9, 9, 9, 9, 9, 4, 9, 6, 9, 9, 2, 6, 1, 3, 6, 0, 9, 2, 1, 1, 6, 2, 3, 9, 0, 9, 2, 3, 0, 7, 3, 8, 0, 2, 3, 8, 8, 1, 3, 2, 3, 3, 8, 3, 1, 8, 0, 2, 8, 8, 1, 3, 3, 8, 3, 2, 8, 8, 1, 8, 8, 3, 0, 3, 3, 8, 3, 8, 8, 8),
)
OPS = len(GATHER_KIND[0])
WORKS = tuple(
    tuple(
        number for number in range(OPS) if parts[number] == 3
    )
    for parts in GATHER_PART
)


def by_place(tables, index):
    place = lax.axis_index("fsdp")
    at_end = (place == 0) | (place == SIDE - 1)
    return jnp.where(at_end, digit(tables[0], index), digit(tables[1], index))


def gather_slot(kind, step):
    ctx, place, twin, across, twin_across = neighbours()
    line = digit_of_row(NEAR, place, step)
    owner = jnp.where(
        kind == 0, ctx, jnp.where(kind == 1, across, jnp.where(kind == 2, twin, twin_across))
    )
    return line, owner * SIDE + line


def work_slot(number):
    kind = by_place(
        tuple(tuple(row[at] for at in places) for row, places in zip(GATHER_KIND, WORKS)), number
    )
    step = by_place(
        tuple(tuple(row[at] for at in places) for row, places in zip(GATHER_STEP, WORKS)), number
    )
    return gather_slot(kind, step)[1]


def gather_blocks(
    land, every, up, down, side, core, arrived, core_arrived, kept, work, tables=None, more=()
):
    ctx, place, twin, across, _ = neighbours()
    kinds, steps, parts = tables or (GATHER_KIND, GATHER_STEP, GATHER_PART)
    at_end = (place == 0) | (place == SIDE - 1)

    def copies(kind, line, slot, part):
        start, size = PARTS[part]
        block = land.at[slot, pl.ds(start, size)]
        row, met = kind * SIDE + line, arrived.at[slot, part]
        return (
            lambda: to_axis(block, block, up.at[row, part], met, "fsdp", place + 1),
            lambda: to_axis(block, block, down.at[row, part], met, "fsdp", place - 1),
            lambda: to_axis(block, block, side.at[line, part], met, "ctx", across),
        )

    def routes(kind, line, part):
        goes_up = (line <= place) & (place < SIDE - 1)
        goes_down = (line >= place) & (place > 0)
        if part == LAST:
            return goes_up, goes_down, (kind == 0) & (line == place)
        return goes_up & (kind == 0), goes_down & (kind == 0), kind == 0

    def core_copy(kind, line, slot):
        block = land.at[slot]
        return to_axis(
            block, block, core.at[kind * SIDE + line], core_arrived.at[slot], "ctx", twin
        )

    def step_op(number, counts):
        worked, made = counts
        kind, step = by_place(kinds, number), by_place(steps, number)
        part = jnp.where(at_end, nibble(parts[0], number), nibble(parts[1], number))
        line, slot = gather_slot(kind, step)
        for which in range(len(PARTS)):

            @pl.when(part == which)
            def _(which=which):
                @pl.when((kind == 1) | (line != place))
                def _():
                    copies(kind, line, slot, which)[2]().wait_recv()

                for copy, goes in zip(
                    copies(kind, line, slot, which), routes(kind, line, which)
                ):

                    @pl.when(goes)
                    def _(copy=copy):
                        copy().start()

        @pl.when(part == 3)
        def _():
            @pl.when(kind <= 1)
            def _():
                core_copy(kind, line, slot).start()

            @pl.when(kind >= 2)
            def _():
                core_copy(kind - 2, line, slot).wait_recv()

            if every is not None:
                pltpu.make_async_copy(land.at[slot], every.at[slot], kept.at[slot]).start()
            work(worked, slot)

        for which, further in enumerate(more):

            @pl.when(part == 4 + which)
            def _(further=further):
                further(step, slot, made)

        return worked + jnp.where(part == 3, 1, 0), made + jnp.where(part == 8, 1, 0)

    lax.fori_loop(0, len(kinds[0]), step_op, (jnp.int32(0), jnp.int32(0)))

    def finish(number, carry):
        kind, line = number // SIDE, lax.rem(number, SIDE)
        slot = jnp.where(kind == 0, ctx, across) * SIDE + line
        for which in range(len(PARTS)):
            for copy, goes in zip(copies(kind, line, slot, which), routes(kind, line, which)):

                @pl.when(goes)
                def _(copy=copy):
                    copy().wait_send()

        core_copy(kind, line, slot).wait_send()
        return carry

    lax.fori_loop(0, 2 * SIDE, finish, 0)

    def finish_kept(slot, carry):
        pltpu.make_async_copy(land.at[slot], every.at[slot], kept.at[slot]).wait()
        return carry

    if every is not None:
        lax.fori_loop(0, GROUP, finish_kept, 0)


def gather_scratch(rows):
    parts = len(PARTS)
    return [
        pltpu.VMEM((GROUP, rows, D), jnp.bfloat16),
        pltpu.SemaphoreType.DMA((2 * SIDE, parts)),
        pltpu.SemaphoreType.DMA((2 * SIDE, parts)),
        pltpu.SemaphoreType.DMA((SIDE, parts)),
        pltpu.SemaphoreType.DMA((2 * SIDE,)),
        pltpu.SemaphoreType.DMA((GROUP, parts)),
        pltpu.SemaphoreType.DMA((GROUP,)),
        pltpu.SemaphoreType.DMA((GROUP,)),
    ]


def spin(values, cosine, sine, sign):
    lane = lax.rem(lax.broadcasted_iota(jnp.int32, values.shape, 1), HEAD_DIM)
    partner = jnp.where(
        lane < ROT // 2,
        -pltpu.roll(values, HEAD_COLS - ROT // 2, 1),
        pltpu.roll(values, ROT // 2, 1),
    )
    return values * cosine + sign * (partner * sine)


STRIP = 32


def each_strip(rows, body, start):
    def step(number, carry):
        return body(pl.ds(pl.multiple_of(number * STRIP, STRIP), STRIP), carry)

    return lax.fori_loop(0, rows // STRIP, step, start)


def column_places(block):
    return [
        (0, pl.multiple_of(part * D + block * HEAD_COLS, HEAD_COLS), part * HEAD_COLS, HEAD_COLS)
        for part in range(3)
    ] + [(1, pl.multiple_of(block * FEED_COLS, FEED_COLS), JOINT_COLS, FEED_COLS)]


PLACES = 4


def plane_swap(swap, sems):
    source, target = swap
    return to_axis(source, target, sems.at[0], sems.at[1], "seq", 1 - lax.axis_index("seq"))


def row_swap(source, target, sems, first, blocks):
    size = source.shape[0] // SWAP_BLOCKS
    return [
        to_axis(
            source.at[pl.ds(block * size, size)],
            target.at[pl.ds((block - first) * size, size)],
            sems.at[0, block],
            sems.at[1, block],
            "seq",
            1 - lax.axis_index("seq"),
        )
        for block in blocks
    ]


SWAP_BLOCKS = 4
SWAP_FIRST = SWAP_BLOCKS // 2


def load_all(pairs, sems):
    copies = [
        pltpu.make_async_copy(source, target, sems.at[number])
        for number, (source, target) in enumerate(pairs)
    ]
    for copy in copies:
        copy.start()
    return copies


def wait_all(copies):
    for copy in copies:
        copy.wait()


def ring_scratch(rows):
    return [
        pltpu.VMEM((2, rows, HEAD_COLS), jnp.bfloat16),
        pltpu.VMEM((2, rows, HEAD_COLS), jnp.bfloat16),
        pltpu.VMEM((2, rows, HEAD_COLS), jnp.bfloat16),
        pltpu.VMEM((2, rows, FEED_COLS), jnp.float32),
        pltpu.VMEM((2, rows, FEED_COLS), jnp.bfloat16),
        pltpu.SemaphoreType.DMA((2, 5)),
    ]


def ring_shapes(rows):
    return [
        jax.ShapeDtypeStruct((GROUP, rows, width), dtype)
        for width, dtype in (
            (HEAD_COLS, jnp.bfloat16),
            (HEAD_COLS, jnp.bfloat16),
            (HEAD_COLS, jnp.bfloat16),
            (FEED_COLS, jnp.float32),
            (FEED_COLS, jnp.bfloat16),
        )
    ]


def ring_product(rings, sems, results, land, columns, bias, cosine, sine):
    query, key, value, inner, active = rings

    def leave(at, slot):
        return [
            pltpu.make_async_copy(ring.at[at], result.at[slot], sems.at[at, which])
            for which, (ring, result) in enumerate(zip(rings, results))
        ]

    def product(number, slot):
        whole = dot(land[slot], columns[...].reshape(D, COLS)) + bias[...]
        one, two = HEAD_COLS, 2 * HEAD_COLS
        at = lax.rem(number, 2)

        @pl.when(number >= 2)
        def _():
            wait_all(leave(at, 0))

        query[at] = spin(whole[:, :one], cosine[slot], sine[slot], 1.0).astype(jnp.bfloat16)
        key[at] = spin(whole[:, one:two], cosine[slot], sine[slot], 1.0).astype(jnp.bfloat16)
        value[at] = whole[:, two:JOINT_COLS].astype(jnp.bfloat16)
        units = whole[:, JOINT_COLS:]
        inner[at] = units
        active[at] = jax.nn.gelu(units, approximate=True).astype(jnp.bfloat16)
        for copy in leave(at, slot):
            copy.start()

    def finish():
        for at in range(2):
            wait_all(leave(at, 0))

    return product, finish


def norm_block(hidden, gain, shift, land, me):
    def strip(part, carry):
        values = hidden[part].astype(jnp.float32)
        centred = values - jnp.mean(values, axis=1, keepdims=True)
        spread = jnp.mean(centred * centred, axis=1, keepdims=True)
        normed = centred * lax.rsqrt(spread + EPS) * gain[...] + shift[...]
        land[me, part] = normed.astype(jnp.bfloat16)
        return carry

    each_strip(hidden.shape[0], strip, 0)


def forward_gather(hidden, gain, shift, bias, tables, halves, layer):
    rows = hidden.shape[0]
    half = SHARE // 2

    def kernel(hidden, gain, shift, bias, turn_a, turn_b, own_half, other_half, *refs):
        every, columns_out, results, refs = refs[0], refs[1], refs[2:7], refs[7:]
        cosine, sine, columns, load_sem, saved = refs[:5]
        rings, ring_sem, refs = refs[5:10], refs[10], refs[11:]
        land, sems = refs[0], refs[1:]
        ctx, place, seq = lax.axis_index("ctx"), lax.axis_index("fsdp"), lax.axis_index("seq")
        part_rows = pl.ds(pl.multiple_of(seq * half, half), half)
        other_rows = pl.ds(pl.multiple_of((1 - seq) * half, half), half)
        loads = load_all(
            (
                (own_half, columns.at[:, part_rows]),
                (other_half, columns.at[:, other_rows]),
                (turn_a, cosine),
                (turn_b, sine),
            ),
            load_sem,
        )
        greet_neighbours()
        norm_block(hidden, gain, shift, land, ctx * SIDE + place)
        save = pltpu.make_async_copy(columns, columns_out, saved)
        product, finish = ring_product(rings, ring_sem, results, land, columns, bias, cosine, sine)

        def work(number, slot):
            @pl.when(number == 0)
            def _():
                wait_all(loads)
                save.start()

            product(number, slot)

        gather_blocks(land, every, *sems, work)
        save.wait()
        finish()

    return pl.pallas_call(
        kernel,
        out_shape=[
            jax.ShapeDtypeStruct((GROUP, rows, D), jnp.bfloat16),
            jax.ShapeDtypeStruct((GROUP, SHARE, COLS), jnp.bfloat16),
        ]
        + ring_shapes(rows),
        in_specs=[VMEM] * 4 + [HBM] * 4,
        out_specs=[HBM] * 7,
        scratch_shapes=[pltpu.VMEM((GROUP, rows, HEAD_COLS), jnp.float32)] * 2
        + [
            pltpu.VMEM((GROUP, SHARE, COLS), jnp.bfloat16),
            pltpu.SemaphoreType.DMA((4,)),
            pltpu.SemaphoreType.DMA,
        ]
        + ring_scratch(rows)
        + gather_scratch(rows),
        compiler_params=pltpu.CompilerParams(
            collective_id=30 + layer, has_side_effects=True, vmem_limit_bytes=ROOM
        ),
    )(hidden, gain, shift, bias, *tables, *halves)


GAIN_ROW, SHIFT_ROW, JOINT_BIAS_ROW, OUT_BIAS_ROW, DOWN_BIAS_ROW, LAYER_ROWS = 0, 1, 2, 5, 6, 7
BEGIN_ROW = LAYERS * LAYER_ROWS


def first_gather(hidden, packed, up_bias, frequency, qkv_weight, up_weight):
    rows = hidden.shape[0]
    half = SHARE // 2

    def kernel(hidden, packed, up_bias, frequency, qkv_weight, up_weight, *refs):
        every, columns_out, results, small, cosine, sine = refs[0], refs[1], refs[2:7], *refs[7:10]
        refs = refs[10:]
        columns, plane_send, plane_recv, cross_send, cross_recv, own_sem, saved = refs[:7]
        small_send, small_recv, gain, shift, bias = refs[7:12]
        rings, ring_sem, refs = refs[12:17], refs[17], refs[18:]
        land, sems = refs[0], refs[1:]
        ctx, place, seq = lax.axis_index("ctx"), lax.axis_index("fsdp"), lax.axis_index("seq")
        me = ctx * SIDE + place
        part_rows = pl.ds(pl.multiple_of(seq * half, half), half)
        sources = (qkv_weight, up_weight)
        greet_plane(GROUP)

        def small_copy(step):
            return to_peer(
                packed,
                small.at[me],
                small_send.at[step],
                small_recv.at[me],
                lax.rem(me + step, GROUP),
            )

        def small_begin(step, carry):
            small_copy(step).start()
            return carry

        lax.fori_loop(1, GROUP, small_begin, 0)
        small[me] = packed[...]

        def piece(step, number):
            peer = lax.rem(me + step, GROUP)
            which, start, at, width = column_places(peer)[number]
            return (
                peer,
                sources[which].at[0, part_rows, pl.ds(start, width)],
                columns.at[me, part_rows, pl.ds(at, width)],
            )

        def send_piece(step, number):
            peer, source, target = piece(step, number)
            return to_peer(
                source, target, plane_send.at[step, number], plane_recv.at[me, number], peer
            )

        def own_piece(number):
            _, source, target = piece(0, number)
            return pltpu.make_async_copy(source, target, own_sem.at[number])

        def cross(source):
            block = columns.at[source, part_rows]
            return to_axis(
                block, block, cross_send.at[source], cross_recv.at[source], "seq", 1 - seq
            )

        for number in range(PLACES):
            own_piece(number).start()

        def send_columns(group, slot, made):
            def send(more, carry):
                step = SIDE * group + more

                @pl.when(step > 0)
                def _():
                    for number in range(PLACES):
                        send_piece(step, number).start()

                return carry

            lax.fori_loop(0, SIDE, send, 0)

        def norm_own(group, slot, made):
            def arrive(step, carry):
                source = lax.rem(me + GROUP - step, GROUP)
                to_peer(
                    packed, small.at[source], small_send.at[step], small_recv.at[source], source
                ).wait_recv()
                return carry

            lax.fori_loop(1, GROUP, arrive, 0)

            def whole_row(row):
                return jnp.concatenate(
                    [small[block, row : row + 1] for block in range(GROUP)], axis=1
                )

            gain[...] = whole_row(GAIN_ROW)
            shift[...] = whole_row(SHIFT_ROW)
            for part in range(3):
                at = part * GROUP + me
                bias[:, part * HEAD_COLS : (part + 1) * HEAD_COLS] = small[
                    at // 3, pl.ds(JOINT_BIAS_ROW + lax.rem(at, 3), 1)
                ]
            bias[:, JOINT_COLS:] = up_bias[...]
            norm_block(hidden, gain, shift, land, me)

        def pass_columns(group, slot, made):
            def pass_on(more, carry):
                step = SIDE * group + more
                source = lax.rem(me + GROUP - step, GROUP)

                @pl.when(step == 0)
                def _():
                    for number in range(PLACES):
                        own_piece(number).wait()

                @pl.when(step > 0)
                def _():
                    for number in range(PLACES):
                        _, _, at, width = column_places(0)[number]
                        target = columns.at[source, part_rows, pl.ds(at, width)]
                        to_peer(
                            target,
                            target,
                            plane_send.at[0, number],
                            plane_recv.at[source, number],
                            source,
                        ).wait_recv()

                cross(source).start()
                return carry

            lax.fori_loop(0, SIDE, pass_on, 0)

        save = pltpu.make_async_copy(columns, columns_out, saved)

        def wait_columns(group, slot, made):
            def arrive(source, carry):
                cross(source).wait_recv()
                return carry

            lax.fori_loop(0, GROUP, arrive, 0)
            save.start()

        product, finish = ring_product(rings, ring_sem, results, land, columns, bias, cosine, sine)

        def next_product(group, slot, made):
            product(made, slot)

        def turn_block(group, slot, made):
            begin = jnp.concatenate(
                [small[slot, BEGIN_ROW + part : BEGIN_ROW + part + 1] for part in range(rows // SHARE)],
                axis=1,
            )
            begin = jnp.broadcast_to(begin, (8, rows)).T[:, :1]
            first = (slot // SIDE) * rows
            token = lax.broadcasted_iota(jnp.int32, (rows, 1), 0) + first
            angle = (token.astype(jnp.float32) - begin) * frequency[...]
            cosine[slot] = jnp.cos(angle)
            sine[slot] = jnp.sin(angle)

        gather_blocks(
            land,
            every,
            *sems,
            lambda number, slot: None,
            (FIRST_KIND, FIRST_STEP, FIRST_WHAT),
            (send_columns, norm_own, pass_columns, wait_columns, next_product, turn_block),
        )
        save.wait()
        finish()

        def end(step, carry):
            cross(step).wait_send()

            @pl.when(step > 0)
            def _():
                small_copy(step).wait_send()
                for number in range(PLACES):
                    send_piece(step, number).wait_send()

            return carry

        lax.fori_loop(0, GROUP, end, 0)

    return pl.pallas_call(
        kernel,
        out_shape=[
            jax.ShapeDtypeStruct((GROUP, rows, D), jnp.bfloat16),
            jax.ShapeDtypeStruct((GROUP, SHARE, COLS), jnp.bfloat16),
        ]
        + ring_shapes(rows)
        + [jax.ShapeDtypeStruct((GROUP,) + packed.shape, packed.dtype)]
        + [jax.ShapeDtypeStruct((GROUP, rows, HEAD_COLS), jnp.float32)] * 2,
        in_specs=[VMEM] * 4 + [HBM] * 2,
        out_specs=[HBM] * 7 + [VMEM] * 3,
        scratch_shapes=[
            pltpu.VMEM((GROUP, SHARE, COLS), jnp.bfloat16),
            pltpu.SemaphoreType.DMA((GROUP, PLACES)),
            pltpu.SemaphoreType.DMA((GROUP, PLACES)),
            pltpu.SemaphoreType.DMA((GROUP,)),
            pltpu.SemaphoreType.DMA((GROUP,)),
            pltpu.SemaphoreType.DMA((PLACES,)),
            pltpu.SemaphoreType.DMA,
            pltpu.SemaphoreType.DMA((GROUP,)),
            pltpu.SemaphoreType.DMA((GROUP,)),
            pltpu.VMEM((1, D), jnp.float32),
            pltpu.VMEM((1, D), jnp.float32),
            pltpu.VMEM((1, COLS), jnp.float32),
        ]
        + ring_scratch(rows)
        + gather_scratch(rows),
        compiler_params=pltpu.CompilerParams(
            collective_id=30, has_side_effects=True, vmem_limit_bytes=ROOM
        ),
    )(hidden, packed, up_bias, frequency, qkv_weight, up_weight)


def backward_gather(grad, out_weight, down_weight, inner, mixed, active, layer, swap=()):
    rows = grad.shape[0]

    def kernel(own, out_weight, down_weight, inner, mixed, active, *refs):
        if swap:
            source, grad_mixed, grad_inner, branch, target, swap_sem = refs[:6]
            refs = refs[6:]
        else:
            grad_mixed, grad_inner, branch = refs[:3]
            refs = refs[3:]
        out_part, down_part, weight_sem, total = refs[:4]
        fetched, fetch_sem, rings, ring_sem = refs[4:7], refs[7], refs[8:10], refs[10]
        land, sems = refs[11], refs[12:]
        inner_part, mixed_part, active_part = fetched
        ctx, place, _, _, _ = neighbours()

        def fetch(number):
            at, slot = lax.rem(number, 2), work_slot(number)
            return [
                pltpu.make_async_copy(source.at[slot], target.at[at], fetch_sem.at[at, which])
                for which, (source, target) in enumerate(zip((inner, mixed, active), fetched))
            ]

        def leave(number):
            at, slot = lax.rem(number, 2), work_slot(number)
            return [
                pltpu.make_async_copy(ring.at[at], result.at[slot], ring_sem.at[at, which])
                for which, (ring, result) in enumerate(zip(rings, (grad_mixed, grad_inner)))
            ]

        weights = load_all(
            ((out_weight.at[layer], out_part), (down_weight.at[layer], down_part)), weight_sem
        )
        for copy in fetch(jnp.int32(0)):
            copy.start()
        greet_neighbours(bool(swap))
        if swap:
            plane_swap((source, target), swap_sem).start()
        land[ctx * SIDE + place] = own[...]
        total[...] = jnp.zeros_like(total)

        def work(number, slot):
            at = lax.rem(number, 2)

            @pl.when(number == 0)
            def _():
                wait_all(weights)

            @pl.when(number + 1 < GROUP)
            def _():
                for copy in fetch(number + 1):
                    copy.start()

            @pl.when(number >= 2)
            def _():
                wait_all(leave(number - 2))

            wait_all(fetch(number))
            block = land[slot]
            rings[0][at] = dot(block, out_part[...], 1, 1)
            value = inner_part[at]
            factor = math.sqrt(2.0 / math.pi)
            square = value * value
            bend = jnp.tanh(factor * value * (1.0 + 0.044715 * square))
            slope = 0.5 * (1.0 + bend) + 0.5 * value * (1.0 - bend * bend) * (
                factor * (1.0 + 3 * 0.044715 * square)
            )
            rings[1][at] = (dot(block, down_part[...], 1, 1) * slope).astype(jnp.bfloat16)
            for copy in leave(number):
                copy.start()
            total[:HEAD_COLS] += dot(mixed_part[at], block, 0, 0)
            total[HEAD_COLS:] += dot(active_part[at], block, 0, 0)

        gather_blocks(land, None, *sems, work)
        branch[...] = total[...].astype(jnp.bfloat16)
        if swap:
            plane_swap((source, target), swap_sem).wait()
        for number in (GROUP - 2, GROUP - 1):
            wait_all(leave(jnp.int32(number)))

    return pl.pallas_call(
        kernel,
        out_shape=(
            jax.ShapeDtypeStruct((GROUP, rows, HEAD_COLS), jnp.float32),
            jax.ShapeDtypeStruct((GROUP, rows, FEED_COLS), jnp.bfloat16),
            jax.ShapeDtypeStruct((BACK_COLS, D), jnp.bfloat16),
        )
        + tuple(jax.ShapeDtypeStruct(array.shape, array.dtype) for array in swap),
        in_specs=[VMEM] + [HBM] * (5 + len(swap)),
        out_specs=(HBM, HBM, VMEM) + (HBM,) * len(swap),
        scratch_shapes=[pltpu.SemaphoreType.DMA((2,))] * len(swap)
        + [
            pltpu.VMEM(out_weight.shape[1:], jnp.bfloat16),
            pltpu.VMEM(down_weight.shape[1:], jnp.bfloat16),
            pltpu.SemaphoreType.DMA((2,)),
            pltpu.VMEM((BACK_COLS, D), jnp.float32),
            pltpu.VMEM((2, rows, FEED_COLS), jnp.float32),
            pltpu.VMEM((2, rows, HEAD_COLS), jnp.bfloat16),
            pltpu.VMEM((2, rows, FEED_COLS), jnp.bfloat16),
            pltpu.SemaphoreType.DMA((2, 3)),
            pltpu.VMEM((2, rows, HEAD_COLS), jnp.float32),
            pltpu.VMEM((2, rows, FEED_COLS), jnp.bfloat16),
            pltpu.SemaphoreType.DMA((2, 2)),
        ]
        + gather_scratch(rows),
        compiler_params=pltpu.CompilerParams(
            collective_id=50 + layer, has_side_effects=True, vmem_limit_bytes=ROOM
        ),
    )(grad, out_weight, down_weight, inner, mixed, active, *swap)


SCATTER_OPS = (
    ((0, 0), (0, 1), (1, 0), (2, 0), (1, 1), (0, 2), (2, 1), (3, 0), (1, 2), (2, 2), (4, 0), (6, 0), (5, 0), (0, 3), (3, 1), (3, 2), (1, 3), (3, 3), (4, 1), (5, 1), (6, 1), (4, 2), (5, 2), (6, 2), (2, 3), (4, 3), (5, 3), (6, 3)),
    ((0, 0), (0, 2), (3, 2), (1, 0), (3, 0), (0, 1), (0, 3), (1, 1), (2, 0), (1, 2), (3, 1), (1, 3), (4, 0), (6, 0), (5, 0), (3, 3), (2, 1), (2, 2), (4, 1), (6, 1), (5, 1), (4, 2), (5, 2), (6, 2), (2, 3), (4, 3), (5, 3), (6, 3)),
)
SCATTER_OPS_WORK = (
    ((0, 0), (0, 1), (1, 0), (2, 0), (1, 1), (0, 2), (2, 1), (3, 0), (1, 2), (2, 2), (4, 0), (6, 0), (7, 0), (5, 0), (0, 3), (3, 1), (3, 2), (1, 3), (3, 3), (4, 1), (7, 0), (5, 1), (7, 0), (7, 0), (7, 0), (7, 0), (7, 0), (6, 1), (4, 2), (7, 0), (5, 2), (7, 0), (7, 0), (7, 0), (6, 2), (2, 3), (7, 0), (7, 0), (7, 0), (7, 0), (7, 0), (4, 3), (5, 3), (6, 3)),
    ((0, 0), (0, 2), (3, 2), (1, 0), (3, 0), (7, 0), (0, 1), (0, 3), (1, 1), (2, 0), (1, 2), (3, 1), (7, 0), (7, 0), (1, 3), (4, 0), (6, 0), (7, 0), (5, 0), (7, 0), (7, 0), (3, 3), (2, 1), (7, 0), (2, 2), (7, 0), (7, 0), (4, 1), (6, 1), (5, 1), (4, 2), (5, 2), (7, 0), (7, 0), (7, 0), (6, 2), (7, 0), (7, 0), (7, 0), (2, 3), (7, 0), (4, 3), (5, 3), (6, 3)),
)
SCATTER_OPS_EARLY = (
    ((0, 0), (0, 1), (1, 0), (3, 0), (2, 0), (0, 2), (1, 1), (2, 1), (1, 2), (2, 2), (0, 3), (4, 0), (6, 0), (7, 0), (7, 0), (7, 0), (5, 0), (7, 0), (3, 1), (1, 3), (7, 0), (7, 0), (7, 0), (4, 1), (7, 0), (7, 0), (7, 0), (6, 1), (7, 0), (5, 1), (7, 0), (7, 0), (7, 0), (7, 0), (7, 0), (3, 2), (3, 3), (2, 3), (4, 2), (5, 2), (6, 2), (8, 0), (8, 1), (8, 2), (8, 3), (4, 3), (5, 3), (6, 3)),
    ((0, 2), (7, 0), (0, 0), (0, 1), (1, 0), (7, 0), (7, 0), (0, 3), (7, 0), (3, 3), (3, 0), (7, 0), (1, 1), (2, 0), (3, 2), (1, 2), (7, 0), (2, 2), (7, 0), (7, 0), (3, 1), (1, 3), (4, 0), (6, 0), (7, 0), (2, 1), (7, 0), (7, 0), (7, 0), (5, 0), (7, 0), (7, 0), (7, 0), (7, 0), (2, 3), (4, 1), (6, 1), (5, 1), (4, 2), (5, 2), (6, 2), (8, 0), (8, 1), (8, 2), (8, 3), (4, 3), (5, 3), (6, 3)),
)
SPLIT = ((0, 208), (208, 48))


def scatter_events(partial, other_work, late_work, ops, scratch):
    total, give, take, side_take, line_take, other_take = scratch[:6]
    core_send, core_recv, side_send, side_recv, line_send, line_recv = scratch[6:12]
    other_send, other_recv = scratch[12:]
    ctx, place, twin, across, twin_across = neighbours()
    below, above = place - 1, place + 1
    has_below, has_above = place > 0, place < SIDE - 1
    at_end = (place == 0) | (place == SIDE - 1)

    def rows_of(part):
        return pl.ds(*SPLIT[part])

    def core_copy(step, store):
        return to_axis(
            give.at[step], take.at[store], core_send.at[store], core_recv.at[store], "ctx", twin
        )

    def side_copy(step, part):
        return to_axis(
            take.at[step, rows_of(part)],
            side_take.at[step, rows_of(part)],
            side_send.at[step, part],
            side_recv.at[step, part],
            "ctx",
            across,
        )

    def line_copy(step, line, slot, target, part):
        return to_axis(
            take.at[SIDE + step, rows_of(part)],
            line_take.at[slot, rows_of(part)],
            line_send.at[line, part],
            line_recv.at[slot, part],
            "fsdp",
            target,
        )

    def other_copy(step, line, slot, target):
        return to_axis(
            take.at[step, rows_of(1)],
            other_take.at[slot],
            other_send.at[line],
            other_recv.at[slot],
            "fsdp",
            target,
        )

    def from_above(line):
        return jnp.where(line == place, SIDE, line)

    def to_below(line):
        return jnp.where(line == place - 1, SIDE, line)

    def one(number, turn):
        def by_end(field):
            ends, middle = (tuple(entry[field] for entry in table) for table in ops)
            return jnp.where(at_end, nibble(ends, number), nibble(middle, number))

        what, step = by_end(0), by_end(1)
        line = digit_of_row(FAR, place, step)

        @pl.when((what <= 1) | (what == 3) | (what == 4))
        def _():
            owner = jnp.where(
                what == 0,
                twin_across,
                jnp.where(what == 1, across, jnp.where(what == 3, twin, ctx)),
            )
            total[...] = partial(owner * SIDE + line)

        @pl.when(what == 0)
        def _():
            give[step] = total[...].astype(jnp.bfloat16)
            core_copy(step, step).start()

        @pl.when(what == 1)
        def _():
            core_copy(step, step).wait_recv()
            take[step] = (total[...] + take[step].astype(jnp.float32)).astype(jnp.bfloat16)
            side_copy(step, 0).start()

        @pl.when(what == 2)
        def _():
            rows = rows_of(1)

            @pl.when((line >= place) & has_below)
            def _():
                other_copy(step, line, line, below).wait_recv()
                take[step, rows] = (
                    take[step, rows].astype(jnp.float32) + other_take[line].astype(jnp.float32)
                ).astype(jnp.bfloat16)

            @pl.when((line <= place) & has_above)
            def _():
                other_copy(step, line, from_above(line), above).wait_recv()
                take[step, rows] = (
                    take[step, rows].astype(jnp.float32)
                    + other_take[from_above(line)].astype(jnp.float32)
                ).astype(jnp.bfloat16)

            @pl.when(line > place)
            def _():
                other_copy(step, line, line, above).start()

            @pl.when(line < place)
            def _():
                other_copy(step, line, to_below(line), below).start()

            @pl.when(line == place)
            def _():
                side_copy(step, 1).start()

        @pl.when(what == 3)
        def _():
            core_copy(step, step).wait_send()
            give[step] = total[...].astype(jnp.bfloat16)
            core_copy(step, SIDE + step).start()

        @pl.when(what == 4)
        def _():
            core_copy(step, SIDE + step).wait_recv()
            total[...] += take[SIDE + step].astype(jnp.float32)

        for part in range(2):
            rows = rows_of(part)

            @pl.when(what == 5 + part)
            def _(rows=rows, part=part):
                crossed = line == place if part == 1 else line >= 0

                @pl.when(crossed)
                def _():
                    side_copy(step, part).wait_recv()
                    total[rows] += side_take[step, rows].astype(jnp.float32)

                @pl.when((line >= place) & has_below)
                def _():
                    line_copy(step, line, line, below, part).wait_recv()
                    total[rows] += line_take[line, rows].astype(jnp.float32)

                @pl.when((line <= place) & has_above)
                def _():
                    line_copy(step, line, from_above(line), above, part).wait_recv()
                    total[rows] += line_take[from_above(line), rows].astype(jnp.float32)

                @pl.when(line > place)
                def _():
                    take[SIDE + step, rows] = total[rows].astype(jnp.bfloat16)
                    line_copy(step, line, line, above, part).start()

                @pl.when(line < place)
                def _():
                    take[SIDE + step, rows] = total[rows].astype(jnp.bfloat16)
                    line_copy(step, line, to_below(line), below, part).start()

        if other_work is not None:

            @pl.when(what == 7)
            def _():
                other_work(turn)

        if late_work is not None:

            @pl.when(what == 8)
            def _():
                late_work(step)

        return turn + jnp.where(what == 7, 1, 0)

    lax.fori_loop(0, len(ops[0]), one, jnp.int32(0))

    def finish(step, carry):
        line = digit_of_row(FAR, place, step)
        core_copy(step, SIDE + step).wait_send()
        side_copy(step, 0).wait_send()

        @pl.when(line == place)
        def _():
            side_copy(step, 1).wait_send()

        @pl.when(line != place)
        def _():
            for part in range(2):
                line_copy(step, line, line, place, part).wait_send()
            other_copy(step, line, line, place).wait_send()

        return carry

    lax.fori_loop(0, SIDE, finish, 0)


def scatter_scratch(rows):
    return [
        pltpu.VMEM((rows, D), jnp.float32),
        pltpu.VMEM((SIDE, rows, D), jnp.bfloat16),
        pltpu.VMEM((2 * SIDE, rows, D), jnp.bfloat16),
        pltpu.VMEM((SIDE, rows, D), jnp.bfloat16),
        pltpu.VMEM((SIDE + 1, rows, D), jnp.bfloat16),
        pltpu.VMEM((SIDE + 1, SPLIT[1][1], D), jnp.bfloat16),
        pltpu.SemaphoreType.DMA((2 * SIDE,)),
        pltpu.SemaphoreType.DMA((2 * SIDE,)),
        pltpu.SemaphoreType.DMA((SIDE, 2)),
        pltpu.SemaphoreType.DMA((SIDE, 2)),
        pltpu.SemaphoreType.DMA((SIDE, 2)),
        pltpu.SemaphoreType.DMA((SIDE + 1, 2)),
        pltpu.SemaphoreType.DMA((SIDE,)),
        pltpu.SemaphoreType.DMA((SIDE + 1,)),
    ]


SMALL_ROWS = 16
PAIRS = GROUP // 2


def norm_back_strip(hidden, grad, total, gain, out, part):
    values = hidden[part].astype(jnp.float32)
    centred = values - jnp.mean(values, axis=1, keepdims=True)
    spread = jnp.mean(centred * centred, axis=1, keepdims=True)
    root = lax.rsqrt(spread + EPS)
    normed = centred * root
    above = total[part]
    scaled = above * gain[...]
    down = jnp.mean(scaled, axis=1, keepdims=True)
    along = jnp.mean(scaled * normed, axis=1, keepdims=True)
    passing = grad[part]
    out[part] = passing + root * (scaled - down - normed * along)
    low = passing.astype(jnp.bfloat16).astype(jnp.float32)
    return tuple(
        jnp.sum(sums.reshape(STRIP // 8, 8, D), axis=0) for sums in (above * normed, above, low)
    )


def small_exchange(shares, land, mine, other, out, sems):
    send, recv, swap_send, swap_recv = sems
    me = lax.axis_index("ctx") * SIDE + lax.axis_index("fsdp")

    def copy(step):
        peer = lax.rem(me + step, GROUP)
        return to_peer(shares.at[peer], land.at[me], send.at[step], recv.at[me], peer)

    def swap():
        return to_axis(mine, other, swap_send, swap_recv, "seq", 1 - lax.axis_index("seq"))

    def begin(sums):
        for number, folded in enumerate(sums):
            row = jnp.sum(folded, axis=0, keepdims=True)
            for block in range(GROUP):
                shares[block, number : number + 1] = row[:, block * SHARE : (block + 1) * SHARE]

        def start(step, carry):
            copy(step).start()
            return carry

        lax.fori_loop(1, GROUP, start, 0)
        land[me] = shares[me]

    def middle():
        def arrive(step, carry):
            source = lax.rem(me + GROUP - step, GROUP)
            to_peer(shares.at[source], land.at[source], send.at[step], recv.at[source], source).wait_recv()
            copy(step).wait_send()
            return carry

        lax.fori_loop(1, GROUP, arrive, 0)
        mine[...] = jnp.sum(land[...], axis=0)
        swap().start()

    def end():
        swap().wait()
        out[...] = mine[...] + other[...]

    return begin, middle, end


def small_scratch():
    small = (SMALL_ROWS, SHARE)
    return [
        pltpu.VMEM((GROUP,) + small, jnp.float32),
        pltpu.VMEM(small, jnp.float32),
        pltpu.VMEM(small, jnp.float32),
        pltpu.SemaphoreType.DMA((GROUP,)),
        pltpu.SemaphoreType.DMA((GROUP,)),
        pltpu.SemaphoreType.DMA,
        pltpu.SemaphoreType.DMA,
    ]


def half_swaps(halves, wholes, sems, pieces=4):
    send, recv, own = sems
    seq = lax.axis_index("seq")
    half = SHARE // 2
    size = half // pieces

    def copies(which):
        return [
            to_axis(
                source.at[pl.ds(piece * size, size)],
                target.at[pl.ds(pl.multiple_of(seq * half + piece * size, size), size)],
                send.at[at, piece],
                recv.at[at, piece],
                "seq",
                1 - seq,
            )
            for at, (source, target) in enumerate(zip(halves, wholes))
            for piece in which
        ]

    def kept():
        rows = pl.ds(pl.multiple_of(seq * half, half), half)
        return [
            pltpu.make_async_copy(source, target.at[rows], own.at[at])
            for at, (source, target) in enumerate(zip(halves, wholes))
        ]

    return copies, kept


def half_sems(pieces=4):
    return [
        pltpu.SemaphoreType.DMA((2, pieces)),
        pltpu.SemaphoreType.DMA((2, pieces)),
        pltpu.SemaphoreType.DMA((2,)),
    ]


WHOLES = (
    jax.ShapeDtypeStruct((SHARE, 3 * D), jnp.bfloat16),
    jax.ShapeDtypeStruct((SHARE, FF), jnp.bfloat16),
)
HALVES = (
    jax.ShapeDtypeStruct((SHARE // 2, 3 * D), jnp.bfloat16),
    jax.ShapeDtypeStruct((SHARE // 2, FF), jnp.bfloat16),
)


def forward_scatter(hidden, bias, mixed, active, out_weight, down_weight, layer, rest=None):
    rows = hidden.shape[0]
    last = rest is not None

    def kernel(hidden, bias, mixed, active, out_weight, down_weight, *refs):
        if last:
            (below_total, below_hidden, below_grad, gain, below_shares, joint, upper, branch), refs = (
                refs[:8],
                refs[8:],
            )
            out, grad_out, small_out, joint_out, upper_out, branch_out = refs[:6]
            refs = refs[6:]
        else:
            out, refs = refs[0], refs[1:]
        hidden_part, mixed_part, active_part, out_part, down_part, load_sem = refs[:6]
        refs = refs[6:]
        loads = load_all(
            (
                (mixed, mixed_part),
                (active, active_part),
                (out_weight.at[layer], out_part),
                (down_weight.at[layer], down_part),
                (hidden, hidden_part),
            ),
            load_sem,
        )
        other_work = None
        if last:
            parts, part_sem, sums, swap_sem = refs[:4], refs[4], refs[5], refs[6]
            shares, small, swap_sems, refs = parts[3], refs[7:14], refs[14:17], refs[17:]
            below = load_all(
                tuple(zip((below_total, below_hidden, below_grad, below_shares), parts)), part_sem
            )
            small_begin, small_middle, small_end = small_exchange(
                shares, small[0], small[1], small[2], small_out, small[3:]
            )
            copies, kept = half_swaps((joint, upper), (joint_out, upper_out), swap_sems)
            greet_plane(GROUP)
            blocks = tuple(range(SWAP_FIRST, SWAP_BLOCKS))
            early, late = (
                row_swap(branch, branch_out, swap_sem, SWAP_FIRST, which)
                for which in (blocks[:-1], blocks[-1:])
            )
            for copy in copies((0, 1, 2, 3)) + kept() + early:
                copy.start()
            sums[...] = jnp.zeros_like(sums)
            strips = rows // STRIP

            def other_work(turn):
                @pl.when(turn == 0)
                def _():
                    wait_all(below)

                @pl.when(turn < strips)
                def _():
                    part = pl.ds(pl.multiple_of(turn * STRIP, STRIP), STRIP)
                    found = norm_back_strip(parts[1], parts[2], parts[0], gain, grad_out, part)
                    for number, folded in enumerate(found):
                        sums[number] += folded

                @pl.when(turn == strips)
                def _():
                    small_begin([sums[number] for number in range(3)])

                @pl.when(turn == GROUP - 4)
                def _():
                    small_middle()
                    for copy in late:
                        copy.start()

        else:
            greet_neighbours()
        scratch = refs
        wait_all(loads[:4])

        def partial(slot):
            return dot(mixed_part[slot], out_part[...]) + dot(active_part[slot], down_part[...])

        scatter_events(
            partial, other_work, None, SCATTER_OPS_WORK if last else SCATTER_OPS, scratch
        )
        loads[4].wait()
        out[...] = hidden_part[...].astype(jnp.float32) + (scratch[0][...] + bias[...])
        if last:
            small_end()
            wait_all(copies((0, 1, 2, 3)) + kept() + early + late)

    out_shape = (jax.ShapeDtypeStruct((rows, D), jnp.float32),)
    out_specs = (VMEM,)
    extra_scratch = []
    if last:
        total, before, grad, _, shares, _, _, branch = rest
        out_shape += (
            (
                jax.ShapeDtypeStruct((rows, D), jnp.float32),
                jax.ShapeDtypeStruct((SMALL_ROWS, SHARE), jnp.float32),
            )
            + WHOLES
            + (jax.ShapeDtypeStruct((BACK_COLS // 2, D), branch.dtype),)
        )
        out_specs += (VMEM, VMEM, HBM, HBM, HBM)
        extra_scratch = (
            [pltpu.VMEM(array.shape, array.dtype) for array in (total, before, grad, shares)]
            + [
                pltpu.SemaphoreType.DMA((4,)),
                pltpu.VMEM((3, 8, D), jnp.float32),
                pltpu.SemaphoreType.DMA((2, SWAP_BLOCKS)),
            ]
            + small_scratch()
            + half_sems()
        )
    return pl.pallas_call(
        kernel,
        out_shape=out_shape,
        in_specs=[HBM, VMEM] + [HBM] * 4 + ([HBM] * 3 + [VMEM] + [HBM] * 4 if last else []),
        out_specs=out_specs,
        scratch_shapes=[pltpu.VMEM(array.shape, array.dtype) for array in (hidden, mixed, active)]
        + [
            pltpu.VMEM(out_weight.shape[1:], jnp.bfloat16),
            pltpu.VMEM(down_weight.shape[1:], jnp.bfloat16),
        ]
        + [pltpu.SemaphoreType.DMA((5,))]
        + extra_scratch
        + scatter_scratch(rows),
        compiler_params=pltpu.CompilerParams(
            collective_id=10 + layer, has_side_effects=True, vmem_limit_bytes=ROOM
        ),
    )(hidden, bias, mixed, active, out_weight, down_weight, *(rest or ()))


def backward_scatter(
    hidden, grad, gain, grad_joint, grad_inner, columns, every, layer, up=None, halves=(), branch=None
):
    rows = grad.shape[0]
    half = SHARE // 2
    collects = up is not None
    made = JOINT_COLS if collects else COLS
    tokens = GROUP * rows

    def kernel(*refs):
        if collects:
            (joint_in, inner_in, columns_in, every, up, *halves), refs = refs[:7], refs[7:]
            branch, out, shares, joint_half, up_half, *wholes = refs[:7]
            branch_out, refs = refs[7], refs[8:]
        else:
            (joint_in, inner_in, columns_in, every, hidden_in, grad_in, gain), refs = refs[:7], refs[7:]
            out, small_out, summed, refs = refs[0], refs[1], refs[2], refs[3:]
        grad_joint, grad_inner, columns, load_sem, strips, load = refs[:6]
        mine, other, cross_send, cross_recv = refs[6:10]
        refs = refs[10:]
        if collects:
            summed, plane_send, plane_recv, plane_own, up_send, up_recv, up_own = refs[:7]
            swap_sems, branch_sem, refs = refs[7:10], refs[10], refs[11:]
            copies, kept = half_swaps(halves, wholes, swap_sems)
            swaps = row_swap(branch, branch_out, branch_sem, 0, range(SWAP_FIRST))
        else:
            hidden, grad, shares, small, refs = refs[0], refs[1], refs[2], refs[3:10], refs[10:]
            small_begin, small_middle, small_end = small_exchange(
                shares, small[0], small[1], small[2], small_out, small[3:]
            )
        scratch = refs
        total = scratch[0]
        ctx, place, seq = lax.axis_index("ctx"), lax.axis_index("fsdp"), lax.axis_index("seq")
        me = ctx * SIDE + place
        part_rows = pl.ds(pl.multiple_of(seq * half, half), half)
        other_rows = pl.ds(pl.multiple_of((1 - seq) * half, half), half)

        def pair_of(turn):
            return lax.rem(me // 2 + 1 + turn, PAIRS)

        def load_strip(turn):
            start = pl.multiple_of(pair_of(turn) * 2 * SHARE, 2 * SHARE)
            buffer = lax.rem(turn, 2)
            return pltpu.make_async_copy(
                every.at[:, :, pl.ds(start, 2 * SHARE)], strips.at[buffer], load.at[buffer]
            )

        pairs = [(joint_in, grad_joint), (inner_in, grad_inner), (columns_in, columns)]
        if not collects:
            pairs += [(hidden_in, hidden), (grad_in, grad)]
        loads = load_all(pairs, load_sem)
        load_strip(jnp.int32(0)).start()
        shares[...] = jnp.zeros_like(shares)
        greet_plane(GROUP)

        def partial(slot):
            return dot(grad_joint[slot], columns[:, :JOINT_COLS], 1, 1) + dot(
                grad_inner[slot], columns[:, JOINT_COLS:], 1, 1
            )

        def product(turn):
            pair = pair_of(turn)
            load_strip(turn).wait()

            @pl.when(turn + 1 < PAIRS)
            def _():
                load_strip(turn + 1).start()

            strip = strips[lax.rem(turn, 2)].reshape(tokens, 2 * SHARE)
            result = dot(strip, grad_joint[...].reshape(tokens, JOINT_COLS), 0, 0).astype(
                jnp.bfloat16
            )
            for which in range(2):
                mine[2 * pair + which, :, :JOINT_COLS] = result[which * SHARE : (which + 1) * SHARE]
            if not collects:
                result = dot(strip, grad_inner[...].reshape(tokens, FEED_COLS), 0, 0).astype(
                    jnp.bfloat16
                )
                for which in range(2):
                    mine[2 * pair + which, :, JOINT_COLS:] = result[
                        which * SHARE : (which + 1) * SHARE
                    ]

        def cross_copy(block):
            return to_axis(
                mine.at[block, other_rows],
                other.at[block],
                cross_send.at[block],
                cross_recv.at[block],
                "seq",
                1 - seq,
            )

        def joint_places():
            return [
                (at, joint_half.at[:, pl.ds(start, width)], pl.ds(at * HEAD_COLS, HEAD_COLS))
                for at, (_, start, _, width) in enumerate(column_places(me)[:3])
            ]

        def plane_copies(block):
            return [
                to_peer(
                    summed.at[block, :, piece],
                    target,
                    plane_send.at[block, at],
                    plane_recv.at[me, at],
                    block,
                )
                for at, target, piece in joint_places()
            ]

        def own_copies():
            return [
                pltpu.make_async_copy(summed.at[me, :, piece], target, plane_own.at[at])
                for at, target, piece in joint_places()
            ]

        def up_place(block):
            return up_half.at[:, pl.ds(pl.multiple_of(block * FEED_COLS, FEED_COLS), FEED_COLS)]

        def up_copy(step):
            peer = lax.rem(me + step, GROUP)
            return to_peer(up.at[peer], up_place(me), up_send.at[step], up_recv.at[me], peer)

        def own_up():
            return pltpu.make_async_copy(up.at[me], up_place(me), up_own)

        def add(turn):
            for which in range(2):
                block = 2 * pair_of(turn) + which
                cross_copy(block).wait_recv()
                summed[block] = (
                    mine[block, part_rows].astype(jnp.float32) + other[block].astype(jnp.float32)
                ).astype(jnp.bfloat16)
                if collects:

                    @pl.when(block != me)
                    def _(block=block):
                        for copy in plane_copies(block):
                            copy.start()

                    @pl.when(block == me)
                    def _(block=block):
                        for copy in own_copies():
                            copy.start()

        def bias_sums():
            ones = jnp.ones((16, tokens), jnp.bfloat16)
            joint_bias = dot(ones, grad_joint[...].reshape(tokens, JOINT_COLS))[:1]
            upper_bias = dot(ones, grad_inner[...].reshape(tokens, FEED_COLS))[:1]
            for part in range(3):
                at = part * GROUP + me
                shares[at // 3, pl.ds(3 + lax.rem(at, 3), 1)] = joint_bias[
                    :, part * HEAD_COLS : (part + 1) * HEAD_COLS
                ]
            for part in range(FEED_COLS // SHARE):
                shares[me, 6 + part : 7 + part] = upper_bias[:, part * SHARE : (part + 1) * SHARE]

        def other_work(turn):
            pl.when(turn == 1)(bias_sums)

            @pl.when(lax.rem(turn, 2) == 0)
            def _():
                product(turn // 2)
                for which in range(2):
                    cross_copy(2 * pair_of(turn // 2) + which).start()

            @pl.when((lax.rem(turn, 2) == 1) & (turn > 4))
            def _():
                add((turn - 5) // 2)

            if collects:

                @pl.when(turn == GROUP - 1)
                def _():
                    for copy in copies((2, 3)) + swaps:
                        copy.start()

        def last_adds(turn, carry):
            add(turn)
            return carry

        def late_work(step):
            @pl.when(step == 0)
            def _():
                lax.fori_loop(PAIRS - 2, PAIRS, last_adds, 0)

        def send_up(step, carry):
            up_copy(step).start()
            return carry

        wait_all(loads[:3])
        if collects:
            own_up().start()
            lax.fori_loop(1, GROUP, send_up, 0)
            for copy in copies((0, 1)) + kept():
                copy.start()
        scatter_events(
            partial,
            other_work,
            late_work if collects else None,
            SCATTER_OPS_EARLY if collects else SCATTER_OPS_WORK,
            scratch,
        )

        def end_cross(block, carry):
            cross_copy(block).wait_send()
            return carry

        def end(step, carry):
            source = lax.rem(me + GROUP - step, GROUP)
            target = up_place(source)
            to_peer(target, target, up_send.at[step], up_recv.at[source], source).wait_recv()
            up_copy(step).wait_send()
            for at, (_, start, _, width) in enumerate(column_places(source)[:3]):
                target = joint_half.at[:, pl.ds(start, width)]
                to_peer(
                    target, target, plane_send.at[source, at], plane_recv.at[source, at], source
                ).wait_recv()
            for copy in plane_copies(lax.rem(me + step, GROUP)):
                copy.wait_send()
            return carry

        if collects:
            out[...] = total[...]
            lax.fori_loop(1, GROUP, end, 0)
            wait_all(own_copies() + [own_up()] + copies((0, 1, 2, 3)) + kept() + swaps)
        else:
            lax.fori_loop(PAIRS - 2, PAIRS, last_adds, 0)
            wait_all(loads[3:])

            def norm_back(part, sums):
                found = norm_back_strip(hidden, grad, total, gain, out, part)
                return tuple(before + more for before, more in zip(sums, found))

            zeros = jnp.zeros((8, D), jnp.float32)
            small_begin(each_strip(rows, norm_back, (zeros, zeros, zeros)))
            small_middle()
            small_end()
        lax.fori_loop(0, GROUP, end_cross, 0)

    def part(width, height=half):
        return pltpu.VMEM((GROUP, height, width), jnp.bfloat16)

    def same(*arrays):
        return [pltpu.VMEM(array.shape, array.dtype) for array in arrays]

    small = (SMALL_ROWS, SHARE)
    shares = (GROUP,) + small
    sixteen = pltpu.SemaphoreType.DMA((GROUP,))
    row_shape = jax.ShapeDtypeStruct((rows, D), jnp.float32)
    common = (
        same(grad_joint, grad_inner, columns)
        + [
            pltpu.SemaphoreType.DMA((5,)),
            pltpu.VMEM((2, GROUP, rows, 2 * SHARE), jnp.bfloat16),
            pltpu.SemaphoreType.DMA((2,)),
            part(made, SHARE),
            part(made),
            sixteen,
            sixteen,
        ]
    )
    if collects:
        out_shape = (row_shape, jax.ShapeDtypeStruct(shares, jnp.float32)) + HALVES + WHOLES
        out_shape += (jax.ShapeDtypeStruct((BACK_COLS // 2, D), branch.dtype),)
        out_specs = (VMEM, VMEM) + (HBM,) * 5
        operands = (grad_joint, grad_inner, columns, every, up, *halves, branch)
        in_specs = [HBM] * 8
        special = [
            part(JOINT_COLS),
            pltpu.SemaphoreType.DMA((GROUP, 3)),
            pltpu.SemaphoreType.DMA((GROUP, 3)),
            pltpu.SemaphoreType.DMA((3,)),
            sixteen,
            sixteen,
            pltpu.SemaphoreType.DMA,
        ] + half_sems() + [pltpu.SemaphoreType.DMA((2, SWAP_BLOCKS))]
    else:
        out_shape = (
            row_shape,
            jax.ShapeDtypeStruct(small, jnp.float32),
            jax.ShapeDtypeStruct((GROUP, half, COLS), jnp.bfloat16),
        )
        out_specs = (VMEM,) * 3
        operands = (grad_joint, grad_inner, columns, every, hidden, grad, gain)
        in_specs = [HBM] * 6 + [VMEM]
        special = same(hidden, grad) + [pltpu.VMEM(shares, jnp.float32)] + small_scratch()
    return pl.pallas_call(
        kernel,
        out_shape=out_shape,
        in_specs=in_specs,
        out_specs=out_specs,
        scratch_shapes=common + special + scatter_scratch(rows),
        compiler_params=pltpu.CompilerParams(
            collective_id=20 + layer, has_side_effects=True, vmem_limit_bytes=ROOM
        ),
    )(*operands)


def mask_rest(rows, begin, spot, first, lead):
    if lead:
        old = jnp.where(spot[:lead] >= begin, rows[:lead], NEG)
    key_at = lax.broadcasted_iota(jnp.int32, (first, first), 0) + lead
    query_at = lax.broadcasted_iota(jnp.int32, (first, first), 1) + lead
    near = spot[lead:]
    seen = ((near >= begin) & (near <= query_at)) | (key_at == query_at)
    new = jnp.where(seen, rows[lead:], NEG)
    return jnp.concatenate([old, new], axis=0) if lead else new


def head_lanes(head, rows):
    lane = lax.broadcasted_iota(jnp.int32, (rows, HEAD_COLS), 1)
    return (lane >= head * HEAD_DIM) & (lane < (head + 1) * HEAD_DIM)


def column_exchange(sources, land, sems, layer):
    plane_send, plane_recv, own_sem = sems
    ctx, place, seq = lax.axis_index("ctx"), lax.axis_index("fsdp"), lax.axis_index("seq")
    me = ctx * SIDE + place
    half = SHARE // 2
    part_rows = pl.ds(pl.multiple_of(seq * half, half), half)

    def piece(peer, number):
        which, start, at, width = column_places(peer)[number]
        return (
            sources[which].at[layer, part_rows, pl.ds(start, width)],
            land.at[me, :, pl.ds(at, width)],
        )

    def send_piece(step, number):
        peer = lax.rem(me + step, GROUP)
        source, target = piece(peer, number)
        return to_peer(source, target, plane_send.at[step, number], plane_recv.at[me, number], peer)

    def own_piece(number):
        return pltpu.make_async_copy(*piece(me, number), own_sem.at[number])

    def begin():
        greet_plane(GROUP, False)

        def send(step, carry):
            for number in range(PLACES):
                send_piece(step, number).start()
            return carry

        lax.fori_loop(1, GROUP, send, 0)
        for number in range(PLACES):
            own_piece(number).start()

    def end():
        def arrive(step, carry):
            source = lax.rem(me + GROUP - step, GROUP)
            for number in range(PLACES):
                _, _, at, width = column_places(0)[number]
                target = land.at[source, :, pl.ds(at, width)]
                to_peer(
                    target, target, plane_send.at[0, number], plane_recv.at[source, number], source
                ).wait_recv()
                send_piece(step, number).wait_send()
            return carry

        lax.fori_loop(1, GROUP, arrive, 0)
        for number in range(PLACES):
            own_piece(number).wait()

    return begin, end


def up_products(every, feed, out, scratch):
    feed_part, strips, mine, other, feed_sem, load, cross_send, cross_recv = scratch
    rows = feed.shape[1]
    tokens = GROUP * rows
    half = SHARE // 2
    seq = lax.axis_index("seq")
    me = lax.axis_index("ctx") * SIDE + lax.axis_index("fsdp")
    part_rows = pl.ds(pl.multiple_of(seq * half, half), half)
    other_rows = pl.ds(pl.multiple_of((1 - seq) * half, half), half)

    def pair_of(turn):
        return lax.rem(me // 2 + 1 + turn, PAIRS)

    def load_strip(turn):
        start = pl.multiple_of(pair_of(turn) * 2 * SHARE, 2 * SHARE)
        buffer = lax.rem(turn, 2)
        return pltpu.make_async_copy(
            every.at[:, :, pl.ds(start, 2 * SHARE)], strips.at[buffer], load.at[buffer]
        )

    def cross_copy(block):
        return to_axis(
            mine.at[block, other_rows],
            other.at[block],
            cross_send.at[block],
            cross_recv.at[block],
            "seq",
            1 - seq,
        )

    def feed_copy():
        return pltpu.make_async_copy(feed, feed_part, feed_sem)

    def begin():
        feed_copy().start()
        load_strip(jnp.int32(0)).start()

    def product(turn, carry):
        pair = pair_of(turn)
        load_strip(turn).wait()

        @pl.when(turn == 0)
        def _():
            feed_copy().wait()

        @pl.when(turn + 1 < PAIRS)
        def _():
            load_strip(turn + 1).start()

        strip = strips[lax.rem(turn, 2)].reshape(tokens, 2 * SHARE)
        made = dot(strip, feed_part[...].reshape(tokens, FEED_COLS), 0, 0).astype(jnp.bfloat16)
        for which in range(2):
            mine[2 * pair + which] = made[which * SHARE : (which + 1) * SHARE]
            cross_copy(2 * pair + which).start()
        return carry

    def add(turn, carry):
        for which in range(2):
            block = 2 * pair_of(turn) + which
            cross_copy(block).wait()
            out[block] = (
                mine[block, part_rows].astype(jnp.float32) + other[block].astype(jnp.float32)
            ).astype(jnp.bfloat16)
        return carry

    each = PAIRS // SIDE

    def make(step):
        lax.fori_loop(each * step, each * step + each, product, 0)
        lax.fori_loop(each * jnp.maximum(step - 1, 0), each * step, add, 0)

    def end():
        lax.fori_loop(PAIRS - each, PAIRS, add, 0)

    return begin, make, end


def row_exchange(summed, outputs, sems):
    plane_send, plane_recv, own_sem = sems
    me = lax.axis_index("ctx") * SIDE + lax.axis_index("fsdp")

    def piece(peer, number):
        which, start, at, width = column_places(me)[number]
        return summed.at[peer, :, pl.ds(at, width)], outputs[which].at[:, pl.ds(start, width)]

    def send_piece(step, number):
        peer = lax.rem(me + step, GROUP)
        source, target = piece(peer, number)
        return to_peer(source, target, plane_send.at[step, number], plane_recv.at[me, number], peer)

    def own_piece(number):
        return pltpu.make_async_copy(*piece(me, number), own_sem.at[number])

    def begin():
        greet_plane(GROUP)

        def send(step, carry):
            for number in range(PLACES):
                send_piece(step, number).start()
            return carry

        lax.fori_loop(1, GROUP, send, 0)
        for number in range(PLACES):
            own_piece(number).start()

    def end():
        def arrive(step, carry):
            source = lax.rem(me + GROUP - step, GROUP)
            for number in range(PLACES):
                which, start, _, width = column_places(source)[number]
                target = outputs[which].at[:, pl.ds(start, width)]
                to_peer(
                    target, target, plane_send.at[0, number], plane_recv.at[source, number], source
                ).wait_recv()
                send_piece(step, number).wait_send()
            return carry

        lax.fori_loop(1, GROUP, arrive, 0)
        for number in range(PLACES):
            own_piece(number).wait()

    return begin, end


EXCHANGE_SEMS = [
    pltpu.SemaphoreType.DMA((GROUP, PLACES)),
    pltpu.SemaphoreType.DMA((GROUP, PLACES)),
    pltpu.SemaphoreType.DMA((PLACES,)),
]


def attend_plane(query, key, value, begin, spot, weights=None, layer=0):
    rows = query.shape[1]
    length = SIDE * rows
    scale = 1.0 / math.sqrt(HEAD_DIM)

    def kernel(query, key, value, begin, spot, *refs):
        if weights is None:
            mixed, turned, stats = refs
        else:
            mixed, turned, stats, land = refs[2:6]
            begin_exchange, end_exchange = column_exchange(refs[:2], land, refs[6:], layer)
            pl.when(pl.program_id(0) == 0)(begin_exchange)
        keys = key[:, 0].reshape(length, HEAD_COLS)
        values = value[:, 0].reshape(length, HEAD_COLS)
        for chunk in range(SIDE):
            lead = chunk * rows
            seen = lead + rows
            scaled = query[chunk, 0] * jnp.bfloat16(scale)
            start = begin[0, :, lead:seen]
            outs = []
            for head in range(OWN):
                own = jnp.where(head_lanes(head, rows), scaled, jnp.bfloat16(0))
                scores = mask_rest(
                    dot(keys[:seen], own, 1, 1), start, spot[0, :seen], rows, lead
                )
                peak = jnp.max(scores, axis=0, keepdims=True)
                probs = jnp.exp(scores - peak)
                norm = jnp.sum(probs, axis=0, keepdims=True)
                stats[0, head : head + 1, lead:seen] = peak
                stats[0, OWN + head : OWN + head + 1, lead:seen] = norm
                whole = dot(values[:seen], probs.astype(jnp.bfloat16), 0, 0)
                outs.append(whole[head * HEAD_DIM : (head + 1) * HEAD_DIM] / norm)
            joined = jnp.concatenate(outs, axis=0)
            turned[chunk, 0] = joined
            mixed[chunk, 0] = joined.T.astype(jnp.bfloat16)
        if weights is not None:
            pl.when(pl.program_id(0) == SIDE - 1)(end_exchange)

    def spec(height, width):
        return pl.BlockSpec((SIDE, 1, height, width), lambda step: (0, step, 0, 0))

    def shape(height, width, dtype):
        return jax.ShapeDtypeStruct((SIDE, SIDE, height, width), dtype)

    extra = weights is not None
    land = (jax.ShapeDtypeStruct((GROUP, SHARE // 2, COLS), jnp.bfloat16),) if extra else ()
    mixed, turned, stats, *land = pl.pallas_call(
        kernel,
        grid=(SIDE,),
        out_shape=(
            shape(rows, HEAD_COLS, jnp.bfloat16),
            shape(HEAD_COLS, rows, jnp.float32),
            jax.ShapeDtypeStruct((SIDE, 2 * OWN, length), jnp.float32),
        )
        + land,
        in_specs=[spec(rows, HEAD_COLS)] * 3
        + [
            pl.BlockSpec((1, 1, length), lambda step: (step, 0, 0)),
            pl.BlockSpec((1, length, 1), lambda step: (step, 0, 0)),
        ]
        + [HBM] * (2 if extra else 0),
        out_specs=(
            spec(rows, HEAD_COLS),
            spec(HEAD_COLS, rows),
            pl.BlockSpec((1, 2 * OWN, length), lambda step: (step, 0, 0)),
        )
        + ((HBM,) if extra else ()),
        scratch_shapes=EXCHANGE_SEMS if extra else [],
        compiler_params=pltpu.CompilerParams(
            collective_id=40, has_side_effects=True, vmem_limit_bytes=ROOM
        )
        if extra
        else pltpu.CompilerParams(vmem_limit_bytes=ROOM),
    )(
        *(array.reshape(SIDE, SIDE, rows, HEAD_COLS) for array in (query, key, value)),
        begin,
        spot,
        *(weights or ()),
    )
    return mixed.reshape(GROUP, rows, HEAD_COLS), turned, stats, *land


def attend_plane_back(
    query, key, value, begin, spot, turned, stats, grad, tables, summed=None, every=None, feed=None
):
    rows = query.shape[1]
    length = SIDE * rows
    scale = 1.0 / math.sqrt(HEAD_DIM)

    extra = summed is not None

    def kernel(query, key, value, grad, cosine, sine, begin, spot, turned, stats, *refs):
        if extra:
            summed, every, feed, out = refs[:4]
            up_out, grad_k, grad_v = refs[6], refs[7], refs[8]
            begin_exchange, end_exchange = row_exchange(summed, refs[4:6], refs[9:12])
            begin_up, make_up, end_up = up_products(every, feed, up_out, refs[12:])

            @pl.when(pl.program_id(0) == 0)
            def _():
                begin_up()
                begin_exchange()

        else:
            out, grad_k, grad_v = refs
        keys = key[:, 0].reshape(length, HEAD_COLS)
        values = value[:, 0].reshape(length, HEAD_COLS)
        for chunk in range(SIDE):
            lead = chunk * rows
            seen = lead + rows
            if chunk == 0:
                grad_k[...] = jnp.zeros_like(grad_k)
                grad_v[...] = jnp.zeros_like(grad_v)
            scaled = query[chunk, 0] * jnp.bfloat16(scale)
            start = begin[0, :, lead:seen]
            flipped = grad[chunk, 0].T
            grad_q, drifts, numers = [], [], []
            for head in range(OWN):
                part = slice(head * HEAD_DIM, (head + 1) * HEAD_DIM)
                norm = stats[0, OWN + head : OWN + head + 1, lead:seen]
                drifts.append(
                    jnp.sum(flipped[part] * turned[chunk, 0, part], axis=0, keepdims=True) / norm
                )
                numers.append(flipped[part] / norm)
            numer = jnp.concatenate(numers, axis=0).T.astype(jnp.bfloat16)
            for head in range(OWN):
                part = slice(head * HEAD_DIM, (head + 1) * HEAD_DIM)
                lanes = head_lanes(head, rows)
                own = jnp.where(lanes, scaled, jnp.bfloat16(0))
                own_numer = jnp.where(lanes, numer, jnp.bfloat16(0))
                scores = mask_rest(
                    dot(keys[:seen], own, 1, 1), start, spot[0, :seen], rows, lead
                )
                probs = jnp.exp(scores - stats[0, head : head + 1, lead:seen])
                grad_probs = dot(values[:seen], own_numer, 1, 1)
                grad_scores = (probs * (grad_probs - drifts[head])).astype(jnp.bfloat16)
                grad_q.append(dot(keys[:seen], grad_scores, 0, 0)[part])
                grad_k[:seen] += dot(grad_scores, own)
                grad_v[:seen] += dot(probs.astype(jnp.bfloat16), own_numer)
            turns = (cosine[chunk, 0], sine[chunk, 0])
            whole = jnp.concatenate(grad_q, axis=0).T * scale
            out[chunk, 0, :, :HEAD_COLS] = spin(whole, *turns, -1.0).astype(jnp.bfloat16)
        for chunk in range(SIDE):
            place = slice(chunk * rows, (chunk + 1) * rows)
            turns = (cosine[chunk, 0], sine[chunk, 0])
            out[chunk, 0, :, HEAD_COLS : 2 * HEAD_COLS] = spin(grad_k[place], *turns, -1.0).astype(
                jnp.bfloat16
            )
            out[chunk, 0, :, 2 * HEAD_COLS :] = grad_v[place].astype(jnp.bfloat16)
        if extra:
            make_up(pl.program_id(0))

            @pl.when(pl.program_id(0) == SIDE - 1)
            def _():
                end_up()
                end_exchange()


    def spec(height, width):
        return pl.BlockSpec((SIDE, 1, height, width), lambda step: (0, step, 0, 0))

    half = SHARE // 2
    halves = (
        jax.ShapeDtypeStruct((half, 3 * D), jnp.bfloat16),
        jax.ShapeDtypeStruct((half, FF), jnp.bfloat16),
        jax.ShapeDtypeStruct((GROUP, half, FEED_COLS), jnp.bfloat16),
    )
    out, *halves = pl.pallas_call(
        kernel,
        grid=(SIDE,),
        out_shape=(jax.ShapeDtypeStruct((SIDE, SIDE, rows, JOINT_COLS), jnp.bfloat16),)
        + (halves if extra else ()),
        in_specs=[spec(rows, HEAD_COLS)] * 6
        + [
            pl.BlockSpec((1, 1, length), lambda step: (step, 0, 0)),
            pl.BlockSpec((1, length, 1), lambda step: (step, 0, 0)),
            spec(HEAD_COLS, rows),
            pl.BlockSpec((1, 2 * OWN, length), lambda step: (step, 0, 0)),
        ]
        + [HBM] * (3 if extra else 0),
        out_specs=(spec(rows, JOINT_COLS),)
        + (
            (HBM, HBM, pl.BlockSpec((GROUP, half, FEED_COLS), lambda step: (0, 0, 0)))
            if extra
            else ()
        ),
        scratch_shapes=[pltpu.VMEM((length, HEAD_COLS), jnp.float32)] * 2
        + (
            EXCHANGE_SEMS
            + [
                pltpu.VMEM((GROUP, rows, FEED_COLS), jnp.bfloat16),
                pltpu.VMEM((2, GROUP, rows, 2 * SHARE), jnp.bfloat16),
                pltpu.VMEM((GROUP, SHARE, FEED_COLS), jnp.bfloat16),
                pltpu.VMEM((GROUP, half, FEED_COLS), jnp.bfloat16),
                pltpu.SemaphoreType.DMA,
                pltpu.SemaphoreType.DMA((2,)),
                pltpu.SemaphoreType.DMA((GROUP,)),
                pltpu.SemaphoreType.DMA((GROUP,)),
            ]
            if extra
            else []
        ),
        compiler_params=pltpu.CompilerParams(
            collective_id=41, has_side_effects=True, vmem_limit_bytes=ROOM
        )
        if extra
        else pltpu.CompilerParams(vmem_limit_bytes=ROOM),
    )(
        *(
            array.reshape(SIDE, SIDE, rows, HEAD_COLS)
            for array in (query, key, value, grad) + tuple(tables)
        ),
        begin,
        spot,
        turned,
        stats,
        *((summed, every, feed) if extra else ()),
    )
    return out.reshape(GROUP, rows, JOINT_COLS), *halves


def on_device_split(
    tokens,
    doc_lengths,
    keep_mask,
    ln_gain,
    ln_bias,
    qkv_weight,
    qkv_bias,
    out_weight,
    out_bias,
    up_weight,
    up_bias,
    down_weight,
    down_bias,
    cotangent,
):
    rows = tokens.shape[1]
    length = SIDE * rows
    me = lax.axis_index("ctx") * SIDE + lax.axis_index("fsdp")

    index = lax.axis_index("ctx") * rows + jnp.arange(rows, dtype=jnp.int32)
    ends = jnp.cumsum(doc_lengths[0])
    begin = jnp.max(jnp.where(index[:, None] >= ends[None, :], ends[None, :], 0), axis=1)
    fields = [ln_gain, ln_bias, qkv_bias, out_bias, down_bias]
    packed = jnp.concatenate(
        [field[layer].astype(jnp.float32) for layer in range(LAYERS) for field in fields]
        + [begin.astype(jnp.float32), keep_mask[0].astype(jnp.float32)]
    )
    packed = jnp.pad(packed, (0, -packed.shape[0] % (8 * SHARE))).reshape(-1, SHARE)
    lane = np.arange(HEAD_COLS) % HEAD_DIM
    inverse = 1.0 / 10000.0 ** (np.arange(0, ROT, 2, dtype=np.float32) / np.float32(ROT))
    inverse = np.where(lane < ROT, inverse[lane % (ROT // 2)], 0.0).astype(np.float32)
    up_bias = up_bias.astype(jnp.float32)

    seq = lax.axis_index("seq")
    half = SHARE // 2
    swap = [(0, 1), (1, 0)]

    def swapped(values):
        return lax.ppermute(values, "seq", swap)

    hidden = tokens[0]
    saved, gains, joint_grads, upper_grads, small_grads = [], [], [], [], []
    for layer in range(LAYERS):
        if layer == 0:
            *out, small, cosine, sine = first_gather(
                hidden, packed, up_bias[:1], jnp.asarray(inverse)[None, :], qkv_weight, up_weight
            )
            tables = (cosine, sine)
            length_rows = rows // SHARE

            def by_sequence(row):
                values = small[:, row : row + length_rows].reshape(SIDE, SIDE, rows)
                return values.transpose(1, 0, 2).reshape(SIDE, length).astype(jnp.int32)

            begin = by_sequence(BEGIN_ROW)[:, None, :]
            keep = by_sequence(BEGIN_ROW + length_rows)
            spot = jnp.where(keep > 0, jnp.arange(length, dtype=jnp.int32)[None, :], -1)[:, :, None]
        else:
            out = forward_gather(
                hidden,
                gain_row,
                row_of(layer, SHIFT_ROW),
                jnp.concatenate([own_bias, up_bias[layer : layer + 1]], axis=1),
                tables,
                halves,
                layer,
            )

        def row_of(layer, row):
            return small[:, layer * LAYER_ROWS + row].reshape(1, D)

        every, columns, query, key, value, inner, active = out
        gains.append(row_of(layer, GAIN_ROW))
        if layer + 1 < LAYERS:
            mixed, turned, stats, arrived = attend_plane(
                query, key, value, begin, spot, (qkv_weight, up_weight), layer + 1
            )
            halves = (arrived, swapped(arrived))
            gain_row = row_of(layer + 1, GAIN_ROW)
            at = (layer + 1) * LAYER_ROWS + JOINT_BIAS_ROW
            own_bias = lax.dynamic_slice_in_dim(
                small[:, at : at + 3].reshape(3, GROUP, HEAD_COLS), me, 1, axis=1
            ).reshape(1, JOINT_COLS)
        else:
            mixed, turned, stats = attend_plane(query, key, value, begin, spot)
        saved.append(
            (hidden, every, columns, query, key, value, inner, active, mixed, turned, stats)
        )
        branches = (
            hidden,
            row_of(layer, OUT_BIAS_ROW) + row_of(layer, DOWN_BIAS_ROW),
            mixed,
            active,
            out_weight,
            down_weight,
            layer,
        )
        if layer + 1 < LAYERS:
            hidden = forward_scatter(*branches)[0]

    grad_hidden = cotangent[0].astype(jnp.float32) * keep_mask[0].astype(jnp.float32)[:, None]
    summed = branch = None
    own_branches, other_branches = [], []
    for layer in reversed(range(LAYERS)):
        before, every, columns, query, key, value, inner, active, mixed, turned, stats = saved[layer]
        grad_mixed, grad_inner, branch, *other = backward_gather(
            grad_hidden.astype(jnp.bfloat16),
            out_weight,
            down_weight,
            inner,
            mixed,
            active,
            layer,
            () if layer + 1 == LAYERS else (branch,),
        )
        own_branches.insert(0, branch)
        other_branches = list(other) + other_branches
        grad_joint, *rest = attend_plane_back(
            query,
            key,
            value,
            begin,
            spot,
            turned,
            stats,
            grad_mixed,
            tables,
            summed,
            every,
            grad_inner,
        )
        grad_above = grad_hidden
        out = backward_scatter(
            before,
            grad_hidden,
            gains[layer],
            grad_joint,
            grad_inner,
            columns.reshape(D, COLS),
            every,
            layer,
            *((rest[2], rest[:2], branch) if rest else ()),
        )
        if layer > 0:
            grad_hidden, small, summed = out
            small_grads.insert(0, small)
            continue
        total, shares, joint, upper, *wholes, first = out
        joint_grads.append(wholes[0])
        upper_grads.append(wholes[1])
        hidden, grad_hidden, small, joint, upper, other = forward_scatter(
            *branches, (total, before, grad_above, gains[layer], shares, joint, upper, branch)
        )
        small_grads.insert(0, small)
        joint_grads.insert(0, joint)
        upper_grads.insert(0, upper)
        other_branches.insert(0, jnp.concatenate([first, other], axis=0))
    here, there = jnp.stack(own_branches), jnp.stack(other_branches)
    result = hidden.astype(jnp.bfloat16)[None]

    def branch_grad(part):
        return here[:, part].astype(jnp.float32) + there[:, part].astype(jnp.float32)

    small = jnp.stack(small_grads)
    return (
        result,
        grad_hidden[None],
        small[:, 0],
        small[:, 1],
        jnp.stack(joint_grads).astype(jnp.float32),
        small[:, 3:6].reshape(LAYERS, JOINT_COLS),
        branch_grad(slice(0, HEAD_COLS)),
        small[:, 2],
        jnp.stack(upper_grads).astype(jnp.float32),
        small[:, 6:10].reshape(LAYERS, FEED_COLS),
        branch_grad(slice(HEAD_COLS, None)),
        small[:, 2],
    )


def solution(mesh):
    small = mesh.shape["ctx"] == SIDE and mesh.shape["fsdp"] == SIDE and mesh.shape["seq"] == 2
    on_device = on_device_split if small else on_device_gathered
    return jax.shard_map(
        on_device,
        mesh=mesh,
        in_specs=(
            P(("seq", "fsdp"), "ctx", None),
            P(("seq", "fsdp"), None),
            P(("seq", "fsdp"), "ctx"),
            P(None, ("ctx", "fsdp")),
            P(None, ("ctx", "fsdp")),
            P(None, ("ctx", "fsdp"), None),
            P(None, ("ctx", "fsdp")),
            P(None, ("ctx", "fsdp"), None),
            P(None, ("ctx", "fsdp")),
            P(None, ("ctx", "fsdp"), None),
            P(None, ("ctx", "fsdp")),
            P(None, ("ctx", "fsdp"), None),
            P(None, ("ctx", "fsdp")),
            P(("seq", "fsdp"), "ctx", None),
        ),
        out_specs=(
            P(("seq", "fsdp"), "ctx", None),
            P(("seq", "fsdp"), "ctx", None),
            P(None, ("ctx", "fsdp")),
            P(None, ("ctx", "fsdp")),
            P(None, ("ctx", "fsdp"), None),
            P(None, ("ctx", "fsdp")),
            P(None, ("ctx", "fsdp"), None),
            P(None, ("ctx", "fsdp")),
            P(None, ("ctx", "fsdp"), None),
            P(None, ("ctx", "fsdp")),
            P(None, ("ctx", "fsdp"), None),
            P(None, ("ctx", "fsdp")),
        ),
        check_vma=False,
    )
```

```python
import functools
import math

import jax
import jax.numpy as jnp
import numpy as np
from jax import lax
from jax.experimental import pallas as pl
from jax.experimental.pallas import tpu as pltpu
from jax.sharding import PartitionSpec as P

D = 2048
HEADS = 32
HEAD_DIM = 64
ROT = 32
FF = 8192
LAYERS = 2


EPS = 1e-05
NEG = -1e30


def place_tokens(token_index, lengths):
    bounds = jnp.cumsum(lengths)
    starts = bounds - lengths
    segment = jnp.sum((token_index[:, None] >= bounds[None, :]).astype(jnp.int32), axis=1)
    chosen = segment[:, None] == jnp.arange(lengths.shape[0], dtype=jnp.int32)[None, :]
    position = token_index - jnp.sum(jnp.where(chosen, starts[None, :], 0), axis=1)
    return (segment, position)


def angles(position):
    indices = jnp.arange(0, ROT, 2, dtype=jnp.float32) / ROT
    inverse = 1.0 / 10000.0**indices
    turned = position.astype(jnp.float32)[:, None] * inverse[None, :]
    turned = jnp.concatenate([turned, turned], axis=1)
    return (jnp.cos(turned), jnp.sin(turned))


def rotate(values, cosine, sine):
    rotary = values[..., :ROT]
    middle = ROT // 2
    turned = jnp.concatenate([-rotary[..., middle:], rotary[..., :middle]], axis=-1)
    mixed = rotary * cosine[:, None, :] + turned * sine[:, None, :]
    return jnp.concatenate([mixed, values[..., ROT:]], axis=-1)


def normalize(hidden, gain_row, shift_row):
    average = jnp.mean(hidden, axis=1, keepdims=True)
    centred = hidden - average
    spread = jnp.mean(centred * centred, axis=1, keepdims=True)
    return centred * lax.rsqrt(spread + EPS) * gain_row + shift_row


def block_scores(queries, travelling, start, query_index, query_segment, lengths):
    key_flat, value_flat, key_keep = travelling
    count = key_flat.shape[0]
    key_index = start + jnp.arange(count, dtype=jnp.int32)
    key_segment = place_tokens(key_index, lengths)[0]
    allowed = (
        (query_segment[:, None] == key_segment[None, :])
        & (key_index[None, :] <= query_index[:, None])
        & ((key_keep[None, :] > 0) | (key_index[None, :] == query_index[:, None]))
    )
    key_rows = key_flat.reshape(count, HEADS, HEAD_DIM)
    value_rows = value_flat.reshape(count, HEADS, HEAD_DIM)
    scores = jnp.einsum("qhd,khd->hqk", queries, key_rows, preferred_element_type=jnp.float32) * (
        1.0 / math.sqrt(HEAD_DIM)
    )
    return (scores, allowed, key_rows, value_rows)


def attend(running, travelling, start, queries, query_index, query_segment, lengths):
    maxima, totals, weighted = running
    scores, allowed, key_rows, value_rows = block_scores(
        queries, travelling, start, query_index, query_segment, lengths
    )
    masked = jnp.where(allowed[None], scores, NEG)
    new_max = jnp.maximum(maxima, jnp.max(masked, axis=2))
    probs = jnp.where(allowed[None], jnp.exp(masked - new_max[:, :, None]), 0.0)
    totals = jnp.sum(probs, axis=2)
    weighted = jnp.einsum(
        "hqk,khd->hqd", probs.astype(jnp.bfloat16), value_rows, preferred_element_type=jnp.float32
    )
    return (new_max, totals, weighted)


def attend_back(
    travelling, start, queries, maxima, grad_numer, drift, query_index, query_segment, lengths
):
    scores, allowed, key_rows, value_rows = block_scores(
        queries, travelling, start, query_index, query_segment, lengths
    )
    count = key_rows.shape[0]
    scale = 1.0 / math.sqrt(HEAD_DIM)
    probs = jnp.where(allowed[None], jnp.exp(scores - maxima[:, :, None]), 0.0)
    grad_probs = jnp.einsum(
        "hqd,khd->hqk", grad_numer, value_rows, preferred_element_type=jnp.float32
    )
    grad_scores = (probs * (grad_probs - drift[:, :, None])).astype(jnp.bfloat16)
    grad_query = (
        jnp.einsum("hqk,khd->qhd", grad_scores, key_rows, preferred_element_type=jnp.float32)
        * scale
    )
    grad_key = (
        jnp.einsum("hqk,qhd->khd", grad_scores, queries, preferred_element_type=jnp.float32) * scale
    )
    grad_value = jnp.einsum(
        "hqk,hqd->khd", probs.astype(jnp.bfloat16), grad_numer, preferred_element_type=jnp.float32
    )
    return (
        grad_query,
        grad_key.reshape(count, HEADS * HEAD_DIM),
        grad_value.reshape(count, HEADS * HEAD_DIM),
    )


def attention_forward(queries, key_flat, value_flat, key_keep, query_index, query_segment, lengths):
    row_count = key_flat.shape[0]
    initial = (
        jnp.full((HEADS, row_count), NEG, jnp.float32),
        jnp.zeros((HEADS, row_count), jnp.float32),
        jnp.zeros((HEADS, row_count, HEAD_DIM), jnp.float32),
    )
    return attend(
        initial,
        (
            lax.all_gather(key_flat, "ctx", axis=0, tiled=True),
            lax.all_gather(value_flat, "ctx", axis=0, tiled=True),
            lax.all_gather(key_keep, "ctx", axis=0, tiled=True),
        ),
        jnp.int32(0),
        queries,
        query_index,
        query_segment,
        lengths,
    )


def attention_backward(
    queries,
    key_flat,
    value_flat,
    key_keep,
    maxima,
    grad_numer,
    drift,
    query_index,
    query_segment,
    lengths,
):
    whole = (
        lax.all_gather(key_flat, "ctx", axis=0, tiled=True),
        lax.all_gather(value_flat, "ctx", axis=0, tiled=True),
        lax.all_gather(key_keep, "ctx", axis=0, tiled=True),
    )
    grad_query, every_key, every_value = attend_back(
        whole, 0, queries, maxima, grad_numer, drift, query_index, query_segment, lengths
    )
    grad_key, grad_value = (
        lax.psum_scatter(
            every_key.astype(jnp.bfloat16), "ctx", scatter_dimension=0, tiled=True
        ).astype(jnp.float32),
        lax.psum_scatter(
            every_value.astype(jnp.bfloat16), "ctx", scatter_dimension=0, tiled=True
        ).astype(jnp.float32),
    )
    return (grad_query, grad_key, grad_value)


def layer_forward(hidden, weights, cosine, sine, key_keep, query_index, query_segment, lengths):
    (
        norm_gain,
        norm_shift,
        joint_weight,
        joint_bias,
        output_weight,
        output_bias,
        upper_weight,
        upper_bias,
        lower_weight,
        lower_bias,
    ) = weights
    row_count = hidden.shape[0]
    width = HEADS * HEAD_DIM
    normed = normalize(
        hidden, norm_gain.astype(jnp.float32), norm_shift.astype(jnp.float32)
    ).astype(jnp.bfloat16)
    joint = jnp.dot(normed, joint_weight, preferred_element_type=jnp.float32) + joint_bias.astype(
        jnp.float32
    )
    queries = rotate(joint[:, :width].reshape(row_count, HEADS, HEAD_DIM), cosine, sine).astype(
        jnp.bfloat16
    )
    key_flat = (
        rotate(joint[:, width : 2 * width].reshape(row_count, HEADS, HEAD_DIM), cosine, sine)
        .astype(jnp.bfloat16)
        .reshape(row_count, width)
    )
    value_flat = joint[:, 2 * width :].astype(jnp.bfloat16)
    maxima, totals, weighted = attention_forward(
        queries, key_flat, value_flat, key_keep, query_index, query_segment, lengths
    )
    mixed = (weighted / totals[:, :, None]).transpose(1, 0, 2).reshape(row_count, width)
    attention_out = jnp.dot(
        mixed.astype(jnp.bfloat16), output_weight, preferred_element_type=jnp.float32
    ) + output_bias.astype(jnp.float32)
    inner = jnp.dot(normed, upper_weight, preferred_element_type=jnp.float32) + upper_bias.astype(
        jnp.float32
    )
    activated = jax.nn.gelu(inner, approximate=True).astype(jnp.bfloat16)
    feed_out = jnp.dot(
        activated, lower_weight, preferred_element_type=jnp.float32
    ) + lower_bias.astype(jnp.float32)
    saved = (hidden, normed, queries, key_flat, value_flat, maxima, totals, mixed, inner, activated)
    return (hidden + (attention_out + feed_out), saved)


def layer_backward(
    grad_out, saved, weights, cosine, sine, key_keep, query_index, query_segment, lengths
):
    hidden, normed, queries, key_flat, value_flat, maxima, totals, mixed, inner, activated = saved
    (
        norm_gain,
        norm_shift,
        joint_weight,
        joint_bias,
        output_weight,
        output_bias,
        upper_weight,
        upper_bias,
        lower_weight,
        lower_bias,
    ) = weights
    row_count = hidden.shape[0]
    width = HEADS * HEAD_DIM
    ratio = FF // D
    grad_branch = grad_out.astype(jnp.bfloat16)
    mixed_low = mixed.astype(jnp.bfloat16)
    branch_bias = jnp.sum(grad_branch, axis=0, dtype=jnp.float32)
    grad_activated = jnp.einsum(
        "td,fd->tf", grad_branch, lower_weight, preferred_element_type=jnp.float32
    )
    gelu_pull = jax.vjp(functools.partial(jax.nn.gelu, approximate=True), inner)[1]
    grad_inner = gelu_pull(grad_activated)[0].astype(jnp.bfloat16)
    upper_bias_grad = jnp.sum(grad_inner, axis=0, dtype=jnp.float32)
    grad_normed = jnp.einsum(
        "tf,df->td", grad_inner, upper_weight, preferred_element_type=jnp.float32
    )
    upper_bias_rows = upper_bias_grad.reshape(D, ratio)
    normed_cols = normed
    upper_part = jnp.einsum(
        "tc,tf->cf", normed_cols, grad_inner, preferred_element_type=jnp.float32
    )
    lower_part = jnp.einsum(
        "tc,td->cd", activated, grad_branch, preferred_element_type=jnp.float32
    ).reshape(lax.axis_size(("ctx", "fsdp")) * (D // lax.axis_size(("ctx", "fsdp"))), ratio * width)
    bias_part = upper_bias_rows
    branch_part = branch_bias[:, None]
    feed_share = lax.psum_scatter(
        jnp.concatenate([upper_part, lower_part, bias_part, branch_part], axis=1),
        ("ctx", "fsdp"),
        scatter_dimension=0,
        tiled=True,
    )
    share_rows = feed_share.shape[0]
    upper_share = feed_share[:, :FF]
    lower_share = feed_share[:, FF : FF + ratio * width].reshape(share_rows * ratio, width)
    upper_bias_share = feed_share[:, FF + ratio * width : FF + ratio * width + ratio].reshape(
        share_rows * ratio
    )
    branch_share = feed_share[:, FF + ratio * width + ratio]
    feed_parts = (upper_share, upper_bias_share, lower_share, branch_share)
    output_share = None
    grad_mixed = jnp.einsum(
        "te,de->td", grad_branch, output_weight, preferred_element_type=jnp.float32
    )
    head_mixed = mixed.reshape(row_count, HEADS, HEAD_DIM).transpose(1, 0, 2)
    head_grad = grad_mixed.reshape(row_count, HEADS, HEAD_DIM).transpose(1, 0, 2)
    drift = jnp.sum(head_grad * head_mixed, axis=2) / totals
    grad_numer = (head_grad / totals[:, :, None]).astype(jnp.bfloat16)
    grad_query, grad_key, grad_value = attention_backward(
        queries,
        key_flat,
        value_flat,
        key_keep,
        maxima,
        grad_numer,
        drift,
        query_index,
        query_segment,
        lengths,
    )
    grad_query = rotate(grad_query, cosine, -sine).reshape(row_count, width)
    grad_key = rotate(grad_key.reshape(row_count, HEADS, HEAD_DIM), cosine, -sine).reshape(
        row_count, width
    )
    grad_joint = jnp.concatenate([grad_query, grad_key, grad_value], axis=1).astype(jnp.bfloat16)
    joint_bias_grad = jnp.sum(grad_joint, axis=0, dtype=jnp.float32)
    grad_normed = grad_normed + jnp.einsum(
        "te,de->td", grad_joint, joint_weight, preferred_element_type=jnp.float32
    )
    norm_pull = jax.vjp(
        normalize, hidden, norm_gain.astype(jnp.float32), norm_shift.astype(jnp.float32)
    )[1]
    grad_hidden, gain_grad, shift_grad = norm_pull(grad_normed)
    joint_bias_rows = joint_bias_grad.reshape(D, 3)
    normed_cols = normed
    joint_part = jnp.einsum(
        "tc,te->ce", normed_cols, grad_joint, preferred_element_type=jnp.float32
    )
    output_part = jnp.einsum(
        "tc,te->ce", mixed_low, grad_branch, preferred_element_type=jnp.float32
    )
    bias_part = joint_bias_rows
    gain_part = gain_grad[:, None]
    shift_part = shift_grad[:, None]
    attn_share = lax.psum_scatter(
        jnp.concatenate([joint_part, output_part, bias_part, gain_part, shift_part], axis=1),
        ("ctx", "fsdp"),
        scatter_dimension=0,
        tiled=True,
    )
    share_rows = attn_share.shape[0]
    joint_share = attn_share[:, : 3 * width]
    output_share = attn_share[:, 3 * width : 4 * width]
    joint_bias_share = attn_share[:, 4 * width : 4 * width + 3].reshape(share_rows * 3)
    gain_share = attn_share[:, 4 * width + 3]
    shift_share = attn_share[:, 4 * width + 4]
    attention_parts = (gain_share, shift_share, joint_share, joint_bias_share, output_share)
    return (grad_out + grad_hidden, attention_parts, feed_parts)


def on_device_gathered(
    tokens,
    doc_lengths,
    keep_mask,
    ln_gain,
    ln_bias,
    qkv_weight,
    qkv_bias,
    out_weight,
    out_bias,
    up_weight,
    up_bias,
    down_weight,
    down_bias,
    cotangent,
):
    row_count = tokens.shape[1]
    position = lax.axis_index("ctx")
    query_index = position * row_count + jnp.arange(row_count, dtype=jnp.int32)
    lengths = doc_lengths[0]
    query_segment, query_position = place_tokens(query_index, lengths)
    cosine, sine = angles(query_position)
    key_keep = keep_mask[0].astype(jnp.bfloat16)
    shards = (
        ln_gain,
        ln_bias,
        qkv_weight,
        qkv_bias,
        out_weight,
        out_bias,
        up_weight,
        up_bias,
        down_weight,
        down_bias,
    )

    def fetch(layer_index):
        return (
            lax.all_gather(shards[0][layer_index], ("ctx", "fsdp"), axis=0, tiled=True),
            lax.all_gather(shards[1][layer_index], ("ctx", "fsdp"), axis=0, tiled=True),
            lax.all_gather(shards[2][layer_index], ("ctx", "fsdp"), axis=0, tiled=True),
            lax.all_gather(shards[3][layer_index], ("ctx", "fsdp"), axis=0, tiled=True),
            lax.all_gather(shards[4][layer_index], ("ctx", "fsdp"), axis=0, tiled=True),
            lax.all_gather(shards[5][layer_index], ("ctx", "fsdp"), axis=0, tiled=True),
            lax.all_gather(shards[6][layer_index], ("ctx", "fsdp"), axis=0, tiled=True),
            lax.all_gather(shards[7][layer_index], ("ctx", "fsdp"), axis=0, tiled=True),
            lax.all_gather(shards[8][layer_index], ("ctx", "fsdp"), axis=0, tiled=True),
            lax.all_gather(shards[9][layer_index], ("ctx", "fsdp"), axis=0, tiled=True),
        )

    hidden = tokens[0].astype(jnp.float32)
    saved_layers = []
    weights = None
    for layer_index in range(LAYERS):
        weights = fetch(layer_index)
        hidden, saved = layer_forward(
            hidden, weights, cosine, sine, key_keep, query_index, query_segment, lengths
        )
        saved_layers.append(saved)
    result = hidden.astype(jnp.bfloat16)[None]
    grad_hidden = cotangent[0].astype(jnp.float32) * keep_mask[0].astype(jnp.float32)[:, None]
    attention_list = [None] * LAYERS
    feed_list = [None] * LAYERS
    for layer_index in reversed(range(LAYERS)):
        weights = weights if layer_index == LAYERS - 1 else fetch(layer_index)
        grad_hidden, attention_parts, feed_parts = layer_backward(
            grad_hidden,
            saved_layers[layer_index],
            weights,
            cosine,
            sine,
            key_keep,
            query_index,
            query_segment,
            lengths,
        )
        attention_list[layer_index] = attention_parts
        feed_list[layer_index] = feed_parts
    gain_stack = jnp.stack([attention_list[layer_index][0] for layer_index in range(LAYERS)])
    shift_stack = jnp.stack([attention_list[layer_index][1] for layer_index in range(LAYERS)])
    joint_stack = jnp.stack([attention_list[layer_index][2] for layer_index in range(LAYERS)])
    joint_bias_stack = jnp.stack([attention_list[layer_index][3] for layer_index in range(LAYERS)])
    output_stack = jnp.stack([attention_list[layer_index][4] for layer_index in range(LAYERS)])
    upper_stack = jnp.stack([feed_list[layer_index][0] for layer_index in range(LAYERS)])
    upper_bias_stack = jnp.stack([feed_list[layer_index][1] for layer_index in range(LAYERS)])
    lower_stack = jnp.stack([feed_list[layer_index][2] for layer_index in range(LAYERS)])
    branch_stack = jnp.stack([feed_list[layer_index][3] for layer_index in range(LAYERS)])
    summed = (
        lax.psum(gain_stack.astype(jnp.bfloat16), "seq").astype(jnp.float32),
        lax.psum(shift_stack.astype(jnp.bfloat16), "seq").astype(jnp.float32),
        lax.psum(joint_stack.astype(jnp.bfloat16), "seq").astype(jnp.float32),
        lax.psum(joint_bias_stack.astype(jnp.bfloat16), "seq").astype(jnp.float32),
        lax.psum(output_stack.astype(jnp.bfloat16), "seq").astype(jnp.float32),
        lax.psum(upper_stack.astype(jnp.bfloat16), "seq").astype(jnp.float32),
        lax.psum(upper_bias_stack.astype(jnp.bfloat16), "seq").astype(jnp.float32),
        lax.psum(lower_stack.astype(jnp.bfloat16), "seq").astype(jnp.float32),
        lax.psum(branch_stack.astype(jnp.bfloat16), "seq").astype(jnp.float32),
    )
    return (
        result,
        grad_hidden[None],
        summed[0],
        summed[1],
        summed[2],
        summed[3],
        summed[4],
        summed[8],
        summed[5],
        summed[6],
        summed[7],
        summed[8],
    )


SIDE = 4
GROUP = SIDE * SIDE
OWN = HEADS // GROUP
HEAD_COLS = OWN * HEAD_DIM
JOINT_COLS = 3 * HEAD_COLS
FEED_COLS = FF // GROUP
COLS = JOINT_COLS + FEED_COLS
BACK_COLS = HEAD_COLS + FEED_COLS
SHARE = D // GROUP
VMEM = pl.BlockSpec(memory_space=pltpu.VMEM)
HBM = pl.BlockSpec(memory_space=pl.ANY)
MESH = pl.DeviceIdType.MESH
ROOM = 60 * 2**20


def dot(left, right, left_dim=1, right_dim=0):
    return lax.dot_general(
        left, right, (((left_dim,), (right_dim,)), ((), ())), preferred_element_type=jnp.float32
    )


def digit(entries, index):
    words = [
        sum(entry << (2 * place) for place, entry in enumerate(entries[start : start + 8]))
        for start in range(0, len(entries), 8)
    ]
    word = jnp.int32(words[0])
    for number in range(1, len(words)):
        word = jnp.where(index >= 8 * number, jnp.int32(words[number]), word)
    return lax.rem(lax.shift_right_logical(word, 2 * lax.rem(index, 8)), 4)


def nibble(entries, index):
    word = jnp.int32(0)
    for start in range(0, len(entries), 7):
        packed = sum(entry << (4 * place) for place, entry in enumerate(entries[start : start + 7]))
        word = jnp.where(index >= start, jnp.int32(packed), word)
    return lax.rem(lax.shift_right_logical(word, 4 * lax.rem(index, 7)), 16)


def digit_of_row(table, row, index):
    value = digit(table[0], index)
    for number in range(1, len(table)):
        value = jnp.where(row == number, digit(table[number], index), value)
    return value


NEAR = ((0, 1, 2, 3), (1, 0, 2, 3), (2, 3, 1, 0), (3, 2, 1, 0))
FAR = ((3, 2, 1, 0), (3, 0, 2, 1), (0, 3, 1, 2), (0, 1, 2, 3))


def neighbours():
    ctx, place = lax.axis_index("ctx"), lax.axis_index("fsdp")
    twin = ctx + 1 - 2 * lax.rem(ctx, 2)
    across = lax.rem(ctx + 2, 4)
    return ctx, place, twin, across, lax.rem(twin + 2, 4)


def greet_neighbours(cross=False):
    ctx, place, twin, across, _ = neighbours()
    barrier = pltpu.get_barrier_semaphore()
    pl.semaphore_signal(barrier, inc=1, device_id={"ctx": twin}, device_id_type=MESH)
    pl.semaphore_signal(barrier, inc=1, device_id={"ctx": across}, device_id_type=MESH)

    @pl.when(place > 0)
    def _():
        pl.semaphore_signal(barrier, inc=1, device_id={"fsdp": place - 1}, device_id_type=MESH)

    @pl.when(place < SIDE - 1)
    def _():
        pl.semaphore_signal(barrier, inc=1, device_id={"fsdp": place + 1}, device_id_type=MESH)

    if cross:
        pl.semaphore_signal(
            barrier, inc=1, device_id={"seq": 1 - lax.axis_index("seq")}, device_id_type=MESH
        )
    inner = jnp.int32(3 if cross else 2) + jnp.where(place > 0, 1, 0) + jnp.where(place < SIDE - 1, 1, 0)
    pl.semaphore_wait(barrier, inner)


def greet_plane(steps, cross=True):
    ctx, place = lax.axis_index("ctx"), lax.axis_index("fsdp")
    me = ctx * SIDE + place
    barrier = pltpu.get_barrier_semaphore()
    for step in range(1, steps):
        peer = lax.rem(me + step, GROUP)
        pl.semaphore_signal(
            barrier,
            inc=1,
            device_id={"ctx": peer // SIDE, "fsdp": lax.rem(peer, SIDE)},
            device_id_type=MESH,
        )
    if cross:
        pl.semaphore_signal(
            barrier, inc=1, device_id={"seq": 1 - lax.axis_index("seq")}, device_id_type=MESH
        )
    pl.semaphore_wait(barrier, steps if cross else steps - 1)


def to_peer(source, target, send, recv, peer):
    return pltpu.make_async_remote_copy(
        src_ref=source,
        dst_ref=target,
        send_sem=send,
        recv_sem=recv,
        device_id={"ctx": peer // SIDE, "fsdp": lax.rem(peer, SIDE)},
        device_id_type=MESH,
    )


def to_axis(source, target, send, recv, axis, index):
    return pltpu.make_async_remote_copy(
        src_ref=source,
        dst_ref=target,
        send_sem=send,
        recv_sem=recv,
        device_id={axis: index},
        device_id_type=MESH,
    )


PARTS = ((0, 112), (112, 96), (208, 48))
LAST = len(PARTS) - 1
GATHER_KIND = (
    (0, 0, 0, 0, 0, 1, 0, 0, 1, 0, 2, 0, 1, 1, 1, 2, 0, 0, 1, 0, 1, 3, 2, 1, 0, 3, 1, 1, 1, 1, 0, 3, 0, 0, 1, 1, 1, 1, 2, 3),
    (0, 0, 0, 1, 0, 0, 0, 0, 0, 0, 0, 0, 1, 0, 2, 1, 2, 1, 0, 1, 1, 2, 0, 3, 1, 1, 0, 1, 1, 1, 3, 1, 1, 0, 1, 3, 1, 1, 2, 3),
)
GATHER_STEP = (
    (0, 0, 1, 0, 0, 0, 1, 1, 0, 1, 0, 2, 0, 0, 1, 1, 2, 2, 1, 2, 1, 0, 2, 1, 3, 1, 2, 2, 2, 2, 3, 2, 3, 3, 3, 3, 3, 3, 3, 3),
    (0, 0, 0, 0, 2, 2, 1, 0, 1, 2, 1, 1, 0, 2, 0, 0, 2, 0, 3, 2, 2, 1, 3, 0, 2, 1, 3, 1, 2, 1, 2, 3, 1, 3, 3, 1, 3, 3, 3, 3),
)
GATHER_PART = (
    (1, 0, 1, 2, 3, 1, 2, 0, 0, 3, 3, 2, 2, 3, 0, 3, 1, 0, 1, 3, 2, 3, 3, 3, 0, 3, 1, 2, 0, 3, 1, 3, 2, 3, 1, 0, 2, 3, 3, 3),
    (1, 0, 2, 0, 2, 0, 2, 3, 1, 1, 0, 3, 2, 3, 3, 1, 3, 3, 0, 0, 2, 3, 1, 3, 1, 1, 2, 2, 3, 0, 3, 2, 3, 3, 0, 3, 1, 3, 3, 3),
)
FIRST_KIND = (
    (0, 0, 0, 0, 0, 0, 0, 0, 0, 1, 3, 2, 3, 2, 0, 1, 3, 1, 0, 1, 0, 0, 0, 1, 1, 0, 0, 3, 0, 0, 2, 2, 0, 1, 0, 0, 1, 1, 1, 0, 0, 1, 1, 2, 2, 3, 3, 0, 1, 0, 0, 0, 0, 1, 1, 3, 2, 1, 0, 1, 1, 2, 0, 2, 2, 0, 1, 3, 0, 1, 0, 0, 3, 3, 2, 1, 1, 1, 2, 1, 3, 3),
    (0, 0, 0, 0, 0, 2, 0, 0, 0, 1, 0, 0, 2, 1, 3, 1, 1, 0, 2, 0, 3, 3, 0, 0, 0, 0, 0, 0, 1, 1, 0, 1, 0, 0, 2, 3, 1, 2, 0, 1, 0, 0, 0, 1, 0, 1, 0, 2, 0, 1, 1, 1, 3, 2, 2, 3, 0, 3, 1, 0, 0, 0, 1, 2, 0, 0, 1, 1, 1, 1, 1, 3, 2, 3, 1, 2, 1, 1, 3, 3, 2, 3),
)
FIRST_STEP = (
    (0, 0, 1, 2, 3, 3, 0, 0, 0, 3, 0, 0, 2, 1, 0, 0, 1, 1, 0, 0, 0, 1, 1, 0, 0, 2, 2, 3, 1, 1, 2, 3, 3, 2, 1, 2, 0, 1, 1, 2, 1, 1, 1, 0, 1, 0, 1, 0, 1, 2, 1, 0, 2, 2, 0, 0, 1, 2, 3, 2, 2, 2, 2, 2, 0, 3, 2, 1, 3, 3, 3, 3, 2, 2, 3, 3, 3, 3, 3, 3, 3, 3),
    (0, 1, 2, 0, 0, 0, 2, 1, 3, 0, 0, 0, 3, 3, 1, 2, 0, 3, 1, 0, 2, 0, 0, 1, 2, 0, 2, 1, 1, 0, 1, 0, 3, 2, 0, 3, 1, 2, 1, 0, 2, 0, 1, 0, 3, 1, 2, 0, 0, 1, 1, 2, 0, 1, 1, 1, 3, 1, 2, 3, 2, 1, 2, 2, 3, 3, 2, 3, 1, 2, 3, 0, 2, 2, 3, 3, 3, 3, 3, 3, 3, 2),
)
FIRST_WHAT = (
    (5, 4, 4, 4, 9, 4, 0, 9, 2, 9, 9, 9, 9, 9, 1, 2, 9, 9, 6, 0, 3, 1, 6, 1, 3, 9, 6, 9, 0, 9, 9, 9, 6, 9, 2, 1, 9, 1, 2, 2, 3, 0, 3, 3, 3, 3, 3, 7, 8, 0, 8, 8, 3, 1, 8, 8, 8, 0, 0, 2, 3, 3, 8, 8, 8, 1, 8, 8, 2, 0, 3, 8, 3, 8, 3, 2, 1, 3, 8, 8, 3, 8),
    (4, 4, 4, 5, 0, 9, 9, 9, 9, 0, 9, 1, 9, 9, 9, 9, 9, 4, 9, 6, 9, 9, 2, 6, 1, 3, 6, 0, 9, 2, 1, 1, 6, 2, 3, 9, 0, 9, 2, 3, 0, 7, 3, 8, 0, 2, 3, 8, 8, 1, 3, 2, 3, 3, 8, 3, 1, 8, 0, 2, 8, 8, 1, 3, 3, 8, 3, 2, 8, 8, 1, 8, 8, 3, 0, 3, 3, 8, 3, 8, 8, 8),
)
OPS = len(GATHER_KIND[0])
WORKS = tuple(
    tuple(
        number for number in range(OPS) if parts[number] == 3
    )
    for parts in GATHER_PART
)


def by_place(tables, index):
    place = lax.axis_index("fsdp")
    at_end = (place == 0) | (place == SIDE - 1)
    return jnp.where(at_end, digit(tables[0], index), digit(tables[1], index))


def gather_slot(kind, step):
    ctx, place, twin, across, twin_across = neighbours()
    line = digit_of_row(NEAR, place, step)
    owner = jnp.where(
        kind == 0, ctx, jnp.where(kind == 1, across, jnp.where(kind == 2, twin, twin_across))
    )
    return line, owner * SIDE + line


def work_slot(number):
    kind = by_place(
        tuple(tuple(row[at] for at in places) for row, places in zip(GATHER_KIND, WORKS)), number
    )
    step = by_place(
        tuple(tuple(row[at] for at in places) for row, places in zip(GATHER_STEP, WORKS)), number
    )
    return gather_slot(kind, step)[1]


def gather_blocks(
    land, every, up, down, side, core, arrived, core_arrived, kept, work, tables=None, more=()
):
    ctx, place, twin, across, _ = neighbours()
    kinds, steps, parts = tables or (GATHER_KIND, GATHER_STEP, GATHER_PART)
    at_end = (place == 0) | (place == SIDE - 1)

    def copies(kind, line, slot, part):
        start, size = PARTS[part]
        block = land.at[slot, pl.ds(start, size)]
        row, met = kind * SIDE + line, arrived.at[slot, part]
        return (
            lambda: to_axis(block, block, up.at[row, part], met, "fsdp", place + 1),
            lambda: to_axis(block, block, down.at[row, part], met, "fsdp", place - 1),
            lambda: to_axis(block, block, side.at[line, part], met, "ctx", across),
        )

    def routes(kind, line, part):
        goes_up = (line <= place) & (place < SIDE - 1)
        goes_down = (line >= place) & (place > 0)
        if part == LAST:
            return goes_up, goes_down, (kind == 0) & (line == place)
        return goes_up & (kind == 0), goes_down & (kind == 0), kind == 0

    def core_copy(kind, line, slot):
        block = land.at[slot]
        return to_axis(
            block, block, core.at[kind * SIDE + line], core_arrived.at[slot], "ctx", twin
        )

    def step_op(number, counts):
        worked, made = counts
        kind, step = by_place(kinds, number), by_place(steps, number)
        part = jnp.where(at_end, nibble(parts[0], number), nibble(parts[1], number))
        line, slot = gather_slot(kind, step)
        for which in range(len(PARTS)):

            @pl.when(part == which)
            def _(which=which):
                @pl.when((kind == 1) | (line != place))
                def _():
                    copies(kind, line, slot, which)[2]().wait_recv()

                for copy, goes in zip(
                    copies(kind, line, slot, which), routes(kind, line, which)
                ):

                    @pl.when(goes)
                    def _(copy=copy):
                        copy().start()

        @pl.when(part == 3)
        def _():
            @pl.when(kind <= 1)
            def _():
                core_copy(kind, line, slot).start()

            @pl.when(kind >= 2)
            def _():
                core_copy(kind - 2, line, slot).wait_recv()

            if every is not None:
                pltpu.make_async_copy(land.at[slot], every.at[slot], kept.at[slot]).start()
            work(worked, slot)

        for which, further in enumerate(more):

            @pl.when(part == 4 + which)
            def _(further=further):
                further(step, slot, made)

        return worked + jnp.where(part == 3, 1, 0), made + jnp.where(part == 8, 1, 0)

    lax.fori_loop(0, len(kinds[0]), step_op, (jnp.int32(0), jnp.int32(0)))

    def finish(number, carry):
        kind, line = number // SIDE, lax.rem(number, SIDE)
        slot = jnp.where(kind == 0, ctx, across) * SIDE + line
        for which in range(len(PARTS)):
            for copy, goes in zip(copies(kind, line, slot, which), routes(kind, line, which)):

                @pl.when(goes)
                def _(copy=copy):
                    copy().wait_send()

        core_copy(kind, line, slot).wait_send()
        return carry

    lax.fori_loop(0, 2 * SIDE, finish, 0)

    def finish_kept(slot, carry):
        pltpu.make_async_copy(land.at[slot], every.at[slot], kept.at[slot]).wait()
        return carry

    if every is not None:
        lax.fori_loop(0, GROUP, finish_kept, 0)


def gather_scratch(rows):
    parts = len(PARTS)
    return [
        pltpu.VMEM((GROUP, rows, D), jnp.bfloat16),
        pltpu.SemaphoreType.DMA((2 * SIDE, parts)),
        pltpu.SemaphoreType.DMA((2 * SIDE, parts)),
        pltpu.SemaphoreType.DMA((SIDE, parts)),
        pltpu.SemaphoreType.DMA((2 * SIDE,)),
        pltpu.SemaphoreType.DMA((GROUP, parts)),
        pltpu.SemaphoreType.DMA((GROUP,)),
        pltpu.SemaphoreType.DMA((GROUP,)),
    ]


def spin(values, cosine, sine, sign):
    lane = lax.rem(lax.broadcasted_iota(jnp.int32, values.shape, 1), HEAD_DIM)
    partner = jnp.where(
        lane < ROT // 2,
        -pltpu.roll(values, HEAD_COLS - ROT // 2, 1),
        pltpu.roll(values, ROT // 2, 1),
    )
    return values * cosine + sign * (partner * sine)


STRIP = 32


def each_strip(rows, body, start):
    def step(number, carry):
        return body(pl.ds(pl.multiple_of(number * STRIP, STRIP), STRIP), carry)

    return lax.fori_loop(0, rows // STRIP, step, start)


def column_places(block):
    return [
        (0, pl.multiple_of(part * D + block * HEAD_COLS, HEAD_COLS), part * HEAD_COLS, HEAD_COLS)
        for part in range(3)
    ] + [(1, pl.multiple_of(block * FEED_COLS, FEED_COLS), JOINT_COLS, FEED_COLS)]


PLACES = 4


def plane_swap(swap, sems):
    source, target = swap
    return to_axis(source, target, sems.at[0], sems.at[1], "seq", 1 - lax.axis_index("seq"))


def row_swap(source, target, sems, first, blocks):
    size = source.shape[0] // SWAP_BLOCKS
    return [
        to_axis(
            source.at[pl.ds(block * size, size)],
            target.at[pl.ds((block - first) * size, size)],
            sems.at[0, block],
            sems.at[1, block],
            "seq",
            1 - lax.axis_index("seq"),
        )
        for block in blocks
    ]


SWAP_BLOCKS = 4
SWAP_FIRST = SWAP_BLOCKS // 2


def load_all(pairs, sems):
    copies = [
        pltpu.make_async_copy(source, target, sems.at[number])
        for number, (source, target) in enumerate(pairs)
    ]
    for copy in copies:
        copy.start()
    return copies


def wait_all(copies):
    for copy in copies:
        copy.wait()


def ring_scratch(rows):
    return [
        pltpu.VMEM((2, rows, HEAD_COLS), jnp.bfloat16),
        pltpu.VMEM((2, rows, HEAD_COLS), jnp.bfloat16),
        pltpu.VMEM((2, rows, HEAD_COLS), jnp.bfloat16),
        pltpu.VMEM((2, rows, FEED_COLS), jnp.float32),
        pltpu.VMEM((2, rows, FEED_COLS), jnp.bfloat16),
        pltpu.SemaphoreType.DMA((2, 5)),
    ]


def ring_shapes(rows):
    return [
        jax.ShapeDtypeStruct((GROUP, rows, width), dtype)
        for width, dtype in (
            (HEAD_COLS, jnp.bfloat16),
            (HEAD_COLS, jnp.bfloat16),
            (HEAD_COLS, jnp.bfloat16),
            (FEED_COLS, jnp.float32),
            (FEED_COLS, jnp.bfloat16),
        )
    ]


def ring_product(rings, sems, results, land, columns, bias, cosine, sine):
    query, key, value, inner, active = rings

    def leave(at, slot):
        return [
            pltpu.make_async_copy(ring.at[at], result.at[slot], sems.at[at, which])
            for which, (ring, result) in enumerate(zip(rings, results))
        ]

    def product(number, slot):
        whole = dot(land[slot], columns[...].reshape(D, COLS)) + bias[...]
        one, two = HEAD_COLS, 2 * HEAD_COLS
        at = lax.rem(number, 2)

        @pl.when(number >= 2)
        def _():
            wait_all(leave(at, 0))

        query[at] = spin(whole[:, :one], cosine[slot], sine[slot], 1.0).astype(jnp.bfloat16)
        key[at] = spin(whole[:, one:two], cosine[slot], sine[slot], 1.0).astype(jnp.bfloat16)
        value[at] = whole[:, two:JOINT_COLS].astype(jnp.bfloat16)
        units = whole[:, JOINT_COLS:]
        inner[at] = units
        active[at] = jax.nn.gelu(units, approximate=True).astype(jnp.bfloat16)
        for copy in leave(at, slot):
            copy.start()

    def finish():
        for at in range(2):
            wait_all(leave(at, 0))

    return product, finish


def norm_block(hidden, gain, shift, land, me):
    def strip(part, carry):
        values = hidden[part].astype(jnp.float32)
        centred = values - jnp.mean(values, axis=1, keepdims=True)
        spread = jnp.mean(centred * centred, axis=1, keepdims=True)
        normed = centred * lax.rsqrt(spread + EPS) * gain[...] + shift[...]
        land[me, part] = normed.astype(jnp.bfloat16)
        return carry

    each_strip(hidden.shape[0], strip, 0)


def forward_gather(hidden, gain, shift, bias, tables, halves, layer):
    rows = hidden.shape[0]
    half = SHARE // 2

    def kernel(hidden, gain, shift, bias, turn_a, turn_b, own_half, other_half, *refs):
        every, columns_out, results, refs = refs[0], refs[1], refs[2:7], refs[7:]
        cosine, sine, columns, load_sem, saved = refs[:5]
        rings, ring_sem, refs = refs[5:10], refs[10], refs[11:]
        land, sems = refs[0], refs[1:]
        ctx, place, seq = lax.axis_index("ctx"), lax.axis_index("fsdp"), lax.axis_index("seq")
        part_rows = pl.ds(pl.multiple_of(seq * half, half), half)
        other_rows = pl.ds(pl.multiple_of((1 - seq) * half, half), half)
        loads = load_all(
            (
                (own_half, columns.at[:, part_rows]),
                (other_half, columns.at[:, other_rows]),
                (turn_a, cosine),
                (turn_b, sine),
            ),
            load_sem,
        )
        greet_neighbours()
        norm_block(hidden, gain, shift, land, ctx * SIDE + place)
        save = pltpu.make_async_copy(columns, columns_out, saved)
        product, finish = ring_product(rings, ring_sem, results, land, columns, bias, cosine, sine)

        def work(number, slot):
            @pl.when(number == 0)
            def _():
                wait_all(loads)
                save.start()

            product(number, slot)

        gather_blocks(land, every, *sems, work)
        save.wait()
        finish()

    return pl.pallas_call(
        kernel,
        out_shape=[
            jax.ShapeDtypeStruct((GROUP, rows, D), jnp.bfloat16),
            jax.ShapeDtypeStruct((GROUP, SHARE, COLS), jnp.bfloat16),
        ]
        + ring_shapes(rows),
        in_specs=[VMEM] * 4 + [HBM] * 4,
        out_specs=[HBM] * 7,
        scratch_shapes=[pltpu.VMEM((GROUP, rows, HEAD_COLS), jnp.float32)] * 2
        + [
            pltpu.VMEM((GROUP, SHARE, COLS), jnp.bfloat16),
            pltpu.SemaphoreType.DMA((4,)),
            pltpu.SemaphoreType.DMA,
        ]
        + ring_scratch(rows)
        + gather_scratch(rows),
        compiler_params=pltpu.CompilerParams(
            collective_id=30 + layer, has_side_effects=True, vmem_limit_bytes=ROOM
        ),
    )(hidden, gain, shift, bias, *tables, *halves)


GAIN_ROW, SHIFT_ROW, JOINT_BIAS_ROW, OUT_BIAS_ROW, DOWN_BIAS_ROW, LAYER_ROWS = 0, 1, 2, 5, 6, 7
BEGIN_ROW = LAYERS * LAYER_ROWS


def first_gather(hidden, packed, up_bias, frequency, qkv_weight, up_weight):
    rows = hidden.shape[0]
    half = SHARE // 2

    def kernel(hidden, packed, up_bias, frequency, qkv_weight, up_weight, *refs):
        every, columns_out, results, small, cosine, sine = refs[0], refs[1], refs[2:7], *refs[7:10]
        refs = refs[10:]
        columns, plane_send, plane_recv, cross_send, cross_recv, own_sem, saved = refs[:7]
        small_send, small_recv, gain, shift, bias = refs[7:12]
        rings, ring_sem, refs = refs[12:17], refs[17], refs[18:]
        land, sems = refs[0], refs[1:]
        ctx, place, seq = lax.axis_index("ctx"), lax.axis_index("fsdp"), lax.axis_index("seq")
        me = ctx * SIDE + place
        part_rows = pl.ds(pl.multiple_of(seq * half, half), half)
        sources = (qkv_weight, up_weight)
        greet_plane(GROUP)

        def small_copy(step):
            return to_peer(
                packed,
                small.at[me],
                small_send.at[step],
                small_recv.at[me],
                lax.rem(me + step, GROUP),
            )

        def small_begin(step, carry):
            small_copy(step).start()
            return carry

        lax.fori_loop(1, GROUP, small_begin, 0)
        small[me] = packed[...]

        def piece(step, number):
            peer = lax.rem(me + step, GROUP)
            which, start, at, width = column_places(peer)[number]
            return (
                peer,
                sources[which].at[0, part_rows, pl.ds(start, width)],
                columns.at[me, part_rows, pl.ds(at, width)],
            )

        def send_piece(step, number):
            peer, source, target = piece(step, number)
            return to_peer(
                source, target, plane_send.at[step, number], plane_recv.at[me, number], peer
            )

        def own_piece(number):
            _, source, target = piece(0, number)
            return pltpu.make_async_copy(source, target, own_sem.at[number])

        def cross(source):
            block = columns.at[source, part_rows]
            return to_axis(
                block, block, cross_send.at[source], cross_recv.at[source], "seq", 1 - seq
            )

        for number in range(PLACES):
            own_piece(number).start()

        def send_columns(group, slot, made):
            def send(more, carry):
                step = SIDE * group + more

                @pl.when(step > 0)
                def _():
                    for number in range(PLACES):
                        send_piece(step, number).start()

                return carry

            lax.fori_loop(0, SIDE, send, 0)

        def norm_own(group, slot, made):
            def arrive(step, carry):
                source = lax.rem(me + GROUP - step, GROUP)
                to_peer(
                    packed, small.at[source], small_send.at[step], small_recv.at[source], source
                ).wait_recv()
                return carry

            lax.fori_loop(1, GROUP, arrive, 0)

            def whole_row(row):
                return jnp.concatenate(
                    [small[block, row : row + 1] for block in range(GROUP)], axis=1
                )

            gain[...] = whole_row(GAIN_ROW)
            shift[...] = whole_row(SHIFT_ROW)
            for part in range(3):
                at = part * GROUP + me
                bias[:, part * HEAD_COLS : (part + 1) * HEAD_COLS] = small[
                    at // 3, pl.ds(JOINT_BIAS_ROW + lax.rem(at, 3), 1)
                ]
            bias[:, JOINT_COLS:] = up_bias[...]
            norm_block(hidden, gain, shift, land, me)

        def pass_columns(group, slot, made):
            def pass_on(more, carry):
                step = SIDE * group + more
                source = lax.rem(me + GROUP - step, GROUP)

                @pl.when(step == 0)
                def _():
                    for number in range(PLACES):
                        own_piece(number).wait()

                @pl.when(step > 0)
                def _():
                    for number in range(PLACES):
                        _, _, at, width = column_places(0)[number]
                        target = columns.at[source, part_rows, pl.ds(at, width)]
                        to_peer(
                            target,
                            target,
                            plane_send.at[0, number],
                            plane_recv.at[source, number],
                            source,
                        ).wait_recv()

                cross(source).start()
                return carry

            lax.fori_loop(0, SIDE, pass_on, 0)

        save = pltpu.make_async_copy(columns, columns_out, saved)

        def wait_columns(group, slot, made):
            def arrive(source, carry):
                cross(source).wait_recv()
                return carry

            lax.fori_loop(0, GROUP, arrive, 0)
            save.start()

        product, finish = ring_product(rings, ring_sem, results, land, columns, bias, cosine, sine)

        def next_product(group, slot, made):
            product(made, slot)

        def turn_block(group, slot, made):
            begin = jnp.concatenate(
                [small[slot, BEGIN_ROW + part : BEGIN_ROW + part + 1] for part in range(rows // SHARE)],
                axis=1,
            )
            begin = jnp.broadcast_to(begin, (8, rows)).T[:, :1]
            first = (slot // SIDE) * rows
            token = lax.broadcasted_iota(jnp.int32, (rows, 1), 0) + first
            angle = (token.astype(jnp.float32) - begin) * frequency[...]
            cosine[slot] = jnp.cos(angle)
            sine[slot] = jnp.sin(angle)

        gather_blocks(
            land,
            every,
            *sems,
            lambda number, slot: None,
            (FIRST_KIND, FIRST_STEP, FIRST_WHAT),
            (send_columns, norm_own, pass_columns, wait_columns, next_product, turn_block),
        )
        save.wait()
        finish()

        def end(step, carry):
            cross(step).wait_send()

            @pl.when(step > 0)
            def _():
                small_copy(step).wait_send()
                for number in range(PLACES):
                    send_piece(step, number).wait_send()

            return carry

        lax.fori_loop(0, GROUP, end, 0)

    return pl.pallas_call(
        kernel,
        out_shape=[
            jax.ShapeDtypeStruct((GROUP, rows, D), jnp.bfloat16),
            jax.ShapeDtypeStruct((GROUP, SHARE, COLS), jnp.bfloat16),
        ]
        + ring_shapes(rows)
        + [jax.ShapeDtypeStruct((GROUP,) + packed.shape, packed.dtype)]
        + [jax.ShapeDtypeStruct((GROUP, rows, HEAD_COLS), jnp.float32)] * 2,
        in_specs=[VMEM] * 4 + [HBM] * 2,
        out_specs=[HBM] * 7 + [VMEM] * 3,
        scratch_shapes=[
            pltpu.VMEM((GROUP, SHARE, COLS), jnp.bfloat16),
            pltpu.SemaphoreType.DMA((GROUP, PLACES)),
            pltpu.SemaphoreType.DMA((GROUP, PLACES)),
            pltpu.SemaphoreType.DMA((GROUP,)),
            pltpu.SemaphoreType.DMA((GROUP,)),
            pltpu.SemaphoreType.DMA((PLACES,)),
            pltpu.SemaphoreType.DMA,
            pltpu.SemaphoreType.DMA((GROUP,)),
            pltpu.SemaphoreType.DMA((GROUP,)),
            pltpu.VMEM((1, D), jnp.float32),
            pltpu.VMEM((1, D), jnp.float32),
            pltpu.VMEM((1, COLS), jnp.float32),
        ]
        + ring_scratch(rows)
        + gather_scratch(rows),
        compiler_params=pltpu.CompilerParams(
            collective_id=30, has_side_effects=True, vmem_limit_bytes=ROOM
        ),
    )(hidden, packed, up_bias, frequency, qkv_weight, up_weight)


def backward_gather(grad, out_weight, down_weight, inner, mixed, active, layer, swap=()):
    rows = grad.shape[0]

    def kernel(own, out_weight, down_weight, inner, mixed, active, *refs):
        if swap:
            source, grad_mixed, grad_inner, branch, target, swap_sem = refs[:6]
            refs = refs[6:]
        else:
            grad_mixed, grad_inner, branch = refs[:3]
            refs = refs[3:]
        out_part, down_part, weight_sem, total = refs[:4]
        fetched, fetch_sem, rings, ring_sem = refs[4:7], refs[7], refs[8:10], refs[10]
        land, sems = refs[11], refs[12:]
        inner_part, mixed_part, active_part = fetched
        ctx, place, _, _, _ = neighbours()

        def fetch(number):
            at, slot = lax.rem(number, 2), work_slot(number)
            return [
                pltpu.make_async_copy(source.at[slot], target.at[at], fetch_sem.at[at, which])
                for which, (source, target) in enumerate(zip((inner, mixed, active), fetched))
            ]

        def leave(number):
            at, slot = lax.rem(number, 2), work_slot(number)
            return [
                pltpu.make_async_copy(ring.at[at], result.at[slot], ring_sem.at[at, which])
                for which, (ring, result) in enumerate(zip(rings, (grad_mixed, grad_inner)))
            ]

        weights = load_all(
            ((out_weight.at[layer], out_part), (down_weight.at[layer], down_part)), weight_sem
        )
        for copy in fetch(jnp.int32(0)):
            copy.start()
        greet_neighbours(bool(swap))
        if swap:
            plane_swap((source, target), swap_sem).start()
        land[ctx * SIDE + place] = own[...]
        total[...] = jnp.zeros_like(total)

        def work(number, slot):
            at = lax.rem(number, 2)

            @pl.when(number == 0)
            def _():
                wait_all(weights)

            @pl.when(number + 1 < GROUP)
            def _():
                for copy in fetch(number + 1):
                    copy.start()

            @pl.when(number >= 2)
            def _():
                wait_all(leave(number - 2))

            wait_all(fetch(number))
            block = land[slot]
            rings[0][at] = dot(block, out_part[...], 1, 1)
            value = inner_part[at]
            factor = math.sqrt(2.0 / math.pi)
            square = value * value
            bend = jnp.tanh(factor * value * (1.0 + 0.044715 * square))
            slope = 0.5 * (1.0 + bend) + 0.5 * value * (1.0 - bend * bend) * (
                factor * (1.0 + 3 * 0.044715 * square)
            )
            rings[1][at] = (dot(block, down_part[...], 1, 1) * slope).astype(jnp.bfloat16)
            for copy in leave(number):
                copy.start()
            total[:HEAD_COLS] += dot(mixed_part[at], block, 0, 0)
            total[HEAD_COLS:] += dot(active_part[at], block, 0, 0)

        gather_blocks(land, None, *sems, work)
        branch[...] = total[...].astype(jnp.bfloat16)
        if swap:
            plane_swap((source, target), swap_sem).wait()
        for number in (GROUP - 2, GROUP - 1):
            wait_all(leave(jnp.int32(number)))

    return pl.pallas_call(
        kernel,
        out_shape=(
            jax.ShapeDtypeStruct((GROUP, rows, HEAD_COLS), jnp.float32),
            jax.ShapeDtypeStruct((GROUP, rows, FEED_COLS), jnp.bfloat16),
            jax.ShapeDtypeStruct((BACK_COLS, D), jnp.bfloat16),
        )
        + tuple(jax.ShapeDtypeStruct(array.shape, array.dtype) for array in swap),
        in_specs=[VMEM] + [HBM] * (5 + len(swap)),
        out_specs=(HBM, HBM, VMEM) + (HBM,) * len(swap),
        scratch_shapes=[pltpu.SemaphoreType.DMA((2,))] * len(swap)
        + [
            pltpu.VMEM(out_weight.shape[1:], jnp.bfloat16),
            pltpu.VMEM(down_weight.shape[1:], jnp.bfloat16),
            pltpu.SemaphoreType.DMA((2,)),
            pltpu.VMEM((BACK_COLS, D), jnp.float32),
            pltpu.VMEM((2, rows, FEED_COLS), jnp.float32),
            pltpu.VMEM((2, rows, HEAD_COLS), jnp.bfloat16),
            pltpu.VMEM((2, rows, FEED_COLS), jnp.bfloat16),
            pltpu.SemaphoreType.DMA((2, 3)),
            pltpu.VMEM((2, rows, HEAD_COLS), jnp.float32),
            pltpu.VMEM((2, rows, FEED_COLS), jnp.bfloat16),
            pltpu.SemaphoreType.DMA((2, 2)),
        ]
        + gather_scratch(rows),
        compiler_params=pltpu.CompilerParams(
            collective_id=50 + layer, has_side_effects=True, vmem_limit_bytes=ROOM
        ),
    )(grad, out_weight, down_weight, inner, mixed, active, *swap)


SCATTER_OPS = (
    ((0, 0), (0, 1), (1, 0), (2, 0), (1, 1), (0, 2), (2, 1), (3, 0), (1, 2), (2, 2), (4, 0), (6, 0), (5, 0), (0, 3), (3, 1), (3, 2), (1, 3), (3, 3), (4, 1), (5, 1), (6, 1), (4, 2), (5, 2), (6, 2), (2, 3), (4, 3), (5, 3), (6, 3)),
    ((0, 0), (0, 2), (3, 2), (1, 0), (3, 0), (0, 1), (0, 3), (1, 1), (2, 0), (1, 2), (3, 1), (1, 3), (4, 0), (6, 0), (5, 0), (3, 3), (2, 1), (2, 2), (4, 1), (6, 1), (5, 1), (4, 2), (5, 2), (6, 2), (2, 3), (4, 3), (5, 3), (6, 3)),
)
SCATTER_OPS_WORK = (
    ((0, 0), (0, 1), (1, 0), (2, 0), (1, 1), (0, 2), (2, 1), (3, 0), (1, 2), (2, 2), (4, 0), (6, 0), (7, 0), (5, 0), (0, 3), (3, 1), (3, 2), (1, 3), (3, 3), (4, 1), (7, 0), (5, 1), (7, 0), (7, 0), (7, 0), (7, 0), (7, 0), (6, 1), (4, 2), (7, 0), (5, 2), (7, 0), (7, 0), (7, 0), (6, 2), (2, 3), (7, 0), (7, 0), (7, 0), (7, 0), (7, 0), (4, 3), (5, 3), (6, 3)),
    ((0, 0), (0, 2), (3, 2), (1, 0), (3, 0), (7, 0), (0, 1), (0, 3), (1, 1), (2, 0), (1, 2), (3, 1), (7, 0), (7, 0), (1, 3), (4, 0), (6, 0), (7, 0), (5, 0), (7, 0), (7, 0), (3, 3), (2, 1), (7, 0), (2, 2), (7, 0), (7, 0), (4, 1), (6, 1), (5, 1), (4, 2), (5, 2), (7, 0), (7, 0), (7, 0), (6, 2), (7, 0), (7, 0), (7, 0), (2, 3), (7, 0), (4, 3), (5, 3), (6, 3)),
)
SCATTER_OPS_EARLY = (
    ((0, 0), (0, 1), (1, 0), (3, 0), (2, 0), (0, 2), (1, 1), (2, 1), (1, 2), (2, 2), (0, 3), (4, 0), (6, 0), (7, 0), (7, 0), (7, 0), (5, 0), (7, 0), (3, 1), (1, 3), (7, 0), (7, 0), (7, 0), (4, 1), (7, 0), (7, 0), (7, 0), (6, 1), (7, 0), (5, 1), (7, 0), (7, 0), (7, 0), (7, 0), (7, 0), (3, 2), (3, 3), (2, 3), (4, 2), (5, 2), (6, 2), (8, 0), (8, 1), (8, 2), (8, 3), (4, 3), (5, 3), (6, 3)),
    ((0, 2), (7, 0), (0, 0), (0, 1), (1, 0), (7, 0), (7, 0), (0, 3), (7, 0), (3, 3), (3, 0), (7, 0), (1, 1), (2, 0), (3, 2), (1, 2), (7, 0), (2, 2), (7, 0), (7, 0), (3, 1), (1, 3), (4, 0), (6, 0), (7, 0), (2, 1), (7, 0), (7, 0), (7, 0), (5, 0), (7, 0), (7, 0), (7, 0), (7, 0), (2, 3), (4, 1), (6, 1), (5, 1), (4, 2), (5, 2), (6, 2), (8, 0), (8, 1), (8, 2), (8, 3), (4, 3), (5, 3), (6, 3)),
)
SPLIT = ((0, 208), (208, 48))


def scatter_events(partial, other_work, late_work, ops, scratch):
    total, give, take, side_take, line_take, other_take = scratch[:6]
    core_send, core_recv, side_send, side_recv, line_send, line_recv = scratch[6:12]
    other_send, other_recv = scratch[12:]
    ctx, place, twin, across, twin_across = neighbours()
    below, above = place - 1, place + 1
    has_below, has_above = place > 0, place < SIDE - 1
    at_end = (place == 0) | (place == SIDE - 1)

    def rows_of(part):
        return pl.ds(*SPLIT[part])

    def core_copy(step, store):
        return to_axis(
            give.at[step], take.at[store], core_send.at[store], core_recv.at[store], "ctx", twin
        )

    def side_copy(step, part):
        return to_axis(
            take.at[step, rows_of(part)],
            side_take.at[step, rows_of(part)],
            side_send.at[step, part],
            side_recv.at[step, part],
            "ctx",
            across,
        )

    def line_copy(step, line, slot, target, part):
        return to_axis(
            take.at[SIDE + step, rows_of(part)],
            line_take.at[slot, rows_of(part)],
            line_send.at[line, part],
            line_recv.at[slot, part],
            "fsdp",
            target,
        )

    def other_copy(step, line, slot, target):
        return to_axis(
            take.at[step, rows_of(1)],
            other_take.at[slot],
            other_send.at[line],
            other_recv.at[slot],
            "fsdp",
            target,
        )

    def from_above(line):
        return jnp.where(line == place, SIDE, line)

    def to_below(line):
        return jnp.where(line == place - 1, SIDE, line)

    def one(number, turn):
        def by_end(field):
            ends, middle = (tuple(entry[field] for entry in table) for table in ops)
            return jnp.where(at_end, nibble(ends, number), nibble(middle, number))

        what, step = by_end(0), by_end(1)
        line = digit_of_row(FAR, place, step)

        @pl.when((what <= 1) | (what == 3) | (what == 4))
        def _():
            owner = jnp.where(
                what == 0,
                twin_across,
                jnp.where(what == 1, across, jnp.where(what == 3, twin, ctx)),
            )
            total[...] = partial(owner * SIDE + line)

        @pl.when(what == 0)
        def _():
            give[step] = total[...].astype(jnp.bfloat16)
            core_copy(step, step).start()

        @pl.when(what == 1)
        def _():
            core_copy(step, step).wait_recv()
            take[step] = (total[...] + take[step].astype(jnp.float32)).astype(jnp.bfloat16)
            side_copy(step, 0).start()

        @pl.when(what == 2)
        def _():
            rows = rows_of(1)

            @pl.when((line >= place) & has_below)
            def _():
                other_copy(step, line, line, below).wait_recv()
                take[step, rows] = (
                    take[step, rows].astype(jnp.float32) + other_take[line].astype(jnp.float32)
                ).astype(jnp.bfloat16)

            @pl.when((line <= place) & has_above)
            def _():
                other_copy(step, line, from_above(line), above).wait_recv()
                take[step, rows] = (
                    take[step, rows].astype(jnp.float32)
                    + other_take[from_above(line)].astype(jnp.float32)
                ).astype(jnp.bfloat16)

            @pl.when(line > place)
            def _():
                other_copy(step, line, line, above).start()

            @pl.when(line < place)
            def _():
                other_copy(step, line, to_below(line), below).start()

            @pl.when(line == place)
            def _():
                side_copy(step, 1).start()

        @pl.when(what == 3)
        def _():
            core_copy(step, step).wait_send()
            give[step] = total[...].astype(jnp.bfloat16)
            core_copy(step, SIDE + step).start()

        @pl.when(what == 4)
        def _():
            core_copy(step, SIDE + step).wait_recv()
            total[...] += take[SIDE + step].astype(jnp.float32)

        for part in range(2):
            rows = rows_of(part)

            @pl.when(what == 5 + part)
            def _(rows=rows, part=part):
                crossed = line == place if part == 1 else line >= 0

                @pl.when(crossed)
                def _():
                    side_copy(step, part).wait_recv()
                    total[rows] += side_take[step, rows].astype(jnp.float32)

                @pl.when((line >= place) & has_below)
                def _():
                    line_copy(step, line, line, below, part).wait_recv()
                    total[rows] += line_take[line, rows].astype(jnp.float32)

                @pl.when((line <= place) & has_above)
                def _():
                    line_copy(step, line, from_above(line), above, part).wait_recv()
                    total[rows] += line_take[from_above(line), rows].astype(jnp.float32)

                @pl.when(line > place)
                def _():
                    take[SIDE + step, rows] = total[rows].astype(jnp.bfloat16)
                    line_copy(step, line, line, above, part).start()

                @pl.when(line < place)
                def _():
                    take[SIDE + step, rows] = total[rows].astype(jnp.bfloat16)
                    line_copy(step, line, to_below(line), below, part).start()

        if other_work is not None:

            @pl.when(what == 7)
            def _():
                other_work(turn)

        if late_work is not None:

            @pl.when(what == 8)
            def _():
                late_work(step)

        return turn + jnp.where(what == 7, 1, 0)

    lax.fori_loop(0, len(ops[0]), one, jnp.int32(0))

    def finish(step, carry):
        line = digit_of_row(FAR, place, step)
        core_copy(step, SIDE + step).wait_send()
        side_copy(step, 0).wait_send()

        @pl.when(line == place)
        def _():
            side_copy(step, 1).wait_send()

        @pl.when(line != place)
        def _():
            for part in range(2):
                line_copy(step, line, line, place, part).wait_send()
            other_copy(step, line, line, place).wait_send()

        return carry

    lax.fori_loop(0, SIDE, finish, 0)


def scatter_scratch(rows):
    return [
        pltpu.VMEM((rows, D), jnp.float32),
        pltpu.VMEM((SIDE, rows, D), jnp.bfloat16),
        pltpu.VMEM((2 * SIDE, rows, D), jnp.bfloat16),
        pltpu.VMEM((SIDE, rows, D), jnp.bfloat16),
        pltpu.VMEM((SIDE + 1, rows, D), jnp.bfloat16),
        pltpu.VMEM((SIDE + 1, SPLIT[1][1], D), jnp.bfloat16),
        pltpu.SemaphoreType.DMA((2 * SIDE,)),
        pltpu.SemaphoreType.DMA((2 * SIDE,)),
        pltpu.SemaphoreType.DMA((SIDE, 2)),
        pltpu.SemaphoreType.DMA((SIDE, 2)),
        pltpu.SemaphoreType.DMA((SIDE, 2)),
        pltpu.SemaphoreType.DMA((SIDE + 1, 2)),
        pltpu.SemaphoreType.DMA((SIDE,)),
        pltpu.SemaphoreType.DMA((SIDE + 1,)),
    ]


SMALL_ROWS = 16
PAIRS = GROUP // 2


def norm_back_strip(hidden, grad, total, gain, out, part):
    values = hidden[part].astype(jnp.float32)
    centred = values - jnp.mean(values, axis=1, keepdims=True)
    spread = jnp.mean(centred * centred, axis=1, keepdims=True)
    root = lax.rsqrt(spread + EPS)
    normed = centred * root
    above = total[part]
    scaled = above * gain[...]
    down = jnp.mean(scaled, axis=1, keepdims=True)
    along = jnp.mean(scaled * normed, axis=1, keepdims=True)
    passing = grad[part]
    out[part] = passing + root * (scaled - down - normed * along)
    low = passing.astype(jnp.bfloat16).astype(jnp.float32)
    return tuple(
        jnp.sum(sums.reshape(STRIP // 8, 8, D), axis=0) for sums in (above * normed, above, low)
    )


def small_exchange(shares, land, mine, other, out, sems):
    send, recv, swap_send, swap_recv = sems
    me = lax.axis_index("ctx") * SIDE + lax.axis_index("fsdp")

    def copy(step):
        peer = lax.rem(me + step, GROUP)
        return to_peer(shares.at[peer], land.at[me], send.at[step], recv.at[me], peer)

    def swap():
        return to_axis(mine, other, swap_send, swap_recv, "seq", 1 - lax.axis_index("seq"))

    def begin(sums):
        for number, folded in enumerate(sums):
            row = jnp.sum(folded, axis=0, keepdims=True)
            for block in range(GROUP):
                shares[block, number : number + 1] = row[:, block * SHARE : (block + 1) * SHARE]

        def start(step, carry):
            copy(step).start()
            return carry

        lax.fori_loop(1, GROUP, start, 0)
        land[me] = shares[me]

    def middle():
        def arrive(step, carry):
            source = lax.rem(me + GROUP - step, GROUP)
            to_peer(shares.at[source], land.at[source], send.at[step], recv.at[source], source).wait_recv()
            copy(step).wait_send()
            return carry

        lax.fori_loop(1, GROUP, arrive, 0)
        mine[...] = jnp.sum(land[...], axis=0)
        swap().start()

    def end():
        swap().wait()
        out[...] = mine[...] + other[...]

    return begin, middle, end


def small_scratch():
    small = (SMALL_ROWS, SHARE)
    return [
        pltpu.VMEM((GROUP,) + small, jnp.float32),
        pltpu.VMEM(small, jnp.float32),
        pltpu.VMEM(small, jnp.float32),
        pltpu.SemaphoreType.DMA((GROUP,)),
        pltpu.SemaphoreType.DMA((GROUP,)),
        pltpu.SemaphoreType.DMA,
        pltpu.SemaphoreType.DMA,
    ]


def half_swaps(halves, wholes, sems, pieces=4):
    send, recv, own = sems
    seq = lax.axis_index("seq")
    half = SHARE // 2
    size = half // pieces

    def copies(which):
        return [
            to_axis(
                source.at[pl.ds(piece * size, size)],
                target.at[pl.ds(pl.multiple_of(seq * half + piece * size, size), size)],
                send.at[at, piece],
                recv.at[at, piece],
                "seq",
                1 - seq,
            )
            for at, (source, target) in enumerate(zip(halves, wholes))
            for piece in which
        ]

    def kept():
        rows = pl.ds(pl.multiple_of(seq * half, half), half)
        return [
            pltpu.make_async_copy(source, target.at[rows], own.at[at])
            for at, (source, target) in enumerate(zip(halves, wholes))
        ]

    return copies, kept


def half_sems(pieces=4):
    return [
        pltpu.SemaphoreType.DMA((2, pieces)),
        pltpu.SemaphoreType.DMA((2, pieces)),
        pltpu.SemaphoreType.DMA((2,)),
    ]


WHOLES = (
    jax.ShapeDtypeStruct((SHARE, 3 * D), jnp.bfloat16),
    jax.ShapeDtypeStruct((SHARE, FF), jnp.bfloat16),
)
HALVES = (
    jax.ShapeDtypeStruct((SHARE // 2, 3 * D), jnp.bfloat16),
    jax.ShapeDtypeStruct((SHARE // 2, FF), jnp.bfloat16),
)


def forward_scatter(hidden, bias, mixed, active, out_weight, down_weight, layer, rest=None):
    rows = hidden.shape[0]
    last = rest is not None

    def kernel(hidden, bias, mixed, active, out_weight, down_weight, *refs):
        if last:
            (below_total, below_hidden, below_grad, gain, below_shares, joint, upper, branch), refs = (
                refs[:8],
                refs[8:],
            )
            out, grad_out, small_out, joint_out, upper_out, branch_out = refs[:6]
            refs = refs[6:]
        else:
            out, refs = refs[0], refs[1:]
        hidden_part, mixed_part, active_part, out_part, down_part, load_sem = refs[:6]
        refs = refs[6:]
        loads = load_all(
            (
                (mixed, mixed_part),
                (active, active_part),
                (out_weight.at[layer], out_part),
                (down_weight.at[layer], down_part),
                (hidden, hidden_part),
            ),
            load_sem,
        )
        other_work = late_work = None
        if last:
            parts, part_sem, sums, swap_sem = refs[:4], refs[4], refs[5], refs[6]
            shares, small, swap_sems, refs = parts[3], refs[7:14], refs[14:17], refs[17:]
            below = load_all(
                tuple(zip((below_total, below_hidden, below_grad, below_shares), parts)), part_sem
            )
            small_begin, small_middle, small_end = small_exchange(
                shares, small[0], small[1], small[2], small_out, small[3:]
            )
            copies, kept = half_swaps((joint, upper), (joint_out, upper_out), swap_sems)
            greet_plane(GROUP)
            swaps = copies((0, 1, 2, 3)) + row_swap(
                branch, branch_out, swap_sem, SWAP_FIRST, range(SWAP_FIRST, SWAP_BLOCKS)
            )
            for copy in swaps + kept():
                copy.start()
            sums[...] = jnp.zeros_like(sums)
            strips = rows // STRIP

            def other_work(turn):
                @pl.when(turn == 0)
                def _():
                    wait_all(below)

                @pl.when(turn < strips)
                def _():
                    part = pl.ds(pl.multiple_of(turn * STRIP, STRIP), STRIP)
                    found = norm_back_strip(parts[1], parts[2], parts[0], gain, grad_out, part)
                    for number, folded in enumerate(found):
                        sums[number] += folded

                @pl.when(turn == strips)
                def _():
                    small_begin([sums[number] for number in range(3)])

            def late_work(step):
                pl.when(step == SIDE - 1)(small_middle)

        else:
            greet_neighbours()
        scratch = refs
        wait_all(loads[:4])

        def partial(slot):
            return dot(mixed_part[slot], out_part[...]) + dot(active_part[slot], down_part[...])

        scatter_events(
            partial, other_work, late_work, SCATTER_OPS_EARLY if last else SCATTER_OPS, scratch
        )
        loads[4].wait()
        out[...] = hidden_part[...].astype(jnp.float32) + (scratch[0][...] + bias[...])
        if last:
            small_end()
            wait_all(swaps + kept())

    out_shape = (jax.ShapeDtypeStruct((rows, D), jnp.float32),)
    out_specs = (VMEM,)
    extra_scratch = []
    if last:
        total, before, grad, _, shares, _, _, branch = rest
        out_shape += (
            (
                jax.ShapeDtypeStruct((rows, D), jnp.float32),
                jax.ShapeDtypeStruct((SMALL_ROWS, SHARE), jnp.float32),
            )
            + WHOLES
            + (jax.ShapeDtypeStruct((BACK_COLS // 2, D), branch.dtype),)
        )
        out_specs += (VMEM, VMEM, HBM, HBM, HBM)
        extra_scratch = (
            [pltpu.VMEM(array.shape, array.dtype) for array in (total, before, grad, shares)]
            + [
                pltpu.SemaphoreType.DMA((4,)),
                pltpu.VMEM((3, 8, D), jnp.float32),
                pltpu.SemaphoreType.DMA((2, SWAP_BLOCKS)),
            ]
            + small_scratch()
            + half_sems()
        )
    return pl.pallas_call(
        kernel,
        out_shape=out_shape,
        in_specs=[HBM, VMEM] + [HBM] * 4 + ([HBM] * 3 + [VMEM] + [HBM] * 4 if last else []),
        out_specs=out_specs,
        scratch_shapes=[pltpu.VMEM(array.shape, array.dtype) for array in (hidden, mixed, active)]
        + [
            pltpu.VMEM(out_weight.shape[1:], jnp.bfloat16),
            pltpu.VMEM(down_weight.shape[1:], jnp.bfloat16),
        ]
        + [pltpu.SemaphoreType.DMA((5,))]
        + extra_scratch
        + scatter_scratch(rows),
        compiler_params=pltpu.CompilerParams(
            collective_id=10 + layer, has_side_effects=True, vmem_limit_bytes=ROOM
        ),
    )(hidden, bias, mixed, active, out_weight, down_weight, *(rest or ()))


def backward_scatter(
    hidden, grad, gain, grad_joint, grad_inner, columns, every, layer, up=None, halves=(), branch=None
):
    rows = grad.shape[0]
    half = SHARE // 2
    collects = up is not None
    made = JOINT_COLS if collects else COLS
    tokens = GROUP * rows

    def kernel(*refs):
        if collects:
            (joint_in, inner_in, columns_in, every, up, *halves), refs = refs[:7], refs[7:]
            branch, out, shares, joint_half, up_half, *wholes = refs[:7]
            branch_out, refs = refs[7], refs[8:]
        else:
            (joint_in, inner_in, columns_in, every, hidden_in, grad_in, gain), refs = refs[:7], refs[7:]
            out, small_out, summed, refs = refs[0], refs[1], refs[2], refs[3:]
        grad_joint, grad_inner, columns, load_sem, strips, load = refs[:6]
        mine, other, cross_send, cross_recv = refs[6:10]
        refs = refs[10:]
        if collects:
            summed, plane_send, plane_recv, plane_own, up_send, up_recv, up_own = refs[:7]
            swap_sems, branch_sem, refs = refs[7:10], refs[10], refs[11:]
            copies, kept = half_swaps(halves, wholes, swap_sems)
            swaps = row_swap(branch, branch_out, branch_sem, 0, range(SWAP_FIRST))
        else:
            hidden, grad, shares, small, refs = refs[0], refs[1], refs[2], refs[3:10], refs[10:]
            small_begin, small_middle, small_end = small_exchange(
                shares, small[0], small[1], small[2], small_out, small[3:]
            )
        scratch = refs
        total = scratch[0]
        ctx, place, seq = lax.axis_index("ctx"), lax.axis_index("fsdp"), lax.axis_index("seq")
        me = ctx * SIDE + place
        part_rows = pl.ds(pl.multiple_of(seq * half, half), half)
        other_rows = pl.ds(pl.multiple_of((1 - seq) * half, half), half)

        def pair_of(turn):
            return lax.rem(me // 2 + 1 + turn, PAIRS)

        def load_strip(turn):
            start = pl.multiple_of(pair_of(turn) * 2 * SHARE, 2 * SHARE)
            buffer = lax.rem(turn, 2)
            return pltpu.make_async_copy(
                every.at[:, :, pl.ds(start, 2 * SHARE)], strips.at[buffer], load.at[buffer]
            )

        pairs = [(joint_in, grad_joint), (inner_in, grad_inner), (columns_in, columns)]
        if not collects:
            pairs += [(hidden_in, hidden), (grad_in, grad)]
        loads = load_all(pairs, load_sem)
        load_strip(jnp.int32(0)).start()
        shares[...] = jnp.zeros_like(shares)
        greet_plane(GROUP)

        def partial(slot):
            return dot(grad_joint[slot], columns[:, :JOINT_COLS], 1, 1) + dot(
                grad_inner[slot], columns[:, JOINT_COLS:], 1, 1
            )

        def product(turn):
            pair = pair_of(turn)
            load_strip(turn).wait()

            @pl.when(turn + 1 < PAIRS)
            def _():
                load_strip(turn + 1).start()

            strip = strips[lax.rem(turn, 2)].reshape(tokens, 2 * SHARE)
            result = dot(strip, grad_joint[...].reshape(tokens, JOINT_COLS), 0, 0).astype(
                jnp.bfloat16
            )
            for which in range(2):
                mine[2 * pair + which, :, :JOINT_COLS] = result[which * SHARE : (which + 1) * SHARE]
            if not collects:
                result = dot(strip, grad_inner[...].reshape(tokens, FEED_COLS), 0, 0).astype(
                    jnp.bfloat16
                )
                for which in range(2):
                    mine[2 * pair + which, :, JOINT_COLS:] = result[
                        which * SHARE : (which + 1) * SHARE
                    ]

        def cross_copy(block):
            return to_axis(
                mine.at[block, other_rows],
                other.at[block],
                cross_send.at[block],
                cross_recv.at[block],
                "seq",
                1 - seq,
            )

        def joint_places():
            return [
                (at, joint_half.at[:, pl.ds(start, width)], pl.ds(at * HEAD_COLS, HEAD_COLS))
                for at, (_, start, _, width) in enumerate(column_places(me)[:3])
            ]

        def plane_copies(block):
            return [
                to_peer(
                    summed.at[block, :, piece],
                    target,
                    plane_send.at[block, at],
                    plane_recv.at[me, at],
                    block,
                )
                for at, target, piece in joint_places()
            ]

        def own_copies():
            return [
                pltpu.make_async_copy(summed.at[me, :, piece], target, plane_own.at[at])
                for at, target, piece in joint_places()
            ]

        def up_place(block):
            return up_half.at[:, pl.ds(pl.multiple_of(block * FEED_COLS, FEED_COLS), FEED_COLS)]

        def up_copy(step):
            peer = lax.rem(me + step, GROUP)
            return to_peer(up.at[peer], up_place(me), up_send.at[step], up_recv.at[me], peer)

        def own_up():
            return pltpu.make_async_copy(up.at[me], up_place(me), up_own)

        def add(turn):
            for which in range(2):
                block = 2 * pair_of(turn) + which
                cross_copy(block).wait_recv()
                summed[block] = (
                    mine[block, part_rows].astype(jnp.float32) + other[block].astype(jnp.float32)
                ).astype(jnp.bfloat16)
                if collects:

                    @pl.when(block != me)
                    def _(block=block):
                        for copy in plane_copies(block):
                            copy.start()

                    @pl.when(block == me)
                    def _(block=block):
                        for copy in own_copies():
                            copy.start()

        def bias_sums():
            ones = jnp.ones((16, tokens), jnp.bfloat16)
            joint_bias = dot(ones, grad_joint[...].reshape(tokens, JOINT_COLS))[:1]
            upper_bias = dot(ones, grad_inner[...].reshape(tokens, FEED_COLS))[:1]
            for part in range(3):
                at = part * GROUP + me
                shares[at // 3, pl.ds(3 + lax.rem(at, 3), 1)] = joint_bias[
                    :, part * HEAD_COLS : (part + 1) * HEAD_COLS
                ]
            for part in range(FEED_COLS // SHARE):
                shares[me, 6 + part : 7 + part] = upper_bias[:, part * SHARE : (part + 1) * SHARE]

        def other_work(turn):
            pl.when(turn == 1)(bias_sums)

            @pl.when(lax.rem(turn, 2) == 0)
            def _():
                product(turn // 2)
                for which in range(2):
                    cross_copy(2 * pair_of(turn // 2) + which).start()

            @pl.when((lax.rem(turn, 2) == 1) & (turn > 4))
            def _():
                add((turn - 5) // 2)

            if collects:

                @pl.when(turn == GROUP - 1)
                def _():
                    for copy in copies((2, 3)) + swaps:
                        copy.start()

        def last_adds(turn, carry):
            add(turn)
            return carry

        def late_work(step):
            @pl.when(step == 0)
            def _():
                lax.fori_loop(PAIRS - 2, PAIRS, last_adds, 0)

        def send_up(step, carry):
            up_copy(step).start()
            return carry

        wait_all(loads[:3])
        if collects:
            own_up().start()
            lax.fori_loop(1, GROUP, send_up, 0)
            for copy in copies((0, 1)) + kept():
                copy.start()
        scatter_events(
            partial,
            other_work,
            late_work if collects else None,
            SCATTER_OPS_EARLY if collects else SCATTER_OPS_WORK,
            scratch,
        )

        def end_cross(block, carry):
            cross_copy(block).wait_send()
            return carry

        def end(step, carry):
            source = lax.rem(me + GROUP - step, GROUP)
            target = up_place(source)
            to_peer(target, target, up_send.at[step], up_recv.at[source], source).wait_recv()
            up_copy(step).wait_send()
            for at, (_, start, _, width) in enumerate(column_places(source)[:3]):
                target = joint_half.at[:, pl.ds(start, width)]
                to_peer(
                    target, target, plane_send.at[source, at], plane_recv.at[source, at], source
                ).wait_recv()
            for copy in plane_copies(lax.rem(me + step, GROUP)):
                copy.wait_send()
            return carry

        if collects:
            out[...] = total[...]
            lax.fori_loop(1, GROUP, end, 0)
            wait_all(own_copies() + [own_up()] + copies((0, 1, 2, 3)) + kept() + swaps)
        else:
            lax.fori_loop(PAIRS - 2, PAIRS, last_adds, 0)
            wait_all(loads[3:])

            def norm_back(part, sums):
                found = norm_back_strip(hidden, grad, total, gain, out, part)
                return tuple(before + more for before, more in zip(sums, found))

            zeros = jnp.zeros((8, D), jnp.float32)
            small_begin(each_strip(rows, norm_back, (zeros, zeros, zeros)))
            small_middle()
            small_end()
        lax.fori_loop(0, GROUP, end_cross, 0)

    def part(width, height=half):
        return pltpu.VMEM((GROUP, height, width), jnp.bfloat16)

    def same(*arrays):
        return [pltpu.VMEM(array.shape, array.dtype) for array in arrays]

    small = (SMALL_ROWS, SHARE)
    shares = (GROUP,) + small
    sixteen = pltpu.SemaphoreType.DMA((GROUP,))
    row_shape = jax.ShapeDtypeStruct((rows, D), jnp.float32)
    common = (
        same(grad_joint, grad_inner, columns)
        + [
            pltpu.SemaphoreType.DMA((5,)),
            pltpu.VMEM((2, GROUP, rows, 2 * SHARE), jnp.bfloat16),
            pltpu.SemaphoreType.DMA((2,)),
            part(made, SHARE),
            part(made),
            sixteen,
            sixteen,
        ]
    )
    if collects:
        out_shape = (row_shape, jax.ShapeDtypeStruct(shares, jnp.float32)) + HALVES + WHOLES
        out_shape += (jax.ShapeDtypeStruct((BACK_COLS // 2, D), branch.dtype),)
        out_specs = (VMEM, VMEM) + (HBM,) * 5
        operands = (grad_joint, grad_inner, columns, every, up, *halves, branch)
        in_specs = [HBM] * 8
        special = [
            part(JOINT_COLS),
            pltpu.SemaphoreType.DMA((GROUP, 3)),
            pltpu.SemaphoreType.DMA((GROUP, 3)),
            pltpu.SemaphoreType.DMA((3,)),
            sixteen,
            sixteen,
            pltpu.SemaphoreType.DMA,
        ] + half_sems() + [pltpu.SemaphoreType.DMA((2, SWAP_BLOCKS))]
    else:
        out_shape = (
            row_shape,
            jax.ShapeDtypeStruct(small, jnp.float32),
            jax.ShapeDtypeStruct((GROUP, half, COLS), jnp.bfloat16),
        )
        out_specs = (VMEM,) * 3
        operands = (grad_joint, grad_inner, columns, every, hidden, grad, gain)
        in_specs = [HBM] * 6 + [VMEM]
        special = same(hidden, grad) + [pltpu.VMEM(shares, jnp.float32)] + small_scratch()
    return pl.pallas_call(
        kernel,
        out_shape=out_shape,
        in_specs=in_specs,
        out_specs=out_specs,
        scratch_shapes=common + special + scatter_scratch(rows),
        compiler_params=pltpu.CompilerParams(
            collective_id=20 + layer, has_side_effects=True, vmem_limit_bytes=ROOM
        ),
    )(*operands)


def mask_rest(rows, begin, spot, first, lead):
    if lead:
        old = jnp.where(spot[:lead] >= begin, rows[:lead], NEG)
    key_at = lax.broadcasted_iota(jnp.int32, (first, first), 0) + lead
    query_at = lax.broadcasted_iota(jnp.int32, (first, first), 1) + lead
    near = spot[lead:]
    seen = ((near >= begin) & (near <= query_at)) | (key_at == query_at)
    new = jnp.where(seen, rows[lead:], NEG)
    return jnp.concatenate([old, new], axis=0) if lead else new


def head_lanes(head, rows):
    lane = lax.broadcasted_iota(jnp.int32, (rows, HEAD_COLS), 1)
    return (lane >= head * HEAD_DIM) & (lane < (head + 1) * HEAD_DIM)


def column_exchange(sources, land, sems, layer):
    plane_send, plane_recv, own_sem = sems
    ctx, place, seq = lax.axis_index("ctx"), lax.axis_index("fsdp"), lax.axis_index("seq")
    me = ctx * SIDE + place
    half = SHARE // 2
    part_rows = pl.ds(pl.multiple_of(seq * half, half), half)

    def piece(peer, number):
        which, start, at, width = column_places(peer)[number]
        return (
            sources[which].at[layer, part_rows, pl.ds(start, width)],
            land.at[me, :, pl.ds(at, width)],
        )

    def send_piece(step, number):
        peer = lax.rem(me + step, GROUP)
        source, target = piece(peer, number)
        return to_peer(source, target, plane_send.at[step, number], plane_recv.at[me, number], peer)

    def own_piece(number):
        return pltpu.make_async_copy(*piece(me, number), own_sem.at[number])

    def begin():
        greet_plane(GROUP, False)

        def send(step, carry):
            for number in range(PLACES):
                send_piece(step, number).start()
            return carry

        lax.fori_loop(1, GROUP, send, 0)
        for number in range(PLACES):
            own_piece(number).start()

    def end():
        def arrive(step, carry):
            source = lax.rem(me + GROUP - step, GROUP)
            for number in range(PLACES):
                _, _, at, width = column_places(0)[number]
                target = land.at[source, :, pl.ds(at, width)]
                to_peer(
                    target, target, plane_send.at[0, number], plane_recv.at[source, number], source
                ).wait_recv()
                send_piece(step, number).wait_send()
            return carry

        lax.fori_loop(1, GROUP, arrive, 0)
        for number in range(PLACES):
            own_piece(number).wait()

    return begin, end


def up_products(every, feed, out, scratch):
    feed_part, strips, mine, other, feed_sem, load, cross_send, cross_recv = scratch
    rows = feed.shape[1]
    tokens = GROUP * rows
    half = SHARE // 2
    seq = lax.axis_index("seq")
    me = lax.axis_index("ctx") * SIDE + lax.axis_index("fsdp")
    part_rows = pl.ds(pl.multiple_of(seq * half, half), half)
    other_rows = pl.ds(pl.multiple_of((1 - seq) * half, half), half)

    def pair_of(turn):
        return lax.rem(me // 2 + 1 + turn, PAIRS)

    def load_strip(turn):
        start = pl.multiple_of(pair_of(turn) * 2 * SHARE, 2 * SHARE)
        buffer = lax.rem(turn, 2)
        return pltpu.make_async_copy(
            every.at[:, :, pl.ds(start, 2 * SHARE)], strips.at[buffer], load.at[buffer]
        )

    def cross_copy(block):
        return to_axis(
            mine.at[block, other_rows],
            other.at[block],
            cross_send.at[block],
            cross_recv.at[block],
            "seq",
            1 - seq,
        )

    def feed_copy():
        return pltpu.make_async_copy(feed, feed_part, feed_sem)

    def begin():
        feed_copy().start()
        load_strip(jnp.int32(0)).start()

    def product(turn, carry):
        pair = pair_of(turn)
        load_strip(turn).wait()

        @pl.when(turn == 0)
        def _():
            feed_copy().wait()

        @pl.when(turn + 1 < PAIRS)
        def _():
            load_strip(turn + 1).start()

        strip = strips[lax.rem(turn, 2)].reshape(tokens, 2 * SHARE)
        made = dot(strip, feed_part[...].reshape(tokens, FEED_COLS), 0, 0).astype(jnp.bfloat16)
        for which in range(2):
            mine[2 * pair + which] = made[which * SHARE : (which + 1) * SHARE]
            cross_copy(2 * pair + which).start()
        return carry

    def add(turn, carry):
        for which in range(2):
            block = 2 * pair_of(turn) + which
            cross_copy(block).wait()
            out[block] = (
                mine[block, part_rows].astype(jnp.float32) + other[block].astype(jnp.float32)
            ).astype(jnp.bfloat16)
        return carry

    each = PAIRS // SIDE

    def make(step):
        lax.fori_loop(each * step, each * step + each, product, 0)
        lax.fori_loop(each * jnp.maximum(step - 1, 0), each * step, add, 0)

    def end():
        lax.fori_loop(PAIRS - each, PAIRS, add, 0)

    return begin, make, end


def row_exchange(summed, outputs, sems):
    plane_send, plane_recv, own_sem = sems
    me = lax.axis_index("ctx") * SIDE + lax.axis_index("fsdp")

    def piece(peer, number):
        which, start, at, width = column_places(me)[number]
        return summed.at[peer, :, pl.ds(at, width)], outputs[which].at[:, pl.ds(start, width)]

    def send_piece(step, number):
        peer = lax.rem(me + step, GROUP)
        source, target = piece(peer, number)
        return to_peer(source, target, plane_send.at[step, number], plane_recv.at[me, number], peer)

    def own_piece(number):
        return pltpu.make_async_copy(*piece(me, number), own_sem.at[number])

    def begin():
        greet_plane(GROUP)

        def send(step, carry):
            for number in range(PLACES):
                send_piece(step, number).start()
            return carry

        lax.fori_loop(1, GROUP, send, 0)
        for number in range(PLACES):
            own_piece(number).start()

    def end():
        def arrive(step, carry):
            source = lax.rem(me + GROUP - step, GROUP)
            for number in range(PLACES):
                which, start, _, width = column_places(source)[number]
                target = outputs[which].at[:, pl.ds(start, width)]
                to_peer(
                    target, target, plane_send.at[0, number], plane_recv.at[source, number], source
                ).wait_recv()
                send_piece(step, number).wait_send()
            return carry

        lax.fori_loop(1, GROUP, arrive, 0)
        for number in range(PLACES):
            own_piece(number).wait()

    return begin, end


EXCHANGE_SEMS = [
    pltpu.SemaphoreType.DMA((GROUP, PLACES)),
    pltpu.SemaphoreType.DMA((GROUP, PLACES)),
    pltpu.SemaphoreType.DMA((PLACES,)),
]


def attend_plane(query, key, value, begin, spot, weights=None, layer=0):
    rows = query.shape[1]
    length = SIDE * rows
    scale = 1.0 / math.sqrt(HEAD_DIM)

    def kernel(query, key, value, begin, spot, *refs):
        if weights is None:
            mixed, turned, stats = refs
        else:
            mixed, turned, stats, land = refs[2:6]
            begin_exchange, end_exchange = column_exchange(refs[:2], land, refs[6:], layer)
            pl.when(pl.program_id(0) == 0)(begin_exchange)
        keys = key[:, 0].reshape(length, HEAD_COLS)
        values = value[:, 0].reshape(length, HEAD_COLS)
        for chunk in range(SIDE):
            lead = chunk * rows
            seen = lead + rows
            scaled = query[chunk, 0] * jnp.bfloat16(scale)
            start = begin[0, :, lead:seen]
            outs = []
            for head in range(OWN):
                own = jnp.where(head_lanes(head, rows), scaled, jnp.bfloat16(0))
                scores = mask_rest(
                    dot(keys[:seen], own, 1, 1), start, spot[0, :seen], rows, lead
                )
                peak = jnp.max(scores, axis=0, keepdims=True)
                probs = jnp.exp(scores - peak)
                norm = jnp.sum(probs, axis=0, keepdims=True)
                stats[0, head : head + 1, lead:seen] = peak
                stats[0, OWN + head : OWN + head + 1, lead:seen] = norm
                whole = dot(values[:seen], probs.astype(jnp.bfloat16), 0, 0)
                outs.append(whole[head * HEAD_DIM : (head + 1) * HEAD_DIM] / norm)
            joined = jnp.concatenate(outs, axis=0)
            turned[chunk, 0] = joined
            mixed[chunk, 0] = joined.T.astype(jnp.bfloat16)
        if weights is not None:
            pl.when(pl.program_id(0) == SIDE - 1)(end_exchange)

    def spec(height, width):
        return pl.BlockSpec((SIDE, 1, height, width), lambda step: (0, step, 0, 0))

    def shape(height, width, dtype):
        return jax.ShapeDtypeStruct((SIDE, SIDE, height, width), dtype)

    extra = weights is not None
    land = (jax.ShapeDtypeStruct((GROUP, SHARE // 2, COLS), jnp.bfloat16),) if extra else ()
    mixed, turned, stats, *land = pl.pallas_call(
        kernel,
        grid=(SIDE,),
        out_shape=(
            shape(rows, HEAD_COLS, jnp.bfloat16),
            shape(HEAD_COLS, rows, jnp.float32),
            jax.ShapeDtypeStruct((SIDE, 2 * OWN, length), jnp.float32),
        )
        + land,
        in_specs=[spec(rows, HEAD_COLS)] * 3
        + [
            pl.BlockSpec((1, 1, length), lambda step: (step, 0, 0)),
            pl.BlockSpec((1, length, 1), lambda step: (step, 0, 0)),
        ]
        + [HBM] * (2 if extra else 0),
        out_specs=(
            spec(rows, HEAD_COLS),
            spec(HEAD_COLS, rows),
            pl.BlockSpec((1, 2 * OWN, length), lambda step: (step, 0, 0)),
        )
        + ((HBM,) if extra else ()),
        scratch_shapes=EXCHANGE_SEMS if extra else [],
        compiler_params=pltpu.CompilerParams(
            collective_id=40, has_side_effects=True, vmem_limit_bytes=ROOM
        )
        if extra
        else pltpu.CompilerParams(vmem_limit_bytes=ROOM),
    )(
        *(array.reshape(SIDE, SIDE, rows, HEAD_COLS) for array in (query, key, value)),
        begin,
        spot,
        *(weights or ()),
    )
    return mixed.reshape(GROUP, rows, HEAD_COLS), turned, stats, *land


def attend_plane_back(
    query, key, value, begin, spot, turned, stats, grad, tables, summed=None, every=None, feed=None
):
    rows = query.shape[1]
    length = SIDE * rows
    scale = 1.0 / math.sqrt(HEAD_DIM)

    extra = summed is not None

    def kernel(query, key, value, grad, cosine, sine, begin, spot, turned, stats, *refs):
        if extra:
            summed, every, feed, out = refs[:4]
            up_out, grad_k, grad_v = refs[6], refs[7], refs[8]
            begin_exchange, end_exchange = row_exchange(summed, refs[4:6], refs[9:12])
            begin_up, make_up, end_up = up_products(every, feed, up_out, refs[12:])

            @pl.when(pl.program_id(0) == 0)
            def _():
                begin_up()
                begin_exchange()

        else:
            out, grad_k, grad_v = refs
        keys = key[:, 0].reshape(length, HEAD_COLS)
        values = value[:, 0].reshape(length, HEAD_COLS)
        for chunk in range(SIDE):
            lead = chunk * rows
            seen = lead + rows
            if chunk == 0:
                grad_k[...] = jnp.zeros_like(grad_k)
                grad_v[...] = jnp.zeros_like(grad_v)
            scaled = query[chunk, 0] * jnp.bfloat16(scale)
            start = begin[0, :, lead:seen]
            flipped = grad[chunk, 0].T
            grad_q, drifts, numers = [], [], []
            for head in range(OWN):
                part = slice(head * HEAD_DIM, (head + 1) * HEAD_DIM)
                norm = stats[0, OWN + head : OWN + head + 1, lead:seen]
                drifts.append(
                    jnp.sum(flipped[part] * turned[chunk, 0, part], axis=0, keepdims=True) / norm
                )
                numers.append(flipped[part] / norm)
            numer = jnp.concatenate(numers, axis=0).T.astype(jnp.bfloat16)
            for head in range(OWN):
                part = slice(head * HEAD_DIM, (head + 1) * HEAD_DIM)
                lanes = head_lanes(head, rows)
                own = jnp.where(lanes, scaled, jnp.bfloat16(0))
                own_numer = jnp.where(lanes, numer, jnp.bfloat16(0))
                scores = mask_rest(
                    dot(keys[:seen], own, 1, 1), start, spot[0, :seen], rows, lead
                )
                probs = jnp.exp(scores - stats[0, head : head + 1, lead:seen])
                grad_probs = dot(values[:seen], own_numer, 1, 1)
                grad_scores = (probs * (grad_probs - drifts[head])).astype(jnp.bfloat16)
                grad_q.append(dot(keys[:seen], grad_scores, 0, 0)[part])
                grad_k[:seen] += dot(grad_scores, own)
                grad_v[:seen] += dot(probs.astype(jnp.bfloat16), own_numer)
            turns = (cosine[chunk, 0], sine[chunk, 0])
            whole = jnp.concatenate(grad_q, axis=0).T * scale
            out[chunk, 0, :, :HEAD_COLS] = spin(whole, *turns, -1.0).astype(jnp.bfloat16)
        for chunk in range(SIDE):
            place = slice(chunk * rows, (chunk + 1) * rows)
            turns = (cosine[chunk, 0], sine[chunk, 0])
            out[chunk, 0, :, HEAD_COLS : 2 * HEAD_COLS] = spin(grad_k[place], *turns, -1.0).astype(
                jnp.bfloat16
            )
            out[chunk, 0, :, 2 * HEAD_COLS :] = grad_v[place].astype(jnp.bfloat16)
        if extra:
            make_up(pl.program_id(0))

            @pl.when(pl.program_id(0) == SIDE - 1)
            def _():
                end_up()
                end_exchange()


    def spec(height, width):
        return pl.BlockSpec((SIDE, 1, height, width), lambda step: (0, step, 0, 0))

    half = SHARE // 2
    halves = (
        jax.ShapeDtypeStruct((half, 3 * D), jnp.bfloat16),
        jax.ShapeDtypeStruct((half, FF), jnp.bfloat16),
        jax.ShapeDtypeStruct((GROUP, half, FEED_COLS), jnp.bfloat16),
    )
    out, *halves = pl.pallas_call(
        kernel,
        grid=(SIDE,),
        out_shape=(jax.ShapeDtypeStruct((SIDE, SIDE, rows, JOINT_COLS), jnp.bfloat16),)
        + (halves if extra else ()),
        in_specs=[spec(rows, HEAD_COLS)] * 6
        + [
            pl.BlockSpec((1, 1, length), lambda step: (step, 0, 0)),
            pl.BlockSpec((1, length, 1), lambda step: (step, 0, 0)),
            spec(HEAD_COLS, rows),
            pl.BlockSpec((1, 2 * OWN, length), lambda step: (step, 0, 0)),
        ]
        + [HBM] * (3 if extra else 0),
        out_specs=(spec(rows, JOINT_COLS),)
        + (
            (HBM, HBM, pl.BlockSpec((GROUP, half, FEED_COLS), lambda step: (0, 0, 0)))
            if extra
            else ()
        ),
        scratch_shapes=[pltpu.VMEM((length, HEAD_COLS), jnp.float32)] * 2
        + (
            EXCHANGE_SEMS
            + [
                pltpu.VMEM((GROUP, rows, FEED_COLS), jnp.bfloat16),
                pltpu.VMEM((2, GROUP, rows, 2 * SHARE), jnp.bfloat16),
                pltpu.VMEM((GROUP, SHARE, FEED_COLS), jnp.bfloat16),
                pltpu.VMEM((GROUP, half, FEED_COLS), jnp.bfloat16),
                pltpu.SemaphoreType.DMA,
                pltpu.SemaphoreType.DMA((2,)),
                pltpu.SemaphoreType.DMA((GROUP,)),
                pltpu.SemaphoreType.DMA((GROUP,)),
            ]
            if extra
            else []
        ),
        compiler_params=pltpu.CompilerParams(
            collective_id=41, has_side_effects=True, vmem_limit_bytes=ROOM
        )
        if extra
        else pltpu.CompilerParams(vmem_limit_bytes=ROOM),
    )(
        *(
            array.reshape(SIDE, SIDE, rows, HEAD_COLS)
            for array in (query, key, value, grad) + tuple(tables)
        ),
        begin,
        spot,
        turned,
        stats,
        *((summed, every, feed) if extra else ()),
    )
    return out.reshape(GROUP, rows, JOINT_COLS), *halves


def on_device_split(
    tokens,
    doc_lengths,
    keep_mask,
    ln_gain,
    ln_bias,
    qkv_weight,
    qkv_bias,
    out_weight,
    out_bias,
    up_weight,
    up_bias,
    down_weight,
    down_bias,
    cotangent,
):
    rows = tokens.shape[1]
    length = SIDE * rows
    me = lax.axis_index("ctx") * SIDE + lax.axis_index("fsdp")

    index = lax.axis_index("ctx") * rows + jnp.arange(rows, dtype=jnp.int32)
    ends = jnp.cumsum(doc_lengths[0])
    begin = jnp.max(jnp.where(index[:, None] >= ends[None, :], ends[None, :], 0), axis=1)
    fields = [ln_gain, ln_bias, qkv_bias, out_bias, down_bias]
    packed = jnp.concatenate(
        [field[layer].astype(jnp.float32) for layer in range(LAYERS) for field in fields]
        + [begin.astype(jnp.float32), keep_mask[0].astype(jnp.float32)]
    )
    packed = jnp.pad(packed, (0, -packed.shape[0] % (8 * SHARE))).reshape(-1, SHARE)
    lane = np.arange(HEAD_COLS) % HEAD_DIM
    inverse = 1.0 / 10000.0 ** (np.arange(0, ROT, 2, dtype=np.float32) / np.float32(ROT))
    inverse = np.where(lane < ROT, inverse[lane % (ROT // 2)], 0.0).astype(np.float32)
    up_bias = up_bias.astype(jnp.float32)

    seq = lax.axis_index("seq")
    half = SHARE // 2
    swap = [(0, 1), (1, 0)]

    def swapped(values):
        return lax.ppermute(values, "seq", swap)

    hidden = tokens[0]
    saved, gains, joint_grads, upper_grads, small_grads = [], [], [], [], []
    for layer in range(LAYERS):
        if layer == 0:
            *out, small, cosine, sine = first_gather(
                hidden, packed, up_bias[:1], jnp.asarray(inverse)[None, :], qkv_weight, up_weight
            )
            tables = (cosine, sine)
            length_rows = rows // SHARE

            def by_sequence(row):
                values = small[:, row : row + length_rows].reshape(SIDE, SIDE, rows)
                return values.transpose(1, 0, 2).reshape(SIDE, length).astype(jnp.int32)

            begin = by_sequence(BEGIN_ROW)[:, None, :]
            keep = by_sequence(BEGIN_ROW + length_rows)
            spot = jnp.where(keep > 0, jnp.arange(length, dtype=jnp.int32)[None, :], -1)[:, :, None]
        else:
            out = forward_gather(
                hidden,
                gain_row,
                row_of(layer, SHIFT_ROW),
                jnp.concatenate([own_bias, up_bias[layer : layer + 1]], axis=1),
                tables,
                halves,
                layer,
            )

        def row_of(layer, row):
            return small[:, layer * LAYER_ROWS + row].reshape(1, D)

        every, columns, query, key, value, inner, active = out
        gains.append(row_of(layer, GAIN_ROW))
        if layer + 1 < LAYERS:
            mixed, turned, stats, arrived = attend_plane(
                query, key, value, begin, spot, (qkv_weight, up_weight), layer + 1
            )
            halves = (arrived, swapped(arrived))
            gain_row = row_of(layer + 1, GAIN_ROW)
            at = (layer + 1) * LAYER_ROWS + JOINT_BIAS_ROW
            own_bias = lax.dynamic_slice_in_dim(
                small[:, at : at + 3].reshape(3, GROUP, HEAD_COLS), me, 1, axis=1
            ).reshape(1, JOINT_COLS)
        else:
            mixed, turned, stats = attend_plane(query, key, value, begin, spot)
        saved.append(
            (hidden, every, columns, query, key, value, inner, active, mixed, turned, stats)
        )
        branches = (
            hidden,
            row_of(layer, OUT_BIAS_ROW) + row_of(layer, DOWN_BIAS_ROW),
            mixed,
            active,
            out_weight,
            down_weight,
            layer,
        )
        if layer + 1 < LAYERS:
            hidden = forward_scatter(*branches)[0]

    grad_hidden = cotangent[0].astype(jnp.float32) * keep_mask[0].astype(jnp.float32)[:, None]
    summed = branch = None
    own_branches, other_branches = [], []
    for layer in reversed(range(LAYERS)):
        before, every, columns, query, key, value, inner, active, mixed, turned, stats = saved[layer]
        grad_mixed, grad_inner, branch, *other = backward_gather(
            grad_hidden.astype(jnp.bfloat16),
            out_weight,
            down_weight,
            inner,
            mixed,
            active,
            layer,
            () if layer + 1 == LAYERS else (branch,),
        )
        own_branches.insert(0, branch)
        other_branches = list(other) + other_branches
        grad_joint, *rest = attend_plane_back(
            query,
            key,
            value,
            begin,
            spot,
            turned,
            stats,
            grad_mixed,
            tables,
            summed,
            every,
            grad_inner,
        )
        grad_above = grad_hidden
        out = backward_scatter(
            before,
            grad_hidden,
            gains[layer],
            grad_joint,
            grad_inner,
            columns.reshape(D, COLS),
            every,
            layer,
            *((rest[2], rest[:2], branch) if rest else ()),
        )
        if layer > 0:
            grad_hidden, small, summed = out
            small_grads.insert(0, small)
            continue
        total, shares, joint, upper, *wholes, first = out
        joint_grads.append(wholes[0])
        upper_grads.append(wholes[1])
        hidden, grad_hidden, small, joint, upper, other = forward_scatter(
            *branches, (total, before, grad_above, gains[layer], shares, joint, upper, branch)
        )
        small_grads.insert(0, small)
        joint_grads.insert(0, joint)
        upper_grads.insert(0, upper)
        other_branches.insert(0, jnp.concatenate([first, other], axis=0))
    here, there = jnp.stack(own_branches), jnp.stack(other_branches)
    result = hidden.astype(jnp.bfloat16)[None]

    def branch_grad(part):
        return here[:, part].astype(jnp.float32) + there[:, part].astype(jnp.float32)

    small = jnp.stack(small_grads)
    return (
        result,
        grad_hidden[None],
        small[:, 0],
        small[:, 1],
        jnp.stack(joint_grads).astype(jnp.float32),
        small[:, 3:6].reshape(LAYERS, JOINT_COLS),
        branch_grad(slice(0, HEAD_COLS)),
        small[:, 2],
        jnp.stack(upper_grads).astype(jnp.float32),
        small[:, 6:10].reshape(LAYERS, FEED_COLS),
        branch_grad(slice(HEAD_COLS, None)),
        small[:, 2],
    )


def solution(mesh):
    small = mesh.shape["ctx"] == SIDE and mesh.shape["fsdp"] == SIDE and mesh.shape["seq"] == 2
    on_device = on_device_split if small else on_device_gathered
    return jax.shard_map(
        on_device,
        mesh=mesh,
        in_specs=(
            P(("seq", "fsdp"), "ctx", None),
            P(("seq", "fsdp"), None),
            P(("seq", "fsdp"), "ctx"),
            P(None, ("ctx", "fsdp")),
            P(None, ("ctx", "fsdp")),
            P(None, ("ctx", "fsdp"), None),
            P(None, ("ctx", "fsdp")),
            P(None, ("ctx", "fsdp"), None),
            P(None, ("ctx", "fsdp")),
            P(None, ("ctx", "fsdp"), None),
            P(None, ("ctx", "fsdp")),
            P(None, ("ctx", "fsdp"), None),
            P(None, ("ctx", "fsdp")),
            P(("seq", "fsdp"), "ctx", None),
        ),
        out_specs=(
            P(("seq", "fsdp"), "ctx", None),
            P(("seq", "fsdp"), "ctx", None),
            P(None, ("ctx", "fsdp")),
            P(None, ("ctx", "fsdp")),
            P(None, ("ctx", "fsdp"), None),
            P(None, ("ctx", "fsdp")),
            P(None, ("ctx", "fsdp"), None),
            P(None, ("ctx", "fsdp")),
            P(None, ("ctx", "fsdp"), None),
            P(None, ("ctx", "fsdp")),
            P(None, ("ctx", "fsdp"), None),
            P(None, ("ctx", "fsdp")),
        ),
        check_vma=False,
    )
```
